32 devices in a mesh: dp: 8 (over z, x), mp: 4 (over y, core).
Axes of the slice: x: 2, y: 2, z: 4, core: 2. Of those that a mesh axis runs over, the one named last changes fastest.
Arguments:
- tokens: bfloat16 [32, 197, 768], P(('dp', 'mp')), may hold values from -6 to 6
- keep_mask: int32 [32, 197], P(('dp', 'mp')), may hold values from 0 to 1, as said below
- cotangent: bfloat16 [32, 197, 768], P(('dp', 'mp')), may hold values from -6 to 6
- w_attn: float32 [16, 384, 384], P('mp', 'dp')
- w_fc1: float32 [16, 384, 384], P('mp', 'dp'), may hold values from -0.21875 to 0.21875
- w_fc2: float32 [16, 384, 384], P('mp', 'dp'), may hold values from -0.109375 to 0.109375
- vectors: float32 [13, 768], replicated, as said below
- left_attn: float32 [16, 384, 384], P('mp', 'dp'), as said below
- right_attn: float32 [16, 384, 384], P('mp', 'dp'), as said below
- root_left_attn: float32 [16, 384, 384], P('mp', 'dp'), as said below
- root_right_attn: float32 [16, 384, 384], P('mp', 'dp'), as said below
- left_fc1: float32 [16, 384, 384], P('mp', 'dp'), as said below
- right_fc1: float32 [16, 384, 384], P('mp', 'dp'), as said below
- root_left_fc1: float32 [16, 384, 384], P('mp', 'dp'), as said below
- root_right_fc1: float32 [16, 384, 384], P('mp', 'dp'), as said below
- left_fc2: float32 [16, 384, 384], P('mp', 'dp'), as said below
- right_fc2: float32 [16, 384, 384], P('mp', 'dp'), as said below
- root_left_fc2: float32 [16, 384, 384], P('mp', 'dp'), as said below
- root_right_fc2: float32 [16, 384, 384], P('mp', 'dp'), as said below
Outputs:
- block_out: bfloat16 [32, 197, 768], P(('dp', 'mp'))
- input_grad: float32 [32, 197, 768], P(('dp', 'mp'))
- grad_attn: float32 [16, 384, 384], P('mp', 'dp')
- grad_fc1: float32 [16, 384, 384], P('mp', 'dp')
- grad_fc2: float32 [16, 384, 384], P('mp', 'dp')
- new_left_attn: float32 [16, 384, 384], P('mp', 'dp')
- new_right_attn: float32 [16, 384, 384], P('mp', 'dp')
- new_left_fc1: float32 [16, 384, 384], P('mp', 'dp')
- new_right_fc1: float32 [16, 384, 384], P('mp', 'dp')
- new_left_fc2: float32 [16, 384, 384], P('mp', 'dp')
- new_right_fc2: float32 [16, 384, 384], P('mp', 'dp')
- new_attn: float32 [16, 384, 384], P('mp', 'dp')
- new_fc1: float32 [16, 384, 384], P('mp', 'dp')
- new_fc2: float32 [16, 384, 384], P('mp', 'dp')
- half_attn: bfloat16 [16, 384, 384], P('mp', 'dp')
- half_fc1: bfloat16 [16, 384, 384], P('mp', 'dp')
- half_fc2: bfloat16 [16, 384, 384], P('mp', 'dp')
- vector_grad: float32 [13, 768], replicated
- new_vectors: float32 [13, 768], replicated
The draws below stay inside these ranges and needn't reach their ends.
Inputs may be any that keep to these rules, and one draw needn't show every extreme that they name: `keep_mask`: each image keeps at least a fifth of its 197 patches, rounded up, and at most 157; both counts occur in every draw. `vectors`: rows as listed in its meaning. `left_attn`: every block is symmetric. `right_attn`: every block is symmetric. `root_left_attn`: every block is symmetric. `root_right_attn`: every block is symmetric. `left_fc1`: every block is symmetric. `right_fc1`: every block is symmetric. `root_left_fc1`: every block is symmetric. `root_right_fc1`: every block is symmetric. `left_fc2`: every block is symmetric. `right_fc2`: every block is symmetric. `root_left_fc2`: every block is symmetric. `root_right_fc2`: every block is symmetric.
All inputs are finite; a program needn't handle non-finite values.
Results may differ from the reference program's by a relative error of at most 0.014.
Values may be sent and summed in bfloat16 or wider, within the bound.
No kernel may reach another device: no remote copies, remote signals or barrier semaphores. Data moves between devices by JAX's collectives and lax.ppermute only.
A program may use at most 128 MiB of HBM per device.

```python
import math
import jax
import jax.numpy as jnp
from jax import lax

D = 768
HEADS = 12
FF = 3072
PATCHES = 197
SB = 384
VECTORS = 13
BLOCK_VEC = 128
IMAGES = 32
ROW_BLOCKS = 2
ATT_BLOCKS = 16
FC_BLOCKS = 16
N_MP = 4


def symmetric_noise(key, block_count, block_order):
    off_noise = jax.random.uniform(key, (block_count, block_order, block_order), minval=-1.0, maxval=1.0)
    return off_noise + jnp.swapaxes(off_noise, 1, 2)


def statistic(key, stat_scale, block_count, block_order):
    key_diag, key_noise = jax.random.split(key)
    diagonal = stat_scale * jnp.exp(jax.random.uniform(key_diag, (block_count, block_order, 1), minval=0.0, maxval=math.log(4.0)))
    identity = jnp.eye(block_order, dtype=jnp.float32)
    spread = symmetric_noise(key_noise, block_count, block_order) * (0.3 / math.sqrt(block_order)) * stat_scale
    return (identity * diagonal + (1.0 - identity) * spread).astype(jnp.float32)


def inverse_root(key, block_count, block_order):
    key_diag, key_noise = jax.random.split(key)
    rising = 0.5 + lax.broadcasted_iota(jnp.float32, (1, block_order, 1), 1) / block_order
    diagonal = jax.random.uniform(key_diag, (block_count, block_order, 1), minval=0.5, maxval=2.0) * rising
    identity = jnp.eye(block_order, dtype=jnp.float32)
    spread = symmetric_noise(key_noise, block_count, block_order) * (0.25 / math.sqrt(block_order))
    return (identity * diagonal + (1.0 - identity) * spread).astype(jnp.float32)


def stat_level(factor):
    grad_entry = factor * math.sqrt(IMAGES * PATCHES)
    return 0.05 / 0.95 * SB * grad_entry * grad_entry


def attn_levels():
    column_block = lax.broadcasted_iota(jnp.int32, (ATT_BLOCKS, 1, 1), 0) // ROW_BLOCKS
    return jnp.where(column_block < 3 * ROW_BLOCKS, stat_level(0.4), stat_level(0.06)).astype(jnp.float32)


def draw_keep_mask(key, part):
    key = jax.random.fold_in(key, 5)
    key_count, key_order, key_pick = jax.random.split(key, 3)
    lowest = (PATCHES + 4) // 5
    largest = 4 * PATCHES // 5
    kept_count = jax.random.randint(key_count, (IMAGES,), lowest, largest + 1)
    picked = jax.random.permutation(key_pick, IMAGES)
    image_index = lax.broadcasted_iota(jnp.int32, (IMAGES,), 0)
    kept_count = jnp.where(image_index == picked[0], largest, kept_count)
    kept_count = jnp.where(image_index == picked[1], lowest, kept_count)
    orders = jax.vmap(lambda image_key: jax.random.permutation(image_key, PATCHES))(jax.random.split(key_order, IMAGES))
    return (orders < kept_count[:, None]).astype(jnp.int32)


def draw_vectors(key, part):
    key = jax.random.fold_in(key, 11)
    key_gain, key_rest = jax.random.split(key)
    row_index = lax.broadcasted_iota(jnp.int32, (VECTORS, D), 0)
    gain_values = 1.0 + jax.random.uniform(key_gain, (VECTORS, D), minval=-0.3, maxval=0.3)
    normal_values = jax.random.normal(key_rest, (VECTORS, D))
    is_gain = (row_index == 0) | (row_index == 2)
    spread = jnp.where(row_index == 8, D ** (-0.5), 0.2)
    return jnp.where(is_gain, gain_values, normal_values * spread).astype(jnp.float32)


def draw_w_attn(key, part):
    key = jax.random.fold_in(key, 41)
    values = jnp.clip(jax.random.normal(key, (ATT_BLOCKS, SB, SB)), -6.0, 6.0)
    column_block = lax.broadcasted_iota(jnp.int32, (ATT_BLOCKS, 1, 1), 0) // ROW_BLOCKS
    scale = jnp.where(column_block < 3 * ROW_BLOCKS, D ** (-0.5), (D // 16) ** (-0.5))
    return (values * scale).astype(jnp.float32)


def draw_left_attn(key, part):
    key = jax.random.fold_in(key, 21)
    return statistic(key, attn_levels(), ATT_BLOCKS, SB)


def draw_right_attn(key, part):
    key = jax.random.fold_in(key, 22)
    return statistic(key, attn_levels(), ATT_BLOCKS, SB)


def draw_root_left_attn(key, part):
    key = jax.random.fold_in(key, 23)
    return inverse_root(key, ATT_BLOCKS, SB)


def draw_root_right_attn(key, part):
    key = jax.random.fold_in(key, 24)
    return inverse_root(key, ATT_BLOCKS, SB)


def draw_left_fc1(key, part):
    key = jax.random.fold_in(key, 29)
    return statistic(key, stat_level(0.2), FC_BLOCKS, SB)


def draw_right_fc1(key, part):
    key = jax.random.fold_in(key, 30)
    return statistic(key, stat_level(0.2), FC_BLOCKS, SB)


def draw_root_left_fc1(key, part):
    key = jax.random.fold_in(key, 31)
    return inverse_root(key, FC_BLOCKS, SB)


def draw_root_right_fc1(key, part):
    key = jax.random.fold_in(key, 32)
    return inverse_root(key, FC_BLOCKS, SB)


def draw_left_fc2(key, part):
    key = jax.random.fold_in(key, 33)
    return statistic(key, stat_level(0.23), FC_BLOCKS, SB)


def draw_right_fc2(key, part):
    key = jax.random.fold_in(key, 34)
    return statistic(key, stat_level(0.23), FC_BLOCKS, SB)


def draw_root_left_fc2(key, part):
    key = jax.random.fold_in(key, 35)
    return inverse_root(key, FC_BLOCKS, SB)


def draw_root_right_fc2(key, part):
    key = jax.random.fold_in(key, 36)
    return inverse_root(key, FC_BLOCKS, SB)


def block_levels(key, dims, cuts, least, high):
    factor_of, own = 1.0, jax.random.fold_in(key, 6)
    for dim, shards_of in cuts:
        heights = jnp.exp(jax.random.uniform(jax.random.fold_in(own, dim), (shards_of,), jnp.float32, least / len(cuts), high / len(cuts)))
        factor_of = factor_of * jnp.repeat(heights, dims[dim] // shards_of).reshape([-1 if axis == dim else 1 for axis in range(len(dims))])
    return factor_of


def noise(own_key, dims, scale, limit, pieces=(), kind=jnp.bfloat16):
    result = scale * jax.random.normal(own_key, dims, jnp.float32)
    if pieces:
        result = result * block_levels(own_key, dims, pieces, -0.22, 0.18)
    return jnp.clip(result, -limit, limit).astype(kind)


def setup_inputs(seed: int = 0) -> dict:
    key_of = jax.random.split(jax.random.key(seed), 20)
    tokens = noise(key_of[0], (IMAGES, PATCHES, D), 1.0, 6.0, ((0, 32),))
    keep_mask = draw_keep_mask(jax.random.fold_in(key_of[19], 71), 0)
    cotangent = noise(key_of[2], (IMAGES, PATCHES, D), 1.0, 6.0, ((0, 32),))
    w_attn = draw_w_attn(jax.random.fold_in(key_of[19], 71), 0)
    w_fc1 = noise(key_of[4], (FC_BLOCKS, SB, SB), D ** -0.5, 0.21875, ((0, 4), (1, 8)), jnp.float32)
    w_fc2 = noise(key_of[5], (FC_BLOCKS, SB, SB), FF ** -0.5, 0.109375, ((0, 4), (1, 8)), jnp.float32)
    vectors = draw_vectors(jax.random.fold_in(key_of[19], 71), 0)
    left_attn = draw_left_attn(jax.random.fold_in(key_of[19], 71), 0)
    right_attn = draw_right_attn(jax.random.fold_in(key_of[19], 71), 0)
    root_left_attn = draw_root_left_attn(jax.random.fold_in(key_of[19], 71), 0)
    root_right_attn = draw_root_right_attn(jax.random.fold_in(key_of[19], 71), 0)
    left_fc1 = draw_left_fc1(jax.random.fold_in(key_of[19], 71), 0)
    right_fc1 = draw_right_fc1(jax.random.fold_in(key_of[19], 71), 0)
    root_left_fc1 = draw_root_left_fc1(jax.random.fold_in(key_of[19], 71), 0)
    root_right_fc1 = draw_root_right_fc1(jax.random.fold_in(key_of[19], 71), 0)
    left_fc2 = draw_left_fc2(jax.random.fold_in(key_of[19], 71), 0)
    right_fc2 = draw_right_fc2(jax.random.fold_in(key_of[19], 71), 0)
    root_left_fc2 = draw_root_left_fc2(jax.random.fold_in(key_of[19], 71), 0)
    root_right_fc2 = draw_root_right_fc2(jax.random.fold_in(key_of[19], 71), 0)
    return dict(tokens=tokens, keep_mask=keep_mask, cotangent=cotangent, w_attn=w_attn, w_fc1=w_fc1, w_fc2=w_fc2, vectors=vectors, left_attn=left_attn, right_attn=right_attn, root_left_attn=root_left_attn, root_right_attn=root_right_attn, left_fc1=left_fc1, right_fc1=right_fc1, root_left_fc1=root_left_fc1, root_right_fc1=root_right_fc1, left_fc2=left_fc2, right_fc2=right_fc2, root_left_fc2=root_left_fc2, root_right_fc2=root_right_fc2)


@jax.custom_vjp
def low(v):
    return lax.optimization_barrier(v.astype(jnp.bfloat16)).astype(jnp.float32)

@jax.custom_vjp
def low_back(v):
    return v

def low_keep(v):
    return (low(v), None)

def low_pass(kept, grad):
    return (grad,)

def back_keep(v):
    return (v, None)

def back_low(kept, grad):
    return (low(grad),)
low.defvjp(low_keep, low_pass)
low_back.defvjp(back_keep, back_low)
highest = lax.Precision.HIGHEST
masked_score = -1e+30

def layer_norm(values, gain_row, shift_row):
    centered = values - lax.optimization_barrier(jnp.mean(values, axis=-1, keepdims=True))
    variance = lax.optimization_barrier(jnp.mean(centered * centered, axis=-1, keepdims=True))
    return centered * lax.rsqrt(variance + 1e-06) * gain_row + shift_row

def matmul(left_side, right_side):
    return jnp.dot(left_side, right_side, precision=highest)

def cols_whole(blocks, row_blocks):
    block_count, block_order, _ = blocks.shape
    col_blocks = block_count // row_blocks
    return blocks.reshape(col_blocks, row_blocks, block_order, block_order).transpose(1, 2, 0, 3).reshape(row_blocks * block_order, col_blocks * block_order)

def rows_whole(blocks, col_blocks):
    block_count, block_order, _ = blocks.shape
    row_blocks = block_count // col_blocks
    return blocks.reshape(row_blocks, col_blocks, block_order, block_order).transpose(0, 2, 1, 3).reshape(row_blocks * block_order, col_blocks * block_order)

def one_image(params, image, keep_row):
    w_qkv, w_out, w_fc1, w_fc2, vectors = params
    width = image.shape[-1]
    patch_count = image.shape[0]
    head_size = width // HEADS
    row_gate = jax.nn.sigmoid(jnp.dot(image, vectors[8], precision=highest))
    normed = low(layer_norm(image, vectors[0], vectors[1]))
    qkv_bias = jnp.concatenate([vectors[4], jnp.zeros_like(vectors[4]), vectors[5]])
    mixed = low_back(low(matmul(normed, w_qkv) + qkv_bias)).reshape(patch_count, 3, HEADS, head_size)
    scale_factor = head_size ** (-0.5)
    scores = low_back(jnp.einsum('qhd,khd->hqk', mixed[:, 0], mixed[:, 1], precision=highest) * scale_factor)
    scores = jnp.where(keep_row[None, None, :] > 0, scores, masked_score)
    shifted = jnp.exp(scores - lax.optimization_barrier(jnp.max(scores, axis=-1, keepdims=True)))
    probs = low(shifted / lax.optimization_barrier(jnp.sum(shifted, axis=-1, keepdims=True)))
    attended = jnp.einsum('hqk,khd->qhd', probs, mixed[:, 2], precision=highest)
    attended = low_back(low(attended)).reshape(patch_count, width)
    branch = low_back(matmul(attended, w_out) + vectors[6])
    middle = image + branch
    normed_two = low(layer_norm(middle, vectors[2], vectors[3]))
    up_bias = vectors[9:].reshape(-1)
    group_width = w_fc1.shape[1] // N_MP
    feed_sum = jnp.zeros((patch_count, width), jnp.float32)
    for group in range(N_MP):
        first = group * group_width
        hidden = low_back(matmul(low_back(normed_two), w_fc1[:, first:first + group_width]) + up_bias[first:first + group_width])
        activated = low(jax.nn.gelu(hidden, approximate=False))
        feed_sum = feed_sum + low(matmul(activated, w_fc2[first:first + group_width]))
    feed = low_back(feed_sum + vectors[7])
    row_scale = keep_row * row_gate
    return image + row_scale[:, None] * (branch + feed)

def block_rates(block_count, row_blocks, split_col, first_rate, second_rate):
    column_block = jnp.arange(block_count, dtype=jnp.int32) // row_blocks
    return jnp.where(column_block < split_col, first_rate, second_rate)

def precondition(weight, gradient, left_stat, right_stat, left_root, right_root, step_rates):
    left_term = jnp.einsum('bij,bkj->bik', gradient, gradient, precision=highest)
    right_term = jnp.einsum('bji,bjk->bik', gradient, gradient, precision=highest)
    new_left = 0.95 * left_stat + 0.05 * left_term
    new_right = 0.95 * right_stat + 0.05 * right_term
    update_step = jnp.einsum('bij,bjk->bik', left_root, gradient, precision=highest)
    update_step = jnp.einsum('bij,bjk->bik', update_step, right_root, precision=highest)
    update_scale = lax.rsqrt(lax.optimization_barrier(jnp.mean(update_step * update_step, axis=(1, 2), keepdims=True)) + 1e-06)
    return (new_left, new_right, weight - step_rates[:, None, None] * update_step * update_scale)

def reference(tokens, keep_mask, cotangent, w_attn, w_fc1, w_fc2, vectors, left_attn, right_attn, root_left_attn, root_right_attn, left_fc1, right_fc1, root_left_fc1, root_right_fc1, left_fc2, right_fc2, root_left_fc2, root_right_fc2):
    token_values = tokens.astype(jnp.float32)
    mask_values = keep_mask.astype(jnp.float32)
    row_blocks = D // SB

    def forward(inputs, params):
        attn_blocks, fc1_blocks, fc2_blocks, vector_values = params
        attn_whole = cols_whole(low(attn_blocks), row_blocks)
        matrices = (attn_whole[:, :3 * D], attn_whole[:, 3 * D:], cols_whole(low(fc1_blocks), row_blocks), rows_whole(low(fc2_blocks), row_blocks), vector_values)
        image_pass = jax.checkpoint(one_image)
        return lax.map(lambda members: image_pass(matrices, members[0], members[1]), (inputs, mask_values))
    outputs, backward = jax.vjp(forward, token_values, (w_attn, w_fc1, w_fc2, vectors))
    input_grad, grads = backward(cotangent.astype(jnp.float32))
    grad_attn, grad_fc1, grad_fc2, vector_grad = grads
    attn_rates = block_rates(ATT_BLOCKS, row_blocks, 3 * row_blocks, 0.5 * D ** (-0.5), 0.5 * (D // 16) ** (-0.5))
    fc1_rates = block_rates(FC_BLOCKS, row_blocks, FF, 0.5 * D ** (-0.5), 0.5 * D ** (-0.5))
    fc2_rates = block_rates(FC_BLOCKS, row_blocks, FF, 0.5 * FF ** (-0.5), 0.5 * FF ** (-0.5))
    new_left_attn, new_right_attn, new_attn = precondition(w_attn, grad_attn, left_attn, right_attn, root_left_attn, root_right_attn, attn_rates)
    new_left_fc1, new_right_fc1, new_fc1 = precondition(w_fc1, grad_fc1, left_fc1, right_fc1, root_left_fc1, root_right_fc1, fc1_rates)
    new_left_fc2, new_right_fc2, new_fc2 = precondition(w_fc2, grad_fc2, left_fc2, right_fc2, root_left_fc2, root_right_fc2, fc2_rates)
    vector_blocks = vector_grad.reshape(VECTORS, D // BLOCK_VEC, BLOCK_VEC)
    block_scale = lax.rsqrt(lax.optimization_barrier(jnp.mean(vector_blocks * vector_blocks, axis=-1, keepdims=True)) + 1e-06)
    new_vectors = vectors - 0.05 * (vector_blocks * block_scale).reshape(VECTORS, D)
    return (outputs.astype(jnp.bfloat16), input_grad, grad_attn, grad_fc1, grad_fc2, new_left_attn, new_right_attn, new_left_fc1, new_right_fc1, new_left_fc2, new_right_fc2, new_attn, new_fc1, new_fc2, new_attn.astype(jnp.bfloat16), new_fc1.astype(jnp.bfloat16), new_fc2.astype(jnp.bfloat16), vector_grad, new_vectors)
```

```python
import jax
import jax.numpy as jnp
from jax import lax
from jax.sharding import PartitionSpec as P

D = 768
HEADS = 12
FF = 3072
BLOCK_VEC = 128
KEPT_MOST = 157
SLOTS = 160
PAIR = 2

highest = lax.Precision.HIGHEST
masked_score = -1e30
half = jnp.bfloat16
full = jnp.float32


def to_half(values):
    return values.astype(half)


def layer_norm(values, gain_row, shift_row):
    centered = values - jnp.mean(values, axis=-1, keepdims=True)
    variance = jnp.mean(centered * centered, axis=-1, keepdims=True)
    return centered * lax.rsqrt(variance + 1e-06) * gain_row + shift_row


def exact_gelu(values):
    return jax.nn.gelu(values, approximate=False)


def dot32(left, right):
    return jnp.dot(left, right, preferred_element_type=full)


def row_product(left_half, right_half):
    return lax.dot_general(
        left_half, right_half, (((0,), (0,)), ((), ())), preferred_element_type=full
    )


def times_transpose(left_half, right_half):
    return lax.dot_general(
        left_half, right_half, (((1,), (1,)), ((), ())), preferred_element_type=full
    )


def swap_low(values, axis):
    count = lax.axis_size(axis)
    return lax.ppermute(values, axis, [(s, s ^ 1) for s in range(count)])


def shift_high(values, axis, step):
    count = lax.axis_size(axis)
    return lax.ppermute(values, axis, [(s, (s + step * PAIR) % count) for s in range(count)])


def high_index(axis):
    return lax.axis_index(axis) // PAIR


def low_index(axis):
    return lax.axis_index(axis) % PAIR


def high_size(axis):
    return lax.axis_size(axis) // PAIR


def pick(values, index, dim=0):
    return lax.dynamic_index_in_dim(values, index, dim, keepdims=False)


def ordered(pieces, index):
    count = len(pieces)
    if count == 2:
        first = index == 0
        return jnp.stack(
            [jnp.where(first, pieces[0], pieces[1]), jnp.where(first, pieces[1], pieces[0])]
        )
    return lax.dynamic_slice_in_dim(jnp.stack(pieces + pieces), (count - index) % count, count, 0)


def gather_low(values, axis):
    return ordered([values, swap_low(values, axis)], low_index(axis))


def gather_high(values, axis):
    count = high_size(axis)
    pieces = [values] + [shift_high(values, axis, -k) for k in range(1, count)]
    return ordered(pieces, high_index(axis))


def scatter_low(values, axis):
    low = low_index(axis)
    arrived = swap_low(pick(values, 1 - low), axis)
    return pick(values, low).astype(full) + arrived.astype(full)


def scatter_high(values, axis):
    count, high = high_size(axis), high_index(axis)
    total = pick(values, high).astype(full)
    for k in range(1, count):
        total = total + shift_high(pick(values, (high + k) % count), axis, k).astype(full)
    return total


def attend(queries, key_part, values, allowed):
    scale_factor = queries.shape[-1] ** (-0.5)
    scores = jnp.einsum("qhd,khd->hqk", queries, key_part, preferred_element_type=full)
    scores = jnp.where(allowed[None, None, :] > 0, scores * scale_factor, masked_score)
    shifted = jnp.exp(scores - jnp.max(scores, axis=-1, keepdims=True))
    probs = shifted / jnp.sum(shifted, axis=-1, keepdims=True)
    attended = jnp.einsum("hqk,khd->qhd", to_half(probs), values, preferred_element_type=full)
    return (to_half(attended), probs)


def attend_back(queries, key_part, values, probs, grad_attended):
    scale_factor = queries.shape[-1] ** (-0.5)
    grad_values = jnp.einsum(
        "hqk,qhd->khd", to_half(probs), grad_attended, preferred_element_type=full
    )
    grad_probs = jnp.einsum("qhd,khd->hqk", grad_attended, values, preferred_element_type=full)
    row_inner = jnp.sum(probs * grad_probs, axis=-1, keepdims=True)
    grad_scores = to_half(probs * (grad_probs - row_inner))
    grad_queries = (
        jnp.einsum("hqk,khd->qhd", grad_scores, key_part, preferred_element_type=full)
        * scale_factor
    )
    grad_keys = (
        jnp.einsum("hqk,qhd->khd", grad_scores, queries, preferred_element_type=full)
        * scale_factor
    )
    return jnp.stack([grad_queries, grad_keys, grad_values], axis=1)


def gather_group(rows):
    pair = jnp.stack([rows, swap_low(rows, "mp")])
    pieces = [pair] + [shift_high(pair, "mp", -k) for k in range(1, high_size("mp"))]
    return jnp.concatenate(pieces, axis=0).reshape(-1, rows.shape[-1])


def scatter_group(rows, row_count):
    pieces = rows.reshape(high_size("mp"), PAIR, row_count, rows.shape[-1])
    pairs = pieces[:, 0].astype(full) + swap_low(pieces[:, 1], "mp").astype(full)
    total = pairs[0]
    for k in range(1, high_size("mp")):
        total = total + shift_high(to_half(pairs[k]), "mp", k).astype(full)
    return total


def halves(values, dim):
    count = values.shape[dim] // 2
    return (
        lax.slice_in_dim(values, 0, count, axis=dim),
        lax.slice_in_dim(values, count, 2 * count, axis=dim),
    )


def gather_attn(blocks):
    local, piece, order = blocks.shape
    lines = gather_high(to_half(blocks), "dp")
    first, second = halves(lines, 0)
    first = gather_high(gather_low(first, "dp"), "mp")
    second = gather_low(gather_high(second, "mp"), "dp")
    both = jnp.concatenate([first, second.swapaxes(0, 1)], axis=2)
    both = gather_low(both, "mp")
    row_blocks = D // order
    both = both.transpose(1, 0, 4, 3, 2, 5, 6)
    both = both.reshape(-1, row_blocks, order, order)
    return both.transpose(1, 2, 0, 3).reshape(D, -1)


def gather_fc(blocks):
    lines = gather_low(gather_high(to_half(blocks), "dp"), "dp")
    lines = lines.transpose(2, 1, 0, 3, 4)
    return lines.reshape(blocks.shape[0], -1, blocks.shape[2])


def split_cols(matrix, order):
    rows, cols = matrix.shape
    return (
        matrix.reshape(rows // order, order, cols // order, order)
        .transpose(2, 0, 1, 3)
        .reshape(-1, order, order)
    )


def split_rows(matrix, order):
    rows, cols = matrix.shape
    return (
        matrix.reshape(rows // order, order, cols // order, order)
        .transpose(0, 2, 1, 3)
        .reshape(-1, order, order)
    )


def join_cols(blocks, row_blocks):
    count, order, _ = blocks.shape
    return (
        blocks.reshape(-1, row_blocks, order, order)
        .transpose(1, 2, 0, 3)
        .reshape(row_blocks * order, -1)
    )


def join_rows(blocks, col_blocks):
    count, order, _ = blocks.shape
    return (
        blocks.reshape(-1, col_blocks, order, order)
        .transpose(0, 2, 1, 3)
        .reshape(-1, col_blocks * order)
    )


def scatter_z(blocks):
    local, order, _ = blocks.shape
    count = high_size("dp")
    by_rows = to_half(blocks).reshape(local, count, order // count, order).swapaxes(0, 1)
    return scatter_high(by_rows, "dp")


def scatter_fc(blocks):
    local, order, _ = blocks.shape
    by_x = to_half(blocks).reshape(PAIR, local // PAIR, order, order)
    return scatter_z(scatter_low(by_x, "dp"))


def scatter_attn(blocks):
    count, order, _ = blocks.shape
    y_count = high_size("mp")
    local = count // (y_count * PAIR)
    by_core = to_half(blocks).reshape(y_count, PAIR, local, order, order).swapaxes(0, 1)
    kept = to_half(scatter_low(by_core, "mp")).reshape(
        y_count, PAIR, local // PAIR, order, order
    )
    first, second = halves(kept, 3)
    first = to_half(scatter_low(first.swapaxes(0, 1), "dp"))
    second = to_half(scatter_high(second, "mp"))
    first = scatter_high(first, "mp")
    second = scatter_low(second, "dp")
    return scatter_z(jnp.concatenate([first, second], axis=1))


def gather_z(rows):
    local, _, order = rows.shape
    return gather_high(to_half(rows), "dp").swapaxes(0, 1).reshape(local, -1, order)


def to_pair(pieces):
    local, piece, order = pieces.shape
    by_x = to_half(pieces).reshape(PAIR, local // PAIR, piece, order)
    low = low_index("dp")
    both = ordered([pick(by_x, low), swap_low(pick(by_x, 1 - low), "dp")], low)
    return both.swapaxes(0, 1).reshape(local // PAIR, PAIR * piece, order)


def from_pair(rows):
    n, local, piece, order = rows.shape
    by_x = to_half(rows).reshape(n, local, PAIR, piece // PAIR, order)
    low = low_index("dp")
    both = ordered([pick(by_x, low, 2), swap_low(pick(by_x, 1 - low, 2), "dp")], low)
    return both.swapaxes(0, 1).reshape(n, PAIR * local, piece // PAIR, order)


def shampoo_rows(grad_rows, left_root, right_root):
    grad_half = to_half(grad_rows)
    whole = gather_z(grad_half)
    rows = grad_rows.shape[1]
    cols = lax.dynamic_slice_in_dim(whole, high_index("dp") * rows, rows, 2)
    left_term = jnp.einsum("bij,bkj->bik", grad_half, whole, preferred_element_type=full)
    right_term = jnp.einsum("bji,bjk->bik", cols, whole, preferred_element_type=full)
    step = to_half(jnp.einsum("bij,bjk->bik", left_root, whole, preferred_element_type=full))
    step = jnp.einsum("bij,bjk->bik", step, right_root, preferred_element_type=full)
    squares = jnp.sum(step * step, axis=(1, 2))
    squares = gather_low(squares, "dp").reshape(-1)
    total = squares
    for k in range(1, high_size("dp")):
        total = total + shift_high(squares, "dp", k)
    sent = from_pair(jnp.stack([grad_rows, left_term, right_term, step]))
    return sent, total


def apply_step(weight, left_stat, right_stat, sent, square_total, step_rates):
    order = weight.shape[2]
    sent = sent.astype(full)
    update_scale = lax.rsqrt(square_total / (order * order) + 1e-06) * step_rates
    return (
        sent[0],
        0.95 * left_stat + 0.05 * sent[1],
        0.95 * right_stat + 0.05 * sent[2],
        weight - sent[3] * update_scale[:, None, None],
    )


def sum_all(values):
    values = values + swap_low(values, "mp")
    for axis in ("mp", "dp"):
        if axis == "dp":
            values = values + swap_low(values, "dp")
        base = values
        for k in range(1, high_size(axis)):
            values = values + shift_high(base, axis, k)
    return values


def body(
    tokens,
    keep_mask,
    cotangent,
    w_attn,
    w_fc1,
    w_fc2,
    vectors,
    left_attn,
    right_attn,
    root_left_attn,
    root_right_attn,
    left_fc1,
    right_fc1,
    root_left_fc1,
    root_right_fc1,
    left_fc2,
    right_fc2,
    root_left_fc2,
    root_right_fc2,
):
    image_count, patch_count, width = tokens.shape
    row_count = image_count * patch_count
    order = w_attn.shape[2]
    row_blocks = width // order
    attn_used = gather_attn(w_attn)
    qkv_full = attn_used[:, : 3 * width]
    out_full = attn_used[:, 3 * width :]
    fc1_used = join_cols(gather_fc(w_fc1), row_blocks)
    fc2_used = join_rows(gather_fc(w_fc2), row_blocks)
    left_roots = [to_pair(v) for v in (root_left_attn, root_left_fc1, root_left_fc2)]
    right_roots = [gather_z(to_pair(v)) for v in (root_right_attn, root_right_fc1, root_right_fc2)]
    hidden_local = fc1_used.shape[1]
    flat = tokens.reshape(row_count, width).astype(full)
    keep_rows = keep_mask.reshape(row_count).astype(full)
    row_gate = jax.nn.sigmoid(jnp.sum(flat * vectors[8], axis=-1))
    row_scale = keep_rows * row_gate
    grad_output = cotangent.reshape(row_count, width).astype(full)
    grad_change = row_scale[:, None] * grad_output
    grad_feed = to_half(grad_change)
    slot = jnp.cumsum(keep_mask, axis=1) - 1
    chosen = (
        (slot[:, None, :] == lax.broadcasted_iota(jnp.int32, (1, SLOTS, 1), 1))
        & (keep_mask[:, None, :] > 0)
    ).astype(half)

    def compact(rows):
        rows = rows.reshape(image_count, patch_count, width)
        picked = jnp.einsum("bsr,brd->bsd", chosen, rows, preferred_element_type=full)
        return to_half(picked).reshape(image_count * SLOTS, width)

    def spread(rows):
        rows = rows.reshape(image_count, SLOTS, width)
        return jnp.einsum(
            "bsr,bsd->brd", chosen.astype(full), rows, precision=highest
        ).reshape(row_count, width)

    group_grads = gather_group(compact(grad_feed))
    normed, first_norm_back = jax.vjp(layer_norm, flat, vectors[0], vectors[1])
    normed_half = to_half(normed)
    qkv_bias = jnp.concatenate([vectors[4], jnp.zeros_like(vectors[4]), vectors[5]])
    mixed_half = to_half(dot32(normed_half, qkv_full) + qkv_bias)
    heads_view = mixed_half.reshape(image_count, patch_count, 3, HEADS, width // HEADS)
    queries = heads_view[:, :, 0]
    key_part = heads_view[:, :, 1]
    values = heads_view[:, :, 2]
    attended_half, probs = jax.vmap(attend)(queries, key_part, values, keep_mask)
    attended_flat = attended_half.reshape(row_count, width)
    branch = dot32(attended_flat, out_full) + vectors[6]
    middle = flat + branch
    normed_two, second_norm_back = jax.vjp(layer_norm, middle, vectors[2], vectors[3])
    group_rows = gather_group(compact(to_half(normed_two)))
    up_bias = vectors[9:].reshape(-1)
    offset = lax.axis_index("mp") * hidden_local
    local_bias = lax.dynamic_slice_in_dim(up_bias, offset, hidden_local)
    hidden = dot32(group_rows, fc1_used) + local_bias
    activated, gelu_back = jax.vjp(exact_gelu, hidden)
    activated = to_half(activated)
    grad_active = times_transpose(group_grads, fc2_used)
    grad_hidden = to_half(gelu_back(grad_active)[0])
    mlp_count = image_count * SLOTS
    grad_rows_back = scatter_group(to_half(times_transpose(grad_hidden, fc1_used)), mlp_count)
    feed = spread(scatter_group(to_half(dot32(activated, fc2_used)), mlp_count)) + vectors[7]
    change = branch + feed
    block_out = to_half(flat + row_scale[:, None] * change).reshape(tokens.shape)
    grad_logit = keep_rows * row_gate * (1.0 - row_gate) * jnp.sum(grad_output * change, axis=-1)
    fc1_rows = scatter_fc(split_cols(row_product(group_rows, grad_hidden), order))
    fc2_rows = scatter_fc(split_rows(row_product(activated, group_grads), order))
    up_part = jnp.sum(grad_hidden, axis=0, dtype=full)
    up_bias_grad = lax.dynamic_update_slice_in_dim(jnp.zeros_like(up_bias), up_part, offset, 0)
    sent_fc1, total_fc1 = shampoo_rows(fc1_rows, left_roots[1], right_roots[1])
    sent_fc2, total_fc2 = shampoo_rows(fc2_rows, left_roots[2], right_roots[2])

    grad_normed_two = spread(grad_rows_back)
    grad_middle, grad_gain_two, grad_shift_two = second_norm_back(grad_normed_two)
    grad_branch = to_half(grad_change + grad_middle)
    grad_attended = to_half(times_transpose(grad_branch, out_full))
    grad_out_full = row_product(attended_flat, grad_branch)
    grad_heads = jax.vmap(attend_back)(
        queries,
        key_part,
        values,
        probs,
        grad_attended.reshape(image_count, patch_count, HEADS, -1),
    )
    grad_mixed = to_half(grad_heads.reshape(row_count, 3 * width))
    grad_qkv_full = row_product(normed_half, grad_mixed)
    attn_rows = scatter_attn(
        split_cols(jnp.concatenate([grad_qkv_full, grad_out_full], axis=1), order)
    )
    sent_attn, total_attn = shampoo_rows(attn_rows, left_roots[0], right_roots[0])
    grad_normed = times_transpose(grad_mixed, qkv_full)
    grad_flat, grad_gain_one, grad_shift_one = first_norm_back(grad_normed)
    input_grad = (grad_output + grad_middle + grad_flat + grad_logit[:, None] * vectors[8]).reshape(
        tokens.shape
    )
    mixed_sums = jnp.sum(grad_mixed, axis=0, dtype=full)
    vector_rows = jnp.stack(
        [
            grad_gain_one,
            grad_shift_one,
            grad_gain_two,
            grad_shift_two,
            mixed_sums[:width],
            mixed_sums[2 * width :],
            jnp.sum(grad_branch, axis=0, dtype=full),
            jnp.sum(grad_feed, axis=0, dtype=full),
            jnp.sum(grad_logit[:, None] * flat, axis=0),
        ]
    )
    vector_part = jnp.concatenate([vector_rows, up_bias_grad.reshape(-1, width)], axis=0)
    vector_grad = sum_all(vector_part)

    attn_local = w_attn.shape[0]
    block_index = lax.axis_index("mp") * attn_local + lax.broadcasted_iota(
        jnp.int32, (attn_local,), 0
    )
    attn_rates = jnp.where(
        block_index // row_blocks < 3 * row_blocks, 0.5 * D ** (-0.5), 0.5 * (D // 16) ** (-0.5)
    )
    fc1_rates = jnp.full((w_fc1.shape[0],), 0.5 * D ** (-0.5), full)
    fc2_rates = jnp.full((w_fc2.shape[0],), 0.5 * FF ** (-0.5), full)
    grad_attn, new_left_attn, new_right_attn, new_attn = apply_step(
        w_attn, left_attn, right_attn, sent_attn, total_attn, attn_rates
    )
    grad_fc1, new_left_fc1, new_right_fc1, new_fc1 = apply_step(
        w_fc1, left_fc1, right_fc1, sent_fc1, total_fc1, fc1_rates
    )
    grad_fc2, new_left_fc2, new_right_fc2, new_fc2 = apply_step(
        w_fc2, left_fc2, right_fc2, sent_fc2, total_fc2, fc2_rates
    )
    vector_blocks = vector_grad.reshape(vector_grad.shape[0], -1, BLOCK_VEC)
    block_scale = lax.rsqrt(jnp.mean(vector_blocks * vector_blocks, axis=-1, keepdims=True) + 1e-06)
    new_vectors = vectors - 0.05 * (vector_blocks * block_scale).reshape(vectors.shape)
    return (
        block_out,
        input_grad,
        grad_attn,
        grad_fc1,
        grad_fc2,
        new_left_attn,
        new_right_attn,
        new_left_fc1,
        new_right_fc1,
        new_left_fc2,
        new_right_fc2,
        new_attn,
        new_fc1,
        new_fc2,
        to_half(new_attn),
        to_half(new_fc1),
        to_half(new_fc2),
        vector_grad,
        new_vectors,
    )


def solution(mesh):
    rows = P(("dp", "mp"), None, None)
    blocks = P("mp", "dp", None)
    return jax.shard_map(
        body,
        mesh=mesh,
        in_specs=(rows, P(("dp", "mp"), None), rows)
        + (blocks,) * 3
        + (P(),)
        + (blocks,) * 12,
        out_specs=(rows, rows) + (blocks,) * 15 + (P(), P()),
        check_vma=False,
    )
```

```python
import jax
import jax.numpy as jnp
from jax import lax
from jax.experimental import pallas as pl
from jax.experimental.pallas import tpu as pltpu
from jax.sharding import PartitionSpec as P

D = 768
HEADS = 12
FF = 3072
BLOCK_VEC = 128
KEPT_MOST = 157
SLOTS = 160
PAIR = 2

highest = lax.Precision.HIGHEST
masked_score = -1e30
half = jnp.bfloat16
full = jnp.float32


def to_half(values):
    return values.astype(half)


def layer_norm(values, gain_row, shift_row):
    centered = values - jnp.mean(values, axis=-1, keepdims=True)
    variance = jnp.mean(centered * centered, axis=-1, keepdims=True)
    return centered * lax.rsqrt(variance + 1e-06) * gain_row + shift_row


def exact_gelu(values):
    return jax.nn.gelu(values, approximate=False)


def dot32(left, right):
    return jnp.dot(left, right, preferred_element_type=full)


def row_product(left_half, right_half):
    return lax.dot_general(
        left_half, right_half, (((0,), (0,)), ((), ())), preferred_element_type=full
    )


def times_transpose(left_half, right_half):
    return lax.dot_general(
        left_half, right_half, (((1,), (1,)), ((), ())), preferred_element_type=full
    )


def swap_low(values, axis):
    count = lax.axis_size(axis)
    return lax.ppermute(values, axis, [(s, s ^ 1) for s in range(count)])


def shift_high(values, axis, step):
    count = lax.axis_size(axis)
    return lax.ppermute(values, axis, [(s, (s + step * PAIR) % count) for s in range(count)])


def high_index(axis):
    return lax.axis_index(axis) // PAIR


def low_index(axis):
    return lax.axis_index(axis) % PAIR


def high_size(axis):
    return lax.axis_size(axis) // PAIR


def pick(values, index, dim=0):
    return lax.dynamic_index_in_dim(values, index, dim, keepdims=False)


def ordered(pieces, index):
    count = len(pieces)
    if count == 2:
        first = index == 0
        return jnp.stack(
            [jnp.where(first, pieces[0], pieces[1]), jnp.where(first, pieces[1], pieces[0])]
        )
    return lax.dynamic_slice_in_dim(jnp.stack(pieces + pieces), (count - index) % count, count, 0)


def gather_low(values, axis):
    return ordered([values, swap_low(values, axis)], low_index(axis))


def gather_high(values, axis):
    count = high_size(axis)
    pieces = [values] + [shift_high(values, axis, -k) for k in range(1, count)]
    return ordered(pieces, high_index(axis))


def scatter_low(values, axis):
    low = low_index(axis)
    arrived = swap_low(pick(values, 1 - low), axis)
    return pick(values, low).astype(full) + arrived.astype(full)


def scatter_high(values, axis):
    count, high = high_size(axis), high_index(axis)
    total = pick(values, high).astype(full)
    for k in range(1, count):
        total = total + shift_high(pick(values, (high + k) % count), axis, k).astype(full)
    return total


def attend(queries, key_part, values, allowed):
    scale_factor = queries.shape[-1] ** (-0.5)
    scores = jnp.einsum("qhd,khd->hqk", queries, key_part, preferred_element_type=full)
    scores = jnp.where(allowed[None, None, :] > 0, scores * scale_factor, masked_score)
    shifted = jnp.exp(scores - jnp.max(scores, axis=-1, keepdims=True))
    probs = shifted / jnp.sum(shifted, axis=-1, keepdims=True)
    attended = jnp.einsum("hqk,khd->qhd", to_half(probs), values, preferred_element_type=full)
    return (to_half(attended), probs)


def attend_back(queries, key_part, values, probs, grad_attended):
    scale_factor = queries.shape[-1] ** (-0.5)
    grad_values = jnp.einsum(
        "hqk,qhd->khd", to_half(probs), grad_attended, preferred_element_type=full
    )
    grad_probs = jnp.einsum("qhd,khd->hqk", grad_attended, values, preferred_element_type=full)
    row_inner = jnp.sum(probs * grad_probs, axis=-1, keepdims=True)
    grad_scores = to_half(probs * (grad_probs - row_inner))
    grad_queries = (
        jnp.einsum("hqk,khd->qhd", grad_scores, key_part, preferred_element_type=full)
        * scale_factor
    )
    grad_keys = (
        jnp.einsum("hqk,qhd->khd", grad_scores, queries, preferred_element_type=full)
        * scale_factor
    )
    return jnp.stack([grad_queries, grad_keys, grad_values], axis=1)


def gather_group(rows):
    pair = jnp.stack([rows, swap_low(rows, "mp")])
    pieces = [pair] + [shift_high(pair, "mp", -k) for k in range(1, high_size("mp"))]
    return jnp.concatenate(pieces, axis=0).reshape(-1, rows.shape[-1])


def scatter_group(rows, row_count):
    pieces = rows.reshape(high_size("mp"), PAIR, row_count, rows.shape[-1])
    pairs = pieces[:, 0].astype(full) + swap_low(pieces[:, 1], "mp").astype(full)
    total = pairs[0]
    for k in range(1, high_size("mp")):
        total = total + shift_high(to_half(pairs[k]), "mp", k).astype(full)
    return total


def halves(values, dim):
    count = values.shape[dim] // 2
    return (
        lax.slice_in_dim(values, 0, count, axis=dim),
        lax.slice_in_dim(values, count, 2 * count, axis=dim),
    )


def gather_attn(blocks):
    local, piece, order = blocks.shape
    lines = gather_high(to_half(blocks), "dp")
    first, second = halves(lines, 0)
    first = gather_high(gather_low(first, "dp"), "mp")
    second = gather_low(gather_high(second, "mp"), "dp")
    both = jnp.concatenate([first, second.swapaxes(0, 1)], axis=2)
    both = gather_low(both, "mp")
    row_blocks = D // order
    both = both.transpose(1, 0, 4, 3, 2, 5, 6)
    both = both.reshape(-1, row_blocks, order, order)
    return both.transpose(1, 2, 0, 3).reshape(D, -1)


def gather_fc(blocks):
    lines = gather_low(gather_high(to_half(blocks), "dp"), "dp")
    lines = lines.transpose(2, 1, 0, 3, 4)
    return lines.reshape(blocks.shape[0], -1, blocks.shape[2])


def split_cols(matrix, order):
    rows, cols = matrix.shape
    return (
        matrix.reshape(rows // order, order, cols // order, order)
        .transpose(2, 0, 1, 3)
        .reshape(-1, order, order)
    )


def split_rows(matrix, order):
    rows, cols = matrix.shape
    return (
        matrix.reshape(rows // order, order, cols // order, order)
        .transpose(0, 2, 1, 3)
        .reshape(-1, order, order)
    )


def join_cols(blocks, row_blocks):
    count, order, _ = blocks.shape
    return (
        blocks.reshape(-1, row_blocks, order, order)
        .transpose(1, 2, 0, 3)
        .reshape(row_blocks * order, -1)
    )


def join_rows(blocks, col_blocks):
    count, order, _ = blocks.shape
    return (
        blocks.reshape(-1, col_blocks, order, order)
        .transpose(0, 2, 1, 3)
        .reshape(-1, col_blocks * order)
    )


def scatter_z(blocks):
    local, order, _ = blocks.shape
    count = high_size("dp")
    by_rows = to_half(blocks).reshape(local, count, order // count, order).swapaxes(0, 1)
    return scatter_high(by_rows, "dp")


def scatter_fc(blocks):
    local, order, _ = blocks.shape
    by_x = to_half(blocks).reshape(PAIR, local // PAIR, order, order)
    return scatter_z(scatter_low(by_x, "dp"))


def scatter_attn(blocks):
    count, order, _ = blocks.shape
    y_count = high_size("mp")
    local = count // (y_count * PAIR)
    by_core = to_half(blocks).reshape(y_count, PAIR, local, order, order).swapaxes(0, 1)
    kept = to_half(scatter_low(by_core, "mp")).reshape(
        y_count, PAIR, local // PAIR, order, order
    )
    first, second = halves(kept, 3)
    first = to_half(scatter_low(first.swapaxes(0, 1), "dp"))
    second = to_half(scatter_high(second, "mp"))
    first = scatter_high(first, "mp")
    second = scatter_low(second, "dp")
    return scatter_z(jnp.concatenate([first, second], axis=1))


def gather_z(rows):
    local, _, order = rows.shape
    return gather_high(to_half(rows), "dp").swapaxes(0, 1).reshape(local, -1, order)


def to_pair(pieces):
    local, piece, order = pieces.shape
    by_x = to_half(pieces).reshape(PAIR, local // PAIR, piece, order)
    low = low_index("dp")
    both = ordered([pick(by_x, low), swap_low(pick(by_x, 1 - low), "dp")], low)
    return both.swapaxes(0, 1).reshape(local // PAIR, PAIR * piece, order)


def from_pair(rows):
    n, local, piece, order = rows.shape
    by_x = to_half(rows).reshape(n, local, PAIR, piece // PAIR, order)
    low = low_index("dp")
    both = ordered([pick(by_x, low, 2), swap_low(pick(by_x, 1 - low, 2), "dp")], low)
    return both.swapaxes(0, 1).reshape(n, PAIR * local, piece // PAIR, order)


def shampoo_rows(grad_rows, left_root, right_root):
    grad_half = to_half(grad_rows)
    whole = gather_z(grad_half)
    rows = grad_rows.shape[1]
    cols = lax.dynamic_slice_in_dim(whole, high_index("dp") * rows, rows, 2)
    left_term = jnp.einsum("bij,bkj->bik", grad_half, whole, preferred_element_type=full)
    right_term = jnp.einsum("bji,bjk->bik", cols, whole, preferred_element_type=full)
    step = to_half(jnp.einsum("bij,bjk->bik", left_root, whole, preferred_element_type=full))
    step = jnp.einsum("bij,bjk->bik", step, right_root, preferred_element_type=full)
    squares = jnp.sum(step * step, axis=(1, 2))
    squares = gather_low(squares, "dp").reshape(-1)
    total = squares
    for k in range(1, high_size("dp")):
        total = total + shift_high(squares, "dp", k)
    sent = from_pair(jnp.stack([grad_rows, left_term, right_term, step]))
    return sent, total


def apply_step(weight, left_stat, right_stat, sent, square_total, step_rates):
    order = weight.shape[2]
    sent = sent.astype(full)
    update_scale = lax.rsqrt(square_total / (order * order) + 1e-06) * step_rates
    return (
        sent[0],
        0.95 * left_stat + 0.05 * sent[1],
        0.95 * right_stat + 0.05 * sent[2],
        weight - sent[3] * update_scale[:, None, None],
    )


def sum_all(values):
    values = values + swap_low(values, "mp")
    for axis in ("mp", "dp"):
        if axis == "dp":
            values = values + swap_low(values, "dp")
        base = values
        for k in range(1, high_size(axis)):
            values = values + shift_high(base, axis, k)
    return values


def body_plain(
    tokens,
    keep_mask,
    cotangent,
    w_attn,
    w_fc1,
    w_fc2,
    vectors,
    left_attn,
    right_attn,
    root_left_attn,
    root_right_attn,
    left_fc1,
    right_fc1,
    root_left_fc1,
    root_right_fc1,
    left_fc2,
    right_fc2,
    root_left_fc2,
    root_right_fc2,
):
    image_count, patch_count, width = tokens.shape
    row_count = image_count * patch_count
    order = w_attn.shape[2]
    row_blocks = width // order
    attn_used = gather_attn(w_attn)
    qkv_full = attn_used[:, : 3 * width]
    out_full = attn_used[:, 3 * width :]
    fc1_used = join_cols(gather_fc(w_fc1), row_blocks)
    fc2_used = join_rows(gather_fc(w_fc2), row_blocks)
    left_roots = [to_pair(v) for v in (root_left_attn, root_left_fc1, root_left_fc2)]
    right_roots = [gather_z(to_pair(v)) for v in (root_right_attn, root_right_fc1, root_right_fc2)]
    hidden_local = fc1_used.shape[1]
    flat = tokens.reshape(row_count, width).astype(full)
    keep_rows = keep_mask.reshape(row_count).astype(full)
    row_gate = jax.nn.sigmoid(jnp.sum(flat * vectors[8], axis=-1))
    row_scale = keep_rows * row_gate
    grad_output = cotangent.reshape(row_count, width).astype(full)
    grad_change = row_scale[:, None] * grad_output
    grad_feed = to_half(grad_change)
    slot = jnp.cumsum(keep_mask, axis=1) - 1
    chosen = (
        (slot[:, None, :] == lax.broadcasted_iota(jnp.int32, (1, SLOTS, 1), 1))
        & (keep_mask[:, None, :] > 0)
    ).astype(half)

    def compact(rows):
        rows = rows.reshape(image_count, patch_count, width)
        picked = jnp.einsum("bsr,brd->bsd", chosen, rows, preferred_element_type=full)
        return to_half(picked).reshape(image_count * SLOTS, width)

    def spread(rows):
        rows = rows.reshape(image_count, SLOTS, width)
        return jnp.einsum(
            "bsr,bsd->brd", chosen.astype(full), rows, precision=highest
        ).reshape(row_count, width)

    group_grads = gather_group(compact(grad_feed))
    normed, first_norm_back = jax.vjp(layer_norm, flat, vectors[0], vectors[1])
    normed_half = to_half(normed)
    qkv_bias = jnp.concatenate([vectors[4], jnp.zeros_like(vectors[4]), vectors[5]])
    mixed_half = to_half(dot32(normed_half, qkv_full) + qkv_bias)
    heads_view = mixed_half.reshape(image_count, patch_count, 3, HEADS, width // HEADS)
    queries = heads_view[:, :, 0]
    key_part = heads_view[:, :, 1]
    values = heads_view[:, :, 2]
    attended_half, probs = jax.vmap(attend)(queries, key_part, values, keep_mask)
    attended_flat = attended_half.reshape(row_count, width)
    branch = dot32(attended_flat, out_full) + vectors[6]
    middle = flat + branch
    normed_two, second_norm_back = jax.vjp(layer_norm, middle, vectors[2], vectors[3])
    group_rows = gather_group(compact(to_half(normed_two)))
    up_bias = vectors[9:].reshape(-1)
    offset = lax.axis_index("mp") * hidden_local
    local_bias = lax.dynamic_slice_in_dim(up_bias, offset, hidden_local)
    hidden = dot32(group_rows, fc1_used) + local_bias
    activated, gelu_back = jax.vjp(exact_gelu, hidden)
    activated = to_half(activated)
    grad_active = times_transpose(group_grads, fc2_used)
    grad_hidden = to_half(gelu_back(grad_active)[0])
    mlp_count = image_count * SLOTS
    grad_rows_back = scatter_group(to_half(times_transpose(grad_hidden, fc1_used)), mlp_count)
    feed = spread(scatter_group(to_half(dot32(activated, fc2_used)), mlp_count)) + vectors[7]
    change = branch + feed
    block_out = to_half(flat + row_scale[:, None] * change).reshape(tokens.shape)
    grad_logit = keep_rows * row_gate * (1.0 - row_gate) * jnp.sum(grad_output * change, axis=-1)
    fc1_rows = scatter_fc(split_cols(row_product(group_rows, grad_hidden), order))
    fc2_rows = scatter_fc(split_rows(row_product(activated, group_grads), order))
    up_part = jnp.sum(grad_hidden, axis=0, dtype=full)
    up_bias_grad = lax.dynamic_update_slice_in_dim(jnp.zeros_like(up_bias), up_part, offset, 0)
    sent_fc1, total_fc1 = shampoo_rows(fc1_rows, left_roots[1], right_roots[1])
    sent_fc2, total_fc2 = shampoo_rows(fc2_rows, left_roots[2], right_roots[2])

    grad_normed_two = spread(grad_rows_back)
    grad_middle, grad_gain_two, grad_shift_two = second_norm_back(grad_normed_two)
    grad_branch = to_half(grad_change + grad_middle)
    grad_attended = to_half(times_transpose(grad_branch, out_full))
    grad_out_full = row_product(attended_flat, grad_branch)
    grad_heads = jax.vmap(attend_back)(
        queries,
        key_part,
        values,
        probs,
        grad_attended.reshape(image_count, patch_count, HEADS, -1),
    )
    grad_mixed = to_half(grad_heads.reshape(row_count, 3 * width))
    grad_qkv_full = row_product(normed_half, grad_mixed)
    attn_rows = scatter_attn(
        split_cols(jnp.concatenate([grad_qkv_full, grad_out_full], axis=1), order)
    )
    sent_attn, total_attn = shampoo_rows(attn_rows, left_roots[0], right_roots[0])
    grad_normed = times_transpose(grad_mixed, qkv_full)
    grad_flat, grad_gain_one, grad_shift_one = first_norm_back(grad_normed)
    input_grad = (grad_output + grad_middle + grad_flat + grad_logit[:, None] * vectors[8]).reshape(
        tokens.shape
    )
    mixed_sums = jnp.sum(grad_mixed, axis=0, dtype=full)
    vector_rows = jnp.stack(
        [
            grad_gain_one,
            grad_shift_one,
            grad_gain_two,
            grad_shift_two,
            mixed_sums[:width],
            mixed_sums[2 * width :],
            jnp.sum(grad_branch, axis=0, dtype=full),
            jnp.sum(grad_feed, axis=0, dtype=full),
            jnp.sum(grad_logit[:, None] * flat, axis=0),
        ]
    )
    vector_part = jnp.concatenate([vector_rows, up_bias_grad.reshape(-1, width)], axis=0)
    vector_grad = sum_all(vector_part)

    attn_local = w_attn.shape[0]
    block_index = lax.axis_index("mp") * attn_local + lax.broadcasted_iota(
        jnp.int32, (attn_local,), 0
    )
    attn_rates = jnp.where(
        block_index // row_blocks < 3 * row_blocks, 0.5 * D ** (-0.5), 0.5 * (D // 16) ** (-0.5)
    )
    fc1_rates = jnp.full((w_fc1.shape[0],), 0.5 * D ** (-0.5), full)
    fc2_rates = jnp.full((w_fc2.shape[0],), 0.5 * FF ** (-0.5), full)
    grad_attn, new_left_attn, new_right_attn, new_attn = apply_step(
        w_attn, left_attn, right_attn, sent_attn, total_attn, attn_rates
    )
    grad_fc1, new_left_fc1, new_right_fc1, new_fc1 = apply_step(
        w_fc1, left_fc1, right_fc1, sent_fc1, total_fc1, fc1_rates
    )
    grad_fc2, new_left_fc2, new_right_fc2, new_fc2 = apply_step(
        w_fc2, left_fc2, right_fc2, sent_fc2, total_fc2, fc2_rates
    )
    vector_blocks = vector_grad.reshape(vector_grad.shape[0], -1, BLOCK_VEC)
    block_scale = lax.rsqrt(jnp.mean(vector_blocks * vector_blocks, axis=-1, keepdims=True) + 1e-06)
    new_vectors = vectors - 0.05 * (vector_blocks * block_scale).reshape(vectors.shape)
    return (
        block_out,
        input_grad,
        grad_attn,
        grad_fc1,
        grad_fc2,
        new_left_attn,
        new_right_attn,
        new_left_fc1,
        new_right_fc1,
        new_left_fc2,
        new_right_fc2,
        new_attn,
        new_fc1,
        new_fc2,
        to_half(new_attn),
        to_half(new_fc1),
        to_half(new_fc2),
        vector_grad,
        new_vectors,
    )


def normalized(values):
    centered = values - jnp.mean(values, axis=-1, keepdims=True)
    variance = jnp.mean(centered * centered, axis=-1, keepdims=True)
    scale = lax.rsqrt(variance + 1e-06)
    return centered * scale, scale


def norm_back(grad_hat, hat, scale):
    first = jnp.mean(grad_hat, axis=-1, keepdims=True)
    second = jnp.mean(grad_hat * hat, axis=-1, keepdims=True)
    return scale * (grad_hat - first - hat * second)


def col_sum(values):
    return jnp.sum(values, axis=0, keepdims=True)


def shape(dims, kind=half):
    return jax.ShapeDtypeStruct(dims, kind)


def local_call(kernel, args, outs, scratch=(), in_hbm=(), out_hbm=(), in_smem=(0,), mib=12, micros=1):
    def place_of(index, hbm, smem):
        if index in hbm:
            return pl.BlockSpec(memory_space=pltpu.HBM)
        if index in smem:
            return pl.BlockSpec(memory_space=pltpu.SMEM)
        return pl.BlockSpec(memory_space=pltpu.VMEM)

    moved = sum(v.size * v.dtype.itemsize for v in list(args) + list(outs))
    return pl.pallas_call(
        kernel,
        out_shape=list(outs),
        in_specs=[place_of(i, in_hbm, in_smem) for i in range(len(args))],
        out_specs=[place_of(i, out_hbm, ()) for i in range(len(outs))],
        scratch_shapes=list(scratch),
        compiler_params=pltpu.CompilerParams(vmem_limit_bytes=mib * 2**20),
        cost_estimate=pl.CostEstimate(
            flops=int(micros * 1e9), bytes_accessed=moved, transcendentals=0
        ),
    )(*args)


def gate_of(tokens, vec_ref):
    return jax.nn.sigmoid(jnp.sum(tokens * vec_ref[8:9, :], axis=-1, keepdims=True))


def keep_of(chosen):
    ones = jnp.ones((chosen.shape[0], 128), half)
    return row_product(chosen, ones)[:, :1]


def prepare_kernel(mask_ref, tok_ref, cot_ref, vec_ref, normed_ref, grad_ref, chosen_ref):
    rows = tok_ref.shape[0]
    tokens = tok_ref[...].astype(full)
    hat, _ = normalized(tokens)
    normed_ref[...] = to_half(hat * vec_ref[0:1, :] + vec_ref[1:2, :])
    mask = mask_ref[...].astype(full)
    upper = lax.broadcasted_iota(jnp.int32, (rows, rows), 0) <= lax.broadcasted_iota(
        jnp.int32, (rows, rows), 1
    )
    count = dot32(
        to_half(jnp.broadcast_to(mask, (16, rows))), jnp.where(upper, 1.0, 0.0).astype(half)
    )
    slot = count[0:1, :] - 1.0
    wanted = lax.broadcasted_iota(jnp.int32, (SLOTS, rows), 0).astype(full)
    chosen = jnp.where((slot == wanted) & (mask > 0.0), 1.0, 0.0).astype(half)
    chosen_ref[...] = chosen
    scale = keep_of(chosen) * gate_of(tokens, vec_ref)
    grad_feed = to_half(scale * cot_ref[...].astype(full))
    grad_ref[...] = to_half(dot32(chosen, grad_feed))


def head_parts(values):
    lane = lax.broadcasted_iota(jnp.int32, values.shape, 1)
    first = lane < values.shape[1] // 2
    zero = jnp.zeros_like(values)
    return jnp.where(first, values, zero), jnp.where(first, zero, values)


def copy_all(copies):
    for copy in copies:
        copy.start()
    for copy in copies:
        copy.wait()


def forward_kernel(order, pieces, place_ref, *refs):
    piece_refs, refs = refs[: len(pieces)], refs[len(pieces) :]
    normed_ref, tok_ref, mask_ref, chosen_ref, vec_ref = refs[:5]
    rows_ref, qkv_ref, probs_ref, attended_ref, branch_ref, weights_hbm = refs[5:11]
    weights, probs_all, sems, out_sem, probs_sems = refs[11:]
    z, x, m = place_ref[0], place_ref[1], place_ref[2]
    local, piece = piece_refs[0].shape[1], piece_refs[0].shape[2]
    copies = []
    for ref, (slots, dx, dm) in zip(piece_refs, pieces):
        for index, slot in enumerate(slots):
            row = pl.multiple_of(((z ^ slot) * PAIR + (x ^ dx)) * piece, 16)
            target = weights.at[pl.ds((m ^ dm) * local, local), pl.ds(row, piece), :]
            copies.append(pltpu.make_async_copy(ref.at[index], target, sems.at[len(copies)]))
    copy_all(copies)
    keep_whole = pltpu.make_async_copy(weights, weights_hbm, out_sem)
    keep_whole.start()
    width = normed_ref.shape[1]
    row_blocks = width // order
    normed = normed_ref[...]
    for col in range(3 * row_blocks):
        part = jnp.zeros((normed.shape[0], order), full)
        for row in range(row_blocks):
            part = part + dot32(
                normed[:, row * order : (row + 1) * order], weights[col * row_blocks + row]
            )
        kind, start = col // row_blocks, (col % row_blocks) * order
        if kind != 1:
            bias_row = 4 if kind == 0 else 5
            part = part + vec_ref[bias_row : bias_row + 1, start : start + order]
        qkv_ref[:, col * order : (col + 1) * order] = to_half(part)
    keep_probs = []
    head = width // HEADS
    scale = head ** (-0.5)
    allowed = mask_ref[...] > 0
    for slab in range(width // (2 * head)):
        lanes = slice(slab * 2 * head, (slab + 1) * 2 * head)
        queries = head_parts(qkv_ref[:, lanes])
        keys = qkv_ref[:, width + lanes.start : width + lanes.stop]
        values = head_parts(qkv_ref[:, 2 * width + lanes.start : 2 * width + lanes.stop])
        total = None
        for index in range(2):
            scores = times_transpose(queries[index], keys) * scale
            scores = jnp.where(allowed, scores, masked_score)
            raised = jnp.exp(scores - jnp.max(scores, axis=-1, keepdims=True))
            probs = raised / jnp.sum(raised, axis=-1, keepdims=True)
            probs_all[2 * slab + index] = probs
            part = dot32(to_half(probs), values[index])
            total = part if total is None else total + part
        attended_ref[:, lanes] = to_half(total)
        pair = pl.ds(2 * slab, 2)
        keep_probs.append(
            pltpu.make_async_copy(probs_all.at[pair], probs_ref.at[pair], probs_sems.at[slab])
        )
        keep_probs[-1].start()
    attended = attended_ref[...]
    for col in range(row_blocks):
        part = jnp.zeros((normed.shape[0], order), full)
        for row in range(row_blocks):
            part = part + dot32(
                attended[:, row * order : (row + 1) * order],
                weights[(3 * row_blocks + col) * row_blocks + row],
            )
        lanes = slice(col * order, (col + 1) * order)
        branch_ref[:, lanes] = part + vec_ref[6:7, lanes]
    hat, _ = normalized(tok_ref[...].astype(full) + branch_ref[...])
    second = to_half(hat * vec_ref[2:3, :] + vec_ref[3:4, :])
    rows_ref[...] = to_half(dot32(chosen_ref[...], second))
    keep_whole.wait()
    for copy in keep_probs:
        copy.wait()


def bias_row(m, values, count):
    row = lax.broadcasted_iota(jnp.int32, (count, values.shape[1]), 0)
    return jnp.where(row == m, values, 0.0)


def gelu_parts(values):
    cdf = 0.5 * (1.0 + lax.erf(values * 0.7071067811865476))
    density = jnp.exp(-0.5 * values * values) * 0.3989422804014327
    return values * cdf, cdf + values * density


def hidden_kernel(order, group, pieces, place_ref, *refs):
    piece_refs, refs = refs[: len(pieces)], refs[len(pieces) :]
    row_refs, refs = refs[:group], refs[group:]
    grad_refs, refs = refs[:group], refs[group:]
    vec_ref = refs[0]
    back_refs, refs = refs[1 : 1 + group], refs[1 + group :]
    rows_ref, grads_ref, active_ref, hidden_ref, down_hbm = refs[:5]
    weights, sems, out_sem = refs[5:]
    z, x, m = place_ref[0], place_ref[1], place_ref[2]
    piece = piece_refs[0].shape[2]
    bias = jnp.sum(bias_row(m, vec_ref[9:, :], vec_ref.shape[0] - 9), axis=0, keepdims=True)
    copies = []
    for ref, (slots, dx) in zip(piece_refs, pieces):
        for index, slot in enumerate(slots):
            row = pl.multiple_of(((z ^ slot) * PAIR + (x ^ dx)) * piece, 16)
            target = weights.at[:, pl.ds(row, piece), :]
            copies.append(pltpu.make_async_copy(ref.at[index], target, sems.at[len(copies)]))
    for copy in copies:
        copy.start()
    count = row_refs[0].shape[0]
    for index in range(group):
        rows_ref[index * count : (index + 1) * count, :] = row_refs[index][...]
        grads_ref[index * count : (index + 1) * count, :] = grad_refs[index][...]
    for copy in copies:
        copy.wait()
    local = weights.shape[0] // 2
    keep_down = pltpu.make_async_copy(weights.at[pl.ds(local, local)], down_hbm, out_sem)
    keep_down.start()
    row_blocks = rows_ref.shape[1] // order
    for col in range(local // row_blocks):
        lanes = slice(col * order, (col + 1) * order)
        hidden = bias[:, lanes]
        for row in range(row_blocks):
            hidden = hidden + dot32(
                rows_ref[:, row * order : (row + 1) * order], weights[col * row_blocks + row]
            )
        active, slope = gelu_parts(hidden)
        active_ref[:, lanes] = to_half(active)
        grad = jnp.zeros_like(slope)
        for row in range(row_blocks):
            grad = grad + times_transpose(
                grads_ref[:, row * order : (row + 1) * order],
                weights[local + col * row_blocks + row],
            )
        hidden_ref[:, lanes] = to_half(grad * slope)
    for row in range(row_blocks):
        total = None
        for col in range(local // row_blocks):
            part = times_transpose(
                hidden_ref[:, col * order : (col + 1) * order], weights[col * row_blocks + row]
            )
            total = part if total is None else total + part
        for index in range(group):
            back_refs[index][:, row * order : (row + 1) * order] = to_half(
                total[index * count : (index + 1) * count, :]
            )
    keep_down.wait()


def share_blocks(place_ref, blocks, kept_ref, sent_ref):
    own, x = kept_ref.shape[0], place_ref[1]
    kept_ref[...] = blocks[pl.ds(x * own, own)]
    sent_ref[...] = blocks[pl.ds((1 - x) * own, own)]


def up_grads_kernel(order, place_ref, rows_ref, hidden_ref, kept_ref, sent_ref, bias_ref, blocks):
    row_blocks = rows_ref.shape[1] // order
    for col in range(blocks.shape[0] // row_blocks):
        lanes = slice(col * order, (col + 1) * order)
        for row in range(row_blocks):
            others = slice(row * order, (row + 1) * order)
            blocks[col * row_blocks + row] = to_half(
                row_product(rows_ref[:, others], hidden_ref[:, lanes])
            )
    share_blocks(place_ref, blocks, kept_ref, sent_ref)
    bias_ref[...] = col_sum(hidden_ref[...].astype(full))


def down_grads_kernel(order, group, place_ref, grads_ref, active_ref, down_ref, *refs):
    feed_refs, (kept_ref, sent_ref, blocks) = refs[:group], refs[group:]
    count = grads_ref.shape[0] // group
    row_blocks = grads_ref.shape[1] // order
    col_blocks = down_ref.shape[0] // row_blocks
    for row in range(row_blocks):
        total = None
        for col in range(col_blocks):
            part = dot32(
                active_ref[:, col * order : (col + 1) * order], down_ref[col * row_blocks + row]
            )
            total = part if total is None else total + part
        for index in range(group):
            feed_refs[index][:, row * order : (row + 1) * order] = to_half(
                total[index * count : (index + 1) * count, :]
            )
    for col in range(col_blocks):
        lanes = slice(col * order, (col + 1) * order)
        for row in range(row_blocks):
            others = slice(row * order, (row + 1) * order)
            blocks[col * row_blocks + row] = to_half(
                row_product(active_ref[:, lanes], grads_ref[:, others])
            )
    share_blocks(place_ref, blocks, kept_ref, sent_ref)


def backward_kernel(order, group, place_ref, *refs):
    back_refs, refs = refs[:group], refs[group:]
    chosen_ref, tok_ref, cot_ref, branch_ref, vec_ref = refs[:5]
    qkv_ref, probs_ref, attended_ref, normed_ref, weights_hbm = refs[5:10]
    kept_ref, sent_ref, mixed_ref, middle_ref, sums_ref = refs[10:15]
    weights, left, right, grad_attended, probs_all, sem, probs_sem = refs[15:]
    width = tok_ref.shape[1]
    row_blocks = width // order
    local = weights.shape[0]
    fetch = pltpu.make_async_copy(weights_hbm.at[pl.ds(3 * local, local)], weights, sem)
    fetch.start()
    fetch_probs = pltpu.make_async_copy(probs_ref, probs_all, probs_sem)
    fetch_probs.start()
    chosen = chosen_ref[...]
    arrived = back_refs[0][...].astype(full)
    for ref in back_refs[1:]:
        arrived = arrived + ref[...].astype(full)
    high = to_half(arrived)
    low = to_half(arrived - high.astype(full))
    grad_second = row_product(chosen, high) + row_product(chosen, low)
    tokens = tok_ref[...].astype(full)
    hat, scale = normalized(tokens + branch_ref[...])
    grad_middle = norm_back(grad_second * vec_ref[2:3, :], hat, scale)
    middle_ref[...] = grad_middle
    change = keep_of(chosen) * gate_of(tokens, vec_ref) * cot_ref[...].astype(full)
    grad_branch = to_half(change + grad_middle)
    sums_ref[0:1, :] = col_sum(grad_second * hat)
    sums_ref[1:2, :] = col_sum(grad_second)
    sums_ref[2:3, :] = col_sum(grad_branch.astype(full))
    sums_ref[3:4, :] = col_sum(to_half(change).astype(full))
    left[0] = normed_ref[...]
    left[1] = attended_ref[...]
    right[3] = grad_branch
    fetch.wait()
    for row in range(row_blocks):
        total = None
        for col in range(row_blocks):
            part = times_transpose(
                grad_branch[:, col * order : (col + 1) * order], weights[col * row_blocks + row]
            )
            total = part if total is None else total + part
        grad_attended[:, row * order : (row + 1) * order] = to_half(total)
    fetch_probs.wait()
    head = width // HEADS
    factor = head ** (-0.5)
    for slab in range(width // (2 * head)):
        start, stop = slab * 2 * head, (slab + 1) * 2 * head
        queries = head_parts(qkv_ref[:, start:stop])
        key_pair = qkv_ref[:, width + start : width + stop]
        keys = head_parts(key_pair)
        values = qkv_ref[:, 2 * width + start : 2 * width + stop]
        grads = head_parts(grad_attended[:, start:stop])
        sums = [None] * 3
        for index in range(2):
            probs = probs_all[2 * slab + index]
            grad_probs = times_transpose(grads[index], values)
            inner = jnp.sum(probs * grad_probs, axis=-1, keepdims=True)
            grad_scores = to_half(probs * (grad_probs - inner))
            parts = (
                dot32(grad_scores, keys[index]),
                row_product(grad_scores, queries[index]),
                row_product(to_half(probs), grads[index]),
            )
            sums = [p if s is None else s + p for s, p in zip(sums, parts)]
        right[0, :, start:stop] = to_half(sums[0] * factor)
        right[1, :, start:stop] = to_half(sums[1] * factor)
        right[2, :, start:stop] = to_half(sums[2])
    for kind in range(3):
        mixed_ref[:, kind * width : (kind + 1) * width] = right[kind]
    core = place_ref[3]
    for high_part in range(kept_ref.shape[0]):
        for target, low_part in ((kept_ref, core), (sent_ref, 1 - core)):
            kind = high_part * PAIR + low_part
            rows = left[kind // 3]
            cols = right[kind]
            for col in range(row_blocks):
                for row in range(row_blocks):
                    target[high_part, col * row_blocks + row] = to_half(
                        row_product(
                            rows[:, row * order : (row + 1) * order],
                            cols[:, col * order : (col + 1) * order],
                        )
                    )


def input_kernel(order, group, *refs):
    feed_refs, refs = refs[:group], refs[group:]
    mixed_ref, middle_ref, tok_ref, cot_ref, chosen_ref, vec_ref, branch_ref, weights_hbm = refs[:8]
    out_ref, grad_ref, sums_ref, weights, sem = refs[8:]
    width = tok_ref.shape[1]
    row_blocks = width // order
    fetch = pltpu.make_async_copy(weights_hbm.at[pl.ds(0, weights.shape[0])], weights, sem)
    fetch.start()
    patches = out_ref.shape[0]
    chosen = chosen_ref[...]
    tokens = tok_ref[...].astype(full)
    cotangent = cot_ref[...].astype(full)
    arrived = feed_refs[0][...].astype(full)
    for ref in feed_refs[1:]:
        arrived = arrived + ref[...].astype(full)
    high = to_half(arrived)
    low = to_half(arrived - high.astype(full))
    feed = row_product(chosen, high) + row_product(chosen, low) + vec_ref[7:8, :]
    change = branch_ref[...] + feed
    gate = gate_of(tokens, vec_ref)
    keep = keep_of(chosen)
    out_ref[...] = to_half(tokens + keep * gate * change)[:patches]
    logit = keep * gate * (1.0 - gate) * jnp.sum(cotangent * change, axis=-1, keepdims=True)
    base = cotangent + middle_ref[...] + logit * vec_ref[8:9, :]
    sums_ref[4:5, :] = col_sum(logit * tokens)
    sums_ref[2:3, :] = col_sum(mixed_ref[:, :width].astype(full))
    sums_ref[3:4, :] = col_sum(mixed_ref[:, 2 * width :].astype(full))
    hat, scale = normalized(tokens)
    fetch.wait()
    parts = []
    for row in range(row_blocks):
        total = None
        for col in range(3 * row_blocks):
            part = times_transpose(
                mixed_ref[:, col * order : (col + 1) * order], weights[col * row_blocks + row]
            )
            total = part if total is None else total + part
        parts.append(total)
    grad_normed = jnp.concatenate(parts, axis=1)
    sums_ref[0:1, :] = col_sum(grad_normed * hat)
    sums_ref[1:2, :] = col_sum(grad_normed)
    grad = base + norm_back(grad_normed * vec_ref[0:1, :], hat, scale)
    grad_ref[...] = grad[:patches]


def core_sum_kernel(place_ref, kept_ref, came_ref, *out_refs):
    x, m = place_ref[1], place_ref[2]
    own = kept_ref.shape[1] // PAIR
    for index, out_ref in enumerate(out_refs):
        dy, dx = index // PAIR, index % PAIR
        high = (m // PAIR) ^ dy
        for block in range(own):
            at = (x ^ dx) * own + block
            out_ref[block] = to_half(
                kept_ref[high, at].astype(full) + came_ref[high, at].astype(full)
            )


def row_sum_kernel(count, place_ref, *refs):
    ins, outs = refs[:count], refs[count:]
    rows = outs[0].shape[1]
    for slot, out_ref in enumerate(outs):
        start = pl.multiple_of((place_ref[0] ^ slot) * rows, 16)
        for block in range(out_ref.shape[0]):
            total = ins[0][block, pl.ds(start, rows), :].astype(full)
            for ref in ins[1:]:
                total = total + ref[block, pl.ds(start, rows), :].astype(full)
            out_ref[block] = to_half(total)


def whole_step_kernel(count, first, place_ref, *refs):
    grad_refs, refs = refs[:count], refs[count:]
    root_refs, refs = refs[:count], refs[count:]
    kept_ref, sent_ref, grads, rights, lefts, terms, found = refs
    z, x = place_ref[0], place_ref[1]
    blocks, rows, order = grad_refs[0].shape
    for slot in range(count):
        start = pl.multiple_of((z ^ slot) * rows, 16)
        for block in range(blocks):
            grads[block, pl.ds(start, rows), :] = grad_refs[slot][block]
            rights[block, pl.ds(start, rows), :] = root_refs[slot][block]
            lefts[block, pl.ds(start, rows), :] = root_refs[slot][first + block]
    mine = pl.multiple_of(z * rows, 16)
    for block in range(blocks):
        whole = grads[block]
        own = grad_refs[0][block]
        step = to_half(dot32(lefts[block], whole))
        step = dot32(step, rights[block])
        mean = jnp.mean(jnp.mean(step * step, axis=1, keepdims=True), axis=0, keepdims=True)
        terms[0] = row_product(whole, whole)
        terms[1] = step * lax.rsqrt(mean + 1e-06)
        found[0] = own.astype(full)
        found[1] = times_transpose(own, whole)
        found[2] = terms[0, pl.ds(mine, rows), :]
        found[3] = terms[1, pl.ds(mine, rows), :]
        half_rows = rows // PAIR
        for target, part in ((kept_ref, x), (sent_ref, 1 - x)):
            start = pl.multiple_of(part * half_rows, 16)
            for kind in range(4):
                target[kind, block] = to_half(found[kind, pl.ds(start, half_rows), :])


def step_kernel(count, first, place_ref, *refs):
    grad_refs, refs = refs[:count], refs[count:]
    right_refs, refs = refs[:count], refs[count:]
    left_ref, kept_ref, sent_ref, square_ref, grads, rights, terms, found = refs
    z, x = place_ref[0], place_ref[1]
    blocks, rows, order = grad_refs[0].shape
    for slot in range(count):
        start = pl.multiple_of((z ^ slot) * rows, 16)
        for block in range(blocks):
            grads[block, pl.ds(start, rows), :] = grad_refs[slot][block]
            rights[block, pl.ds(start, rows), :] = right_refs[slot][first + block]
    mine = pl.multiple_of(z * rows, 16)
    square_ref[...] = jnp.zeros_like(square_ref)
    for block in range(blocks):
        whole = grads[block]
        own = grad_refs[0][block]
        step = to_half(dot32(left_ref[first + block], whole))
        step = dot32(step, rights[block])
        square_ref[block : block + 1, :] = jnp.broadcast_to(
            jnp.sum(jnp.sum(step * step, axis=1, keepdims=True), axis=0, keepdims=True), (1, 128)
        )
        terms[...] = row_product(whole, whole)
        found[0] = own.astype(full)
        found[1] = times_transpose(own, whole)
        found[2] = terms[pl.ds(mine, rows), :]
        found[3] = step
        half_rows = rows // PAIR
        for target, part in ((kept_ref, x), (sent_ref, 1 - x)):
            start = pl.multiple_of(part * half_rows, 16)
            for kind in range(4):
                target[kind, block] = to_half(found[kind, pl.ds(start, half_rows), :])


def apply_kernel(
    first, order, rates, place_ref, weight_ref, left_ref, right_ref, kept_ref, came_ref, *refs
):
    total_ref = refs[0] if len(refs) == 6 else None
    grad_ref, new_left_ref, new_right_ref, new_ref, half_ref = refs[-5:]
    x, m = place_ref[1], place_ref[2]
    local = weight_ref.shape[0]
    own = local // PAIR
    for side, ref in ((0, kept_ref), (1, came_ref)):
        for block in range(own):
            at = (x ^ side) * own + block
            index = first + block
            rate = jnp.where(m * local + at < rates[0], rates[1], rates[2])
            scale = 1.0
            if total_ref is not None:
                scale = lax.rsqrt(total_ref[side, index : index + 1, 0:1] / (order * order) + 1e-06)
            grad_ref[at] = ref[0, index].astype(full)
            new_left_ref[at] = 0.95 * left_ref[at] + 0.05 * ref[1, index].astype(full)
            new_right_ref[at] = 0.95 * right_ref[at] + 0.05 * ref[2, index].astype(full)
            new = weight_ref[at] - (rate * scale) * ref[3, index].astype(full)
            new_ref[at] = new
            half_ref[at] = to_half(new)


def vector_part_kernel(place_ref, one_ref, two_ref, bias_ref, out_ref):
    out_ref[0:2, :] = one_ref[0:2, :]
    out_ref[2:4, :] = two_ref[0:2, :]
    out_ref[4:6, :] = one_ref[2:4, :]
    out_ref[6:8, :] = two_ref[2:4, :]
    out_ref[8:9, :] = one_ref[4:5, :]
    out_ref[9:, :] = bias_row(place_ref[2], bias_ref[...], out_ref.shape[0] - 9)


def vector_step_kernel(vec_ref, *refs):
    part_refs, (grad_ref, new_ref) = refs[:-2], refs[-2:]
    grad = part_refs[0][...]
    for ref in part_refs[1:]:
        grad = grad + ref[...]
    grad_ref[...] = grad
    for start in range(0, grad.shape[1], BLOCK_VEC):
        lanes = slice(start, start + BLOCK_VEC)
        block = grad[:, lanes]
        scale = lax.rsqrt(jnp.mean(block * block, axis=-1, keepdims=True) + 1e-06)
        new_ref[:, lanes] = vec_ref[:, lanes] - 0.05 * (block * scale)


def weights_kernel(attn_ref, up_ref, down_ref, attn_out, feed_out):
    attn_out[...] = to_half(attn_ref[...])
    local = up_ref.shape[0]
    feed_out[:local] = to_half(up_ref[...])
    feed_out[local:] = to_half(down_ref[...])


def roots_kernel(place_ref, *refs):
    ins, (kept_ref, sent_ref) = refs[:6], refs[6:]
    x = place_ref[1]
    own = ins[0].shape[0] // PAIR
    for index, ref in enumerate(ins):
        kept_ref[index] = to_half(ref[pl.ds(x * own, own)])
        sent_ref[index] = to_half(ref[pl.ds((1 - x) * own, own)])


def roots_join_kernel(place_ref, kept_ref, came_ref, left_ref, right_ref):
    x = place_ref[1]
    kinds, own, piece, order = kept_ref.shape
    for index in range(kinds):
        for block in range(own):
            at = (index % 3) * own + block
            targets = [(left_ref, at)] if index < 3 else [(right_ref, at)]
            if index == 0:
                targets.append((right_ref, 3 * own + block))
            for target, place in targets:
                for side, ref in ((0, kept_ref), (1, came_ref)):
                    start = pl.multiple_of((x ^ side) * piece, 16)
                    target[place, pl.ds(start, piece), :] = ref[index, block]


def move(values, dp_mask, mp_mask):
    dp, mp = lax.axis_size("dp"), lax.axis_size("mp")
    if mp_mask == 0:
        return lax.ppermute(values, "dp", [(s, s ^ dp_mask) for s in range(dp)])
    if dp_mask == 0:
        return lax.ppermute(values, "mp", [(s, s ^ mp_mask) for s in range(mp)])
    mask = dp_mask * mp + mp_mask
    return lax.ppermute(values, ("dp", "mp"), [(s, s ^ mask) for s in range(dp * mp)])


def phase(*values):
    return lax.optimization_barrier(values)


def after(values, *others):
    return lax.optimization_barrier((values,) + others)[0]


def body_lines(
    tokens,
    keep_mask,
    cotangent,
    w_attn,
    w_fc1,
    w_fc2,
    vectors,
    left_attn,
    right_attn,
    root_left_attn,
    root_right_attn,
    left_fc1,
    right_fc1,
    root_left_fc1,
    root_right_fc1,
    left_fc2,
    right_fc2,
    root_left_fc2,
    root_right_fc2,
):
    _, patches, width = tokens.shape
    local, piece, order = w_attn.shape
    z_count, group = high_size("dp"), lax.axis_size("mp")
    row_blocks = width // order
    own = local // PAIR
    rows = patches
    line_rows = order // z_count
    total_rows = group * SLOTS
    hidden_width = local // row_blocks * order
    heads = (HEADS, rows, rows)
    others = range(1, group)
    lines = range(1, z_count)
    tok, cot, mask = tokens[0], cotangent[0], keep_mask
    line, member = lax.axis_index("dp"), lax.axis_index("mp")
    place = jnp.stack([line >> 1, line & 1, member, member & 1]).astype(jnp.int32)
    w_attn_first, place = phase(w_attn, place)

    attn_half, feed_half = local_call(
        weights_kernel,
        (w_attn_first, w_fc1, w_fc2),
        (shape((local, piece, order)), shape((2 * local, piece, order))),
        in_smem=(),
    )
    line_came = [move(attn_half, k * PAIR, 0) for k in lines]
    plane = [(dx, high * PAIR) for high in range(group // PAIR) for dx in range(PAIR)]
    first = attn_half[None]
    first_pieces = [first] + [move(first, dx, dm) for dx, dm in plane[1:]]
    root_kept, root_sent = local_call(
        roots_kernel,
        (
            place,
            root_left_attn,
            root_left_fc1,
            root_left_fc2,
            root_right_attn,
            root_right_fc1,
            root_right_fc2,
        ),
        (shape((6, own, piece, order)),) * 2,
    )
    root_came = move(root_sent, 1, 0)
    second = jnp.stack(line_came)
    second, first_pieces, root_came, feed_half = phase(
        second, first_pieces, root_came, feed_half
    )

    feed_far, feed_near = move(feed_half, 2 * PAIR, 0), move(feed_half, PAIR, 0)
    second_pieces = [second] + [move(second, dx, dm) for dx, dm in plane[1:]]
    pieces, piece_info = [], []
    for slots, found in (((0,), first_pieces), (tuple(lines), second_pieces)):
        for (dx, dm), part in zip(plane, found):
            pieces += [part, move(part, 0, 1)]
            piece_info += [(slots, dx, dm), (slots, dx, dm + 1)]
    normed, grad_sent, chosen = local_call(
        prepare_kernel,
        (mask, tok, cot, vectors),
        (shape((rows, width)), shape((SLOTS, width)), shape((SLOTS, rows))),
        in_smem=(),
        micros=1.5,
    )
    feed_near = jnp.stack([feed_half, feed_near])
    pieces, feed_near, feed_far, normed, grad_sent, chosen = phase(
        pieces, feed_near, feed_far, normed, grad_sent, chosen
    )

    near_came = move(feed_near, 1, 0)
    feed_last = move(feed_far, PAIR, 0)
    group_grads = [grad_sent] + [move(grad_sent, 0, k) for k in others]
    count = len(pieces)
    rows_sent, qkv, probs, attended, branch, weights = local_call(
        lambda *refs: forward_kernel(order, piece_info, *refs),
        (place, *pieces, normed, tok, mask, chosen, vectors),
        (
            shape((SLOTS, width)),
            shape((rows, 3 * width)),
            shape(heads, full),
            shape((rows, width)),
            shape((rows, width), full),
            shape((group * local, order, order)),
        ),
        scratch=(
            pltpu.VMEM((group * local, order, order), half),
            pltpu.VMEM(heads, full),
            pltpu.SemaphoreType.DMA((count * z_count // 2,)),
            pltpu.SemaphoreType.DMA(()),
            pltpu.SemaphoreType.DMA((HEADS // 2,)),
        ),
        in_hbm=range(1, 1 + count),
        out_hbm=(2, 5),
        micros=8,
    )
    feed_far = jnp.stack([feed_far, feed_last])
    rows_sent, near_came, feed_far, group_grads = phase(
        rows_sent, near_came, feed_far, group_grads
    )

    group_rows = [rows_sent] + [move(rows_sent, 0, k) for k in others]
    far_came = move(feed_far, 1, 0)
    left_roots, right_root = local_call(
        roots_join_kernel,
        (place, root_kept, root_came),
        (shape((3 * own, PAIR * piece, order)), shape((4 * own, PAIR * piece, order))),
    )
    roots_far = move(right_root, 2 * PAIR, 0)
    roots_near = move(right_root, PAIR, 0)
    group_rows, far_came, roots_far, roots_near = phase(
        group_rows, far_came, roots_far, roots_near
    )

    feed_pieces = [feed_near, near_came, feed_far, far_came]
    near_slots, far_slots = (0, 1), (2, 3)
    feed_info = [(near_slots, 0), (near_slots, 1), (far_slots, 0), (far_slots, 1)]
    count = len(feed_pieces)
    outs = local_call(
        lambda *refs: hidden_kernel(order, group, feed_info, *refs),
        (place, *feed_pieces, *group_rows, *group_grads, vectors),
        (shape((SLOTS, width)),) * group
        + (shape((total_rows, width)),) * 2
        + (shape((total_rows, hidden_width)),) * 2
        + (shape((local, order, order)),),
        scratch=(
            pltpu.VMEM((2 * local, order, order), half),
            pltpu.SemaphoreType.DMA((PAIR * z_count,)),
            pltpu.SemaphoreType.DMA(()),
        ),
        in_hbm=range(1, 1 + count),
        out_hbm=(group + 4,),
        micros=5,
    )
    back, (all_rows, all_grads, active, grad_hidden, down) = outs[:group], outs[group:]
    back, all_rows = phase(back, all_rows)

    back = [back[0]] + [move(back[k], 0, k) for k in others]
    roots_last = move(roots_far, PAIR, 0)
    right_roots = [right_root, roots_near, roots_far, roots_last]
    up_kept, up_sent, bias_sums = local_call(
        lambda *refs: up_grads_kernel(order, *refs),
        (place, all_rows, grad_hidden),
        (shape((own, order, order)),) * 2 + (shape((1, hidden_width), full),),
        scratch=(pltpu.VMEM((local, order, order), half),),
        micros=1,
    )
    up_came = move(up_sent, 1, 0)
    outs = local_call(
        lambda *refs: down_grads_kernel(order, group, *refs),
        (place, all_grads, active, down),
        (shape((SLOTS, width)),) * group + (shape((own, order, order)),) * 2,
        scratch=(pltpu.VMEM((local, order, order), half),),
        micros=2,
    )
    feed, down_kept, down_sent = outs[:group], outs[group], outs[group + 1]
    back, up_came, down_sent, feed, roots_last = phase(back, up_came, down_sent, feed, roots_last)

    def split_rows_of(parts):
        return local_call(
            lambda *refs: row_sum_kernel(len(parts), *refs),
            (place, *parts),
            (shape((own, line_rows, order)),) * z_count,
        )

    def total_of(split):
        parts = [split[0]] + [move(split[k], k * PAIR, 0) for k in lines]
        total = parts[0].astype(full)
        for part in parts[1:]:
            total = total + part.astype(full)
        return to_half(total)

    up_rows = total_of(split_rows_of([up_kept, up_came]))
    down_came = move(down_sent, 1, 0)
    feed = [feed[0]] + [move(feed[k], 0, k) for k in others]
    attn_kept, attn_sent, mixed, grad_middle, sums_two = local_call(
        lambda *refs: backward_kernel(order, group, *refs),
        (place, *back, chosen, tok, cot, branch, vectors, qkv, probs, attended, normed, weights),
        (
            shape((group // PAIR, local, order, order)),
            shape((group // PAIR, local, order, order)),
            shape((rows, 3 * width)),
            shape((rows, width), full),
            shape((4, width), full),
        ),
        scratch=(
            pltpu.VMEM((local, order, order), half),
            pltpu.VMEM((2, rows, width), half),
            pltpu.VMEM((4, rows, width), half),
            pltpu.VMEM((rows, width), half),
            pltpu.VMEM(heads, full),
            pltpu.SemaphoreType.DMA(()),
            pltpu.SemaphoreType.DMA(()),
        ),
        in_hbm=(1 + group + 6, 1 + group + 9),
        micros=8,
    )
    attn_sent, up_rows, down_came, feed = phase(attn_sent, up_rows, down_came, feed)

    attn_came = move(attn_sent, 0, 1)
    block_out, input_grad, sums_one = local_call(
        lambda *refs: input_kernel(order, group, *refs),
        (*feed, mixed, grad_middle, tok, cot, chosen, vectors, branch, weights),
        (
            shape((patches, width)),
            shape((patches, width), full),
            shape((5, width), full),
        ),
        scratch=(
            pltpu.VMEM((3 * local, order, order), half),
            pltpu.SemaphoreType.DMA(()),
        ),
        in_hbm=(group + 7,),
        in_smem=(),
        micros=4,
    )
    (vector_sum,) = local_call(
        vector_part_kernel,
        (place, sums_one, sums_two, bias_sums),
        (shape(vectors.shape, full),),
    )
    down_split = split_rows_of([down_kept, down_came])
    core_parts = local_call(
        core_sum_kernel,
        (place, attn_kept, attn_came),
        (shape((own, order, order)),) * group,
    )
    core_parts, down_split, vector_sum = phase(core_parts, down_split, vector_sum)

    attn_parts = [core_parts[0]]
    for (dx, dm), part in zip(plane[1:], core_parts[1:]):
        attn_parts.append(move(part, dx, dm))
    up_near, up_far = move(up_rows, PAIR, 0), move(up_rows, 2 * PAIR, 0)
    down_rows = total_of(down_split)
    up_last = move(up_far, PAIR, 0)
    vector_sum = vector_sum + move(vector_sum, 0, 1)
    attn_split = split_rows_of(attn_parts)
    up_parts = [up_rows, up_near, up_far, up_last]
    attn_split, up_parts, down_rows, vector_sum = phase(
        attn_split, up_parts, down_rows, vector_sum
    )

    def step_of(parts, first):
        return local_call(
            lambda *refs: step_kernel(z_count, first, *refs),
            (place, *parts, *right_roots, left_roots),
            (shape((4, own, line_rows // PAIR, order)),) * 2 + (shape((8, 128), full),),
            scratch=(
                pltpu.VMEM((own, order, order), half),
                pltpu.VMEM((own, order, order), half),
                pltpu.VMEM((order, order), full),
                pltpu.VMEM((4, line_rows, order), full),
            ),
            micros=2,
        )

    def line_total(values):
        total = values
        for k in lines:
            total = total + move(values, k * PAIR, 0)
        return total

    attn_rows = total_of(attn_split)
    down_near, down_far = move(down_rows, PAIR, 0), move(down_rows, 2 * PAIR, 0)
    up_mine, up_sent, up_squares = step_of(up_parts, own)
    up_squares = jnp.stack([up_squares, move(up_squares, 1, 0)])
    up_found = move(up_sent, 1, 0)
    for dm in range(PAIR, group, PAIR):
        vector_sum = vector_sum + move(vector_sum, 0, dm)
    attn_rows, down_near, down_far, up_squares, up_found, vector_sum = phase(
        attn_rows, down_near, down_far, up_squares, up_found, vector_sum
    )

    attn_near, attn_far = move(attn_rows, PAIR, 0), move(attn_rows, 2 * PAIR, 0)
    down_last = move(down_far, PAIR, 0)
    attn_last = move(attn_far, PAIR, 0)
    vector_sum = vector_sum + move(vector_sum, 1, 0)
    up_total = line_total(up_squares)
    attn_near, attn_far, attn_last, down_last, vector_sum, up_total = phase(
        attn_near, attn_far, attn_last, down_last, vector_sum, up_total
    )

    kept, sent = local_call(
        lambda *refs: whole_step_kernel(z_count, 3 * own, *refs),
        (place, attn_rows, attn_near, attn_far, attn_last, *right_roots),
        (shape((4, own, line_rows // PAIR, order)),) * 2,
        scratch=(pltpu.VMEM((own, order, order), half),) * 3
        + (pltpu.VMEM((2, order, order), full), pltpu.VMEM((4, line_rows, order), full)),
        micros=2,
    )
    down_mine, down_sent, down_squares = step_of(
        [down_rows, down_near, down_far, down_last], 2 * own
    )
    down_squares = jnp.stack([down_squares, move(down_squares, 1, 0)])
    came = move(after(sent, down_squares), 1, 0)
    down_found = move(after(down_sent, down_squares), 1, 0)
    vector_parts = [vector_sum] + [move(vector_sum, k * PAIR, 0) for k in lines]
    down_total = line_total(down_squares)

    def apply(first, rates, weight, left, right, found):
        stat = shape(weight.shape, full)
        return local_call(
            lambda *refs: apply_kernel(first, order, rates, *refs),
            (place, weight, left, right, *found),
            (stat,) * 4 + (shape(weight.shape),),
        )

    attn_rates = (3 * row_blocks * row_blocks, 0.5 * D ** (-0.5), 0.5 * (D // 16) ** (-0.5))
    fc1_rates = (0, 0.0, 0.5 * D ** (-0.5))
    fc2_rates = (0, 0.0, 0.5 * FF ** (-0.5))
    vector_grad, new_vectors = local_call(
        vector_step_kernel,
        (vectors, *vector_parts),
        (shape(vectors.shape, full),) * 2,
        in_smem=(),
    )
    done_attn = apply(0, attn_rates, w_attn, left_attn, right_attn, (kept, came))
    done_fc1 = apply(0, fc1_rates, w_fc1, left_fc1, right_fc1, (up_mine, up_found, up_total))
    done_fc2 = apply(
        0, fc2_rates, w_fc2, left_fc2, right_fc2, (down_mine, down_found, down_total)
    )
    return (
        block_out[None],
        input_grad[None],
        done_attn[0],
        done_fc1[0],
        done_fc2[0],
        *done_attn[1:3],
        *done_fc1[1:3],
        *done_fc2[1:3],
        done_attn[3],
        done_fc1[3],
        done_fc2[3],
        done_attn[4],
        done_fc1[4],
        done_fc2[4],
        vector_grad,
        new_vectors,
    )


def body(tokens, keep_mask, cotangent, w_attn, *rest):
    local, piece, _ = w_attn.shape
    group = lax.axis_size("mp")
    tiled = piece % 16 == 0 and tokens.shape[0] == 1 and local % (2 * PAIR) == 0
    tiled = tiled and group == 4 and high_size("dp") == 4
    chosen_body = body_lines if tiled else body_plain
    return chosen_body(tokens, keep_mask, cotangent, w_attn, *rest)


def solution(mesh):
    rows = P(("dp", "mp"), None, None)
    blocks = P("mp", "dp", None)
    return jax.shard_map(
        body,
        mesh=mesh,
        in_specs=(rows, P(("dp", "mp"), None), rows)
        + (blocks,) * 3
        + (P(),)
        + (blocks,) * 12,
        out_specs=(rows, rows) + (blocks,) * 15 + (P(), P()),
        check_vma=False,
    )
```

```python
import jax
import jax.numpy as jnp
from jax import lax
from jax.experimental import pallas as pl
from jax.experimental.pallas import tpu as pltpu
from jax.sharding import PartitionSpec as P

D = 768
HEADS = 12
FF = 3072
BLOCK_VEC = 128
KEPT_MOST = 157
SLOTS = 160
PAIR = 2

highest = lax.Precision.HIGHEST
masked_score = -1e30
half = jnp.bfloat16
full = jnp.float32


def to_half(values):
    return values.astype(half)


def layer_norm(values, gain_row, shift_row):
    centered = values - jnp.mean(values, axis=-1, keepdims=True)
    variance = jnp.mean(centered * centered, axis=-1, keepdims=True)
    return centered * lax.rsqrt(variance + 1e-06) * gain_row + shift_row


def exact_gelu(values):
    return jax.nn.gelu(values, approximate=False)


def dot32(left, right):
    return jnp.dot(left, right, preferred_element_type=full)


def row_product(left_half, right_half):
    return lax.dot_general(
        left_half, right_half, (((0,), (0,)), ((), ())), preferred_element_type=full
    )


def times_transpose(left_half, right_half):
    return lax.dot_general(
        left_half, right_half, (((1,), (1,)), ((), ())), preferred_element_type=full
    )


def swap_low(values, axis):
    count = lax.axis_size(axis)
    return lax.ppermute(values, axis, [(s, s ^ 1) for s in range(count)])


def shift_high(values, axis, step):
    count = lax.axis_size(axis)
    return lax.ppermute(values, axis, [(s, (s + step * PAIR) % count) for s in range(count)])


def high_index(axis):
    return lax.axis_index(axis) // PAIR


def low_index(axis):
    return lax.axis_index(axis) % PAIR


def high_size(axis):
    return lax.axis_size(axis) // PAIR


def pick(values, index, dim=0):
    return lax.dynamic_index_in_dim(values, index, dim, keepdims=False)


def ordered(pieces, index):
    count = len(pieces)
    if count == 2:
        first = index == 0
        return jnp.stack(
            [jnp.where(first, pieces[0], pieces[1]), jnp.where(first, pieces[1], pieces[0])]
        )
    return lax.dynamic_slice_in_dim(jnp.stack(pieces + pieces), (count - index) % count, count, 0)


def gather_low(values, axis):
    return ordered([values, swap_low(values, axis)], low_index(axis))


def gather_high(values, axis):
    count = high_size(axis)
    pieces = [values] + [shift_high(values, axis, -k) for k in range(1, count)]
    return ordered(pieces, high_index(axis))


def scatter_low(values, axis):
    low = low_index(axis)
    arrived = swap_low(pick(values, 1 - low), axis)
    return pick(values, low).astype(full) + arrived.astype(full)


def scatter_high(values, axis):
    count, high = high_size(axis), high_index(axis)
    total = pick(values, high).astype(full)
    for k in range(1, count):
        total = total + shift_high(pick(values, (high + k) % count), axis, k).astype(full)
    return total


def attend(queries, key_part, values, allowed):
    scale_factor = queries.shape[-1] ** (-0.5)
    scores = jnp.einsum("qhd,khd->hqk", queries, key_part, preferred_element_type=full)
    scores = jnp.where(allowed[None, None, :] > 0, scores * scale_factor, masked_score)
    shifted = jnp.exp(scores - jnp.max(scores, axis=-1, keepdims=True))
    probs = shifted / jnp.sum(shifted, axis=-1, keepdims=True)
    attended = jnp.einsum("hqk,khd->qhd", to_half(probs), values, preferred_element_type=full)
    return (to_half(attended), probs)


def attend_back(queries, key_part, values, probs, grad_attended):
    scale_factor = queries.shape[-1] ** (-0.5)
    grad_values = jnp.einsum(
        "hqk,qhd->khd", to_half(probs), grad_attended, preferred_element_type=full
    )
    grad_probs = jnp.einsum("qhd,khd->hqk", grad_attended, values, preferred_element_type=full)
    row_inner = jnp.sum(probs * grad_probs, axis=-1, keepdims=True)
    grad_scores = to_half(probs * (grad_probs - row_inner))
    grad_queries = (
        jnp.einsum("hqk,khd->qhd", grad_scores, key_part, preferred_element_type=full)
        * scale_factor
    )
    grad_keys = (
        jnp.einsum("hqk,qhd->khd", grad_scores, queries, preferred_element_type=full)
        * scale_factor
    )
    return jnp.stack([grad_queries, grad_keys, grad_values], axis=1)


def gather_group(rows):
    pair = jnp.stack([rows, swap_low(rows, "mp")])
    pieces = [pair] + [shift_high(pair, "mp", -k) for k in range(1, high_size("mp"))]
    return jnp.concatenate(pieces, axis=0).reshape(-1, rows.shape[-1])


def scatter_group(rows, row_count):
    pieces = rows.reshape(high_size("mp"), PAIR, row_count, rows.shape[-1])
    pairs = pieces[:, 0].astype(full) + swap_low(pieces[:, 1], "mp").astype(full)
    total = pairs[0]
    for k in range(1, high_size("mp")):
        total = total + shift_high(to_half(pairs[k]), "mp", k).astype(full)
    return total


def halves(values, dim):
    count = values.shape[dim] // 2
    return (
        lax.slice_in_dim(values, 0, count, axis=dim),
        lax.slice_in_dim(values, count, 2 * count, axis=dim),
    )


def gather_attn(blocks):
    local, piece, order = blocks.shape
    lines = gather_high(to_half(blocks), "dp")
    first, second = halves(lines, 0)
    first = gather_high(gather_low(first, "dp"), "mp")
    second = gather_low(gather_high(second, "mp"), "dp")
    both = jnp.concatenate([first, second.swapaxes(0, 1)], axis=2)
    both = gather_low(both, "mp")
    row_blocks = D // order
    both = both.transpose(1, 0, 4, 3, 2, 5, 6)
    both = both.reshape(-1, row_blocks, order, order)
    return both.transpose(1, 2, 0, 3).reshape(D, -1)


def gather_fc(blocks):
    lines = gather_low(gather_high(to_half(blocks), "dp"), "dp")
    lines = lines.transpose(2, 1, 0, 3, 4)
    return lines.reshape(blocks.shape[0], -1, blocks.shape[2])


def split_cols(matrix, order):
    rows, cols = matrix.shape
    return (
        matrix.reshape(rows // order, order, cols // order, order)
        .transpose(2, 0, 1, 3)
        .reshape(-1, order, order)
    )


def split_rows(matrix, order):
    rows, cols = matrix.shape
    return (
        matrix.reshape(rows // order, order, cols // order, order)
        .transpose(0, 2, 1, 3)
        .reshape(-1, order, order)
    )


def join_cols(blocks, row_blocks):
    count, order, _ = blocks.shape
    return (
        blocks.reshape(-1, row_blocks, order, order)
        .transpose(1, 2, 0, 3)
        .reshape(row_blocks * order, -1)
    )


def join_rows(blocks, col_blocks):
    count, order, _ = blocks.shape
    return (
        blocks.reshape(-1, col_blocks, order, order)
        .transpose(0, 2, 1, 3)
        .reshape(-1, col_blocks * order)
    )


def scatter_z(blocks):
    local, order, _ = blocks.shape
    count = high_size("dp")
    by_rows = to_half(blocks).reshape(local, count, order // count, order).swapaxes(0, 1)
    return scatter_high(by_rows, "dp")


def scatter_fc(blocks):
    local, order, _ = blocks.shape
    by_x = to_half(blocks).reshape(PAIR, local // PAIR, order, order)
    return scatter_z(scatter_low(by_x, "dp"))


def scatter_attn(blocks):
    count, order, _ = blocks.shape
    y_count = high_size("mp")
    local = count // (y_count * PAIR)
    by_core = to_half(blocks).reshape(y_count, PAIR, local, order, order).swapaxes(0, 1)
    kept = to_half(scatter_low(by_core, "mp")).reshape(
        y_count, PAIR, local // PAIR, order, order
    )
    first, second = halves(kept, 3)
    first = to_half(scatter_low(first.swapaxes(0, 1), "dp"))
    second = to_half(scatter_high(second, "mp"))
    first = scatter_high(first, "mp")
    second = scatter_low(second, "dp")
    return scatter_z(jnp.concatenate([first, second], axis=1))


def gather_z(rows):
    local, _, order = rows.shape
    return gather_high(to_half(rows), "dp").swapaxes(0, 1).reshape(local, -1, order)


def to_pair(pieces):
    local, piece, order = pieces.shape
    by_x = to_half(pieces).reshape(PAIR, local // PAIR, piece, order)
    low = low_index("dp")
    both = ordered([pick(by_x, low), swap_low(pick(by_x, 1 - low), "dp")], low)
    return both.swapaxes(0, 1).reshape(local // PAIR, PAIR * piece, order)


def from_pair(rows):
    n, local, piece, order = rows.shape
    by_x = to_half(rows).reshape(n, local, PAIR, piece // PAIR, order)
    low = low_index("dp")
    both = ordered([pick(by_x, low, 2), swap_low(pick(by_x, 1 - low, 2), "dp")], low)
    return both.swapaxes(0, 1).reshape(n, PAIR * local, piece // PAIR, order)


def shampoo_rows(grad_rows, left_root, right_root):
    grad_half = to_half(grad_rows)
    whole = gather_z(grad_half)
    rows = grad_rows.shape[1]
    cols = lax.dynamic_slice_in_dim(whole, high_index("dp") * rows, rows, 2)
    left_term = jnp.einsum("bij,bkj->bik", grad_half, whole, preferred_element_type=full)
    right_term = jnp.einsum("bji,bjk->bik", cols, whole, preferred_element_type=full)
    step = to_half(jnp.einsum("bij,bjk->bik", left_root, whole, preferred_element_type=full))
    step = jnp.einsum("bij,bjk->bik", step, right_root, preferred_element_type=full)
    squares = jnp.sum(step * step, axis=(1, 2))
    squares = gather_low(squares, "dp").reshape(-1)
    total = squares
    for k in range(1, high_size("dp")):
        total = total + shift_high(squares, "dp", k)
    sent = from_pair(jnp.stack([grad_rows, left_term, right_term, step]))
    return sent, total


def apply_step(weight, left_stat, right_stat, sent, square_total, step_rates):
    order = weight.shape[2]
    sent = sent.astype(full)
    update_scale = lax.rsqrt(square_total / (order * order) + 1e-06) * step_rates
    return (
        sent[0],
        0.95 * left_stat + 0.05 * sent[1],
        0.95 * right_stat + 0.05 * sent[2],
        weight - sent[3] * update_scale[:, None, None],
    )


def sum_all(values):
    values = values + swap_low(values, "mp")
    for axis in ("mp", "dp"):
        if axis == "dp":
            values = values + swap_low(values, "dp")
        base = values
        for k in range(1, high_size(axis)):
            values = values + shift_high(base, axis, k)
    return values


def body_plain(
    tokens,
    keep_mask,
    cotangent,
    w_attn,
    w_fc1,
    w_fc2,
    vectors,
    left_attn,
    right_attn,
    root_left_attn,
    root_right_attn,
    left_fc1,
    right_fc1,
    root_left_fc1,
    root_right_fc1,
    left_fc2,
    right_fc2,
    root_left_fc2,
    root_right_fc2,
):
    image_count, patch_count, width = tokens.shape
    row_count = image_count * patch_count
    order = w_attn.shape[2]
    row_blocks = width // order
    attn_used = gather_attn(w_attn)
    qkv_full = attn_used[:, : 3 * width]
    out_full = attn_used[:, 3 * width :]
    fc1_used = join_cols(gather_fc(w_fc1), row_blocks)
    fc2_used = join_rows(gather_fc(w_fc2), row_blocks)
    left_roots = [to_pair(v) for v in (root_left_attn, root_left_fc1, root_left_fc2)]
    right_roots = [gather_z(to_pair(v)) for v in (root_right_attn, root_right_fc1, root_right_fc2)]
    hidden_local = fc1_used.shape[1]
    flat = tokens.reshape(row_count, width).astype(full)
    keep_rows = keep_mask.reshape(row_count).astype(full)
    row_gate = jax.nn.sigmoid(jnp.sum(flat * vectors[8], axis=-1))
    row_scale = keep_rows * row_gate
    grad_output = cotangent.reshape(row_count, width).astype(full)
    grad_change = row_scale[:, None] * grad_output
    grad_feed = to_half(grad_change)
    slot = jnp.cumsum(keep_mask, axis=1) - 1
    chosen = (
        (slot[:, None, :] == lax.broadcasted_iota(jnp.int32, (1, SLOTS, 1), 1))
        & (keep_mask[:, None, :] > 0)
    ).astype(half)

    def compact(rows):
        rows = rows.reshape(image_count, patch_count, width)
        picked = jnp.einsum("bsr,brd->bsd", chosen, rows, preferred_element_type=full)
        return to_half(picked).reshape(image_count * SLOTS, width)

    def spread(rows):
        rows = rows.reshape(image_count, SLOTS, width)
        return jnp.einsum(
            "bsr,bsd->brd", chosen.astype(full), rows, precision=highest
        ).reshape(row_count, width)

    group_grads = gather_group(compact(grad_feed))
    normed, first_norm_back = jax.vjp(layer_norm, flat, vectors[0], vectors[1])
    normed_half = to_half(normed)
    qkv_bias = jnp.concatenate([vectors[4], jnp.zeros_like(vectors[4]), vectors[5]])
    mixed_half = to_half(dot32(normed_half, qkv_full) + qkv_bias)
    heads_view = mixed_half.reshape(image_count, patch_count, 3, HEADS, width // HEADS)
    queries = heads_view[:, :, 0]
    key_part = heads_view[:, :, 1]
    values = heads_view[:, :, 2]
    attended_half, probs = jax.vmap(attend)(queries, key_part, values, keep_mask)
    attended_flat = attended_half.reshape(row_count, width)
    branch = dot32(attended_flat, out_full) + vectors[6]
    middle = flat + branch
    normed_two, second_norm_back = jax.vjp(layer_norm, middle, vectors[2], vectors[3])
    group_rows = gather_group(compact(to_half(normed_two)))
    up_bias = vectors[9:].reshape(-1)
    offset = lax.axis_index("mp") * hidden_local
    local_bias = lax.dynamic_slice_in_dim(up_bias, offset, hidden_local)
    hidden = dot32(group_rows, fc1_used) + local_bias
    activated, gelu_back = jax.vjp(exact_gelu, hidden)
    activated = to_half(activated)
    grad_active = times_transpose(group_grads, fc2_used)
    grad_hidden = to_half(gelu_back(grad_active)[0])
    mlp_count = image_count * SLOTS
    grad_rows_back = scatter_group(to_half(times_transpose(grad_hidden, fc1_used)), mlp_count)
    feed = spread(scatter_group(to_half(dot32(activated, fc2_used)), mlp_count)) + vectors[7]
    change = branch + feed
    block_out = to_half(flat + row_scale[:, None] * change).reshape(tokens.shape)
    grad_logit = keep_rows * row_gate * (1.0 - row_gate) * jnp.sum(grad_output * change, axis=-1)
    fc1_rows = scatter_fc(split_cols(row_product(group_rows, grad_hidden), order))
    fc2_rows = scatter_fc(split_rows(row_product(activated, group_grads), order))
    up_part = jnp.sum(grad_hidden, axis=0, dtype=full)
    up_bias_grad = lax.dynamic_update_slice_in_dim(jnp.zeros_like(up_bias), up_part, offset, 0)
    sent_fc1, total_fc1 = shampoo_rows(fc1_rows, left_roots[1], right_roots[1])
    sent_fc2, total_fc2 = shampoo_rows(fc2_rows, left_roots[2], right_roots[2])

    grad_normed_two = spread(grad_rows_back)
    grad_middle, grad_gain_two, grad_shift_two = second_norm_back(grad_normed_two)
    grad_branch = to_half(grad_change + grad_middle)
    grad_attended = to_half(times_transpose(grad_branch, out_full))
    grad_out_full = row_product(attended_flat, grad_branch)
    grad_heads = jax.vmap(attend_back)(
        queries,
        key_part,
        values,
        probs,
        grad_attended.reshape(image_count, patch_count, HEADS, -1),
    )
    grad_mixed = to_half(grad_heads.reshape(row_count, 3 * width))
    grad_qkv_full = row_product(normed_half, grad_mixed)
    attn_rows = scatter_attn(
        split_cols(jnp.concatenate([grad_qkv_full, grad_out_full], axis=1), order)
    )
    sent_attn, total_attn = shampoo_rows(attn_rows, left_roots[0], right_roots[0])
    grad_normed = times_transpose(grad_mixed, qkv_full)
    grad_flat, grad_gain_one, grad_shift_one = first_norm_back(grad_normed)
    input_grad = (grad_output + grad_middle + grad_flat + grad_logit[:, None] * vectors[8]).reshape(
        tokens.shape
    )
    mixed_sums = jnp.sum(grad_mixed, axis=0, dtype=full)
    vector_rows = jnp.stack(
        [
            grad_gain_one,
            grad_shift_one,
            grad_gain_two,
            grad_shift_two,
            mixed_sums[:width],
            mixed_sums[2 * width :],
            jnp.sum(grad_branch, axis=0, dtype=full),
            jnp.sum(grad_feed, axis=0, dtype=full),
            jnp.sum(grad_logit[:, None] * flat, axis=0),
        ]
    )
    vector_part = jnp.concatenate([vector_rows, up_bias_grad.reshape(-1, width)], axis=0)
    vector_grad = sum_all(vector_part)

    attn_local = w_attn.shape[0]
    block_index = lax.axis_index("mp") * attn_local + lax.broadcasted_iota(
        jnp.int32, (attn_local,), 0
    )
    attn_rates = jnp.where(
        block_index // row_blocks < 3 * row_blocks, 0.5 * D ** (-0.5), 0.5 * (D // 16) ** (-0.5)
    )
    fc1_rates = jnp.full((w_fc1.shape[0],), 0.5 * D ** (-0.5), full)
    fc2_rates = jnp.full((w_fc2.shape[0],), 0.5 * FF ** (-0.5), full)
    grad_attn, new_left_attn, new_right_attn, new_attn = apply_step(
        w_attn, left_attn, right_attn, sent_attn, total_attn, attn_rates
    )
    grad_fc1, new_left_fc1, new_right_fc1, new_fc1 = apply_step(
        w_fc1, left_fc1, right_fc1, sent_fc1, total_fc1, fc1_rates
    )
    grad_fc2, new_left_fc2, new_right_fc2, new_fc2 = apply_step(
        w_fc2, left_fc2, right_fc2, sent_fc2, total_fc2, fc2_rates
    )
    vector_blocks = vector_grad.reshape(vector_grad.shape[0], -1, BLOCK_VEC)
    block_scale = lax.rsqrt(jnp.mean(vector_blocks * vector_blocks, axis=-1, keepdims=True) + 1e-06)
    new_vectors = vectors - 0.05 * (vector_blocks * block_scale).reshape(vectors.shape)
    return (
        block_out,
        input_grad,
        grad_attn,
        grad_fc1,
        grad_fc2,
        new_left_attn,
        new_right_attn,
        new_left_fc1,
        new_right_fc1,
        new_left_fc2,
        new_right_fc2,
        new_attn,
        new_fc1,
        new_fc2,
        to_half(new_attn),
        to_half(new_fc1),
        to_half(new_fc2),
        vector_grad,
        new_vectors,
    )


def normalized(values):
    centered = values - jnp.mean(values, axis=-1, keepdims=True)
    variance = jnp.mean(centered * centered, axis=-1, keepdims=True)
    scale = lax.rsqrt(variance + 1e-06)
    return centered * scale, scale


def norm_back(grad_hat, hat, scale):
    first = jnp.mean(grad_hat, axis=-1, keepdims=True)
    second = jnp.mean(grad_hat * hat, axis=-1, keepdims=True)
    return scale * (grad_hat - first - hat * second)


def col_sum(values):
    return jnp.sum(values, axis=0, keepdims=True)


def shape(dims, kind=half):
    return jax.ShapeDtypeStruct(dims, kind)


def local_call(kernel, args, outs, scratch=(), in_hbm=(), out_hbm=(), in_smem=(0,), mib=12, micros=1):
    def place_of(index, hbm, smem):
        if index in hbm:
            return pl.BlockSpec(memory_space=pltpu.HBM)
        if index in smem:
            return pl.BlockSpec(memory_space=pltpu.SMEM)
        return pl.BlockSpec(memory_space=pltpu.VMEM)

    moved = sum(v.size * v.dtype.itemsize for v in list(args) + list(outs))
    return pl.pallas_call(
        kernel,
        out_shape=list(outs),
        in_specs=[place_of(i, in_hbm, in_smem) for i in range(len(args))],
        out_specs=[place_of(i, out_hbm, ()) for i in range(len(outs))],
        scratch_shapes=list(scratch),
        compiler_params=pltpu.CompilerParams(vmem_limit_bytes=mib * 2**20),
        cost_estimate=pl.CostEstimate(
            flops=int(micros * 1e9), bytes_accessed=moved, transcendentals=0
        ),
    )(*args)


def gate_of(tokens, vec_ref):
    return jax.nn.sigmoid(jnp.sum(tokens * vec_ref[8:9, :], axis=-1, keepdims=True))


def keep_of(chosen):
    ones = jnp.ones((chosen.shape[0], 128), half)
    return row_product(chosen, ones)[:, :1]


def prepare_kernel(mask_ref, tok_ref, cot_ref, vec_ref, normed_ref, grad_ref, chosen_ref):
    rows = tok_ref.shape[0]
    tokens = tok_ref[...].astype(full)
    hat, _ = normalized(tokens)
    normed_ref[...] = to_half(hat * vec_ref[0:1, :] + vec_ref[1:2, :])
    mask = mask_ref[...].astype(full)
    upper = lax.broadcasted_iota(jnp.int32, (rows, rows), 0) <= lax.broadcasted_iota(
        jnp.int32, (rows, rows), 1
    )
    count = dot32(
        to_half(jnp.broadcast_to(mask, (16, rows))), jnp.where(upper, 1.0, 0.0).astype(half)
    )
    slot = count[0:1, :] - 1.0
    wanted = lax.broadcasted_iota(jnp.int32, (SLOTS, rows), 0).astype(full)
    chosen = jnp.where((slot == wanted) & (mask > 0.0), 1.0, 0.0).astype(half)
    chosen_ref[...] = chosen
    scale = keep_of(chosen) * gate_of(tokens, vec_ref)
    grad_feed = to_half(scale * cot_ref[...].astype(full))
    grad_ref[...] = to_half(dot32(chosen, grad_feed))


def head_parts(values):
    lane = lax.broadcasted_iota(jnp.int32, values.shape, 1)
    first = lane < values.shape[1] // 2
    zero = jnp.zeros_like(values)
    return jnp.where(first, values, zero), jnp.where(first, zero, values)


def copy_all(copies):
    for copy in copies:
        copy.start()
    for copy in copies:
        copy.wait()


def forward_kernel(order, pieces, place_ref, *refs):
    piece_refs, refs = refs[: len(pieces)], refs[len(pieces) :]
    normed_ref, tok_ref, mask_ref, chosen_ref, vec_ref = refs[:5]
    rows_ref, qkv_ref, probs_ref, attended_ref, branch_ref, weights_hbm = refs[5:11]
    weights, probs_all, sems, out_sem, probs_sems = refs[11:]
    z, x, m = place_ref[0], place_ref[1], place_ref[2]
    local, piece = piece_refs[0].shape[1], piece_refs[0].shape[2]
    copies = []
    for ref, (slots, dx, dm) in zip(piece_refs, pieces):
        for index, slot in enumerate(slots):
            row = pl.multiple_of(((z ^ slot) * PAIR + (x ^ dx)) * piece, 16)
            target = weights.at[pl.ds((m ^ dm) * local, local), pl.ds(row, piece), :]
            copies.append(pltpu.make_async_copy(ref.at[index], target, sems.at[len(copies)]))
    copy_all(copies)
    keep_whole = pltpu.make_async_copy(weights, weights_hbm, out_sem)
    keep_whole.start()
    width = normed_ref.shape[1]
    row_blocks = width // order
    normed = normed_ref[...]
    for col in range(3 * row_blocks):
        part = jnp.zeros((normed.shape[0], order), full)
        for row in range(row_blocks):
            part = part + dot32(
                normed[:, row * order : (row + 1) * order], weights[col * row_blocks + row]
            )
        kind, start = col // row_blocks, (col % row_blocks) * order
        if kind != 1:
            bias_row = 4 if kind == 0 else 5
            part = part + vec_ref[bias_row : bias_row + 1, start : start + order]
        qkv_ref[:, col * order : (col + 1) * order] = to_half(part)
    keep_probs = []
    head = width // HEADS
    scale = head ** (-0.5)
    allowed = mask_ref[...] > 0
    for slab in range(width // (2 * head)):
        lanes = slice(slab * 2 * head, (slab + 1) * 2 * head)
        queries = head_parts(qkv_ref[:, lanes])
        keys = qkv_ref[:, width + lanes.start : width + lanes.stop]
        values = head_parts(qkv_ref[:, 2 * width + lanes.start : 2 * width + lanes.stop])
        total = None
        for index in range(2):
            scores = times_transpose(queries[index], keys) * scale
            scores = jnp.where(allowed, scores, masked_score)
            raised = jnp.exp(scores - jnp.max(scores, axis=-1, keepdims=True))
            probs = raised / jnp.sum(raised, axis=-1, keepdims=True)
            probs_all[2 * slab + index] = probs
            part = dot32(to_half(probs), values[index])
            total = part if total is None else total + part
        attended_ref[:, lanes] = to_half(total)
        pair = pl.ds(2 * slab, 2)
        keep_probs.append(
            pltpu.make_async_copy(probs_all.at[pair], probs_ref.at[pair], probs_sems.at[slab])
        )
        keep_probs[-1].start()
    attended = attended_ref[...]
    for col in range(row_blocks):
        part = jnp.zeros((normed.shape[0], order), full)
        for row in range(row_blocks):
            part = part + dot32(
                attended[:, row * order : (row + 1) * order],
                weights[(3 * row_blocks + col) * row_blocks + row],
            )
        lanes = slice(col * order, (col + 1) * order)
        branch_ref[:, lanes] = part + vec_ref[6:7, lanes]
    hat, _ = normalized(tok_ref[...].astype(full) + branch_ref[...])
    second = to_half(hat * vec_ref[2:3, :] + vec_ref[3:4, :])
    rows_ref[...] = to_half(dot32(chosen_ref[...], second))
    keep_whole.wait()
    for copy in keep_probs:
        copy.wait()


def bias_row(m, values, count):
    row = lax.broadcasted_iota(jnp.int32, (count, values.shape[1]), 0)
    return jnp.where(row == m, values, 0.0)


def gelu_parts(values):
    cdf = 0.5 * (1.0 + lax.erf(values * 0.7071067811865476))
    density = jnp.exp(-0.5 * values * values) * 0.3989422804014327
    return values * cdf, cdf + values * density


def hidden_kernel(order, group, pieces, place_ref, *refs):
    piece_refs, refs = refs[: len(pieces)], refs[len(pieces) :]
    row_refs, refs = refs[:group], refs[group:]
    grad_refs, refs = refs[: group // PAIR], refs[group // PAIR :]
    vec_ref = refs[0]
    back_refs, refs = refs[1 : 1 + group], refs[1 + group :]
    rows_ref, grads_ref, active_ref, hidden_ref, down_hbm = refs[:5]
    weights, sems, out_sem = refs[5:]
    z, x, m = place_ref[0], place_ref[1], place_ref[2]
    piece = piece_refs[0].shape[2]
    local = weights.shape[0] // 2
    bias = jnp.sum(bias_row(m, vec_ref[9:, :], vec_ref.shape[0] - 9), axis=0, keepdims=True)
    copies = []
    for ref, (slots, dx) in zip(piece_refs, pieces):
        for index, slot in enumerate(slots):
            row = pl.multiple_of(((z ^ slot) * PAIR + (x ^ dx)) * piece, 16)
            target = weights.at[:, pl.ds(row, piece), :]
            copies.append(pltpu.make_async_copy(ref.at[index], target, sems.at[len(copies)]))
    for copy in copies:
        copy.start()
    count = row_refs[0].shape[0]
    for index in range(group):
        rows_ref[index * count : (index + 1) * count, :] = row_refs[index][...]
        grads_ref[index * count : (index + 1) * count, :] = grad_refs[index // PAIR][index % PAIR]
    for copy in copies:
        copy.wait()
    local = weights.shape[0] // 2
    keep_down = pltpu.make_async_copy(weights.at[pl.ds(local, local)], down_hbm, out_sem)
    keep_down.start()
    row_blocks = rows_ref.shape[1] // order
    for col in range(local // row_blocks):
        lanes = slice(col * order, (col + 1) * order)
        hidden = bias[:, lanes]
        for row in range(row_blocks):
            hidden = hidden + dot32(
                rows_ref[:, row * order : (row + 1) * order], weights[col * row_blocks + row]
            )
        active, slope = gelu_parts(hidden)
        active_ref[:, lanes] = to_half(active)
        grad = jnp.zeros_like(slope)
        for row in range(row_blocks):
            grad = grad + times_transpose(
                grads_ref[:, row * order : (row + 1) * order],
                weights[local + col * row_blocks + row],
            )
        hidden_ref[:, lanes] = to_half(grad * slope)
    for row in range(row_blocks):
        total = None
        for col in range(local // row_blocks):
            part = times_transpose(
                hidden_ref[:, col * order : (col + 1) * order], weights[col * row_blocks + row]
            )
            total = part if total is None else total + part
        for index in range(group):
            back_refs[index][:, row * order : (row + 1) * order] = to_half(
                total[index * count : (index + 1) * count, :]
            )
    keep_down.wait()


def share_blocks(place_ref, blocks, kept_ref, *sent_refs):
    own, x = kept_ref.shape[0], place_ref[1]
    kept_ref[...] = blocks[pl.ds(x * own, own)]
    count = own // len(sent_refs)
    for index, ref in enumerate(sent_refs):
        ref[...] = blocks[pl.ds((1 - x) * own + index * count, count)]


def up_grads_kernel(order, place_ref, rows_ref, hidden_ref, kept_ref, sent_ref, bias_ref, blocks):
    row_blocks = rows_ref.shape[1] // order
    for col in range(blocks.shape[0] // row_blocks):
        lanes = slice(col * order, (col + 1) * order)
        for row in range(row_blocks):
            others = slice(row * order, (row + 1) * order)
            blocks[col * row_blocks + row] = to_half(
                row_product(rows_ref[:, others], hidden_ref[:, lanes])
            )
    share_blocks(place_ref, blocks, kept_ref, sent_ref)
    bias_ref[...] = col_sum(hidden_ref[...].astype(full))


def down_grads_kernel(order, group, place_ref, grads_ref, active_ref, down_ref, *refs):
    feed_kept_ref, feed_sent_ref, kept_ref, first_ref, second_ref, blocks = refs
    count = grads_ref.shape[0] // group
    row_blocks = grads_ref.shape[1] // order
    col_blocks = down_ref.shape[0] // row_blocks
    for row in range(row_blocks):
        total = None
        for col in range(col_blocks):
            part = dot32(
                active_ref[:, col * order : (col + 1) * order], down_ref[col * row_blocks + row]
            )
            total = part if total is None else total + part
        for index in range(group):
            target = (feed_kept_ref, feed_sent_ref)[index % PAIR]
            target[index // PAIR, :, row * order : (row + 1) * order] = to_half(
                total[index * count : (index + 1) * count, :]
            )
    for col in range(col_blocks):
        lanes = slice(col * order, (col + 1) * order)
        for row in range(row_blocks):
            others = slice(row * order, (row + 1) * order)
            blocks[col * row_blocks + row] = to_half(
                row_product(active_ref[:, lanes], grads_ref[:, others])
            )
    share_blocks(place_ref, blocks, kept_ref, first_ref, second_ref)


def backward_kernel(order, group, place_ref, *refs):
    back_refs, refs = refs[:group], refs[group:]
    chosen_ref, tok_ref, cot_ref, branch_ref, vec_ref = refs[:5]
    qkv_ref, probs_ref, attended_ref, normed_ref, weights_hbm = refs[5:10]
    kept_ref, sent_ref, mixed_ref, middle_ref, sums_ref = refs[10:15]
    weights, left, right, grad_attended, probs_all, sem, probs_sem = refs[15:]
    width = tok_ref.shape[1]
    row_blocks = width // order
    local = weights.shape[0]
    fetch = pltpu.make_async_copy(weights_hbm.at[pl.ds(3 * local, local)], weights, sem)
    fetch.start()
    fetch_probs = pltpu.make_async_copy(probs_ref, probs_all, probs_sem)
    fetch_probs.start()
    chosen = chosen_ref[...]
    arrived = back_refs[0][...].astype(full)
    for ref in back_refs[1:]:
        arrived = arrived + ref[...].astype(full)
    high = to_half(arrived)
    low = to_half(arrived - high.astype(full))
    grad_second = row_product(chosen, high) + row_product(chosen, low)
    tokens = tok_ref[...].astype(full)
    hat, scale = normalized(tokens + branch_ref[...])
    grad_middle = norm_back(grad_second * vec_ref[2:3, :], hat, scale)
    middle_ref[...] = grad_middle
    change = keep_of(chosen) * gate_of(tokens, vec_ref) * cot_ref[...].astype(full)
    grad_branch = to_half(change + grad_middle)
    sums_ref[0:1, :] = col_sum(grad_second * hat)
    sums_ref[1:2, :] = col_sum(grad_second)
    sums_ref[2:3, :] = col_sum(grad_branch.astype(full))
    sums_ref[3:4, :] = col_sum(to_half(change).astype(full))
    left[0] = normed_ref[...]
    left[1] = attended_ref[...]
    right[3] = grad_branch
    fetch.wait()
    for row in range(row_blocks):
        total = None
        for col in range(row_blocks):
            part = times_transpose(
                grad_branch[:, col * order : (col + 1) * order], weights[col * row_blocks + row]
            )
            total = part if total is None else total + part
        grad_attended[:, row * order : (row + 1) * order] = to_half(total)
    fetch_probs.wait()
    head = width // HEADS
    factor = head ** (-0.5)
    for slab in range(width // (2 * head)):
        start, stop = slab * 2 * head, (slab + 1) * 2 * head
        queries = head_parts(qkv_ref[:, start:stop])
        key_pair = qkv_ref[:, width + start : width + stop]
        keys = head_parts(key_pair)
        values = qkv_ref[:, 2 * width + start : 2 * width + stop]
        grads = head_parts(grad_attended[:, start:stop])
        sums = [None] * 3
        for index in range(2):
            probs = probs_all[2 * slab + index]
            grad_probs = times_transpose(grads[index], values)
            inner = jnp.sum(probs * grad_probs, axis=-1, keepdims=True)
            grad_scores = to_half(probs * (grad_probs - inner))
            parts = (
                dot32(grad_scores, keys[index]),
                row_product(grad_scores, queries[index]),
                row_product(to_half(probs), grads[index]),
            )
            sums = [p if s is None else s + p for s, p in zip(sums, parts)]
        right[0, :, start:stop] = to_half(sums[0] * factor)
        right[1, :, start:stop] = to_half(sums[1] * factor)
        right[2, :, start:stop] = to_half(sums[2])
    for kind in range(3):
        mixed_ref[:, kind * width : (kind + 1) * width] = right[kind]
    core = place_ref[3]
    for high_part in range(kept_ref.shape[0]):
        for target, low_part in ((kept_ref, core), (sent_ref, 1 - core)):
            kind = high_part * PAIR + low_part
            rows = left[kind // 3]
            cols = right[kind]
            for col in range(row_blocks):
                for row in range(row_blocks):
                    target[high_part, col * row_blocks + row] = to_half(
                        row_product(
                            rows[:, row * order : (row + 1) * order],
                            cols[:, col * order : (col + 1) * order],
                        )
                    )


def input_kernel(order, group, *refs):
    feed_refs, refs = refs[:group], refs[group:]
    mixed_ref, middle_ref, tok_ref, cot_ref, chosen_ref, vec_ref, branch_ref, weights_hbm = refs[:8]
    out_ref, grad_ref, sums_ref, weights, sem = refs[8:]
    width = tok_ref.shape[1]
    row_blocks = width // order
    fetch = pltpu.make_async_copy(weights_hbm.at[pl.ds(0, weights.shape[0])], weights, sem)
    fetch.start()
    patches = out_ref.shape[0]
    chosen = chosen_ref[...]
    tokens = tok_ref[...].astype(full)
    cotangent = cot_ref[...].astype(full)
    arrived = feed_refs[0][...].astype(full)
    for ref in feed_refs[1:]:
        arrived = arrived + ref[...].astype(full)
    high = to_half(arrived)
    low = to_half(arrived - high.astype(full))
    feed = row_product(chosen, high) + row_product(chosen, low) + vec_ref[7:8, :]
    change = branch_ref[...] + feed
    gate = gate_of(tokens, vec_ref)
    keep = keep_of(chosen)
    out_ref[...] = to_half(tokens + keep * gate * change)[:patches]
    logit = keep * gate * (1.0 - gate) * jnp.sum(cotangent * change, axis=-1, keepdims=True)
    base = cotangent + middle_ref[...] + logit * vec_ref[8:9, :]
    sums_ref[4:5, :] = col_sum(logit * tokens)
    sums_ref[2:3, :] = col_sum(mixed_ref[:, :width].astype(full))
    sums_ref[3:4, :] = col_sum(mixed_ref[:, 2 * width :].astype(full))
    hat, scale = normalized(tokens)
    fetch.wait()
    parts = []
    for row in range(row_blocks):
        total = None
        for col in range(3 * row_blocks):
            part = times_transpose(
                mixed_ref[:, col * order : (col + 1) * order], weights[col * row_blocks + row]
            )
            total = part if total is None else total + part
        parts.append(total)
    grad_normed = jnp.concatenate(parts, axis=1)
    sums_ref[0:1, :] = col_sum(grad_normed * hat)
    sums_ref[1:2, :] = col_sum(grad_normed)
    grad = base + norm_back(grad_normed * vec_ref[0:1, :], hat, scale)
    grad_ref[...] = grad[:patches]


def core_sum_kernel(place_ref, kept_ref, came_ref, *out_refs):
    x, m = place_ref[1], place_ref[2]
    own = kept_ref.shape[1] // PAIR
    chips = len(out_refs) // 2
    for index in range(chips):
        dy, dx = index // PAIR, index % PAIR
        high = (m // PAIR) ^ dy
        for block in range(own):
            at = (x ^ dx) * own + block
            out_ref = out_refs[block // (own // 2) * chips + index]
            out_ref[block % (own // 2)] = to_half(
                kept_ref[high, at].astype(full) + came_ref[high, at].astype(full)
            )


def row_sum_kernel(groups, count, place_ref, *refs):
    ins, outs = refs[: groups * count], refs[groups * count :]
    rows = outs[0].shape[-2]
    near = len(outs) == 2
    slots = outs[0].shape[0] * 2 if near else len(outs)
    for slot in range(slots):
        out_ref = outs[slot % 2].at[slot // 2] if near else outs[slot]
        start = pl.multiple_of((place_ref[0] ^ slot) * rows, 16)
        at = 0
        for group in range(groups):
            parts = ins[group * count : (group + 1) * count]
            for block in range(parts[0].shape[0]):
                total = parts[0][block, pl.ds(start, rows), :].astype(full)
                for ref in parts[1:]:
                    total = total + ref[block, pl.ds(start, rows), :].astype(full)
                out_ref[at] = to_half(total)
                at += 1


def line_blocks(z, refs, target, first=0):
    for slot, ref in enumerate(refs):
        rows = ref.shape[-2]
        start = pl.multiple_of((z ^ slot) * rows, 16)
        for block in range(target.shape[0]):
            target[block, pl.ds(start, rows), :] = ref[first + block]


def line_roots(z, refs, target, first):
    for slot, ref in enumerate(refs):
        rows = ref.shape[1]
        for block in range(target.shape[0]):
            for part in range(PAIR):
                start = pl.multiple_of((z ^ slot) * (PAIR * rows) + part * rows, 16)
                at = (first + block) * PAIR + part
                target[block, pl.ds(start, rows), :] = ref[at]


def step_parts(z, x, own, whole, step, terms, found, block, kept_ref, sent_ref):
    rows, order = own.shape
    mine = pl.multiple_of(z * rows, 16)
    half_rows = rows // PAIR
    terms[...] = row_product(whole, whole)
    found[0] = own.astype(full)
    found[1] = times_transpose(own, whole)
    found[2] = terms[pl.ds(mine, rows), :]
    found[3] = step
    for target, part in ((kept_ref, x), (sent_ref, 1 - x)):
        start = pl.multiple_of(part * half_rows, 16)
        for kind in range(4):
            target[kind, block] = to_half(found[kind, pl.ds(start, half_rows), :])


def whole_step_kernel(count, left_first, place_ref, *refs):
    grad_refs, refs = refs[:count], refs[count:]
    root_refs, refs = refs[:count], refs[count:]
    kept_ref, sent_ref, grads, lefts, rights, terms, found, steps = refs
    z, x = place_ref[0], place_ref[1]
    blocks, rows, order = grad_refs[0].shape
    line_blocks(z, grad_refs, grads)
    line_roots(z, root_refs, rights, 0)
    line_roots(z, root_refs, lefts, left_first)
    mine = pl.multiple_of(z * rows, 16)
    for block in range(blocks):
        whole = grads[block]
        step = to_half(dot32(lefts[block], whole))
        step = dot32(step, rights[block])
        mean = jnp.mean(jnp.mean(step * step, axis=1, keepdims=True), axis=0, keepdims=True)
        steps[...] = step * lax.rsqrt(mean + 1e-06)
        step = steps[pl.ds(mine, rows), :]
        step_parts(z, x, grad_refs[0][block], whole, step, terms, found, block, kept_ref, sent_ref)


def step_kernel(count, first, place_ref, *refs):
    grad_refs, refs = refs[:count], refs[count:]
    root_refs, refs = refs[:count], refs[count:]
    left_ref, kept_ref, sent_ref, square_ref, grads, rights, terms, found = refs
    z, x = place_ref[0], place_ref[1]
    blocks, rows, order = grad_refs[0].shape
    line_blocks(z, grad_refs, grads)
    line_roots(z, root_refs, rights, first)
    square_ref[...] = jnp.zeros_like(square_ref)
    for block in range(blocks):
        whole = grads[block]
        step = to_half(dot32(left_ref[first + block], whole))
        step = dot32(step, rights[block])
        total = jnp.sum(jnp.sum(step * step, axis=1, keepdims=True), axis=0, keepdims=True)
        square_ref[block : block + 1, :] = jnp.broadcast_to(total, (1, 128))
        step_parts(z, x, grad_refs[0][block], whole, step, terms, found, block, kept_ref, sent_ref)
        total = jnp.broadcast_to(total, (16, order))
        terms_of = jnp.zeros((16, order), full)
        row = lax.broadcasted_iota(jnp.int32, (16, order), 0)
        for index in range(3):
            part = to_half(total).astype(full)
            terms_of = jnp.where(row == index, part, terms_of)
            total = total - part
        sent_ref[4, block, :16, :] = to_half(terms_of)
        sent_ref[4, block, 16:, :] = jnp.zeros((sent_ref.shape[2] - 16, order), half)


def squares_kernel(*refs):
    count = len(refs) // 2
    mine_refs, came_refs, out_ref = refs[:count], refs[count:-1], refs[-1]
    blocks = came_refs[0].shape[1]
    for matrix in range(count):
        for block in range(blocks):
            at = matrix * blocks + block
            out_ref[at : at + 1, :] = mine_refs[matrix][block : block + 1, :]
            terms = came_refs[matrix][4, block, 0:16, 0:128].astype(full)
            at += count * blocks
            out_ref[at : at + 1, :] = jnp.sum(terms, axis=0, keepdims=True)


def apply_kernel(
    order, rates, matrix, place_ref, weight_ref, left_ref, right_ref, kept_ref, came_ref, *refs
):
    total_ref = refs[0] if len(refs) == 6 else None
    grad_ref, new_left_ref, new_right_ref, new_ref, half_ref = refs[-5:]
    x, m = place_ref[1], place_ref[2]
    local = weight_ref.shape[0]
    own = local // PAIR
    for side, ref in ((0, kept_ref), (1, came_ref)):
        for block in range(own):
            at = (x ^ side) * own + block
            rate = jnp.where(m * local + at < rates[0], rates[1], rates[2])
            if total_ref is not None:
                row = (side * 2 + matrix) * own + block
                total = total_ref[row : row + 1, 0:1]
                rate = rate * lax.rsqrt(total / (order * order) + 1e-06)
            grad_ref[at] = ref[0, block].astype(full)
            new_left_ref[at] = 0.95 * left_ref[at] + 0.05 * ref[1, block].astype(full)
            new_right_ref[at] = 0.95 * right_ref[at] + 0.05 * ref[2, block].astype(full)
            new = weight_ref[at] - rate * ref[3, block].astype(full)
            new_ref[at] = new
            half_ref[at] = to_half(new)


def vector_part_kernel(place_ref, one_ref, two_ref, bias_ref, out_ref):
    out_ref[0:2, :] = one_ref[0:2, :]
    out_ref[2:4, :] = two_ref[0:2, :]
    out_ref[4:6, :] = one_ref[2:4, :]
    out_ref[6:8, :] = two_ref[2:4, :]
    out_ref[8:9, :] = one_ref[4:5, :]
    out_ref[9:, :] = bias_row(place_ref[2], bias_ref[...], out_ref.shape[0] - 9)


def vector_step_kernel(vec_ref, *refs):
    part_refs, (grad_ref, new_ref) = refs[:-2], refs[-2:]
    grad = part_refs[0][...]
    for ref in part_refs[1:]:
        grad = grad + ref[...]
    grad_ref[...] = grad
    for start in range(0, grad.shape[1], BLOCK_VEC):
        lanes = slice(start, start + BLOCK_VEC)
        block = grad[:, lanes]
        scale = lax.rsqrt(jnp.mean(block * block, axis=-1, keepdims=True) + 1e-06)
        new_ref[:, lanes] = vec_ref[:, lanes] - 0.05 * (block * scale)


def first_kernel(place_ref, *refs):
    ins, refs = refs[:9], refs[9:]
    attn_out, feed_out, kept_ref, sent_ref = refs[:4]
    held, sems = refs[4:]
    copies = [
        pltpu.make_async_copy(ref, held.at[index], sems.at[index])
        for index, ref in enumerate(ins)
    ]
    for copy in copies:
        copy.start()
    local, own = attn_out.shape[0], kept_ref.shape[1]
    x = place_ref[1]
    for index, copy in enumerate(copies):
        copy.wait()
        if index == 0:
            attn_out[...] = to_half(held[index])
        elif index < 3:
            feed_out[(index - 1) * local : index * local] = to_half(held[index])
        else:
            kept_ref[index - 3] = to_half(held[index, pl.ds(x * own, own)])
            sent_ref[index - 3] = to_half(held[index, pl.ds((1 - x) * own, own)])


def bundle_kernel(place_ref, kept_ref, came_ref, feed_ref, left_ref, bundle_ref):
    x = place_ref[1]
    kinds, own, piece, order = kept_ref.shape
    feed = feed_ref.shape[0]
    bundle_ref[:feed] = feed_ref[...]
    for index in range(kinds):
        for block in range(own):
            for side, ref in ((0, kept_ref), (1, came_ref)):
                value = ref[index, block]
                if index < 3:
                    start = pl.multiple_of((x ^ side) * piece, 16)
                    left_ref[index * own + block, pl.ds(start, piece), :] = value
                if index == 0 or index >= 3:
                    at = (index - 3 if index else 3) * own + block
                    bundle_ref[feed + at * PAIR + (x ^ side)] = value


def move(values, dp_mask, mp_mask):
    dp, mp = lax.axis_size("dp"), lax.axis_size("mp")
    if mp_mask == 0:
        return lax.ppermute(values, "dp", [(s, s ^ dp_mask) for s in range(dp)])
    if dp_mask == 0:
        return lax.ppermute(values, "mp", [(s, s ^ mp_mask) for s in range(mp)])
    mask = dp_mask * mp + mp_mask
    return lax.ppermute(values, ("dp", "mp"), [(s, s ^ mask) for s in range(dp * mp)])


def phase(*values):
    return lax.optimization_barrier(values)


def after(values, *others):
    return lax.optimization_barrier((values,) + others)[0]


def body_lines(
    tokens,
    keep_mask,
    cotangent,
    w_attn,
    w_fc1,
    w_fc2,
    vectors,
    left_attn,
    right_attn,
    root_left_attn,
    root_right_attn,
    left_fc1,
    right_fc1,
    root_left_fc1,
    root_right_fc1,
    left_fc2,
    right_fc2,
    root_left_fc2,
    root_right_fc2,
):
    _, patches, width = tokens.shape
    local, piece, order = w_attn.shape
    z_count, group = high_size("dp"), lax.axis_size("mp")
    row_blocks = width // order
    own = local // PAIR
    rows = patches
    line_rows = order // z_count
    total_rows = group * SLOTS
    hidden_width = local // row_blocks * order
    heads = (HEADS, rows, rows)
    others = range(1, group)
    lines = range(1, z_count)
    tok, cot, mask = tokens[0], cotangent[0], keep_mask
    line, member = lax.axis_index("dp"), lax.axis_index("mp")
    place = jnp.stack([line >> 1, line & 1, member, member & 1]).astype(jnp.int32)

    attn_half, feed_half, root_kept, root_sent = local_call(
        first_kernel,
        (
            place,
            *[
                pltpu.with_memory_space_constraint(value, pltpu.HBM)
                for value in (
                    w_attn,
                    w_fc1,
                    w_fc2,
                    root_left_attn,
                    root_left_fc1,
                    root_left_fc2,
                    root_right_attn,
                    root_right_fc1,
                    root_right_fc2,
                )
            ],
        ),
        (
            shape((local, piece, order)),
            shape((2 * local, piece, order)),
            shape((6, own, piece, order)),
            shape((6, own, piece, order)),
        ),
        scratch=(pltpu.VMEM((9, local, piece, order), full), pltpu.SemaphoreType.DMA((9,))),
        in_hbm=range(1, 10),
    )
    line_came = [move(attn_half, k * PAIR, 0) for k in lines]
    root_came = move(root_sent, 1, 0)
    line_came, root_came, attn_half, mask = phase(line_came, root_came, attn_half, mask)

    plane = [(dx, high * PAIR) for high in range(group // PAIR) for dx in range(PAIR)]
    feed_far = move(feed_half, 2 * PAIR, 0)
    left_roots, bundle = local_call(
        bundle_kernel,
        (place, root_kept, root_came, feed_half),
        (
            shape((3 * own, PAIR * piece, order)),
            shape((2 * local + 4 * own * PAIR, piece, order)),
        ),
    )
    bundle_near = move(bundle, PAIR, 0)
    stack = jnp.stack([attn_half, *line_came])
    found = [stack] + [move(stack, dx, dm) for dx, dm in plane[1:]]
    normed, grad_sent, chosen = local_call(
        prepare_kernel,
        (mask, tok, cot, vectors),
        (shape((rows, width)), shape((SLOTS, width)), shape((SLOTS, rows))),
        in_smem=(),
        micros=1.5,
    )
    found, grad_sent, normed, chosen, feed_far, bundle_near = phase(
        found, grad_sent, normed, chosen, feed_far, bundle_near
    )

    pieces, piece_info = [], []
    for (dx, dm), part in zip(plane, found):
        pieces += [part, move(part, 0, 1)]
        piece_info += [(range(z_count), dx, dm), (range(z_count), dx, dm + 1)]
    grad_came = move(grad_sent, 0, 1)
    feed_count = 2 * local
    feed_near = jnp.stack([feed_half, bundle_near[:feed_count]])
    roots, roots_near = bundle[feed_count:], bundle_near[feed_count:]
    half_roots = roots.shape[0] // 2
    roots_first, roots_second = roots[:half_roots], roots[half_roots:]
    pieces, grad_came, feed_near, roots_first, roots_second, roots, roots_near = phase(
        pieces, grad_came, feed_near, roots_first, roots_second, roots, roots_near
    )

    feed_near_came = move(feed_near, 1, 0)
    feed_last = move(feed_far, PAIR, 0)
    roots_first_far = move(roots_first, 2 * PAIR, 0)
    pair = jnp.stack([grad_sent, grad_came])
    group_grads = [pair] + [move(pair, 0, dm) for dm in range(PAIR, group, PAIR)]
    count = len(pieces)
    rows_sent, qkv, probs, attended, branch, weights = local_call(
        lambda *refs: forward_kernel(order, piece_info, *refs),
        (place, *pieces, normed, tok, mask, chosen, vectors),
        (
            shape((SLOTS, width)),
            shape((rows, 3 * width)),
            shape(heads, full),
            shape((rows, width)),
            shape((rows, width), full),
            shape((group * local, order, order)),
        ),
        scratch=(
            pltpu.VMEM((group * local, order, order), half),
            pltpu.VMEM(heads, full),
            pltpu.SemaphoreType.DMA((count * z_count,)),
            pltpu.SemaphoreType.DMA(()),
            pltpu.SemaphoreType.DMA((HEADS // 2,)),
        ),
        in_hbm=range(1, 1 + count),
        out_hbm=(2, 5),
        micros=8,
    )
    rows_sent, group_grads, feed_near_came, feed_last, roots_first_far = phase(
        rows_sent, group_grads, feed_near_came, feed_last, roots_first_far
    )

    group_rows = [rows_sent] + [move(rows_sent, 0, k) for k in others]
    feed_far = jnp.stack([feed_far, feed_last])
    feed_far_came = move(feed_far, 1, 0)
    roots_second_far = move(roots_second, 2 * PAIR, 0)
    group_rows, feed_far_came, roots_second_far = phase(
        group_rows, feed_far_came, roots_second_far
    )

    feed_pieces = [feed_near, feed_near_came, feed_far, feed_far_came]
    feed_info = [((0, 1), 0), ((0, 1), 1), ((2, 3), 0), ((2, 3), 1)]
    outs = local_call(
        lambda *refs: hidden_kernel(order, group, feed_info, *refs),
        (place, *feed_pieces, *group_rows, *group_grads, vectors),
        (shape((SLOTS, width)),) * group
        + (shape((total_rows, width)),) * 2
        + (shape((total_rows, hidden_width)),) * 2
        + (shape((local, order, order)),),
        scratch=(
            pltpu.VMEM((2 * local, order, order), half),
            pltpu.SemaphoreType.DMA((PAIR * z_count,)),
            pltpu.SemaphoreType.DMA(()),
        ),
        in_hbm=(1, 2, 3, 4),
        out_hbm=(group + 4,),
        micros=5,
    )
    back, (all_rows, all_grads, active, grad_hidden, down) = outs[:group], outs[group:]
    back, all_rows = phase(back, all_rows)

    back = [back[0]] + [move(back[k], 0, k) for k in others]
    roots_far = jnp.concatenate([roots_first_far, roots_second_far])
    roots_last = move(roots_far, PAIR, 0)
    all_roots = [roots, roots_near, roots_far, roots_last]
    up_kept, up_sent, bias_sums = local_call(
        lambda *refs: up_grads_kernel(order, *refs),
        (place, all_rows, grad_hidden),
        (shape((own, order, order)),) * 2 + (shape((1, hidden_width), full),),
        scratch=(pltpu.VMEM((local, order, order), half),),
        micros=1,
    )
    up_came = move(up_sent, 1, 0)
    feed_kept, feed_sent, down_kept, down_first, down_second = local_call(
        lambda *refs: down_grads_kernel(order, group, *refs),
        (place, all_grads, active, down),
        (shape((group // PAIR, SLOTS, width)),) * 2
        + (shape((own, order, order)),)
        + (shape((own // 2, order, order)),) * 2,
        scratch=(pltpu.VMEM((local, order, order), half),),
        micros=2,
    )
    back, up_came, down_first, down_second, feed_sent, all_roots = phase(
        back, up_came, down_first, down_second, feed_sent, all_roots
    )

    def rows_of(*groups):
        blocks = sum(parts[0].shape[0] for parts in groups)
        return local_call(
            lambda *refs: row_sum_kernel(len(groups), len(groups[0]), *refs),
            (place, *[part for parts in groups for part in parts]),
            (shape((blocks, line_rows, order)),) * z_count,
        )

    def pairs_of(*groups):
        blocks = sum(parts[0].shape[0] for parts in groups)
        return local_call(
            lambda *refs: row_sum_kernel(len(groups), len(groups[0]), *refs),
            (place, *[part for parts in groups for part in parts]),
            (shape((z_count // 2, blocks, line_rows, order)),) * 2,
        )

    def add_near(kept, came):
        return [
            to_half(kept[k].astype(full) + came[k].astype(full)) for k in range(z_count // 2)
        ]

    def total_of(parts):
        total = parts[0].astype(full)
        for part in parts[1:]:
            total = total + part.astype(full)
        return to_half(total)

    def step_of(parts, matrix):
        return local_call(
            lambda *refs: step_kernel(z_count, matrix * own, *refs),
            (place, *parts, *all_roots, left_roots),
            (
                shape((4, own, piece, order)),
                shape((5, own, piece, order)),
                shape((8, 128), full),
            ),
            scratch=(
                pltpu.VMEM((own, order, order), half),
                pltpu.VMEM((own, order, order), half),
                pltpu.VMEM((order, order), full),
                pltpu.VMEM((4, line_rows, order), full),
            ),
            micros=2,
        )

    up_near_kept, up_near_sent = pairs_of((up_kept, up_came))
    up_near = move(up_near_sent, PAIR, 0)
    down_first_came = move(down_first, 1, 0)
    feed_came = move(feed_sent, 0, 1)
    attn_kept, attn_sent, mixed, grad_middle, sums_two = local_call(
        lambda *refs: backward_kernel(order, group, *refs),
        (place, *back, chosen, tok, cot, branch, vectors, qkv, probs, attended, normed, weights),
        (
            shape((group // PAIR, local, order, order)),
            shape((group // PAIR, local, order, order)),
            shape((rows, 3 * width)),
            shape((rows, width), full),
            shape((4, width), full),
        ),
        scratch=(
            pltpu.VMEM((local, order, order), half),
            pltpu.VMEM((2, rows, width), half),
            pltpu.VMEM((4, rows, width), half),
            pltpu.VMEM((rows, width), half),
            pltpu.VMEM(heads, full),
            pltpu.SemaphoreType.DMA(()),
            pltpu.SemaphoreType.DMA(()),
        ),
        in_hbm=(1 + group + 6, 1 + group + 9),
        micros=8,
    )
    attn_sent, up_near, down_first_came, feed_came = phase(
        attn_sent, up_near, down_first_came, feed_came
    )

    attn_came = move(attn_sent, 0, 1)
    up_mine, up_other = add_near(up_near_kept, up_near)
    up_far = move(up_other, 2 * PAIR, 0)
    down_second_came = move(down_second, 1, 0)
    feed_pairs = [
        to_half(feed_kept[k].astype(full) + feed_came[k].astype(full))
        for k in range(group // PAIR)
    ]
    feed = [feed_pairs[0]] + [
        move(part, 0, (k + 1) * PAIR) for k, part in enumerate(feed_pairs[1:])
    ]
    core_parts = local_call(
        core_sum_kernel,
        (place, attn_kept, attn_came),
        (shape((own // 2, order, order)),) * (2 * group),
    )
    core_parts, up_far, up_mine, down_second_came, feed = phase(
        core_parts, up_far, up_mine, down_second_came, feed
    )
    first_half, second_half = core_parts[:group], core_parts[group:]

    first_came = [move(part, dx, dm) for (dx, dm), part in zip(plane[1:], first_half[1:])]
    middle = own // 2
    down_near_kept, down_near_sent = pairs_of(
        (down_kept[:middle], down_first_came), (down_kept[middle:], down_second_came)
    )
    down_near = move(down_near_sent, PAIR, 0)
    up_rows = total_of([up_mine, up_far])
    up_whole_far = move(up_rows, 2 * PAIR, 0)
    block_out, input_grad, sums_one = local_call(
        lambda *refs: input_kernel(order, group // PAIR, *refs),
        (*feed, mixed, grad_middle, tok, cot, chosen, vectors, branch, weights),
        (
            shape((patches, width)),
            shape((patches, width), full),
            shape((5, width), full),
        ),
        scratch=(
            pltpu.VMEM((3 * local, order, order), half),
            pltpu.SemaphoreType.DMA(()),
        ),
        in_hbm=(group // PAIR + 7,),
        in_smem=(),
        micros=2,
    )
    (vector_sum,) = local_call(
        vector_part_kernel,
        (place, sums_one, sums_two, bias_sums),
        (shape(vectors.shape, full),),
    )
    first_came, down_near, up_whole_far, up_rows, vector_sum = phase(
        first_came, down_near, up_whole_far, up_rows, vector_sum
    )
    second_came = [move(part, dx, dm) for (dx, dm), part in zip(plane[1:], second_half[1:])]
    down_mine, down_other = add_near(down_near_kept, down_near)
    down_far = move(down_other, 2 * PAIR, 0)
    up_pair = jnp.stack([up_rows, up_whole_far])
    up_pair_came = move(up_pair, PAIR, 0)
    second_came, down_far, up_pair_came, down_mine = phase(
        second_came, down_far, up_pair_came, down_mine
    )

    attn_split = rows_of((first_half[0], *first_came), (second_half[0], *second_came))
    attn_split = [attn_split[0]] + [move(attn_split[k], k * PAIR, 0) for k in lines]
    down_rows = total_of([down_mine, down_far])
    down_whole_far = move(down_rows, 2 * PAIR, 0)
    vector_came = move(vector_sum, 0, 1)
    up_mine, up_sent, up_squares = step_of(
        [up_rows, up_pair_came[0], up_whole_far, up_pair_came[1]], 1
    )
    attn_split, down_whole_far, vector_came, up_sent, up_mine, up_squares = phase(
        attn_split, down_whole_far, vector_came, up_sent, up_mine, up_squares
    )

    attn_rows = total_of(attn_split)
    attn_far = move(attn_rows, 2 * PAIR, 0)
    up_found = move(up_sent, 1, 0)
    down_pair = jnp.stack([down_rows, down_whole_far])
    down_pair_came = move(down_pair, PAIR, 0)
    vector_sum = vector_sum + vector_came
    vector_later = [move(vector_sum, 0, dm) for dm in range(PAIR, group, PAIR)]
    attn_far, up_found, down_pair_came, vector_later = phase(
        attn_far, up_found, down_pair_came, vector_later
    )
    attn_pair = jnp.stack([attn_rows, attn_far])
    attn_pair_came = move(attn_pair, PAIR, 0)
    down_mine, down_sent, down_squares = step_of(
        [down_rows, down_pair_came[0], down_whole_far, down_pair_came[1]], 2
    )
    down_found = move(down_sent, 1, 0)
    vector_sum = sum(vector_later, vector_sum)
    vector_line = [move(vector_sum, k * PAIR, 0) for k in lines]
    attn_pair_came, down_found, vector_line = phase(attn_pair_came, down_found, vector_line)

    kept, sent = local_call(
        lambda *refs: whole_step_kernel(z_count, 3 * own, *refs),
        (place, attn_rows, attn_pair_came[0], attn_far, attn_pair_came[1], *all_roots),
        (shape((4, own, piece, order)),) * 2,
        scratch=(pltpu.VMEM((own, order, order), half),) * 3
        + (
            pltpu.VMEM((order, order), full),
            pltpu.VMEM((4, line_rows, order), full),
            pltpu.VMEM((order, order), full),
        ),
        micros=2,
    )
    sent, down_found, vector_line = phase(sent, down_found, vector_line)
    came = move(sent, 1, 0)
    (squares,) = local_call(
        squares_kernel,
        (up_squares, down_squares, up_found, down_found),
        (shape((8, 128), full),),
        in_smem=(),
    )
    total = squares
    for k in lines:
        total = total + move(squares, k * PAIR, 0)
    vector_sum = sum(vector_line, vector_sum)
    vector_parts = [vector_sum, move(vector_sum, 1, 0)]

    def apply(rates, matrix, weight, left, right, *found):
        stat = shape(weight.shape, full)
        return local_call(
            lambda *refs: apply_kernel(order, rates, matrix, *refs),
            (place, weight, left, right, *found),
            (stat,) * 4 + (shape(weight.shape),),
        )

    attn_rates = (3 * row_blocks * row_blocks, 0.5 * D ** (-0.5), 0.5 * (D // 16) ** (-0.5))
    fc1_rates = (0, 0.0, 0.5 * D ** (-0.5))
    fc2_rates = (0, 0.0, 0.5 * FF ** (-0.5))
    vector_grad, new_vectors = local_call(
        vector_step_kernel,
        (vectors, *vector_parts),
        (shape(vectors.shape, full),) * 2,
        in_smem=(),
    )
    done_attn = apply(attn_rates, 0, w_attn, left_attn, right_attn, kept, came)
    done_fc1 = apply(fc1_rates, 0, w_fc1, left_fc1, right_fc1, up_mine, up_found, total)
    done_fc2 = apply(fc2_rates, 1, w_fc2, left_fc2, right_fc2, down_mine, down_found, total)
    return (
        block_out[None],
        input_grad[None],
        done_attn[0],
        done_fc1[0],
        done_fc2[0],
        *done_attn[1:3],
        *done_fc1[1:3],
        *done_fc2[1:3],
        done_attn[3],
        done_fc1[3],
        done_fc2[3],
        done_attn[4],
        done_fc1[4],
        done_fc2[4],
        vector_grad,
        new_vectors,
    )


def body(tokens, keep_mask, cotangent, w_attn, *rest):
    local, piece, _ = w_attn.shape
    group = lax.axis_size("mp")
    tiled = piece % 16 == 0 and tokens.shape[0] == 1 and local % (2 * PAIR) == 0
    tiled = tiled and group == 4 and high_size("dp") == 4
    chosen_body = body_lines if tiled else body_plain
    return chosen_body(tokens, keep_mask, cotangent, w_attn, *rest)


def solution(mesh):
    rows = P(("dp", "mp"), None, None)
    blocks = P("mp", "dp", None)
    return jax.shard_map(
        body,
        mesh=mesh,
        in_specs=(rows, P(("dp", "mp"), None), rows)
        + (blocks,) * 3
        + (P(),)
        + (blocks,) * 12,
        out_specs=(rows, rows) + (blocks,) * 15 + (P(), P()),
        check_vma=False,
    )
```

```python
import jax
import jax.numpy as jnp
from jax import lax
from jax.experimental import pallas as pl
from jax.experimental.pallas import tpu as pltpu
from jax.sharding import PartitionSpec as P

D = 768
HEADS = 12
FF = 3072
BLOCK_VEC = 128
KEPT_MOST = 157
SLOTS = 160
PAIR = 2

highest = lax.Precision.HIGHEST
masked_score = -1e30
half = jnp.bfloat16
full = jnp.float32


def to_half(values):
    return values.astype(half)


def layer_norm(values, gain_row, shift_row):
    centered = values - jnp.mean(values, axis=-1, keepdims=True)
    variance = jnp.mean(centered * centered, axis=-1, keepdims=True)
    return centered * lax.rsqrt(variance + 1e-06) * gain_row + shift_row


def exact_gelu(values):
    return jax.nn.gelu(values, approximate=False)


def dot32(left, right):
    return jnp.dot(left, right, preferred_element_type=full)


def row_product(left_half, right_half):
    return lax.dot_general(
        left_half, right_half, (((0,), (0,)), ((), ())), preferred_element_type=full
    )


def times_transpose(left_half, right_half):
    return lax.dot_general(
        left_half, right_half, (((1,), (1,)), ((), ())), preferred_element_type=full
    )


def swap_low(values, axis):
    count = lax.axis_size(axis)
    return lax.ppermute(values, axis, [(s, s ^ 1) for s in range(count)])


def shift_high(values, axis, step):
    count = lax.axis_size(axis)
    return lax.ppermute(values, axis, [(s, (s + step * PAIR) % count) for s in range(count)])


def high_index(axis):
    return lax.axis_index(axis) // PAIR


def low_index(axis):
    return lax.axis_index(axis) % PAIR


def high_size(axis):
    return lax.axis_size(axis) // PAIR


def pick(values, index, dim=0):
    return lax.dynamic_index_in_dim(values, index, dim, keepdims=False)


def ordered(pieces, index):
    count = len(pieces)
    if count == 2:
        first = index == 0
        return jnp.stack(
            [jnp.where(first, pieces[0], pieces[1]), jnp.where(first, pieces[1], pieces[0])]
        )
    return lax.dynamic_slice_in_dim(jnp.stack(pieces + pieces), (count - index) % count, count, 0)


def gather_low(values, axis):
    return ordered([values, swap_low(values, axis)], low_index(axis))


def gather_high(values, axis):
    count = high_size(axis)
    pieces = [values] + [shift_high(values, axis, -k) for k in range(1, count)]
    return ordered(pieces, high_index(axis))


def scatter_low(values, axis):
    low = low_index(axis)
    arrived = swap_low(pick(values, 1 - low), axis)
    return pick(values, low).astype(full) + arrived.astype(full)


def scatter_high(values, axis):
    count, high = high_size(axis), high_index(axis)
    total = pick(values, high).astype(full)
    for k in range(1, count):
        total = total + shift_high(pick(values, (high + k) % count), axis, k).astype(full)
    return total


def attend(queries, key_part, values, allowed):
    scale_factor = queries.shape[-1] ** (-0.5)
    scores = jnp.einsum("qhd,khd->hqk", queries, key_part, preferred_element_type=full)
    scores = jnp.where(allowed[None, None, :] > 0, scores * scale_factor, masked_score)
    shifted = jnp.exp(scores - jnp.max(scores, axis=-1, keepdims=True))
    probs = shifted / jnp.sum(shifted, axis=-1, keepdims=True)
    attended = jnp.einsum("hqk,khd->qhd", to_half(probs), values, preferred_element_type=full)
    return (to_half(attended), probs)


def attend_back(queries, key_part, values, probs, grad_attended):
    scale_factor = queries.shape[-1] ** (-0.5)
    grad_values = jnp.einsum(
        "hqk,qhd->khd", to_half(probs), grad_attended, preferred_element_type=full
    )
    grad_probs = jnp.einsum("qhd,khd->hqk", grad_attended, values, preferred_element_type=full)
    row_inner = jnp.sum(probs * grad_probs, axis=-1, keepdims=True)
    grad_scores = to_half(probs * (grad_probs - row_inner))
    grad_queries = (
        jnp.einsum("hqk,khd->qhd", grad_scores, key_part, preferred_element_type=full)
        * scale_factor
    )
    grad_keys = (
        jnp.einsum("hqk,qhd->khd", grad_scores, queries, preferred_element_type=full)
        * scale_factor
    )
    return jnp.stack([grad_queries, grad_keys, grad_values], axis=1)


def gather_group(rows):
    pair = jnp.stack([rows, swap_low(rows, "mp")])
    pieces = [pair] + [shift_high(pair, "mp", -k) for k in range(1, high_size("mp"))]
    return jnp.concatenate(pieces, axis=0).reshape(-1, rows.shape[-1])


def scatter_group(rows, row_count):
    pieces = rows.reshape(high_size("mp"), PAIR, row_count, rows.shape[-1])
    pairs = pieces[:, 0].astype(full) + swap_low(pieces[:, 1], "mp").astype(full)
    total = pairs[0]
    for k in range(1, high_size("mp")):
        total = total + shift_high(to_half(pairs[k]), "mp", k).astype(full)
    return total


def halves(values, dim):
    count = values.shape[dim] // 2
    return (
        lax.slice_in_dim(values, 0, count, axis=dim),
        lax.slice_in_dim(values, count, 2 * count, axis=dim),
    )


def gather_attn(blocks):
    local, piece, order = blocks.shape
    lines = gather_high(to_half(blocks), "dp")
    first, second = halves(lines, 0)
    first = gather_high(gather_low(first, "dp"), "mp")
    second = gather_low(gather_high(second, "mp"), "dp")
    both = jnp.concatenate([first, second.swapaxes(0, 1)], axis=2)
    both = gather_low(both, "mp")
    row_blocks = D // order
    both = both.transpose(1, 0, 4, 3, 2, 5, 6)
    both = both.reshape(-1, row_blocks, order, order)
    return both.transpose(1, 2, 0, 3).reshape(D, -1)


def gather_fc(blocks):
    lines = gather_low(gather_high(to_half(blocks), "dp"), "dp")
    lines = lines.transpose(2, 1, 0, 3, 4)
    return lines.reshape(blocks.shape[0], -1, blocks.shape[2])


def split_cols(matrix, order):
    rows, cols = matrix.shape
    return (
        matrix.reshape(rows // order, order, cols // order, order)
        .transpose(2, 0, 1, 3)
        .reshape(-1, order, order)
    )


def split_rows(matrix, order):
    rows, cols = matrix.shape
    return (
        matrix.reshape(rows // order, order, cols // order, order)
        .transpose(0, 2, 1, 3)
        .reshape(-1, order, order)
    )


def join_cols(blocks, row_blocks):
    count, order, _ = blocks.shape
    return (
        blocks.reshape(-1, row_blocks, order, order)
        .transpose(1, 2, 0, 3)
        .reshape(row_blocks * order, -1)
    )


def join_rows(blocks, col_blocks):
    count, order, _ = blocks.shape
    return (
        blocks.reshape(-1, col_blocks, order, order)
        .transpose(0, 2, 1, 3)
        .reshape(-1, col_blocks * order)
    )


def scatter_z(blocks):
    local, order, _ = blocks.shape
    count = high_size("dp")
    by_rows = to_half(blocks).reshape(local, count, order // count, order).swapaxes(0, 1)
    return scatter_high(by_rows, "dp")


def scatter_fc(blocks):
    local, order, _ = blocks.shape
    by_x = to_half(blocks).reshape(PAIR, local // PAIR, order, order)
    return scatter_z(scatter_low(by_x, "dp"))


def scatter_attn(blocks):
    count, order, _ = blocks.shape
    y_count = high_size("mp")
    local = count // (y_count * PAIR)
    by_core = to_half(blocks).reshape(y_count, PAIR, local, order, order).swapaxes(0, 1)
    kept = to_half(scatter_low(by_core, "mp")).reshape(
        y_count, PAIR, local // PAIR, order, order
    )
    first, second = halves(kept, 3)
    first = to_half(scatter_low(first.swapaxes(0, 1), "dp"))
    second = to_half(scatter_high(second, "mp"))
    first = scatter_high(first, "mp")
    second = scatter_low(second, "dp")
    return scatter_z(jnp.concatenate([first, second], axis=1))


def gather_z(rows):
    local, _, order = rows.shape
    return gather_high(to_half(rows), "dp").swapaxes(0, 1).reshape(local, -1, order)


def to_pair(pieces):
    local, piece, order = pieces.shape
    by_x = to_half(pieces).reshape(PAIR, local // PAIR, piece, order)
    low = low_index("dp")
    both = ordered([pick(by_x, low), swap_low(pick(by_x, 1 - low), "dp")], low)
    return both.swapaxes(0, 1).reshape(local // PAIR, PAIR * piece, order)


def from_pair(rows):
    n, local, piece, order = rows.shape
    by_x = to_half(rows).reshape(n, local, PAIR, piece // PAIR, order)
    low = low_index("dp")
    both = ordered([pick(by_x, low, 2), swap_low(pick(by_x, 1 - low, 2), "dp")], low)
    return both.swapaxes(0, 1).reshape(n, PAIR * local, piece // PAIR, order)


def shampoo_rows(grad_rows, left_root, right_root):
    grad_half = to_half(grad_rows)
    whole = gather_z(grad_half)
    rows = grad_rows.shape[1]
    cols = lax.dynamic_slice_in_dim(whole, high_index("dp") * rows, rows, 2)
    left_term = jnp.einsum("bij,bkj->bik", grad_half, whole, preferred_element_type=full)
    right_term = jnp.einsum("bji,bjk->bik", cols, whole, preferred_element_type=full)
    step = to_half(jnp.einsum("bij,bjk->bik", left_root, whole, preferred_element_type=full))
    step = jnp.einsum("bij,bjk->bik", step, right_root, preferred_element_type=full)
    squares = jnp.sum(step * step, axis=(1, 2))
    squares = gather_low(squares, "dp").reshape(-1)
    total = squares
    for k in range(1, high_size("dp")):
        total = total + shift_high(squares, "dp", k)
    sent = from_pair(jnp.stack([grad_rows, left_term, right_term, step]))
    return sent, total


def apply_step(weight, left_stat, right_stat, sent, square_total, step_rates):
    order = weight.shape[2]
    sent = sent.astype(full)
    update_scale = lax.rsqrt(square_total / (order * order) + 1e-06) * step_rates
    return (
        sent[0],
        0.95 * left_stat + 0.05 * sent[1],
        0.95 * right_stat + 0.05 * sent[2],
        weight - sent[3] * update_scale[:, None, None],
    )


def sum_all(values):
    values = values + swap_low(values, "mp")
    for axis in ("mp", "dp"):
        if axis == "dp":
            values = values + swap_low(values, "dp")
        base = values
        for k in range(1, high_size(axis)):
            values = values + shift_high(base, axis, k)
    return values


def body_plain(
    tokens,
    keep_mask,
    cotangent,
    w_attn,
    w_fc1,
    w_fc2,
    vectors,
    left_attn,
    right_attn,
    root_left_attn,
    root_right_attn,
    left_fc1,
    right_fc1,
    root_left_fc1,
    root_right_fc1,
    left_fc2,
    right_fc2,
    root_left_fc2,
    root_right_fc2,
):
    image_count, patch_count, width = tokens.shape
    row_count = image_count * patch_count
    order = w_attn.shape[2]
    row_blocks = width // order
    attn_used = gather_attn(w_attn)
    qkv_full = attn_used[:, : 3 * width]
    out_full = attn_used[:, 3 * width :]
    fc1_used = join_cols(gather_fc(w_fc1), row_blocks)
    fc2_used = join_rows(gather_fc(w_fc2), row_blocks)
    left_roots = [to_pair(v) for v in (root_left_attn, root_left_fc1, root_left_fc2)]
    right_roots = [gather_z(to_pair(v)) for v in (root_right_attn, root_right_fc1, root_right_fc2)]
    hidden_local = fc1_used.shape[1]
    flat = tokens.reshape(row_count, width).astype(full)
    keep_rows = keep_mask.reshape(row_count).astype(full)
    row_gate = jax.nn.sigmoid(jnp.sum(flat * vectors[8], axis=-1))
    row_scale = keep_rows * row_gate
    grad_output = cotangent.reshape(row_count, width).astype(full)
    grad_change = row_scale[:, None] * grad_output
    grad_feed = to_half(grad_change)
    slot = jnp.cumsum(keep_mask, axis=1) - 1
    chosen = (
        (slot[:, None, :] == lax.broadcasted_iota(jnp.int32, (1, SLOTS, 1), 1))
        & (keep_mask[:, None, :] > 0)
    ).astype(half)

    def compact(rows):
        rows = rows.reshape(image_count, patch_count, width)
        picked = jnp.einsum("bsr,brd->bsd", chosen, rows, preferred_element_type=full)
        return to_half(picked).reshape(image_count * SLOTS, width)

    def spread(rows):
        rows = rows.reshape(image_count, SLOTS, width)
        return jnp.einsum(
            "bsr,bsd->brd", chosen.astype(full), rows, precision=highest
        ).reshape(row_count, width)

    group_grads = gather_group(compact(grad_feed))
    normed, first_norm_back = jax.vjp(layer_norm, flat, vectors[0], vectors[1])
    normed_half = to_half(normed)
    qkv_bias = jnp.concatenate([vectors[4], jnp.zeros_like(vectors[4]), vectors[5]])
    mixed_half = to_half(dot32(normed_half, qkv_full) + qkv_bias)
    heads_view = mixed_half.reshape(image_count, patch_count, 3, HEADS, width // HEADS)
    queries = heads_view[:, :, 0]
    key_part = heads_view[:, :, 1]
    values = heads_view[:, :, 2]
    attended_half, probs = jax.vmap(attend)(queries, key_part, values, keep_mask)
    attended_flat = attended_half.reshape(row_count, width)
    branch = dot32(attended_flat, out_full) + vectors[6]
    middle = flat + branch
    normed_two, second_norm_back = jax.vjp(layer_norm, middle, vectors[2], vectors[3])
    group_rows = gather_group(compact(to_half(normed_two)))
    up_bias = vectors[9:].reshape(-1)
    offset = lax.axis_index("mp") * hidden_local
    local_bias = lax.dynamic_slice_in_dim(up_bias, offset, hidden_local)
    hidden = dot32(group_rows, fc1_used) + local_bias
    activated, gelu_back = jax.vjp(exact_gelu, hidden)
    activated = to_half(activated)
    grad_active = times_transpose(group_grads, fc2_used)
    grad_hidden = to_half(gelu_back(grad_active)[0])
    mlp_count = image_count * SLOTS
    grad_rows_back = scatter_group(to_half(times_transpose(grad_hidden, fc1_used)), mlp_count)
    feed = spread(scatter_group(to_half(dot32(activated, fc2_used)), mlp_count)) + vectors[7]
    change = branch + feed
    block_out = to_half(flat + row_scale[:, None] * change).reshape(tokens.shape)
    grad_logit = keep_rows * row_gate * (1.0 - row_gate) * jnp.sum(grad_output * change, axis=-1)
    fc1_rows = scatter_fc(split_cols(row_product(group_rows, grad_hidden), order))
    fc2_rows = scatter_fc(split_rows(row_product(activated, group_grads), order))
    up_part = jnp.sum(grad_hidden, axis=0, dtype=full)
    up_bias_grad = lax.dynamic_update_slice_in_dim(jnp.zeros_like(up_bias), up_part, offset, 0)
    sent_fc1, total_fc1 = shampoo_rows(fc1_rows, left_roots[1], right_roots[1])
    sent_fc2, total_fc2 = shampoo_rows(fc2_rows, left_roots[2], right_roots[2])

    grad_normed_two = spread(grad_rows_back)
    grad_middle, grad_gain_two, grad_shift_two = second_norm_back(grad_normed_two)
    grad_branch = to_half(grad_change + grad_middle)
    grad_attended = to_half(times_transpose(grad_branch, out_full))
    grad_out_full = row_product(attended_flat, grad_branch)
    grad_heads = jax.vmap(attend_back)(
        queries,
        key_part,
        values,
        probs,
        grad_attended.reshape(image_count, patch_count, HEADS, -1),
    )
    grad_mixed = to_half(grad_heads.reshape(row_count, 3 * width))
    grad_qkv_full = row_product(normed_half, grad_mixed)
    attn_rows = scatter_attn(
        split_cols(jnp.concatenate([grad_qkv_full, grad_out_full], axis=1), order)
    )
    sent_attn, total_attn = shampoo_rows(attn_rows, left_roots[0], right_roots[0])
    grad_normed = times_transpose(grad_mixed, qkv_full)
    grad_flat, grad_gain_one, grad_shift_one = first_norm_back(grad_normed)
    input_grad = (grad_output + grad_middle + grad_flat + grad_logit[:, None] * vectors[8]).reshape(
        tokens.shape
    )
    mixed_sums = jnp.sum(grad_mixed, axis=0, dtype=full)
    vector_rows = jnp.stack(
        [
            grad_gain_one,
            grad_shift_one,
            grad_gain_two,
            grad_shift_two,
            mixed_sums[:width],
            mixed_sums[2 * width :],
            jnp.sum(grad_branch, axis=0, dtype=full),
            jnp.sum(grad_feed, axis=0, dtype=full),
            jnp.sum(grad_logit[:, None] * flat, axis=0),
        ]
    )
    vector_part = jnp.concatenate([vector_rows, up_bias_grad.reshape(-1, width)], axis=0)
    vector_grad = sum_all(vector_part)

    attn_local = w_attn.shape[0]
    block_index = lax.axis_index("mp") * attn_local + lax.broadcasted_iota(
        jnp.int32, (attn_local,), 0
    )
    attn_rates = jnp.where(
        block_index // row_blocks < 3 * row_blocks, 0.5 * D ** (-0.5), 0.5 * (D // 16) ** (-0.5)
    )
    fc1_rates = jnp.full((w_fc1.shape[0],), 0.5 * D ** (-0.5), full)
    fc2_rates = jnp.full((w_fc2.shape[0],), 0.5 * FF ** (-0.5), full)
    grad_attn, new_left_attn, new_right_attn, new_attn = apply_step(
        w_attn, left_attn, right_attn, sent_attn, total_attn, attn_rates
    )
    grad_fc1, new_left_fc1, new_right_fc1, new_fc1 = apply_step(
        w_fc1, left_fc1, right_fc1, sent_fc1, total_fc1, fc1_rates
    )
    grad_fc2, new_left_fc2, new_right_fc2, new_fc2 = apply_step(
        w_fc2, left_fc2, right_fc2, sent_fc2, total_fc2, fc2_rates
    )
    vector_blocks = vector_grad.reshape(vector_grad.shape[0], -1, BLOCK_VEC)
    block_scale = lax.rsqrt(jnp.mean(vector_blocks * vector_blocks, axis=-1, keepdims=True) + 1e-06)
    new_vectors = vectors - 0.05 * (vector_blocks * block_scale).reshape(vectors.shape)
    return (
        block_out,
        input_grad,
        grad_attn,
        grad_fc1,
        grad_fc2,
        new_left_attn,
        new_right_attn,
        new_left_fc1,
        new_right_fc1,
        new_left_fc2,
        new_right_fc2,
        new_attn,
        new_fc1,
        new_fc2,
        to_half(new_attn),
        to_half(new_fc1),
        to_half(new_fc2),
        vector_grad,
        new_vectors,
    )


def normalized(values):
    centered = values - jnp.mean(values, axis=-1, keepdims=True)
    variance = jnp.mean(centered * centered, axis=-1, keepdims=True)
    scale = lax.rsqrt(variance + 1e-06)
    return centered * scale, scale


def norm_back(grad_hat, hat, scale):
    first = jnp.mean(grad_hat, axis=-1, keepdims=True)
    second = jnp.mean(grad_hat * hat, axis=-1, keepdims=True)
    return scale * (grad_hat - first - hat * second)


def col_sum(values):
    return jnp.sum(values, axis=0, keepdims=True)


def shape(dims, kind=half):
    return jax.ShapeDtypeStruct(dims, kind)


def local_call(kernel, args, outs, scratch=(), in_hbm=(), out_hbm=(), in_smem=(0,), mib=12, micros=0.05):
    def place_of(index, hbm, smem):
        if index in hbm:
            return pl.BlockSpec(memory_space=pltpu.HBM)
        if index in smem:
            return pl.BlockSpec(memory_space=pltpu.SMEM)
        return pl.BlockSpec(memory_space=pltpu.VMEM)

    return pl.pallas_call(
        kernel,
        out_shape=list(outs),
        in_specs=[place_of(i, in_hbm, in_smem) for i in range(len(args))],
        out_specs=[place_of(i, out_hbm, ()) for i in range(len(outs))],
        scratch_shapes=list(scratch),
        compiler_params=pltpu.CompilerParams(vmem_limit_bytes=mib * 2**20),
        cost_estimate=pl.CostEstimate(
            flops=int(micros * 1e9), bytes_accessed=int(micros * 1e6), transcendentals=0
        ),
    )(*args)


def gate_of(tokens, vec_ref):
    return jax.nn.sigmoid(jnp.sum(tokens * vec_ref[8:9, :], axis=-1, keepdims=True))


def keep_of(chosen):
    ones = jnp.ones((chosen.shape[0], 128), half)
    return row_product(chosen, ones)[:, :1]


def prepare_kernel(mask_ref, tok_ref, cot_ref, vec_ref, normed_ref, grad_ref, chosen_ref):
    rows = tok_ref.shape[0]
    tokens = tok_ref[...].astype(full)
    hat, _ = normalized(tokens)
    normed_ref[...] = to_half(hat * vec_ref[0:1, :] + vec_ref[1:2, :])
    mask = mask_ref[...].astype(full)
    upper = lax.broadcasted_iota(jnp.int32, (rows, rows), 0) <= lax.broadcasted_iota(
        jnp.int32, (rows, rows), 1
    )
    count = dot32(
        to_half(jnp.broadcast_to(mask, (16, rows))), jnp.where(upper, 1.0, 0.0).astype(half)
    )
    slot = count[0:1, :] - 1.0
    wanted = lax.broadcasted_iota(jnp.int32, (SLOTS, rows), 0).astype(full)
    chosen = jnp.where((slot == wanted) & (mask > 0.0), 1.0, 0.0).astype(half)
    chosen_ref[...] = chosen
    scale = keep_of(chosen) * gate_of(tokens, vec_ref)
    grad_feed = to_half(scale * cot_ref[...].astype(full))
    grad_ref[...] = to_half(dot32(chosen, grad_feed))


def head_parts(values):
    lane = lax.broadcasted_iota(jnp.int32, values.shape, 1)
    first = lane < values.shape[1] // 2
    zero = jnp.zeros_like(values)
    return jnp.where(first, values, zero), jnp.where(first, zero, values)


def copy_all(copies):
    for copy in copies:
        copy.start()
    for copy in copies:
        copy.wait()


def forward_kernel(order, pieces, place_ref, *refs):
    piece_refs, refs = refs[: len(pieces)], refs[len(pieces) :]
    normed_ref, tok_ref, mask_ref, chosen_ref, vec_ref = refs[:5]
    rows_ref, qkv_ref, probs_ref, attended_ref, branch_ref, weights_hbm = refs[5:11]
    weights, probs_all, sems, out_sem, probs_sems = refs[11:]
    z, x, m = place_ref[0], place_ref[1], place_ref[2]
    local, piece = piece_refs[0].shape[1], piece_refs[0].shape[2]
    copies = []
    for ref, (slots, dx, dm) in zip(piece_refs, pieces):
        for index, slot in enumerate(slots):
            row = pl.multiple_of(((z ^ slot) * PAIR + (x ^ dx)) * piece, 16)
            target = weights.at[pl.ds((m ^ dm) * local, local), pl.ds(row, piece), :]
            copies.append(pltpu.make_async_copy(ref.at[index], target, sems.at[len(copies)]))
    copy_all(copies)
    keep_whole = pltpu.make_async_copy(weights, weights_hbm, out_sem)
    keep_whole.start()
    width = normed_ref.shape[1]
    row_blocks = width // order
    normed = normed_ref[...]
    for col in range(3 * row_blocks):
        part = jnp.zeros((normed.shape[0], order), full)
        for row in range(row_blocks):
            part = part + dot32(
                normed[:, row * order : (row + 1) * order], weights[col * row_blocks + row]
            )
        kind, start = col // row_blocks, (col % row_blocks) * order
        if kind != 1:
            bias_row = 4 if kind == 0 else 5
            part = part + vec_ref[bias_row : bias_row + 1, start : start + order]
        qkv_ref[:, col * order : (col + 1) * order] = to_half(part)
    keep_probs = []
    head = width // HEADS
    scale = head ** (-0.5)
    allowed = mask_ref[...] > 0
    for slab in range(width // (2 * head)):
        lanes = slice(slab * 2 * head, (slab + 1) * 2 * head)
        queries = head_parts(qkv_ref[:, lanes])
        keys = qkv_ref[:, width + lanes.start : width + lanes.stop]
        values = head_parts(qkv_ref[:, 2 * width + lanes.start : 2 * width + lanes.stop])
        total = None
        for index in range(2):
            scores = times_transpose(queries[index], keys) * scale
            scores = jnp.where(allowed, scores, masked_score)
            raised = jnp.exp(scores - jnp.max(scores, axis=-1, keepdims=True))
            probs = raised / jnp.sum(raised, axis=-1, keepdims=True)
            probs_all[2 * slab + index] = probs
            part = dot32(to_half(probs), values[index])
            total = part if total is None else total + part
        attended_ref[:, lanes] = to_half(total)
        pair = pl.ds(2 * slab, 2)
        keep_probs.append(
            pltpu.make_async_copy(probs_all.at[pair], probs_ref.at[pair], probs_sems.at[slab])
        )
        keep_probs[-1].start()
    attended = attended_ref[...]
    for col in range(row_blocks):
        part = jnp.zeros((normed.shape[0], order), full)
        for row in range(row_blocks):
            part = part + dot32(
                attended[:, row * order : (row + 1) * order],
                weights[(3 * row_blocks + col) * row_blocks + row],
            )
        lanes = slice(col * order, (col + 1) * order)
        branch_ref[:, lanes] = part + vec_ref[6:7, lanes]
    hat, _ = normalized(tok_ref[...].astype(full) + branch_ref[...])
    second = to_half(hat * vec_ref[2:3, :] + vec_ref[3:4, :])
    rows_ref[...] = to_half(dot32(chosen_ref[...], second))
    keep_whole.wait()
    for copy in keep_probs:
        copy.wait()


def bias_row(m, values, count):
    row = lax.broadcasted_iota(jnp.int32, (count, values.shape[1]), 0)
    return jnp.where(row == m, values, 0.0)


def gelu_parts(values):
    cdf = 0.5 * (1.0 + lax.erf(values * 0.7071067811865476))
    density = jnp.exp(-0.5 * values * values) * 0.3989422804014327
    return values * cdf, cdf + values * density


def hidden_kernel(order, group, pieces, place_ref, *refs):
    piece_refs, refs = refs[: len(pieces)], refs[len(pieces) :]
    row_refs, refs = refs[:group], refs[group:]
    grad_refs, refs = refs[: group // PAIR], refs[group // PAIR :]
    vec_ref = refs[0]
    back_refs, refs = refs[1 : 1 + group], refs[1 + group :]
    rows_ref, grads_ref, active_ref, hidden_ref, down_hbm = refs[:5]
    weights, sems, out_sem = refs[5:]
    z, x, m = place_ref[0], place_ref[1], place_ref[2]
    piece = piece_refs[0].shape[2]
    local = weights.shape[0] // 2
    bias = jnp.sum(bias_row(m, vec_ref[9:, :], vec_ref.shape[0] - 9), axis=0, keepdims=True)
    copies = []
    for ref, (slots, dx) in zip(piece_refs, pieces):
        for index, slot in enumerate(slots):
            row = pl.multiple_of(((z ^ slot) * PAIR + (x ^ dx)) * piece, 16)
            target = weights.at[:, pl.ds(row, piece), :]
            copies.append(pltpu.make_async_copy(ref.at[index], target, sems.at[len(copies)]))
    for copy in copies:
        copy.start()
    count = row_refs[0].shape[0]
    for index in range(group):
        rows_ref[index * count : (index + 1) * count, :] = row_refs[index][...]
        grads_ref[index * count : (index + 1) * count, :] = grad_refs[index // PAIR][index % PAIR]
    for copy in copies:
        copy.wait()
    local = weights.shape[0] // 2
    keep_down = pltpu.make_async_copy(weights.at[pl.ds(local, local)], down_hbm, out_sem)
    keep_down.start()
    row_blocks = rows_ref.shape[1] // order
    for col in range(local // row_blocks):
        lanes = slice(col * order, (col + 1) * order)
        hidden = bias[:, lanes]
        for row in range(row_blocks):
            hidden = hidden + dot32(
                rows_ref[:, row * order : (row + 1) * order], weights[col * row_blocks + row]
            )
        active, slope = gelu_parts(hidden)
        active_ref[:, lanes] = to_half(active)
        grad = jnp.zeros_like(slope)
        for row in range(row_blocks):
            grad = grad + times_transpose(
                grads_ref[:, row * order : (row + 1) * order],
                weights[local + col * row_blocks + row],
            )
        hidden_ref[:, lanes] = to_half(grad * slope)
    for row in range(row_blocks):
        total = None
        for col in range(local // row_blocks):
            part = times_transpose(
                hidden_ref[:, col * order : (col + 1) * order], weights[col * row_blocks + row]
            )
            total = part if total is None else total + part
        for index in range(group):
            back_refs[index][:, row * order : (row + 1) * order] = to_half(
                total[index * count : (index + 1) * count, :]
            )
    keep_down.wait()


def share_blocks(place_ref, blocks, kept_ref, *sent_refs):
    own, x = kept_ref.shape[0], place_ref[1]
    kept_ref[...] = blocks[pl.ds(x * own, own)]
    count = own // len(sent_refs)
    for index, ref in enumerate(sent_refs):
        ref[...] = blocks[pl.ds((1 - x) * own + index * count, count)]


def up_grads_kernel(order, place_ref, rows_ref, hidden_ref, kept_ref, sent_ref, bias_ref, blocks):
    row_blocks = rows_ref.shape[1] // order
    for col in range(blocks.shape[0] // row_blocks):
        lanes = slice(col * order, (col + 1) * order)
        for row in range(row_blocks):
            others = slice(row * order, (row + 1) * order)
            blocks[col * row_blocks + row] = to_half(
                row_product(rows_ref[:, others], hidden_ref[:, lanes])
            )
    share_blocks(place_ref, blocks, kept_ref, sent_ref)
    bias_ref[...] = col_sum(hidden_ref[...].astype(full))


def down_grads_kernel(order, group, place_ref, grads_ref, active_ref, down_ref, *refs):
    feed_kept_ref, feed_sent_ref, kept_ref, first_ref, second_ref, blocks = refs
    count = grads_ref.shape[0] // group
    row_blocks = grads_ref.shape[1] // order
    col_blocks = down_ref.shape[0] // row_blocks
    for row in range(row_blocks):
        total = None
        for col in range(col_blocks):
            part = dot32(
                active_ref[:, col * order : (col + 1) * order], down_ref[col * row_blocks + row]
            )
            total = part if total is None else total + part
        for index in range(group):
            target = (feed_kept_ref, feed_sent_ref)[index % PAIR]
            target[index // PAIR, :, row * order : (row + 1) * order] = to_half(
                total[index * count : (index + 1) * count, :]
            )
    for col in range(col_blocks):
        lanes = slice(col * order, (col + 1) * order)
        for row in range(row_blocks):
            others = slice(row * order, (row + 1) * order)
            blocks[col * row_blocks + row] = to_half(
                row_product(active_ref[:, lanes], grads_ref[:, others])
            )
    share_blocks(place_ref, blocks, kept_ref, first_ref, second_ref)


def backward_kernel(order, group, place_ref, *refs):
    back_refs, refs = refs[:group], refs[group:]
    chosen_ref, tok_ref, cot_ref, branch_ref, vec_ref = refs[:5]
    qkv_ref, probs_ref, attended_ref, normed_ref, weights_hbm = refs[5:10]
    kept_ref, sent_ref, mixed_ref, middle_ref, sums_ref = refs[10:15]
    weights, left, right, grad_attended, probs_all, sem, probs_sem = refs[15:]
    width = tok_ref.shape[1]
    row_blocks = width // order
    local = weights.shape[0]
    fetch = pltpu.make_async_copy(weights_hbm.at[pl.ds(3 * local, local)], weights, sem)
    fetch.start()
    fetch_probs = pltpu.make_async_copy(probs_ref, probs_all, probs_sem)
    fetch_probs.start()
    chosen = chosen_ref[...]
    arrived = back_refs[0][...].astype(full)
    for ref in back_refs[1:]:
        arrived = arrived + ref[...].astype(full)
    high = to_half(arrived)
    low = to_half(arrived - high.astype(full))
    grad_second = row_product(chosen, high) + row_product(chosen, low)
    tokens = tok_ref[...].astype(full)
    hat, scale = normalized(tokens + branch_ref[...])
    grad_middle = norm_back(grad_second * vec_ref[2:3, :], hat, scale)
    middle_ref[...] = grad_middle
    change = keep_of(chosen) * gate_of(tokens, vec_ref) * cot_ref[...].astype(full)
    grad_branch = to_half(change + grad_middle)
    sums_ref[0:1, :] = col_sum(grad_second * hat)
    sums_ref[1:2, :] = col_sum(grad_second)
    sums_ref[2:3, :] = col_sum(grad_branch.astype(full))
    sums_ref[3:4, :] = col_sum(to_half(change).astype(full))
    left[0] = normed_ref[...]
    left[1] = attended_ref[...]
    right[3] = grad_branch
    fetch.wait()
    for row in range(row_blocks):
        total = None
        for col in range(row_blocks):
            part = times_transpose(
                grad_branch[:, col * order : (col + 1) * order], weights[col * row_blocks + row]
            )
            total = part if total is None else total + part
        grad_attended[:, row * order : (row + 1) * order] = to_half(total)
    fetch_probs.wait()
    head = width // HEADS
    factor = head ** (-0.5)
    for slab in range(width // (2 * head)):
        start, stop = slab * 2 * head, (slab + 1) * 2 * head
        queries = head_parts(qkv_ref[:, start:stop])
        key_pair = qkv_ref[:, width + start : width + stop]
        keys = head_parts(key_pair)
        values = qkv_ref[:, 2 * width + start : 2 * width + stop]
        grads = head_parts(grad_attended[:, start:stop])
        sums = [None] * 3
        for index in range(2):
            probs = probs_all[2 * slab + index]
            grad_probs = times_transpose(grads[index], values)
            inner = jnp.sum(probs * grad_probs, axis=-1, keepdims=True)
            grad_scores = to_half(probs * (grad_probs - inner))
            parts = (
                dot32(grad_scores, keys[index]),
                row_product(grad_scores, queries[index]),
                row_product(to_half(probs), grads[index]),
            )
            sums = [p if s is None else s + p for s, p in zip(sums, parts)]
        right[0, :, start:stop] = to_half(sums[0] * factor)
        right[1, :, start:stop] = to_half(sums[1] * factor)
        right[2, :, start:stop] = to_half(sums[2])
    for kind in range(3):
        mixed_ref[:, kind * width : (kind + 1) * width] = right[kind]
    core = place_ref[3]
    for high_part in range(kept_ref.shape[0]):
        for target, low_part in ((kept_ref, core), (sent_ref, 1 - core)):
            kind = high_part * PAIR + low_part
            rows = left[kind // 3]
            cols = right[kind]
            for col in range(row_blocks):
                for row in range(row_blocks):
                    target[high_part, col * row_blocks + row] = to_half(
                        row_product(
                            rows[:, row * order : (row + 1) * order],
                            cols[:, col * order : (col + 1) * order],
                        )
                    )


def input_kernel(order, group, *refs):
    feed_refs, refs = refs[:group], refs[group:]
    mixed_ref, middle_ref, tok_ref, cot_ref, chosen_ref, vec_ref, branch_ref, weights_hbm = refs[:8]
    out_ref, grad_ref, sums_ref, weights, sem = refs[8:]
    width = tok_ref.shape[1]
    row_blocks = width // order
    fetch = pltpu.make_async_copy(weights_hbm.at[pl.ds(0, weights.shape[0])], weights, sem)
    fetch.start()
    patches = out_ref.shape[0]
    chosen = chosen_ref[...]
    tokens = tok_ref[...].astype(full)
    cotangent = cot_ref[...].astype(full)
    arrived = feed_refs[0][...].astype(full)
    for ref in feed_refs[1:]:
        arrived = arrived + ref[...].astype(full)
    high = to_half(arrived)
    low = to_half(arrived - high.astype(full))
    feed = row_product(chosen, high) + row_product(chosen, low) + vec_ref[7:8, :]
    change = branch_ref[...] + feed
    gate = gate_of(tokens, vec_ref)
    keep = keep_of(chosen)
    out_ref[...] = to_half(tokens + keep * gate * change)[:patches]
    logit = keep * gate * (1.0 - gate) * jnp.sum(cotangent * change, axis=-1, keepdims=True)
    base = cotangent + middle_ref[...] + logit * vec_ref[8:9, :]
    sums_ref[4:5, :] = col_sum(logit * tokens)
    sums_ref[2:3, :] = col_sum(mixed_ref[:, :width].astype(full))
    sums_ref[3:4, :] = col_sum(mixed_ref[:, 2 * width :].astype(full))
    hat, scale = normalized(tokens)
    fetch.wait()
    parts = []
    for row in range(row_blocks):
        total = None
        for col in range(3 * row_blocks):
            part = times_transpose(
                mixed_ref[:, col * order : (col + 1) * order], weights[col * row_blocks + row]
            )
            total = part if total is None else total + part
        parts.append(total)
    grad_normed = jnp.concatenate(parts, axis=1)
    sums_ref[0:1, :] = col_sum(grad_normed * hat)
    sums_ref[1:2, :] = col_sum(grad_normed)
    grad = base + norm_back(grad_normed * vec_ref[0:1, :], hat, scale)
    grad_ref[:, 0, :] = grad[:patches]


def core_sum_kernel(place_ref, kept_ref, came_ref, *out_refs):
    x, m = place_ref[1], place_ref[2]
    own = kept_ref.shape[1] // PAIR
    for index, out_ref in enumerate(out_refs):
        dy, dx = index // PAIR, index % PAIR
        high = (m // PAIR) ^ dy
        for block in range(own):
            at = (x ^ dx) * own + block
            out_ref[block] = to_half(
                kept_ref[high, at].astype(full) + came_ref[high, at].astype(full)
            )


def row_sum_kernel(groups, count, place_ref, *refs):
    ins, outs = refs[: groups * count], refs[groups * count :]
    rows = outs[0].shape[-2]
    near = len(outs) == 2
    slots = outs[0].shape[0] * 2 if near else len(outs)
    for slot in range(slots):
        out_ref = outs[slot % 2].at[slot // 2] if near else outs[slot]
        start = pl.multiple_of((place_ref[0] ^ slot) * rows, 16)
        at = 0
        for group in range(groups):
            parts = ins[group * count : (group + 1) * count]
            for block in range(parts[0].shape[0]):
                total = parts[0][block, pl.ds(start, rows), :].astype(full)
                for ref in parts[1:]:
                    total = total + ref[block, pl.ds(start, rows), :].astype(full)
                out_ref[at] = to_half(total)
                at += 1


def line_blocks(z, refs, target, first=0):
    for slot, ref in enumerate(refs):
        rows = ref.shape[-2]
        start = pl.multiple_of((z ^ slot) * rows, 16)
        for block in range(target.shape[0]):
            target[block, pl.ds(start, rows), :] = ref[first + block]


def line_roots(z, refs, target, first):
    for slot, ref in enumerate(refs):
        rows = ref.shape[1]
        for block in range(target.shape[0]):
            for part in range(PAIR):
                start = pl.multiple_of((z ^ slot) * (PAIR * rows) + part * rows, 16)
                at = (first + block) * PAIR + part
                target[block, pl.ds(start, rows), :] = ref[at]


def step_parts(z, x, own, whole, step, terms, found, block, kept_ref, sent_ref):
    rows, order = own.shape
    mine = pl.multiple_of(z * rows, 16)
    half_rows = rows // PAIR
    terms[...] = row_product(whole, whole)
    found[0] = own.astype(full)
    found[1] = times_transpose(own, whole)
    found[2] = terms[pl.ds(mine, rows), :]
    found[3] = step
    for target, part in ((kept_ref, x), (sent_ref, 1 - x)):
        start = pl.multiple_of(part * half_rows, 16)
        for kind in range(4):
            target[kind, block] = to_half(found[kind, pl.ds(start, half_rows), :])


def whole_step_kernel(count, left_first, place_ref, *refs):
    grad_refs, refs = refs[:count], refs[count:]
    root_refs, refs = refs[:count], refs[count:]
    kept_ref, sent_ref, grads, lefts, rights, terms, found, steps = refs
    z, x = place_ref[0], place_ref[1]
    blocks, rows, order = grad_refs[0].shape
    line_blocks(z, grad_refs, grads)
    line_roots(z, root_refs, rights, 0)
    line_roots(z, root_refs, lefts, left_first)
    mine = pl.multiple_of(z * rows, 16)
    for block in range(blocks):
        whole = grads[block]
        step = to_half(dot32(lefts[block], whole))
        step = dot32(step, rights[block])
        mean = jnp.mean(jnp.mean(step * step, axis=1, keepdims=True), axis=0, keepdims=True)
        steps[...] = step * lax.rsqrt(mean + 1e-06)
        step = steps[pl.ds(mine, rows), :]
        step_parts(z, x, grad_refs[0][block], whole, step, terms, found, block, kept_ref, sent_ref)


def step_kernel(count, first, place_ref, *refs):
    grad_refs, refs = refs[:count], refs[count:]
    root_refs, refs = refs[:count], refs[count:]
    left_ref, kept_ref, sent_ref, square_ref, grads, rights, terms, found = refs
    z, x = place_ref[0], place_ref[1]
    blocks, rows, order = grad_refs[0].shape
    line_blocks(z, grad_refs, grads)
    line_roots(z, root_refs, rights, first)
    square_ref[...] = jnp.zeros_like(square_ref)
    for block in range(blocks):
        whole = grads[block]
        step = to_half(dot32(left_ref[first + block], whole))
        step = dot32(step, rights[block])
        total = jnp.sum(jnp.sum(step * step, axis=1, keepdims=True), axis=0, keepdims=True)
        square_ref[block : block + 1, :] = jnp.broadcast_to(total, (1, 128))
        step_parts(z, x, grad_refs[0][block], whole, step, terms, found, block, kept_ref, sent_ref)
        total = jnp.broadcast_to(total, (16, order))
        terms_of = jnp.zeros((16, order), full)
        row = lax.broadcasted_iota(jnp.int32, (16, order), 0)
        for index in range(3):
            part = to_half(total).astype(full)
            terms_of = jnp.where(row == index, part, terms_of)
            total = total - part
        sent_ref[4, block, :16, :] = to_half(terms_of)
        sent_ref[4, block, 16:, :] = jnp.zeros((sent_ref.shape[2] - 16, order), half)


def last_sums_kernel(vec_ref, vec_came_ref, *refs):
    count = len(refs) // 2
    mine_refs, came_refs, out_ref = refs[:count], refs[count:-1], refs[-1]
    blocks = came_refs[0].shape[1]
    out_ref[...] = jnp.zeros_like(out_ref)
    out_ref[: vec_ref.shape[0], :] = vec_ref[...] + vec_came_ref[...]
    for matrix in range(count):
        for block in range(blocks):
            at = 16 + matrix * blocks + block
            out_ref[at : at + 1, :128] = mine_refs[matrix][block : block + 1, :]
            terms = came_refs[matrix][4, block, 0:16, 0:128].astype(full)
            at += count * blocks
            out_ref[at : at + 1, :128] = jnp.sum(terms, axis=0, keepdims=True)


def apply_kernel(
    order, rates, matrix, place_ref, weight_ref, left_ref, right_ref, kept_ref, came_ref, *refs
):
    total_ref = refs[0] if len(refs) == 6 else None
    grad_ref, new_left_ref, new_right_ref, new_ref, half_ref = refs[-5:]
    x, m = place_ref[1], place_ref[2]
    local = weight_ref.shape[0]
    own = local // PAIR
    for side, ref in ((0, kept_ref), (1, came_ref)):
        for block in range(own):
            at = (x ^ side) * own + block
            rate = jnp.where(m * local + at < rates[0], rates[1], rates[2])
            if total_ref is not None:
                row = 16 + (side * 2 + matrix) * own + block
                total = total_ref[row : row + 1, 0:1]
                rate = rate * lax.rsqrt(total / (order * order) + 1e-06)
            grad_ref[at] = ref[0, block].astype(full)
            new_left_ref[at] = 0.95 * left_ref[at] + 0.05 * ref[1, block].astype(full)
            new_right_ref[at] = 0.95 * right_ref[at] + 0.05 * ref[2, block].astype(full)
            new = weight_ref[at] - rate * ref[3, block].astype(full)
            new_ref[at] = new
            half_ref[at] = to_half(new)


def vector_part_kernel(place_ref, one_ref, two_ref, bias_ref, out_ref):
    out_ref[0:2, :] = one_ref[0:2, :]
    out_ref[2:4, :] = two_ref[0:2, :]
    out_ref[4:6, :] = one_ref[2:4, :]
    out_ref[6:8, :] = two_ref[2:4, :]
    out_ref[8:9, :] = one_ref[4:5, :]
    out_ref[9:, :] = bias_row(place_ref[2], bias_ref[...], out_ref.shape[0] - 9)


def vector_step_kernel(vec_ref, total_ref, grad_ref, new_ref):
    rows = vec_ref.shape[0]
    grad_ref[...] = total_ref[:rows, :]
    for start in range(0, vec_ref.shape[1], BLOCK_VEC):
        lanes = slice(start, start + BLOCK_VEC)
        block = total_ref[:rows, lanes]
        scale = lax.rsqrt(jnp.mean(block * block, axis=-1, keepdims=True) + 1e-06)
        new_ref[:, lanes] = vec_ref[:, lanes] - 0.05 * (block * scale)


def first_kernel(place_ref, *refs):
    ins, refs = refs[:9], refs[9:]
    attn_out, feed_out, kept_ref, sent_ref = refs[:4]
    held, sems = refs[4:]
    copies = [
        pltpu.make_async_copy(ref, held.at[index], sems.at[index])
        for index, ref in enumerate(ins)
    ]
    for copy in copies:
        copy.start()
    local, own = attn_out.shape[0], kept_ref.shape[1]
    x = place_ref[1]
    for index, copy in enumerate(copies):
        copy.wait()
        if index == 0:
            attn_out[...] = to_half(held[index])
        elif index < 3:
            feed_out[(index - 1) * local : index * local] = to_half(held[index])
        else:
            kept_ref[index - 3] = to_half(held[index, pl.ds(x * own, own)])
            sent_ref[index - 3] = to_half(held[index, pl.ds((1 - x) * own, own)])


def bundle_kernel(place_ref, kept_ref, came_ref, feed_ref, left_ref, bundle_ref):
    x = place_ref[1]
    kinds, own, piece, order = kept_ref.shape
    feed = feed_ref.shape[0]
    bundle_ref[:feed] = feed_ref[...]
    for index in range(kinds):
        for block in range(own):
            for side, ref in ((0, kept_ref), (1, came_ref)):
                value = ref[index, block]
                if index < 3:
                    start = pl.multiple_of((x ^ side) * piece, 16)
                    left_ref[index * own + block, pl.ds(start, piece), :] = value
                if index == 0 or index >= 3:
                    at = (index - 3 if index else 3) * own + block
                    bundle_ref[feed + at * PAIR + (x ^ side)] = value


def move(values, dp_mask, mp_mask):
    dp, mp = lax.axis_size("dp"), lax.axis_size("mp")
    if mp_mask == 0:
        return lax.ppermute(values, "dp", [(s, s ^ dp_mask) for s in range(dp)])
    if dp_mask == 0:
        return lax.ppermute(values, "mp", [(s, s ^ mp_mask) for s in range(mp)])
    mask = dp_mask * mp + mp_mask
    return lax.ppermute(values, ("dp", "mp"), [(s, s ^ mask) for s in range(dp * mp)])


def phase(*values):
    return lax.optimization_barrier(values)


def after(values, *others):
    return lax.optimization_barrier((values,) + others)[0]


def body_lines(
    tokens,
    keep_mask,
    cotangent,
    w_attn,
    w_fc1,
    w_fc2,
    vectors,
    left_attn,
    right_attn,
    root_left_attn,
    root_right_attn,
    left_fc1,
    right_fc1,
    root_left_fc1,
    root_right_fc1,
    left_fc2,
    right_fc2,
    root_left_fc2,
    root_right_fc2,
):
    _, patches, width = tokens.shape
    local, piece, order = w_attn.shape
    z_count, group = high_size("dp"), lax.axis_size("mp")
    row_blocks = width // order
    own = local // PAIR
    rows = patches
    line_rows = order // z_count
    total_rows = group * SLOTS
    hidden_width = local // row_blocks * order
    heads = (HEADS, rows, rows)
    others = range(1, group)
    lines = range(1, z_count)
    tok, cot, mask = tokens[0], cotangent[0], keep_mask
    line, member = lax.axis_index("dp"), lax.axis_index("mp")
    place = jnp.stack([line >> 1, line & 1, member, member & 1]).astype(jnp.int32)

    attn_half, feed_half, root_kept, root_sent = local_call(
        first_kernel,
        (
            place,
            *[
                pltpu.with_memory_space_constraint(value, pltpu.HBM)
                for value in (
                    w_attn,
                    w_fc1,
                    w_fc2,
                    root_left_attn,
                    root_left_fc1,
                    root_left_fc2,
                    root_right_attn,
                    root_right_fc1,
                    root_right_fc2,
                )
            ],
        ),
        (
            shape((local, piece, order)),
            shape((2 * local, piece, order)),
            shape((6, own, piece, order)),
            shape((6, own, piece, order)),
        ),
        scratch=(pltpu.VMEM((9, local, piece, order), full), pltpu.SemaphoreType.DMA((9,))),
        in_hbm=range(1, 10),
    )
    line_came = [move(attn_half, k * PAIR, 0) for k in lines]
    root_came = move(root_sent, 1, 0)
    line_came, root_came, attn_half, mask = phase(line_came, root_came, attn_half, mask)

    plane = [(dx, high * PAIR) for high in range(group // PAIR) for dx in range(PAIR)]
    feed_far = move(feed_half, 2 * PAIR, 0)
    left_roots, bundle = local_call(
        bundle_kernel,
        (place, root_kept, root_came, feed_half),
        (
            shape((3 * own, PAIR * piece, order)),
            shape((2 * local + 4 * own * PAIR, piece, order)),
        ),
    )
    bundle_near = move(bundle, PAIR, 0)
    stack = jnp.stack([attn_half, *line_came])
    found = [stack] + [move(stack, dx, dm) for dx, dm in plane[1:]]
    normed, grad_sent, chosen = local_call(
        prepare_kernel,
        (mask, tok, cot, vectors),
        (shape((rows, width)), shape((SLOTS, width)), shape((SLOTS, rows))),
        in_smem=(),
    )
    pieces, piece_info = [], []
    for (dx, dm), part in zip(plane, found):
        pieces += [part, move(part, 0, 1)]
        piece_info += [(range(z_count), dx, dm), (range(z_count), dx, dm + 1)]
    grad_came = move(grad_sent, 0, 1)
    feed_count = 2 * local
    feed_near = jnp.stack([feed_half, bundle_near[:feed_count]])
    roots, roots_near = bundle[feed_count:], bundle_near[feed_count:]
    half_roots = roots.shape[0] // 2
    roots_first, roots_second = roots[:half_roots], roots[half_roots:]

    feed_near_came = move(feed_near, 1, 0)
    feed_last = move(feed_far, PAIR, 0)
    roots_first_far = move(roots_first, 2 * PAIR, 0)
    pair = jnp.stack([grad_sent, grad_came])
    group_grads = [pair] + [move(pair, 0, dm) for dm in range(PAIR, group, PAIR)]
    count = len(pieces)
    rows_sent, qkv, probs, attended, branch, weights = local_call(
        lambda *refs: forward_kernel(order, piece_info, *refs),
        (place, *pieces, normed, tok, mask, chosen, vectors),
        (
            shape((SLOTS, width)),
            shape((rows, 3 * width)),
            shape(heads, full),
            shape((rows, width)),
            shape((rows, width), full),
            shape((group * local, order, order)),
        ),
        scratch=(
            pltpu.VMEM((group * local, order, order), half),
            pltpu.VMEM(heads, full),
            pltpu.SemaphoreType.DMA((count * z_count,)),
            pltpu.SemaphoreType.DMA(()),
            pltpu.SemaphoreType.DMA((HEADS // 2,)),
        ),
        in_hbm=range(1, 1 + count),
        out_hbm=(2, 5),
        micros=8,
    )
    rows_sent, group_grads, feed_near_came, feed_last, roots_first_far = phase(
        rows_sent, group_grads, feed_near_came, feed_last, roots_first_far
    )

    group_rows = [rows_sent] + [move(rows_sent, 0, k) for k in others]
    feed_far = jnp.stack([feed_far, feed_last])
    feed_far_came = move(feed_far, 1, 0)
    roots_second_far = move(roots_second, 2 * PAIR, 0)

    feed_pieces = [feed_near, feed_near_came, feed_far, feed_far_came]
    feed_info = [((0, 1), 0), ((0, 1), 1), ((2, 3), 0), ((2, 3), 1)]
    outs = local_call(
        lambda *refs: hidden_kernel(order, group, feed_info, *refs),
        (place, *feed_pieces, *group_rows, *group_grads, vectors),
        (shape((SLOTS, width)),) * group
        + (shape((total_rows, width)),) * 2
        + (shape((total_rows, hidden_width)),) * 2
        + (shape((local, order, order)),),
        scratch=(
            pltpu.VMEM((2 * local, order, order), half),
            pltpu.SemaphoreType.DMA((PAIR * z_count,)),
            pltpu.SemaphoreType.DMA(()),
        ),
        in_hbm=(1, 2, 3, 4),
        out_hbm=(group + 4,),
        micros=5,
    )
    back, (all_rows, all_grads, active, grad_hidden, down) = outs[:group], outs[group:]
    back, all_rows = phase(back, all_rows)

    back = [back[0]] + [move(back[k], 0, k) for k in others]
    roots_far = jnp.concatenate([roots_first_far, roots_second_far])
    roots_last = move(roots_far, PAIR, 0)
    all_roots = [roots, roots_near, roots_far, roots_last]
    up_kept, up_sent, bias_sums = local_call(
        lambda *refs: up_grads_kernel(order, *refs),
        (place, all_rows, grad_hidden),
        (shape((own, order, order)),) * 2 + (shape((1, hidden_width), full),),
        scratch=(pltpu.VMEM((local, order, order), half),),
    )
    up_came = move(up_sent, 1, 0)
    feed_kept, feed_sent, down_kept, down_first, down_second = local_call(
        lambda *refs: down_grads_kernel(order, group, *refs),
        (place, all_grads, active, down),
        (shape((group // PAIR, SLOTS, width)),) * 2
        + (shape((own, order, order)),)
        + (shape((own // 2, order, order)),) * 2,
        scratch=(pltpu.VMEM((local, order, order), half),),
    )
    back, up_came, down_first, down_second, feed_sent, all_roots = phase(
        back, up_came, down_first, down_second, feed_sent, all_roots
    )

    def rows_of(*groups):
        blocks = sum(parts[0].shape[0] for parts in groups)
        return local_call(
            lambda *refs: row_sum_kernel(len(groups), len(groups[0]), *refs),
            (place, *[part for parts in groups for part in parts]),
            (shape((blocks, line_rows, order)),) * z_count,
        )

    def pairs_of(*groups):
        blocks = sum(parts[0].shape[0] for parts in groups)
        return local_call(
            lambda *refs: row_sum_kernel(len(groups), len(groups[0]), *refs),
            (place, *[part for parts in groups for part in parts]),
            (shape((z_count // 2, blocks, line_rows, order)),) * 2,
        )

    def add_near(kept, came):
        return [
            to_half(kept[k].astype(full) + came[k].astype(full)) for k in range(z_count // 2)
        ]

    def total_of(parts):
        total = parts[0].astype(full)
        for part in parts[1:]:
            total = total + part.astype(full)
        return to_half(total)

    def step_of(parts, matrix):
        return local_call(
            lambda *refs: step_kernel(z_count, matrix * own, *refs),
            (place, *parts, *all_roots, left_roots),
            (
                shape((4, own, piece, order)),
                shape((5, own, piece, order)),
                shape((8, 128), full),
            ),
            scratch=(
                pltpu.VMEM((own, order, order), half),
                pltpu.VMEM((own, order, order), half),
                pltpu.VMEM((order, order), full),
                pltpu.VMEM((4, line_rows, order), full),
            ),
            )

    up_near_kept, up_near_sent = pairs_of((up_kept, up_came))
    up_near = move(up_near_sent, PAIR, 0)
    down_first_came = move(down_first, 1, 0)
    feed_came = move(feed_sent, 0, 1)
    attn_kept, attn_sent, mixed, grad_middle, sums_two = local_call(
        lambda *refs: backward_kernel(order, group, *refs),
        (place, *back, chosen, tok, cot, branch, vectors, qkv, probs, attended, normed, weights),
        (
            shape((group // PAIR, local, order, order)),
            shape((group // PAIR, local, order, order)),
            shape((rows, 3 * width)),
            shape((rows, width), full),
            shape((4, width), full),
        ),
        scratch=(
            pltpu.VMEM((local, order, order), half),
            pltpu.VMEM((2, rows, width), half),
            pltpu.VMEM((4, rows, width), half),
            pltpu.VMEM((rows, width), half),
            pltpu.VMEM(heads, full),
            pltpu.SemaphoreType.DMA(()),
            pltpu.SemaphoreType.DMA(()),
        ),
        in_hbm=(1 + group + 6, 1 + group + 9),
        micros=8,
    )
    attn_sent, up_near, down_first_came, feed_came = phase(
        attn_sent, up_near, down_first_came, feed_came
    )

    attn_came = move(attn_sent, 0, 1)
    up_mine, up_other = add_near(up_near_kept, up_near)
    up_far = move(up_other, 2 * PAIR, 0)
    down_second_came = move(down_second, 1, 0)
    feed_pairs = [
        to_half(feed_kept[k].astype(full) + feed_came[k].astype(full))
        for k in range(group // PAIR)
    ]
    feed = [feed_pairs[0]] + [
        move(part, 0, (k + 1) * PAIR) for k, part in enumerate(feed_pairs[1:])
    ]
    core_parts = local_call(
        core_sum_kernel,
        (place, attn_kept, attn_came),
        (shape((own, order, order)),) * group,
    )
    core_parts, up_far, up_mine, down_second_came, feed = phase(
        core_parts, up_far, up_mine, down_second_came, feed
    )

    attn_came = [move(part, dx, dm) for (dx, dm), part in zip(plane[1:], core_parts[1:])]
    middle = own // 2
    down_near_kept, down_near_sent = pairs_of(
        (down_kept[:middle], down_first_came), (down_kept[middle:], down_second_came)
    )
    down_near = move(down_near_sent, PAIR, 0)
    up_rows = total_of([up_mine, up_far])
    up_whole_far = move(up_rows, 2 * PAIR, 0)
    block_out, input_grad, sums_one = local_call(
        lambda *refs: input_kernel(order, group // PAIR, *refs),
        (*feed, mixed, grad_middle, tok, cot, chosen, vectors, branch, weights),
        (
            shape((patches, width)),
            shape((patches, 1, width), full),
            shape((5, width), full),
        ),
        scratch=(
            pltpu.VMEM((3 * local, order, order), half),
            pltpu.SemaphoreType.DMA(()),
        ),
        in_hbm=(group // PAIR + 7,),
        in_smem=(),
    )
    (vector_sum,) = local_call(
        vector_part_kernel,
        (place, sums_one, sums_two, bias_sums),
        (shape(vectors.shape, full),),
    )
    down_mine, down_other = add_near(down_near_kept, down_near)
    down_far = move(down_other, 2 * PAIR, 0)
    up_pair = jnp.stack([up_rows, up_whole_far])
    up_pair_came = move(up_pair, PAIR, 0)
    up_kept, up_sent, up_squares = step_of(
        [up_rows, up_pair_came[0], up_whole_far, up_pair_came[1]], 1
    )
    down_rows = total_of([down_mine, down_far])
    down_whole_far = move(down_rows, 2 * PAIR, 0)
    attn_came, down_rows, down_whole_far, up_sent, vector_sum = phase(
        attn_came, down_rows, down_whole_far, up_sent, vector_sum
    )

    attn_split = rows_of((core_parts[0], *attn_came))
    attn_split = [attn_split[0]] + [move(attn_split[k], k * PAIR, 0) for k in lines]
    down_pair = jnp.stack([down_rows, down_whole_far])
    down_pair_came = move(down_pair, PAIR, 0)
    up_found = move(up_sent, 1, 0)
    down_kept, down_sent, down_squares = step_of(
        [down_rows, down_pair_came[0], down_whole_far, down_pair_came[1]], 2
    )
    attn_split, up_found, down_sent, vector_sum = phase(
        attn_split, up_found, down_sent, vector_sum
    )

    attn_rows = total_of(attn_split)
    attn_parts = [attn_rows] + [move(attn_rows, k * PAIR, 0) for k in lines]
    down_found = move(down_sent, 1, 0)
    vector_sum = vector_sum + move(vector_sum, 0, 1)
    for dm in range(PAIR, group, PAIR):
        vector_sum = vector_sum + move(vector_sum, 0, dm)
    vector_came = move(vector_sum, 1, 0)
    attn_parts, down_found, vector_came = phase(attn_parts, down_found, vector_came)

    kept, sent = local_call(
        lambda *refs: whole_step_kernel(z_count, 3 * own, *refs),
        (place, *attn_parts, *all_roots),
        (shape((4, own, piece, order)),) * 2,
        scratch=(pltpu.VMEM((own, order, order), half),) * 3
        + (
            pltpu.VMEM((order, order), full),
            pltpu.VMEM((4, line_rows, order), full),
            pltpu.VMEM((order, order), full),
        ),
    )
    came = move(sent, 1, 0)
    (last_sums,) = local_call(
        last_sums_kernel,
        (vector_sum, vector_came, up_squares, down_squares, up_found, down_found),
        (shape((24, width), full),),
        in_smem=(),
    )
    total = last_sums
    for k in lines:
        total = total + move(last_sums, k * PAIR, 0)

    def apply(rates, matrix, weight, left, right, *found):
        stat = shape(weight.shape, full)
        return local_call(
            lambda *refs: apply_kernel(order, rates, matrix, *refs),
            (place, weight, left, right, *found),
            (stat,) * 4 + (shape(weight.shape),),
        )

    attn_rates = (3 * row_blocks * row_blocks, 0.5 * D ** (-0.5), 0.5 * (D // 16) ** (-0.5))
    fc1_rates = (0, 0.0, 0.5 * D ** (-0.5))
    fc2_rates = (0, 0.0, 0.5 * FF ** (-0.5))
    vector_grad, new_vectors = local_call(
        vector_step_kernel,
        (vectors, total),
        (shape(vectors.shape, full),) * 2,
        in_smem=(),
    )
    done_attn = apply(attn_rates, 0, w_attn, left_attn, right_attn, kept, came)
    done_fc1 = apply(fc1_rates, 0, w_fc1, left_fc1, right_fc1, up_kept, up_found, total)
    done_fc2 = apply(fc2_rates, 1, w_fc2, left_fc2, right_fc2, down_kept, down_found, total)
    return (
        block_out[None],
        input_grad.transpose(1, 0, 2),
        done_attn[0],
        done_fc1[0],
        done_fc2[0],
        *done_attn[1:3],
        *done_fc1[1:3],
        *done_fc2[1:3],
        done_attn[3],
        done_fc1[3],
        done_fc2[3],
        done_attn[4],
        done_fc1[4],
        done_fc2[4],
        vector_grad,
        new_vectors,
    )


def body(tokens, keep_mask, cotangent, w_attn, *rest):
    local, piece, _ = w_attn.shape
    group = lax.axis_size("mp")
    tiled = piece % 16 == 0 and tokens.shape[0] == 1 and local % (2 * PAIR) == 0
    tiled = tiled and group == 4 and high_size("dp") == 4
    chosen_body = body_lines if tiled else body_plain
    return chosen_body(tokens, keep_mask, cotangent, w_attn, *rest)


def solution(mesh):
    rows = P(("dp", "mp"), None, None)
    blocks = P("mp", "dp", None)
    return jax.shard_map(
        body,
        mesh=mesh,
        in_specs=(rows, P(("dp", "mp"), None), rows)
        + (blocks,) * 3
        + (P(),)
        + (blocks,) * 12,
        out_specs=(rows, rows) + (blocks,) * 15 + (P(), P()),
        check_vma=False,
    )
```

```python
import jax
import jax.numpy as jnp
from jax import lax
from jax.experimental import pallas as pl
from jax.experimental.pallas import tpu as pltpu
from jax.sharding import PartitionSpec as P

D = 768
HEADS = 12
FF = 3072
BLOCK_VEC = 128
KEPT_MOST = 157
SLOTS = 160
TILE = 256
PAIR = 2

highest = lax.Precision.HIGHEST
masked_score = -1e30
half = jnp.bfloat16
full = jnp.float32


def to_half(values):
    return values.astype(half)


def layer_norm(values, gain_row, shift_row):
    centered = values - jnp.mean(values, axis=-1, keepdims=True)
    variance = jnp.mean(centered * centered, axis=-1, keepdims=True)
    return centered * lax.rsqrt(variance + 1e-06) * gain_row + shift_row


def exact_gelu(values):
    return jax.nn.gelu(values, approximate=False)


def dot32(left, right):
    return jnp.dot(left, right, preferred_element_type=full)


def row_product(left_half, right_half):
    return lax.dot_general(
        left_half, right_half, (((0,), (0,)), ((), ())), preferred_element_type=full
    )


def times_transpose(left_half, right_half):
    return lax.dot_general(
        left_half, right_half, (((1,), (1,)), ((), ())), preferred_element_type=full
    )


def swap_low(values, axis):
    count = lax.axis_size(axis)
    return lax.ppermute(values, axis, [(s, s ^ 1) for s in range(count)])


def shift_high(values, axis, step):
    count = lax.axis_size(axis)
    return lax.ppermute(values, axis, [(s, (s + step * PAIR) % count) for s in range(count)])


def high_index(axis):
    return lax.axis_index(axis) // PAIR


def low_index(axis):
    return lax.axis_index(axis) % PAIR


def high_size(axis):
    return lax.axis_size(axis) // PAIR


def pick(values, index, dim=0):
    return lax.dynamic_index_in_dim(values, index, dim, keepdims=False)


def ordered(pieces, index):
    count = len(pieces)
    if count == 2:
        first = index == 0
        return jnp.stack(
            [jnp.where(first, pieces[0], pieces[1]), jnp.where(first, pieces[1], pieces[0])]
        )
    return lax.dynamic_slice_in_dim(jnp.stack(pieces + pieces), (count - index) % count, count, 0)


def gather_low(values, axis):
    return ordered([values, swap_low(values, axis)], low_index(axis))


def gather_high(values, axis):
    count = high_size(axis)
    pieces = [values] + [shift_high(values, axis, -k) for k in range(1, count)]
    return ordered(pieces, high_index(axis))


def scatter_low(values, axis):
    low = low_index(axis)
    arrived = swap_low(pick(values, 1 - low), axis)
    return pick(values, low).astype(full) + arrived.astype(full)


def scatter_high(values, axis):
    count, high = high_size(axis), high_index(axis)
    total = pick(values, high).astype(full)
    for k in range(1, count):
        total = total + shift_high(pick(values, (high + k) % count), axis, k).astype(full)
    return total


def attend(queries, key_part, values, allowed):
    scale_factor = queries.shape[-1] ** (-0.5)
    scores = jnp.einsum("qhd,khd->hqk", queries, key_part, preferred_element_type=full)
    scores = jnp.where(allowed[None, None, :] > 0, scores * scale_factor, masked_score)
    shifted = jnp.exp(scores - jnp.max(scores, axis=-1, keepdims=True))
    probs = shifted / jnp.sum(shifted, axis=-1, keepdims=True)
    attended = jnp.einsum("hqk,khd->qhd", to_half(probs), values, preferred_element_type=full)
    return (to_half(attended), probs)


def attend_back(queries, key_part, values, probs, grad_attended):
    scale_factor = queries.shape[-1] ** (-0.5)
    grad_values = jnp.einsum(
        "hqk,qhd->khd", to_half(probs), grad_attended, preferred_element_type=full
    )
    grad_probs = jnp.einsum("qhd,khd->hqk", grad_attended, values, preferred_element_type=full)
    row_inner = jnp.sum(probs * grad_probs, axis=-1, keepdims=True)
    grad_scores = to_half(probs * (grad_probs - row_inner))
    grad_queries = (
        jnp.einsum("hqk,khd->qhd", grad_scores, key_part, preferred_element_type=full)
        * scale_factor
    )
    grad_keys = (
        jnp.einsum("hqk,qhd->khd", grad_scores, queries, preferred_element_type=full)
        * scale_factor
    )
    return jnp.stack([grad_queries, grad_keys, grad_values], axis=1)


def gather_group(rows):
    pair = jnp.stack([rows, swap_low(rows, "mp")])
    pieces = [pair] + [shift_high(pair, "mp", -k) for k in range(1, high_size("mp"))]
    return jnp.concatenate(pieces, axis=0).reshape(-1, rows.shape[-1])


def scatter_group(rows, row_count):
    pieces = rows.reshape(high_size("mp"), PAIR, row_count, rows.shape[-1])
    pairs = pieces[:, 0].astype(full) + swap_low(pieces[:, 1], "mp").astype(full)
    total = pairs[0]
    for k in range(1, high_size("mp")):
        total = total + shift_high(to_half(pairs[k]), "mp", k).astype(full)
    return total


def halves(values, dim):
    count = values.shape[dim] // 2
    return (
        lax.slice_in_dim(values, 0, count, axis=dim),
        lax.slice_in_dim(values, count, 2 * count, axis=dim),
    )


def gather_attn(blocks):
    local, piece, order = blocks.shape
    lines = gather_high(to_half(blocks), "dp")
    first, second = halves(lines, 0)
    first = gather_high(gather_low(first, "dp"), "mp")
    second = gather_low(gather_high(second, "mp"), "dp")
    both = jnp.concatenate([first, second.swapaxes(0, 1)], axis=2)
    both = gather_low(both, "mp")
    row_blocks = D // order
    both = both.transpose(1, 0, 4, 3, 2, 5, 6)
    both = both.reshape(-1, row_blocks, order, order)
    return both.transpose(1, 2, 0, 3).reshape(D, -1)


def gather_fc(blocks):
    lines = gather_low(gather_high(to_half(blocks), "dp"), "dp")
    lines = lines.transpose(2, 1, 0, 3, 4)
    return lines.reshape(blocks.shape[0], -1, blocks.shape[2])


def split_cols(matrix, order):
    rows, cols = matrix.shape
    return (
        matrix.reshape(rows // order, order, cols // order, order)
        .transpose(2, 0, 1, 3)
        .reshape(-1, order, order)
    )


def split_rows(matrix, order):
    rows, cols = matrix.shape
    return (
        matrix.reshape(rows // order, order, cols // order, order)
        .transpose(0, 2, 1, 3)
        .reshape(-1, order, order)
    )


def join_cols(blocks, row_blocks):
    count, order, _ = blocks.shape
    return (
        blocks.reshape(-1, row_blocks, order, order)
        .transpose(1, 2, 0, 3)
        .reshape(row_blocks * order, -1)
    )


def join_rows(blocks, col_blocks):
    count, order, _ = blocks.shape
    return (
        blocks.reshape(-1, col_blocks, order, order)
        .transpose(0, 2, 1, 3)
        .reshape(-1, col_blocks * order)
    )


def scatter_z(blocks):
    local, order, _ = blocks.shape
    count = high_size("dp")
    by_rows = to_half(blocks).reshape(local, count, order // count, order).swapaxes(0, 1)
    return scatter_high(by_rows, "dp")


def scatter_fc(blocks):
    local, order, _ = blocks.shape
    by_x = to_half(blocks).reshape(PAIR, local // PAIR, order, order)
    return scatter_z(scatter_low(by_x, "dp"))


def scatter_attn(blocks):
    count, order, _ = blocks.shape
    y_count = high_size("mp")
    local = count // (y_count * PAIR)
    by_core = to_half(blocks).reshape(y_count, PAIR, local, order, order).swapaxes(0, 1)
    kept = to_half(scatter_low(by_core, "mp")).reshape(
        y_count, PAIR, local // PAIR, order, order
    )
    first, second = halves(kept, 3)
    first = to_half(scatter_low(first.swapaxes(0, 1), "dp"))
    second = to_half(scatter_high(second, "mp"))
    first = scatter_high(first, "mp")
    second = scatter_low(second, "dp")
    return scatter_z(jnp.concatenate([first, second], axis=1))


def gather_z(rows):
    local, _, order = rows.shape
    return gather_high(to_half(rows), "dp").swapaxes(0, 1).reshape(local, -1, order)


def to_pair(pieces):
    local, piece, order = pieces.shape
    by_x = to_half(pieces).reshape(PAIR, local // PAIR, piece, order)
    low = low_index("dp")
    both = ordered([pick(by_x, low), swap_low(pick(by_x, 1 - low), "dp")], low)
    return both.swapaxes(0, 1).reshape(local // PAIR, PAIR * piece, order)


def from_pair(rows):
    n, local, piece, order = rows.shape
    by_x = to_half(rows).reshape(n, local, PAIR, piece // PAIR, order)
    low = low_index("dp")
    both = ordered([pick(by_x, low, 2), swap_low(pick(by_x, 1 - low, 2), "dp")], low)
    return both.swapaxes(0, 1).reshape(n, PAIR * local, piece // PAIR, order)


def shampoo_rows(grad_rows, left_root, right_root):
    grad_half = to_half(grad_rows)
    whole = gather_z(grad_half)
    rows = grad_rows.shape[1]
    cols = lax.dynamic_slice_in_dim(whole, high_index("dp") * rows, rows, 2)
    left_term = jnp.einsum("bij,bkj->bik", grad_half, whole, preferred_element_type=full)
    right_term = jnp.einsum("bji,bjk->bik", cols, whole, preferred_element_type=full)
    step = to_half(jnp.einsum("bij,bjk->bik", left_root, whole, preferred_element_type=full))
    step = jnp.einsum("bij,bjk->bik", step, right_root, preferred_element_type=full)
    squares = jnp.sum(step * step, axis=(1, 2))
    squares = gather_low(squares, "dp").reshape(-1)
    total = squares
    for k in range(1, high_size("dp")):
        total = total + shift_high(squares, "dp", k)
    sent = from_pair(jnp.stack([grad_rows, left_term, right_term, step]))
    return sent, total


def apply_step(weight, left_stat, right_stat, sent, square_total, step_rates):
    order = weight.shape[2]
    sent = sent.astype(full)
    update_scale = lax.rsqrt(square_total / (order * order) + 1e-06) * step_rates
    return (
        sent[0],
        0.95 * left_stat + 0.05 * sent[1],
        0.95 * right_stat + 0.05 * sent[2],
        weight - sent[3] * update_scale[:, None, None],
    )


def sum_all(values):
    values = values + swap_low(values, "mp")
    for axis in ("mp", "dp"):
        if axis == "dp":
            values = values + swap_low(values, "dp")
        base = values
        for k in range(1, high_size(axis)):
            values = values + shift_high(base, axis, k)
    return values


def body_plain(
    tokens,
    keep_mask,
    cotangent,
    w_attn,
    w_fc1,
    w_fc2,
    vectors,
    left_attn,
    right_attn,
    root_left_attn,
    root_right_attn,
    left_fc1,
    right_fc1,
    root_left_fc1,
    root_right_fc1,
    left_fc2,
    right_fc2,
    root_left_fc2,
    root_right_fc2,
):
    image_count, patch_count, width = tokens.shape
    row_count = image_count * patch_count
    order = w_attn.shape[2]
    row_blocks = width // order
    attn_used = gather_attn(w_attn)
    qkv_full = attn_used[:, : 3 * width]
    out_full = attn_used[:, 3 * width :]
    fc1_used = join_cols(gather_fc(w_fc1), row_blocks)
    fc2_used = join_rows(gather_fc(w_fc2), row_blocks)
    left_roots = [to_pair(v) for v in (root_left_attn, root_left_fc1, root_left_fc2)]
    right_roots = [gather_z(to_pair(v)) for v in (root_right_attn, root_right_fc1, root_right_fc2)]
    hidden_local = fc1_used.shape[1]
    flat = tokens.reshape(row_count, width).astype(full)
    keep_rows = keep_mask.reshape(row_count).astype(full)
    row_gate = jax.nn.sigmoid(jnp.sum(flat * vectors[8], axis=-1))
    row_scale = keep_rows * row_gate
    grad_output = cotangent.reshape(row_count, width).astype(full)
    grad_change = row_scale[:, None] * grad_output
    grad_feed = to_half(grad_change)
    slot = jnp.cumsum(keep_mask, axis=1) - 1
    chosen = (
        (slot[:, None, :] == lax.broadcasted_iota(jnp.int32, (1, SLOTS, 1), 1))
        & (keep_mask[:, None, :] > 0)
    ).astype(half)

    def compact(rows):
        rows = rows.reshape(image_count, patch_count, width)
        picked = jnp.einsum("bsr,brd->bsd", chosen, rows, preferred_element_type=full)
        return to_half(picked).reshape(image_count * SLOTS, width)

    def spread(rows):
        rows = rows.reshape(image_count, SLOTS, width)
        return jnp.einsum(
            "bsr,bsd->brd", chosen.astype(full), rows, precision=highest
        ).reshape(row_count, width)

    group_grads = gather_group(compact(grad_feed))
    normed, first_norm_back = jax.vjp(layer_norm, flat, vectors[0], vectors[1])
    normed_half = to_half(normed)
    qkv_bias = jnp.concatenate([vectors[4], jnp.zeros_like(vectors[4]), vectors[5]])
    mixed_half = to_half(dot32(normed_half, qkv_full) + qkv_bias)
    heads_view = mixed_half.reshape(image_count, patch_count, 3, HEADS, width // HEADS)
    queries = heads_view[:, :, 0]
    key_part = heads_view[:, :, 1]
    values = heads_view[:, :, 2]
    attended_half, probs = jax.vmap(attend)(queries, key_part, values, keep_mask)
    attended_flat = attended_half.reshape(row_count, width)
    branch = dot32(attended_flat, out_full) + vectors[6]
    middle = flat + branch
    normed_two, second_norm_back = jax.vjp(layer_norm, middle, vectors[2], vectors[3])
    group_rows = gather_group(compact(to_half(normed_two)))
    up_bias = vectors[9:].reshape(-1)
    offset = lax.axis_index("mp") * hidden_local
    local_bias = lax.dynamic_slice_in_dim(up_bias, offset, hidden_local)
    hidden = dot32(group_rows, fc1_used) + local_bias
    activated, gelu_back = jax.vjp(exact_gelu, hidden)
    activated = to_half(activated)
    grad_active = times_transpose(group_grads, fc2_used)
    grad_hidden = to_half(gelu_back(grad_active)[0])
    mlp_count = image_count * SLOTS
    grad_rows_back = scatter_group(to_half(times_transpose(grad_hidden, fc1_used)), mlp_count)
    feed = spread(scatter_group(to_half(dot32(activated, fc2_used)), mlp_count)) + vectors[7]
    change = branch + feed
    block_out = to_half(flat + row_scale[:, None] * change).reshape(tokens.shape)
    grad_logit = keep_rows * row_gate * (1.0 - row_gate) * jnp.sum(grad_output * change, axis=-1)
    fc1_rows = scatter_fc(split_cols(row_product(group_rows, grad_hidden), order))
    fc2_rows = scatter_fc(split_rows(row_product(activated, group_grads), order))
    up_part = jnp.sum(grad_hidden, axis=0, dtype=full)
    up_bias_grad = lax.dynamic_update_slice_in_dim(jnp.zeros_like(up_bias), up_part, offset, 0)
    sent_fc1, total_fc1 = shampoo_rows(fc1_rows, left_roots[1], right_roots[1])
    sent_fc2, total_fc2 = shampoo_rows(fc2_rows, left_roots[2], right_roots[2])

    grad_normed_two = spread(grad_rows_back)
    grad_middle, grad_gain_two, grad_shift_two = second_norm_back(grad_normed_two)
    grad_branch = to_half(grad_change + grad_middle)
    grad_attended = to_half(times_transpose(grad_branch, out_full))
    grad_out_full = row_product(attended_flat, grad_branch)
    grad_heads = jax.vmap(attend_back)(
        queries,
        key_part,
        values,
        probs,
        grad_attended.reshape(image_count, patch_count, HEADS, -1),
    )
    grad_mixed = to_half(grad_heads.reshape(row_count, 3 * width))
    grad_qkv_full = row_product(normed_half, grad_mixed)
    attn_rows = scatter_attn(
        split_cols(jnp.concatenate([grad_qkv_full, grad_out_full], axis=1), order)
    )
    sent_attn, total_attn = shampoo_rows(attn_rows, left_roots[0], right_roots[0])
    grad_normed = times_transpose(grad_mixed, qkv_full)
    grad_flat, grad_gain_one, grad_shift_one = first_norm_back(grad_normed)
    input_grad = (grad_output + grad_middle + grad_flat + grad_logit[:, None] * vectors[8]).reshape(
        tokens.shape
    )
    mixed_sums = jnp.sum(grad_mixed, axis=0, dtype=full)
    vector_rows = jnp.stack(
        [
            grad_gain_one,
            grad_shift_one,
            grad_gain_two,
            grad_shift_two,
            mixed_sums[:width],
            mixed_sums[2 * width :],
            jnp.sum(grad_branch, axis=0, dtype=full),
            jnp.sum(grad_feed, axis=0, dtype=full),
            jnp.sum(grad_logit[:, None] * flat, axis=0),
        ]
    )
    vector_part = jnp.concatenate([vector_rows, up_bias_grad.reshape(-1, width)], axis=0)
    vector_grad = sum_all(vector_part)

    attn_local = w_attn.shape[0]
    block_index = lax.axis_index("mp") * attn_local + lax.broadcasted_iota(
        jnp.int32, (attn_local,), 0
    )
    attn_rates = jnp.where(
        block_index // row_blocks < 3 * row_blocks, 0.5 * D ** (-0.5), 0.5 * (D // 16) ** (-0.5)
    )
    fc1_rates = jnp.full((w_fc1.shape[0],), 0.5 * D ** (-0.5), full)
    fc2_rates = jnp.full((w_fc2.shape[0],), 0.5 * FF ** (-0.5), full)
    grad_attn, new_left_attn, new_right_attn, new_attn = apply_step(
        w_attn, left_attn, right_attn, sent_attn, total_attn, attn_rates
    )
    grad_fc1, new_left_fc1, new_right_fc1, new_fc1 = apply_step(
        w_fc1, left_fc1, right_fc1, sent_fc1, total_fc1, fc1_rates
    )
    grad_fc2, new_left_fc2, new_right_fc2, new_fc2 = apply_step(
        w_fc2, left_fc2, right_fc2, sent_fc2, total_fc2, fc2_rates
    )
    vector_blocks = vector_grad.reshape(vector_grad.shape[0], -1, BLOCK_VEC)
    block_scale = lax.rsqrt(jnp.mean(vector_blocks * vector_blocks, axis=-1, keepdims=True) + 1e-06)
    new_vectors = vectors - 0.05 * (vector_blocks * block_scale).reshape(vectors.shape)
    return (
        block_out,
        input_grad,
        grad_attn,
        grad_fc1,
        grad_fc2,
        new_left_attn,
        new_right_attn,
        new_left_fc1,
        new_right_fc1,
        new_left_fc2,
        new_right_fc2,
        new_attn,
        new_fc1,
        new_fc2,
        to_half(new_attn),
        to_half(new_fc1),
        to_half(new_fc2),
        vector_grad,
        new_vectors,
    )


def normalized(values):
    centered = values - jnp.mean(values, axis=-1, keepdims=True)
    variance = jnp.mean(centered * centered, axis=-1, keepdims=True)
    scale = lax.rsqrt(variance + 1e-06)
    return centered * scale, scale


def norm_back(grad_hat, hat, scale):
    first = jnp.mean(grad_hat, axis=-1, keepdims=True)
    second = jnp.mean(grad_hat * hat, axis=-1, keepdims=True)
    return scale * (grad_hat - first - hat * second)


def col_sum(values):
    return jnp.sum(values, axis=0, keepdims=True)


def shape(dims, kind=half):
    return jax.ShapeDtypeStruct(dims, kind)


def local_call(kernel, args, outs, scratch=(), in_hbm=(), out_hbm=(), in_smem=(0,), mib=20, micros=0.05):
    def place_of(index, hbm, smem):
        if index in hbm:
            return pl.BlockSpec(memory_space=pltpu.HBM)
        if index in smem:
            return pl.BlockSpec(memory_space=pltpu.SMEM)
        return pl.BlockSpec(memory_space=pltpu.VMEM)

    return pl.pallas_call(
        kernel,
        out_shape=list(outs),
        in_specs=[place_of(i, in_hbm, in_smem) for i in range(len(args))],
        out_specs=[place_of(i, out_hbm, ()) for i in range(len(outs))],
        scratch_shapes=list(scratch),
        compiler_params=pltpu.CompilerParams(vmem_limit_bytes=mib * 2**20),
        cost_estimate=pl.CostEstimate(
            flops=int(micros * 1e9), bytes_accessed=int(micros * 1e6), transcendentals=0
        ),
    )(*args)


def gate_of(tokens, vec_ref):
    return jax.nn.sigmoid(jnp.sum(tokens * vec_ref[8:9, :], axis=-1, keepdims=True))


def keep_of(chosen):
    ones = jnp.ones((chosen.shape[0], 128), half)
    return row_product(chosen, ones)[:, :1]


def prepare_kernel(mask_ref, tok_ref, cot_ref, vec_ref, normed_ref, grad_ref, chosen_ref):
    rows = tok_ref.shape[0]
    tokens = tok_ref[...].astype(full)
    hat, _ = normalized(tokens)
    normed_ref[...] = to_half(hat * vec_ref[0:1, :] + vec_ref[1:2, :])
    mask = mask_ref[...].astype(full)
    upper = lax.broadcasted_iota(jnp.int32, (rows, rows), 0) <= lax.broadcasted_iota(
        jnp.int32, (rows, rows), 1
    )
    count = dot32(
        to_half(jnp.broadcast_to(mask, (16, rows))), jnp.where(upper, 1.0, 0.0).astype(half)
    )
    slot = count[0:1, :] - 1.0
    wanted = lax.broadcasted_iota(jnp.int32, (SLOTS, rows), 0).astype(full)
    chosen = jnp.where((slot == wanted) & (mask > 0.0), 1.0, 0.0).astype(half)
    chosen_ref[...] = chosen
    scale = keep_of(chosen) * gate_of(tokens, vec_ref)
    grad_feed = to_half(scale * cot_ref[...].astype(full))
    grad_ref[...] = to_half(dot32(chosen, grad_feed))


def head_parts(values):
    lane = lax.broadcasted_iota(jnp.int32, values.shape, 1)
    first = lane < values.shape[1] // 2
    zero = jnp.zeros_like(values)
    return jnp.where(first, values, zero), jnp.where(first, zero, values)


def copy_all(copies):
    for copy in copies:
        copy.start()
    for copy in copies:
        copy.wait()


def matrix_of(weights, kind, row_blocks):
    blocks = weights[kind * row_blocks : (kind + 1) * row_blocks]
    return blocks.reshape(row_blocks * blocks.shape[1], blocks.shape[2])


def forward_kernel(order, pieces, place_ref, *refs):
    piece_refs, refs = refs[: len(pieces)], refs[len(pieces) :]
    normed_ref, tok_ref, mask_ref, chosen_ref, vec_ref = refs[:5]
    rows_ref, qkv_ref, probs_ref, attended_ref, branch_ref, weights_hbm = refs[5:11]
    weights, probs_all, sems, out_sem, probs_sems = refs[11:]
    z, x, m = place_ref[0], place_ref[1], place_ref[2]
    piece = piece_refs[0].shape[2]
    width = normed_ref.shape[1]
    row_blocks = width // order
    copies = []
    for ref, (slots, dx, dm) in zip(piece_refs, pieces):
        for index, slot in enumerate(slots):
            row = pl.multiple_of(((z ^ slot) * PAIR + (x ^ dx)) * piece, 16)
            for col in range(row_blocks):
                target = weights.at[
                    pl.ds((m ^ dm) * row_blocks, row_blocks),
                    pl.ds(row, piece),
                    pl.ds(col * order, order),
                ]
                source = ref.at[index, pl.ds(col * row_blocks, row_blocks)]
                copies.append(pltpu.make_async_copy(source, target, sems.at[len(copies)]))
    copy_all(copies)
    keep_whole = pltpu.make_async_copy(weights, weights_hbm, out_sem)
    keep_whole.start()
    normed = normed_ref[...]
    for kind in range(3):
        matrix = matrix_of(weights, kind, row_blocks)
        for start in range(0, width, TILE):
            lanes = slice(start, start + TILE)
            part = dot32(normed, matrix[:, lanes])
            if kind != 1:
                bias_row = 4 if kind == 0 else 5
                part = part + vec_ref[bias_row : bias_row + 1, lanes]
            qkv_ref[:, kind * width + start : kind * width + start + TILE] = to_half(part)
    keep_probs = []
    head = width // HEADS
    scale = head ** (-0.5)
    allowed = mask_ref[...] > 0
    for slab in range(width // (2 * head)):
        lanes = slice(slab * 2 * head, (slab + 1) * 2 * head)
        queries = head_parts(qkv_ref[:, lanes])
        keys = qkv_ref[:, width + lanes.start : width + lanes.stop]
        values = head_parts(qkv_ref[:, 2 * width + lanes.start : 2 * width + lanes.stop])
        total = None
        for index in range(2):
            scores = times_transpose(queries[index], keys) * scale
            scores = jnp.where(allowed, scores, masked_score)
            raised = jnp.exp(scores - jnp.max(scores, axis=-1, keepdims=True))
            probs = raised / jnp.sum(raised, axis=-1, keepdims=True)
            probs_all[2 * slab + index] = probs
            part = dot32(to_half(probs), values[index])
            total = part if total is None else total + part
        attended_ref[:, lanes] = to_half(total)
        pair = pl.ds(2 * slab, 2)
        keep_probs.append(
            pltpu.make_async_copy(probs_all.at[pair], probs_ref.at[pair], probs_sems.at[slab])
        )
        keep_probs[-1].start()
    attended = attended_ref[...]
    matrix = matrix_of(weights, 3, row_blocks)
    for start in range(0, width, TILE):
        lanes = slice(start, start + TILE)
        branch_ref[:, lanes] = dot32(attended, matrix[:, lanes]) + vec_ref[6:7, lanes]
    hat, _ = normalized(tok_ref[...].astype(full) + branch_ref[...])
    second = to_half(hat * vec_ref[2:3, :] + vec_ref[3:4, :])
    rows_ref[...] = to_half(dot32(chosen_ref[...], second))
    keep_whole.wait()
    for copy in keep_probs:
        copy.wait()


def bias_row(m, values, count):
    row = lax.broadcasted_iota(jnp.int32, (count, values.shape[1]), 0)
    return jnp.where(row == m, values, 0.0)


def gelu_parts(values):
    cdf = 0.5 * (1.0 + lax.erf(values * 0.7071067811865476))
    density = jnp.exp(-0.5 * values * values) * 0.3989422804014327
    return values * cdf, cdf + values * density


def hidden_kernel(order, group, pieces, place_ref, *refs):
    piece_refs, refs = refs[: len(pieces)], refs[len(pieces) :]
    row_refs, refs = refs[:group], refs[group:]
    grad_refs, refs = refs[: group // PAIR], refs[group // PAIR :]
    vec_ref = refs[0]
    back_refs, refs = refs[1 : 1 + group], refs[1 + group :]
    rows_ref, grads_ref, active_ref, hidden_ref, down_hbm = refs[:5]
    up, down, sems, out_sem = refs[5:]
    z, x, m = place_ref[0], place_ref[1], place_ref[2]
    piece = piece_refs[0].shape[2]
    width = rows_ref.shape[1]
    row_blocks = width // order
    col_blocks = active_ref.shape[1] // order
    local = row_blocks * col_blocks
    bias = jnp.sum(bias_row(m, vec_ref[9:, :], vec_ref.shape[0] - 9), axis=0, keepdims=True)
    copies = []
    for ref, (slots, dx) in zip(piece_refs, pieces):
        for index, slot in enumerate(slots):
            row = pl.multiple_of(((z ^ slot) * PAIR + (x ^ dx)) * piece, 16)
            span = pl.ds(row, piece)
            for col in range(col_blocks):
                lanes = pl.ds(col * order, order)
                source = ref.at[index, pl.ds(col * row_blocks, row_blocks)]
                pairs = [(source, up.at[:, span, lanes])]
                for other in range(row_blocks):
                    source = ref.at[index, local + col * row_blocks + other]
                    pairs.append((source, down.at[col, span, pl.ds(other * order, order)]))
                for source, target in pairs:
                    copies.append(pltpu.make_async_copy(source, target, sems.at[len(copies)]))
    for copy in copies:
        copy.start()
    count = row_refs[0].shape[0]
    for index in range(group):
        rows_ref[index * count : (index + 1) * count, :] = row_refs[index][...]
        grads_ref[index * count : (index + 1) * count, :] = grad_refs[index // PAIR][index % PAIR]
    for copy in copies:
        copy.wait()
    keep_down = pltpu.make_async_copy(down, down_hbm, out_sem)
    keep_down.start()
    up_matrix = matrix_of(up, 0, row_blocks)
    down_matrix = matrix_of(down, 0, col_blocks)
    for start in range(0, active_ref.shape[1], TILE):
        lanes = slice(start, start + TILE)
        hidden = dot32(rows_ref[...], up_matrix[:, lanes]) + bias[:, lanes]
        active, slope = gelu_parts(hidden)
        active_ref[:, lanes] = to_half(active)
        grad = times_transpose(grads_ref[...], down_matrix[lanes, :])
        hidden_ref[:, lanes] = to_half(grad * slope)
    for start in range(0, width, TILE):
        lanes = slice(start, start + TILE)
        total = times_transpose(hidden_ref[...], up_matrix[lanes, :])
        for index in range(group):
            back_refs[index][:, lanes] = to_half(total[index * count : (index + 1) * count, :])
    keep_down.wait()


def share_blocks(place_ref, blocks, kept_ref, *sent_refs):
    own, x = kept_ref.shape[0], place_ref[1]
    kept_ref[...] = blocks[pl.ds(x * own, own)]
    count = own // len(sent_refs)
    for index, ref in enumerate(sent_refs):
        ref[...] = blocks[pl.ds((1 - x) * own + index * count, count)]


def store_blocks(blocks, order, product, by_rows):
    rows, cols = product.shape[0] // order, product.shape[1] // order
    for row in range(rows):
        for col in range(cols):
            at = row * cols + col if by_rows else col * rows + row
            blocks[at] = to_half(
                product[row * order : (row + 1) * order, col * order : (col + 1) * order]
            )


def up_grads_kernel(order, place_ref, rows_ref, hidden_ref, kept_ref, sent_ref, blocks):
    store_blocks(blocks, order, row_product(rows_ref[...], hidden_ref[...]), False)
    share_blocks(place_ref, blocks, kept_ref, sent_ref)


def down_grads_kernel(order, group, place_ref, grads_ref, active_ref, hidden_ref, down_ref, *refs):
    feed_kept_ref, feed_sent_ref, kept_ref, first_ref, second_ref, bias_ref, blocks = refs
    count = grads_ref.shape[0] // group
    down_matrix = matrix_of(down_ref, 0, down_ref.shape[0])
    for start in range(0, down_matrix.shape[1], TILE):
        lanes = slice(start, start + TILE)
        total = dot32(active_ref[...], down_matrix[:, lanes])
        for index in range(group):
            target = (feed_kept_ref, feed_sent_ref)[index % PAIR]
            target[index // PAIR, :, lanes] = to_half(total[index * count : (index + 1) * count, :])
    store_blocks(blocks, order, row_product(active_ref[...], grads_ref[...]), True)
    share_blocks(place_ref, blocks, kept_ref, first_ref, second_ref)
    bias_ref[...] = col_sum(hidden_ref[...].astype(full))


def backward_kernel(order, group, place_ref, *refs):
    back_refs, refs = refs[:group], refs[group:]
    chosen_ref, tok_ref, cot_ref, branch_ref, vec_ref = refs[:5]
    qkv_ref, probs_ref, attended_ref, normed_ref, weights_hbm = refs[5:10]
    kept_ref, sent_ref, mixed_ref, middle_ref, sums_ref = refs[10:15]
    weights, left, right, grad_attended, probs_all, sem, probs_sem = refs[15:]
    width = tok_ref.shape[1]
    row_blocks = width // order
    fetch = pltpu.make_async_copy(
        weights_hbm.at[pl.ds(3 * row_blocks, row_blocks)], weights, sem
    )
    fetch.start()
    fetch_probs = pltpu.make_async_copy(probs_ref, probs_all, probs_sem)
    fetch_probs.start()
    chosen = chosen_ref[...]
    arrived = back_refs[0][...].astype(full)
    for ref in back_refs[1:]:
        arrived = arrived + ref[...].astype(full)
    high = to_half(arrived)
    low = to_half(arrived - high.astype(full))
    grad_second = row_product(chosen, high) + row_product(chosen, low)
    tokens = tok_ref[...].astype(full)
    hat, scale = normalized(tokens + branch_ref[...])
    grad_middle = norm_back(grad_second * vec_ref[2:3, :], hat, scale)
    middle_ref[...] = grad_middle
    change = keep_of(chosen) * gate_of(tokens, vec_ref) * cot_ref[...].astype(full)
    grad_branch = to_half(change + grad_middle)
    sums_ref[0:1, :] = col_sum(grad_second * hat)
    sums_ref[1:2, :] = col_sum(grad_second)
    sums_ref[2:3, :] = col_sum(grad_branch.astype(full))
    sums_ref[3:4, :] = col_sum(to_half(change).astype(full))
    left[0] = normed_ref[...]
    left[1] = attended_ref[...]
    right[3] = grad_branch
    fetch.wait()
    matrix = matrix_of(weights, 0, row_blocks)
    for start in range(0, width, TILE):
        lanes = slice(start, start + TILE)
        grad_attended[:, lanes] = to_half(times_transpose(grad_branch, matrix[lanes, :]))
    fetch_probs.wait()
    head = width // HEADS
    factor = head ** (-0.5)
    for slab in range(width // (2 * head)):
        start, stop = slab * 2 * head, (slab + 1) * 2 * head
        queries = head_parts(qkv_ref[:, start:stop])
        key_pair = qkv_ref[:, width + start : width + stop]
        keys = head_parts(key_pair)
        values = qkv_ref[:, 2 * width + start : 2 * width + stop]
        grads = head_parts(grad_attended[:, start:stop])
        sums = [None] * 3
        for index in range(2):
            probs = probs_all[2 * slab + index]
            grad_probs = times_transpose(grads[index], values)
            inner = jnp.sum(probs * grad_probs, axis=-1, keepdims=True)
            grad_scores = to_half(probs * (grad_probs - inner))
            parts = (
                dot32(grad_scores, keys[index]),
                row_product(grad_scores, queries[index]),
                row_product(to_half(probs), grads[index]),
            )
            sums = [p if s is None else s + p for s, p in zip(sums, parts)]
        right[0, :, start:stop] = to_half(sums[0] * factor)
        right[1, :, start:stop] = to_half(sums[1] * factor)
        right[2, :, start:stop] = to_half(sums[2])
    for kind in range(3):
        mixed_ref[:, kind * width : (kind + 1) * width] = right[kind]
    core = place_ref[3]
    for high_part in range(kept_ref.shape[0]):
        for target, low_part in ((kept_ref, core), (sent_ref, 1 - core)):
            kind = high_part * PAIR + low_part
            product = row_product(left[kind // 3], right[kind])
            store_blocks(target.at[high_part], order, product, False)


def input_kernel(order, group, *refs):
    feed_refs, refs = refs[:group], refs[group:]
    mixed_ref, middle_ref, tok_ref, cot_ref, chosen_ref, vec_ref, branch_ref, weights_hbm = refs[:8]
    out_ref, grad_ref, sums_ref, weights, sem = refs[8:]
    width = tok_ref.shape[1]
    row_blocks = width // order
    fetch = pltpu.make_async_copy(weights_hbm.at[pl.ds(0, weights.shape[0])], weights, sem)
    fetch.start()
    patches = out_ref.shape[0]
    chosen = chosen_ref[...]
    tokens = tok_ref[...].astype(full)
    cotangent = cot_ref[...].astype(full)
    arrived = feed_refs[0][...].astype(full)
    for ref in feed_refs[1:]:
        arrived = arrived + ref[...].astype(full)
    high = to_half(arrived)
    low = to_half(arrived - high.astype(full))
    feed = row_product(chosen, high) + row_product(chosen, low) + vec_ref[7:8, :]
    change = branch_ref[...] + feed
    gate = gate_of(tokens, vec_ref)
    keep = keep_of(chosen)
    out_ref[...] = to_half(tokens + keep * gate * change)[:patches]
    logit = keep * gate * (1.0 - gate) * jnp.sum(cotangent * change, axis=-1, keepdims=True)
    base = cotangent + middle_ref[...] + logit * vec_ref[8:9, :]
    sums_ref[4:5, :] = col_sum(logit * tokens)
    sums_ref[2:3, :] = col_sum(mixed_ref[:, :width].astype(full))
    sums_ref[3:4, :] = col_sum(mixed_ref[:, 2 * width :].astype(full))
    hat, scale = normalized(tokens)
    fetch.wait()
    grad_normed = None
    for kind in range(3):
        part = times_transpose(
            mixed_ref[:, kind * width : (kind + 1) * width], matrix_of(weights, kind, row_blocks)
        )
        grad_normed = part if grad_normed is None else grad_normed + part
    sums_ref[0:1, :] = col_sum(grad_normed * hat)
    sums_ref[1:2, :] = col_sum(grad_normed)
    grad = base + norm_back(grad_normed * vec_ref[0:1, :], hat, scale)
    grad_ref[:, 0, :] = grad[:patches]


def core_sum_kernel(place_ref, kept_ref, came_ref, *out_refs):
    x, m = place_ref[1], place_ref[2]
    own = kept_ref.shape[1] // PAIR
    for index, out_ref in enumerate(out_refs):
        dy, dx = index // PAIR, index % PAIR
        high = (m // PAIR) ^ dy
        for block in range(own):
            at = (x ^ dx) * own + block
            out_ref[block] = to_half(
                kept_ref[high, at].astype(full) + came_ref[high, at].astype(full)
            )


def row_sum_kernel(groups, count, place_ref, *refs):
    ins, outs = refs[: groups * count], refs[groups * count :]
    rows = outs[0].shape[-2]
    near = len(outs) == 2
    slots = outs[0].shape[0] * 2 if near else len(outs)
    for slot in range(slots):
        out_ref = outs[slot % 2].at[slot // 2] if near else outs[slot]
        start = pl.multiple_of((place_ref[0] ^ slot) * rows, 16)
        at = 0
        for group in range(groups):
            parts = ins[group * count : (group + 1) * count]
            for block in range(parts[0].shape[0]):
                total = parts[0][block, pl.ds(start, rows), :].astype(full)
                for ref in parts[1:]:
                    total = total + ref[block, pl.ds(start, rows), :].astype(full)
                out_ref[at] = to_half(total)
                at += 1


def line_blocks(z, refs, target, first=0):
    for slot, ref in enumerate(refs):
        rows = ref.shape[-2]
        start = pl.multiple_of((z ^ slot) * rows, 16)
        for block in range(target.shape[0]):
            target[block, pl.ds(start, rows), :] = ref[first + block]


def line_roots(z, refs, target, first):
    for slot, ref in enumerate(refs):
        rows = ref.shape[1]
        for block in range(target.shape[0]):
            for part in range(PAIR):
                start = pl.multiple_of((z ^ slot) * (PAIR * rows) + part * rows, 16)
                at = (first + block) * PAIR + part
                target[block, pl.ds(start, rows), :] = ref[at]


def step_parts(z, x, own, whole, step, terms, found, block, kept_ref, sent_ref):
    rows, order = own.shape
    mine = pl.multiple_of(z * rows, 16)
    half_rows = rows // PAIR
    terms[...] = row_product(whole, whole)
    found[0] = own.astype(full)
    found[1] = times_transpose(own, whole)
    found[2] = terms[pl.ds(mine, rows), :]
    found[3] = step
    for target, part in ((kept_ref, x), (sent_ref, 1 - x)):
        start = pl.multiple_of(part * half_rows, 16)
        for kind in range(4):
            target[kind, block] = to_half(found[kind, pl.ds(start, half_rows), :])


def whole_step_kernel(count, left_first, place_ref, *refs):
    grad_refs, refs = refs[:count], refs[count:]
    root_refs, refs = refs[:count], refs[count:]
    kept_ref, sent_ref, grads, lefts, rights, terms, found, steps = refs
    z, x = place_ref[0], place_ref[1]
    blocks, rows, order = grad_refs[0].shape
    line_blocks(z, grad_refs, grads)
    line_roots(z, root_refs, rights, 0)
    line_roots(z, root_refs, lefts, left_first)
    mine = pl.multiple_of(z * rows, 16)
    for block in range(blocks):
        whole = grads[block]
        step = to_half(dot32(lefts[block], whole))
        step = dot32(step, rights[block])
        mean = jnp.mean(jnp.mean(step * step, axis=1, keepdims=True), axis=0, keepdims=True)
        steps[...] = step * lax.rsqrt(mean + 1e-06)
        step = steps[pl.ds(mine, rows), :]
        step_parts(z, x, grad_refs[0][block], whole, step, terms, found, block, kept_ref, sent_ref)


def step_kernel(count, first, place_ref, *refs):
    grad_refs, refs = refs[:count], refs[count:]
    root_refs, refs = refs[:count], refs[count:]
    left_ref, kept_ref, sent_ref, square_ref, grads, rights, terms, found = refs
    z, x = place_ref[0], place_ref[1]
    blocks, rows, order = grad_refs[0].shape
    line_blocks(z, grad_refs, grads)
    line_roots(z, root_refs, rights, first)
    square_ref[...] = jnp.zeros_like(square_ref)
    for block in range(blocks):
        whole = grads[block]
        step = to_half(dot32(left_ref[first + block], whole))
        step = dot32(step, rights[block])
        total = jnp.sum(jnp.sum(step * step, axis=1, keepdims=True), axis=0, keepdims=True)
        square_ref[block : block + 1, :] = jnp.broadcast_to(total, (1, 128))
        step_parts(z, x, grad_refs[0][block], whole, step, terms, found, block, kept_ref, sent_ref)
        total = jnp.broadcast_to(total, (16, order))
        terms_of = jnp.zeros((16, order), full)
        row = lax.broadcasted_iota(jnp.int32, (16, order), 0)
        for index in range(3):
            part = to_half(total).astype(full)
            terms_of = jnp.where(row == index, part, terms_of)
            total = total - part
        sent_ref[4, block, :16, :] = to_half(terms_of)
        sent_ref[4, block, 16:, :] = jnp.zeros((sent_ref.shape[2] - 16, order), half)


def last_sums_kernel(vec_ref, vec_came_ref, *refs):
    count = len(refs) // 2
    mine_refs, came_refs, out_ref = refs[:count], refs[count:-1], refs[-1]
    blocks = came_refs[0].shape[1]
    out_ref[...] = jnp.zeros_like(out_ref)
    out_ref[: vec_ref.shape[0], :] = vec_ref[...] + vec_came_ref[...]
    for matrix in range(count):
        for block in range(blocks):
            at = 16 + matrix * blocks + block
            out_ref[at : at + 1, :128] = mine_refs[matrix][block : block + 1, :]
            terms = came_refs[matrix][4, block, 0:16, 0:128].astype(full)
            at += count * blocks
            out_ref[at : at + 1, :128] = jnp.sum(terms, axis=0, keepdims=True)


def apply_kernel(
    order, rates, matrix, place_ref, weight_ref, left_ref, right_ref, kept_ref, came_ref, *refs
):
    total_ref = refs[0] if len(refs) == 6 else None
    grad_ref, new_left_ref, new_right_ref, new_ref, half_ref = refs[-5:]
    x, m = place_ref[1], place_ref[2]
    local = weight_ref.shape[0]
    own = local // PAIR
    for side, ref in ((0, kept_ref), (1, came_ref)):
        for block in range(own):
            at = (x ^ side) * own + block
            rate = jnp.where(m * local + at < rates[0], rates[1], rates[2])
            if total_ref is not None:
                row = 16 + (side * 2 + matrix) * own + block
                total = total_ref[row : row + 1, 0:1]
                rate = rate * lax.rsqrt(total / (order * order) + 1e-06)
            grad_ref[at] = ref[0, block].astype(full)
            new_left_ref[at] = 0.95 * left_ref[at] + 0.05 * ref[1, block].astype(full)
            new_right_ref[at] = 0.95 * right_ref[at] + 0.05 * ref[2, block].astype(full)
            new = weight_ref[at] - rate * ref[3, block].astype(full)
            new_ref[at] = new
            half_ref[at] = to_half(new)


def vector_part_kernel(place_ref, one_ref, two_ref, bias_ref, out_ref):
    out_ref[0:2, :] = one_ref[0:2, :]
    out_ref[2:4, :] = two_ref[0:2, :]
    out_ref[4:6, :] = one_ref[2:4, :]
    out_ref[6:8, :] = two_ref[2:4, :]
    out_ref[8:9, :] = one_ref[4:5, :]
    out_ref[9:, :] = bias_row(place_ref[2], bias_ref[...], out_ref.shape[0] - 9)


def vector_step_kernel(vec_ref, total_ref, grad_ref, new_ref):
    rows = vec_ref.shape[0]
    grad_ref[...] = total_ref[:rows, :]
    for start in range(0, vec_ref.shape[1], BLOCK_VEC):
        lanes = slice(start, start + BLOCK_VEC)
        block = total_ref[:rows, lanes]
        scale = lax.rsqrt(jnp.mean(block * block, axis=-1, keepdims=True) + 1e-06)
        new_ref[:, lanes] = vec_ref[:, lanes] - 0.05 * (block * scale)


def first_kernel(place_ref, *refs):
    ins, refs = refs[:9], refs[9:]
    attn_out, feed_out, kept_ref, sent_ref = refs[:4]
    held, sems = refs[4:]
    copies = [
        pltpu.make_async_copy(ref, held.at[index], sems.at[index])
        for index, ref in enumerate(ins)
    ]
    for copy in copies:
        copy.start()
    local, own = attn_out.shape[0], kept_ref.shape[1]
    x = place_ref[1]
    for index, copy in enumerate(copies):
        copy.wait()
        if index == 0:
            attn_out[...] = to_half(held[index])
        elif index < 3:
            feed_out[(index - 1) * local : index * local] = to_half(held[index])
        else:
            kept_ref[index - 3] = to_half(held[index, pl.ds(x * own, own)])
            sent_ref[index - 3] = to_half(held[index, pl.ds((1 - x) * own, own)])


def bundle_kernel(place_ref, kept_ref, came_ref, feed_ref, left_ref, bundle_ref):
    x = place_ref[1]
    kinds, own, piece, order = kept_ref.shape
    feed = feed_ref.shape[0]
    bundle_ref[:feed] = feed_ref[...]
    for index in range(kinds):
        for block in range(own):
            for side, ref in ((0, kept_ref), (1, came_ref)):
                value = ref[index, block]
                if index < 3:
                    start = pl.multiple_of((x ^ side) * piece, 16)
                    left_ref[index * own + block, pl.ds(start, piece), :] = value
                if index == 0 or index >= 3:
                    at = (index - 3 if index else 3) * own + block
                    bundle_ref[feed + at * PAIR + (x ^ side)] = value


def move(values, dp_mask, mp_mask):
    dp, mp = lax.axis_size("dp"), lax.axis_size("mp")
    if mp_mask == 0:
        return lax.ppermute(values, "dp", [(s, s ^ dp_mask) for s in range(dp)])
    if dp_mask == 0:
        return lax.ppermute(values, "mp", [(s, s ^ mp_mask) for s in range(mp)])
    mask = dp_mask * mp + mp_mask
    return lax.ppermute(values, ("dp", "mp"), [(s, s ^ mask) for s in range(dp * mp)])


def phase(*values):
    return lax.optimization_barrier(values)


def after(values, *others):
    return lax.optimization_barrier((values,) + others)[0]


def body_lines(
    tokens,
    keep_mask,
    cotangent,
    w_attn,
    w_fc1,
    w_fc2,
    vectors,
    left_attn,
    right_attn,
    root_left_attn,
    root_right_attn,
    left_fc1,
    right_fc1,
    root_left_fc1,
    root_right_fc1,
    left_fc2,
    right_fc2,
    root_left_fc2,
    root_right_fc2,
):
    _, patches, width = tokens.shape
    local, piece, order = w_attn.shape
    z_count, group = high_size("dp"), lax.axis_size("mp")
    row_blocks = width // order
    own = local // PAIR
    rows = patches
    line_rows = order // z_count
    total_rows = group * SLOTS
    hidden_width = local // row_blocks * order
    heads = (HEADS, rows, rows)
    others = range(1, group)
    lines = range(1, z_count)
    tok, cot, mask = tokens[0], cotangent[0], keep_mask
    line, member = lax.axis_index("dp"), lax.axis_index("mp")
    place = jnp.stack([line >> 1, line & 1, member, member & 1]).astype(jnp.int32)

    attn_half, feed_half, root_kept, root_sent = local_call(
        first_kernel,
        (
            place,
            *[
                pltpu.with_memory_space_constraint(value, pltpu.HBM)
                for value in (
                    w_attn,
                    w_fc1,
                    w_fc2,
                    root_left_attn,
                    root_left_fc1,
                    root_left_fc2,
                    root_right_attn,
                    root_right_fc1,
                    root_right_fc2,
                )
            ],
        ),
        (
            shape((local, piece, order)),
            shape((2 * local, piece, order)),
            shape((6, own, piece, order)),
            shape((6, own, piece, order)),
        ),
        scratch=(pltpu.VMEM((9, local, piece, order), full), pltpu.SemaphoreType.DMA((9,))),
        in_hbm=range(1, 10),
    )
    line_came = [move(attn_half, k * PAIR, 0) for k in lines]
    root_came = move(root_sent, 1, 0)
    line_came, root_came, attn_half, mask = phase(line_came, root_came, attn_half, mask)

    plane = [(dx, high * PAIR) for high in range(group // PAIR) for dx in range(PAIR)]
    feed_far = move(feed_half, 2 * PAIR, 0)
    left_roots, bundle = local_call(
        bundle_kernel,
        (place, root_kept, root_came, feed_half),
        (
            shape((3 * own, PAIR * piece, order)),
            shape((2 * local + 4 * own * PAIR, piece, order)),
        ),
    )
    bundle_near = move(bundle, PAIR, 0)
    stack = jnp.stack([attn_half, *line_came])
    found = [stack] + [move(stack, dx, dm) for dx, dm in plane[1:]]
    normed, grad_sent, chosen = local_call(
        prepare_kernel,
        (mask, tok, cot, vectors),
        (shape((rows, width)), shape((SLOTS, width)), shape((SLOTS, rows))),
        in_smem=(),
    )
    pieces, piece_info = [], []
    for (dx, dm), part in zip(plane, found):
        pieces += [part, move(part, 0, 1)]
        piece_info += [(range(z_count), dx, dm), (range(z_count), dx, dm + 1)]
    grad_came = move(grad_sent, 0, 1)
    feed_count = 2 * local
    feed_near = jnp.stack([feed_half, bundle_near[:feed_count]])
    roots, roots_near = bundle[feed_count:], bundle_near[feed_count:]
    half_roots = roots.shape[0] // 2
    roots_first, roots_second = roots[:half_roots], roots[half_roots:]

    feed_near_came = move(feed_near, 1, 0)
    feed_last = move(feed_far, PAIR, 0)
    roots_first_far = move(roots_first, 2 * PAIR, 0)
    pair = jnp.stack([grad_sent, grad_came])
    group_grads = [pair] + [move(pair, 0, dm) for dm in range(PAIR, group, PAIR)]
    count = len(pieces)
    rows_sent, qkv, probs, attended, branch, weights = local_call(
        lambda *refs: forward_kernel(order, piece_info, *refs),
        (place, *pieces, normed, tok, mask, chosen, vectors),
        (
            shape((SLOTS, width)),
            shape((rows, 3 * width)),
            shape(heads, full),
            shape((rows, width)),
            shape((rows, width), full),
            shape((group * row_blocks, order, width)),
        ),
        scratch=(
            pltpu.VMEM((group * row_blocks, order, width), half),
            pltpu.VMEM(heads, full),
            pltpu.SemaphoreType.DMA((count * z_count * row_blocks,)),
            pltpu.SemaphoreType.DMA(()),
            pltpu.SemaphoreType.DMA((HEADS // 2,)),
        ),
        in_hbm=range(1, 1 + count),
        out_hbm=(2, 5),
        micros=8,
    )
    rows_sent, group_grads, feed_last, roots_first_far = phase(
        rows_sent, group_grads, feed_last, roots_first_far
    )

    group_rows = [rows_sent] + [move(rows_sent, 0, k) for k in others]
    feed_far = jnp.stack([feed_far, feed_last])
    feed_far_came = move(feed_far, 1, 0)
    roots_second_far = move(roots_second, 2 * PAIR, 0)

    feed_pieces = [feed_near, feed_near_came, feed_far, feed_far_came]
    feed_info = [((0, 1), 0), ((0, 1), 1), ((2, 3), 0), ((2, 3), 1)]
    outs = local_call(
        lambda *refs: hidden_kernel(order, group, feed_info, *refs),
        (place, *feed_pieces, *group_rows, *group_grads, vectors),
        (shape((SLOTS, width)),) * group
        + (shape((total_rows, width)),) * 2
        + (shape((total_rows, hidden_width)),) * 2
        + (shape((local // row_blocks, order, width)),),
        scratch=(
            pltpu.VMEM((row_blocks, order, hidden_width), half),
            pltpu.VMEM((local // row_blocks, order, width), half),
            pltpu.SemaphoreType.DMA((PAIR * z_count * (local // row_blocks + local),)),
            pltpu.SemaphoreType.DMA(()),
        ),
        in_hbm=(1, 2, 3, 4),
        out_hbm=(group + 4,),
        micros=5,
    )
    back, (all_rows, all_grads, active, grad_hidden, down) = outs[:group], outs[group:]
    back, all_rows = phase(back, all_rows)

    back = [back[0]] + [move(back[k], 0, k) for k in others]
    roots_far = jnp.concatenate([roots_first_far, roots_second_far])
    roots_last = move(roots_far, PAIR, 0)
    all_roots = [roots, roots_near, roots_far, roots_last]
    up_kept, up_sent = local_call(
        lambda *refs: up_grads_kernel(order, *refs),
        (place, all_rows, grad_hidden),
        (shape((own, order, order)),) * 2,
        scratch=(pltpu.VMEM((local, order, order), half),),
    )
    up_came = move(up_sent, 1, 0)
    feed_kept, feed_sent, down_kept, down_first, down_second, bias_sums = local_call(
        lambda *refs: down_grads_kernel(order, group, *refs),
        (place, all_grads, active, grad_hidden, down),
        (shape((group // PAIR, SLOTS, width)),) * 2
        + (shape((own, order, order)),)
        + (shape((own // 2, order, order)),) * 2
        + (shape((1, hidden_width), full),),
        scratch=(pltpu.VMEM((local, order, order), half),),
    )
    back, down_first, down_second, feed_sent, all_roots = phase(
        back, down_first, down_second, feed_sent, all_roots
    )

    def rows_of(*groups):
        blocks = sum(parts[0].shape[0] for parts in groups)
        return local_call(
            lambda *refs: row_sum_kernel(len(groups), len(groups[0]), *refs),
            (place, *[part for parts in groups for part in parts]),
            (shape((blocks, line_rows, order)),) * z_count,
        )

    def pairs_of(*groups):
        blocks = sum(parts[0].shape[0] for parts in groups)
        return local_call(
            lambda *refs: row_sum_kernel(len(groups), len(groups[0]), *refs),
            (place, *[part for parts in groups for part in parts]),
            (shape((z_count // 2, blocks, line_rows, order)),) * 2,
        )

    def add_near(kept, came):
        return [
            to_half(kept[k].astype(full) + came[k].astype(full)) for k in range(z_count // 2)
        ]

    def total_of(parts):
        total = parts[0].astype(full)
        for part in parts[1:]:
            total = total + part.astype(full)
        return to_half(total)

    def step_of(parts, matrix):
        return local_call(
            lambda *refs: step_kernel(z_count, matrix * own, *refs),
            (place, *parts, *all_roots, left_roots),
            (
                shape((4, own, piece, order)),
                shape((5, own, piece, order)),
                shape((8, 128), full),
            ),
            scratch=(
                pltpu.VMEM((own, order, order), half),
                pltpu.VMEM((own, order, order), half),
                pltpu.VMEM((order, order), full),
                pltpu.VMEM((4, line_rows, order), full),
            ),
            )

    up_near_kept, up_near_sent = pairs_of((up_kept, up_came))
    up_near = move(up_near_sent, PAIR, 0)
    down_first_came = move(down_first, 1, 0)
    feed_came = move(feed_sent, 0, 1)
    attn_kept, attn_sent, mixed, grad_middle, sums_two = local_call(
        lambda *refs: backward_kernel(order, group, *refs),
        (place, *back, chosen, tok, cot, branch, vectors, qkv, probs, attended, normed, weights),
        (
            shape((group // PAIR, local, order, order)),
            shape((group // PAIR, local, order, order)),
            shape((rows, 3 * width)),
            shape((rows, width), full),
            shape((4, width), full),
        ),
        scratch=(
            pltpu.VMEM((row_blocks, order, width), half),
            pltpu.VMEM((2, rows, width), half),
            pltpu.VMEM((4, rows, width), half),
            pltpu.VMEM((rows, width), half),
            pltpu.VMEM(heads, full),
            pltpu.SemaphoreType.DMA(()),
            pltpu.SemaphoreType.DMA(()),
        ),
        in_hbm=(1 + group + 6, 1 + group + 9),
        micros=8,
    )
    attn_sent, up_near, down_first_came, feed_came = phase(
        attn_sent, up_near, down_first_came, feed_came
    )

    attn_came = move(attn_sent, 0, 1)
    up_mine, up_other = add_near(up_near_kept, up_near)
    up_far = move(up_other, 2 * PAIR, 0)
    down_second_came = move(down_second, 1, 0)
    feed_pairs = [
        to_half(feed_kept[k].astype(full) + feed_came[k].astype(full))
        for k in range(group // PAIR)
    ]
    feed = [feed_pairs[0]] + [
        move(part, 0, (k + 1) * PAIR) for k, part in enumerate(feed_pairs[1:])
    ]
    core_parts = local_call(
        core_sum_kernel,
        (place, attn_kept, attn_came),
        (shape((own, order, order)),) * group,
    )
    core_parts, up_mine, down_second_came, feed = phase(
        core_parts, up_mine, down_second_came, feed
    )

    attn_came = [move(part, dx, dm) for (dx, dm), part in zip(plane[1:], core_parts[1:])]
    middle = own // 2
    down_near_kept, down_near_sent = pairs_of(
        (down_kept[:middle], down_first_came), (down_kept[middle:], down_second_came)
    )
    down_near = move(down_near_sent, PAIR, 0)
    up_rows = total_of([up_mine, up_far])
    up_whole_far = move(up_rows, 2 * PAIR, 0)
    block_out, input_grad, sums_one = local_call(
        lambda *refs: input_kernel(order, group // PAIR, *refs),
        (*feed, mixed, grad_middle, tok, cot, chosen, vectors, branch, weights),
        (
            shape((patches, width)),
            shape((patches, 1, width), full),
            shape((5, width), full),
        ),
        scratch=(
            pltpu.VMEM((3 * row_blocks, order, width), half),
            pltpu.SemaphoreType.DMA(()),
        ),
        in_hbm=(group // PAIR + 7,),
        in_smem=(),
    )
    (vector_sum,) = local_call(
        vector_part_kernel,
        (place, sums_one, sums_two, bias_sums),
        (shape(vectors.shape, full),),
    )
    down_mine, down_other = add_near(down_near_kept, down_near)
    down_far = move(down_other, 2 * PAIR, 0)
    up_pair = jnp.stack([up_rows, up_whole_far])
    up_pair_came = move(up_pair, PAIR, 0)
    up_kept, up_sent, up_squares = step_of(
        [up_rows, up_pair_came[0], up_whole_far, up_pair_came[1]], 1
    )
    down_rows = total_of([down_mine, down_far])
    down_whole_far = move(down_rows, 2 * PAIR, 0)
    attn_came, down_rows, down_whole_far, up_sent, vector_sum = phase(
        attn_came, down_rows, down_whole_far, up_sent, vector_sum
    )

    attn_split = rows_of((core_parts[0], *attn_came))
    attn_split = [attn_split[0]] + [move(attn_split[k], k * PAIR, 0) for k in lines]
    down_pair = jnp.stack([down_rows, down_whole_far])
    down_pair_came = move(down_pair, PAIR, 0)
    up_found = move(up_sent, 1, 0)
    down_kept, down_sent, down_squares = step_of(
        [down_rows, down_pair_came[0], down_whole_far, down_pair_came[1]], 2
    )
    attn_split, up_found, down_sent, vector_sum = phase(
        attn_split, up_found, down_sent, vector_sum
    )

    attn_rows = total_of(attn_split)
    attn_parts = [attn_rows] + [move(attn_rows, k * PAIR, 0) for k in lines]
    down_found = move(down_sent, 1, 0)
    vector_sum = vector_sum + move(vector_sum, 0, 1)
    for dm in range(PAIR, group, PAIR):
        vector_sum = vector_sum + move(vector_sum, 0, dm)
    vector_came = move(vector_sum, 1, 0)
    attn_parts, down_found, vector_came = phase(attn_parts, down_found, vector_came)

    kept, sent = local_call(
        lambda *refs: whole_step_kernel(z_count, 3 * own, *refs),
        (place, *attn_parts, *all_roots),
        (shape((4, own, piece, order)),) * 2,
        scratch=(pltpu.VMEM((own, order, order), half),) * 3
        + (
            pltpu.VMEM((order, order), full),
            pltpu.VMEM((4, line_rows, order), full),
            pltpu.VMEM((order, order), full),
        ),
    )
    came = move(sent, 1, 0)
    (last_sums,) = local_call(
        last_sums_kernel,
        (vector_sum, vector_came, up_squares, down_squares, up_found, down_found),
        (shape((24, width), full),),
        in_smem=(),
    )
    total = last_sums
    for k in lines:
        total = total + move(last_sums, k * PAIR, 0)

    def apply(rates, matrix, weight, left, right, *found):
        stat = shape(weight.shape, full)
        return local_call(
            lambda *refs: apply_kernel(order, rates, matrix, *refs),
            (place, weight, left, right, *found),
            (stat,) * 4 + (shape(weight.shape),),
        )

    attn_rates = (3 * row_blocks * row_blocks, 0.5 * D ** (-0.5), 0.5 * (D // 16) ** (-0.5))
    fc1_rates = (0, 0.0, 0.5 * D ** (-0.5))
    fc2_rates = (0, 0.0, 0.5 * FF ** (-0.5))
    vector_grad, new_vectors = local_call(
        vector_step_kernel,
        (vectors, total),
        (shape(vectors.shape, full),) * 2,
        in_smem=(),
    )
    done_attn = apply(attn_rates, 0, w_attn, left_attn, right_attn, kept, came)
    done_fc1 = apply(fc1_rates, 0, w_fc1, left_fc1, right_fc1, up_kept, up_found, total)
    done_fc2 = apply(fc2_rates, 1, w_fc2, left_fc2, right_fc2, down_kept, down_found, total)
    return (
        block_out[None],
        input_grad.transpose(1, 0, 2),
        done_attn[0],
        done_fc1[0],
        done_fc2[0],
        *done_attn[1:3],
        *done_fc1[1:3],
        *done_fc2[1:3],
        done_attn[3],
        done_fc1[3],
        done_fc2[3],
        done_attn[4],
        done_fc1[4],
        done_fc2[4],
        vector_grad,
        new_vectors,
    )


def body(tokens, keep_mask, cotangent, w_attn, *rest):
    local, piece, _ = w_attn.shape
    group = lax.axis_size("mp")
    tiled = piece % 16 == 0 and tokens.shape[0] == 1 and local % (2 * PAIR) == 0
    tiled = tiled and group == 4 and high_size("dp") == 4
    chosen_body = body_lines if tiled else body_plain
    return chosen_body(tokens, keep_mask, cotangent, w_attn, *rest)


def solution(mesh):
    rows = P(("dp", "mp"), None, None)
    blocks = P("mp", "dp", None)
    return jax.shard_map(
        body,
        mesh=mesh,
        in_specs=(rows, P(("dp", "mp"), None), rows)
        + (blocks,) * 3
        + (P(),)
        + (blocks,) * 12,
        out_specs=(rows, rows) + (blocks,) * 15 + (P(), P()),
        check_vma=False,
    )
```

```python
import jax
import jax.numpy as jnp
from jax import lax
from jax.experimental import pallas as pl
from jax.experimental.pallas import tpu as pltpu
from jax.sharding import PartitionSpec as P

D = 768
HEADS = 12
FF = 3072
BLOCK_VEC = 128
KEPT_MOST = 157
SLOTS = 160
TILE = 256
PAIR = 2

highest = lax.Precision.HIGHEST
masked_score = -1e30
half = jnp.bfloat16
full = jnp.float32


def to_half(values):
    return values.astype(half)


def layer_norm(values, gain_row, shift_row):
    centered = values - jnp.mean(values, axis=-1, keepdims=True)
    variance = jnp.mean(centered * centered, axis=-1, keepdims=True)
    return centered * lax.rsqrt(variance + 1e-06) * gain_row + shift_row


def exact_gelu(values):
    return jax.nn.gelu(values, approximate=False)


def dot32(left, right):
    return jnp.dot(left, right, preferred_element_type=full)


def row_product(left_half, right_half):
    return lax.dot_general(
        left_half, right_half, (((0,), (0,)), ((), ())), preferred_element_type=full
    )


def times_transpose(left_half, right_half):
    return lax.dot_general(
        left_half, right_half, (((1,), (1,)), ((), ())), preferred_element_type=full
    )


def swap_low(values, axis):
    count = lax.axis_size(axis)
    return lax.ppermute(values, axis, [(s, s ^ 1) for s in range(count)])


def shift_high(values, axis, step):
    count = lax.axis_size(axis)
    return lax.ppermute(values, axis, [(s, (s + step * PAIR) % count) for s in range(count)])


def high_index(axis):
    return lax.axis_index(axis) // PAIR


def low_index(axis):
    return lax.axis_index(axis) % PAIR


def high_size(axis):
    return lax.axis_size(axis) // PAIR


def pick(values, index, dim=0):
    return lax.dynamic_index_in_dim(values, index, dim, keepdims=False)


def ordered(pieces, index):
    count = len(pieces)
    if count == 2:
        first = index == 0
        return jnp.stack(
            [jnp.where(first, pieces[0], pieces[1]), jnp.where(first, pieces[1], pieces[0])]
        )
    return lax.dynamic_slice_in_dim(jnp.stack(pieces + pieces), (count - index) % count, count, 0)


def gather_low(values, axis):
    return ordered([values, swap_low(values, axis)], low_index(axis))


def gather_high(values, axis):
    count = high_size(axis)
    pieces = [values] + [shift_high(values, axis, -k) for k in range(1, count)]
    return ordered(pieces, high_index(axis))


def scatter_low(values, axis):
    low = low_index(axis)
    arrived = swap_low(pick(values, 1 - low), axis)
    return pick(values, low).astype(full) + arrived.astype(full)


def scatter_high(values, axis):
    count, high = high_size(axis), high_index(axis)
    total = pick(values, high).astype(full)
    for k in range(1, count):
        total = total + shift_high(pick(values, (high + k) % count), axis, k).astype(full)
    return total


def attend(queries, key_part, values, allowed):
    scale_factor = queries.shape[-1] ** (-0.5)
    scores = jnp.einsum("qhd,khd->hqk", queries, key_part, preferred_element_type=full)
    scores = jnp.where(allowed[None, None, :] > 0, scores * scale_factor, masked_score)
    shifted = jnp.exp(scores - jnp.max(scores, axis=-1, keepdims=True))
    probs = shifted / jnp.sum(shifted, axis=-1, keepdims=True)
    attended = jnp.einsum("hqk,khd->qhd", to_half(probs), values, preferred_element_type=full)
    return (to_half(attended), probs)


def attend_back(queries, key_part, values, probs, grad_attended):
    scale_factor = queries.shape[-1] ** (-0.5)
    grad_values = jnp.einsum(
        "hqk,qhd->khd", to_half(probs), grad_attended, preferred_element_type=full
    )
    grad_probs = jnp.einsum("qhd,khd->hqk", grad_attended, values, preferred_element_type=full)
    row_inner = jnp.sum(probs * grad_probs, axis=-1, keepdims=True)
    grad_scores = to_half(probs * (grad_probs - row_inner))
    grad_queries = (
        jnp.einsum("hqk,khd->qhd", grad_scores, key_part, preferred_element_type=full)
        * scale_factor
    )
    grad_keys = (
        jnp.einsum("hqk,qhd->khd", grad_scores, queries, preferred_element_type=full)
        * scale_factor
    )
    return jnp.stack([grad_queries, grad_keys, grad_values], axis=1)


def gather_group(rows):
    pair = jnp.stack([rows, swap_low(rows, "mp")])
    pieces = [pair] + [shift_high(pair, "mp", -k) for k in range(1, high_size("mp"))]
    return jnp.concatenate(pieces, axis=0).reshape(-1, rows.shape[-1])


def scatter_group(rows, row_count):
    pieces = rows.reshape(high_size("mp"), PAIR, row_count, rows.shape[-1])
    pairs = pieces[:, 0].astype(full) + swap_low(pieces[:, 1], "mp").astype(full)
    total = pairs[0]
    for k in range(1, high_size("mp")):
        total = total + shift_high(to_half(pairs[k]), "mp", k).astype(full)
    return total


def halves(values, dim):
    count = values.shape[dim] // 2
    return (
        lax.slice_in_dim(values, 0, count, axis=dim),
        lax.slice_in_dim(values, count, 2 * count, axis=dim),
    )


def gather_attn(blocks):
    local, piece, order = blocks.shape
    lines = gather_high(to_half(blocks), "dp")
    first, second = halves(lines, 0)
    first = gather_high(gather_low(first, "dp"), "mp")
    second = gather_low(gather_high(second, "mp"), "dp")
    both = jnp.concatenate([first, second.swapaxes(0, 1)], axis=2)
    both = gather_low(both, "mp")
    row_blocks = D // order
    both = both.transpose(1, 0, 4, 3, 2, 5, 6)
    both = both.reshape(-1, row_blocks, order, order)
    return both.transpose(1, 2, 0, 3).reshape(D, -1)


def gather_fc(blocks):
    lines = gather_low(gather_high(to_half(blocks), "dp"), "dp")
    lines = lines.transpose(2, 1, 0, 3, 4)
    return lines.reshape(blocks.shape[0], -1, blocks.shape[2])


def split_cols(matrix, order):
    rows, cols = matrix.shape
    return (
        matrix.reshape(rows // order, order, cols // order, order)
        .transpose(2, 0, 1, 3)
        .reshape(-1, order, order)
    )


def split_rows(matrix, order):
    rows, cols = matrix.shape
    return (
        matrix.reshape(rows // order, order, cols // order, order)
        .transpose(0, 2, 1, 3)
        .reshape(-1, order, order)
    )


def join_cols(blocks, row_blocks):
    count, order, _ = blocks.shape
    return (
        blocks.reshape(-1, row_blocks, order, order)
        .transpose(1, 2, 0, 3)
        .reshape(row_blocks * order, -1)
    )


def join_rows(blocks, col_blocks):
    count, order, _ = blocks.shape
    return (
        blocks.reshape(-1, col_blocks, order, order)
        .transpose(0, 2, 1, 3)
        .reshape(-1, col_blocks * order)
    )


def scatter_z(blocks):
    local, order, _ = blocks.shape
    count = high_size("dp")
    by_rows = to_half(blocks).reshape(local, count, order // count, order).swapaxes(0, 1)
    return scatter_high(by_rows, "dp")


def scatter_fc(blocks):
    local, order, _ = blocks.shape
    by_x = to_half(blocks).reshape(PAIR, local // PAIR, order, order)
    return scatter_z(scatter_low(by_x, "dp"))


def scatter_attn(blocks):
    count, order, _ = blocks.shape
    y_count = high_size("mp")
    local = count // (y_count * PAIR)
    by_core = to_half(blocks).reshape(y_count, PAIR, local, order, order).swapaxes(0, 1)
    kept = to_half(scatter_low(by_core, "mp")).reshape(
        y_count, PAIR, local // PAIR, order, order
    )
    first, second = halves(kept, 3)
    first = to_half(scatter_low(first.swapaxes(0, 1), "dp"))
    second = to_half(scatter_high(second, "mp"))
    first = scatter_high(first, "mp")
    second = scatter_low(second, "dp")
    return scatter_z(jnp.concatenate([first, second], axis=1))


def gather_z(rows):
    local, _, order = rows.shape
    return gather_high(to_half(rows), "dp").swapaxes(0, 1).reshape(local, -1, order)


def to_pair(pieces):
    local, piece, order = pieces.shape
    by_x = to_half(pieces).reshape(PAIR, local // PAIR, piece, order)
    low = low_index("dp")
    both = ordered([pick(by_x, low), swap_low(pick(by_x, 1 - low), "dp")], low)
    return both.swapaxes(0, 1).reshape(local // PAIR, PAIR * piece, order)


def from_pair(rows):
    n, local, piece, order = rows.shape
    by_x = to_half(rows).reshape(n, local, PAIR, piece // PAIR, order)
    low = low_index("dp")
    both = ordered([pick(by_x, low, 2), swap_low(pick(by_x, 1 - low, 2), "dp")], low)
    return both.swapaxes(0, 1).reshape(n, PAIR * local, piece // PAIR, order)


def shampoo_rows(grad_rows, left_root, right_root):
    grad_half = to_half(grad_rows)
    whole = gather_z(grad_half)
    rows = grad_rows.shape[1]
    cols = lax.dynamic_slice_in_dim(whole, high_index("dp") * rows, rows, 2)
    left_term = jnp.einsum("bij,bkj->bik", grad_half, whole, preferred_element_type=full)
    right_term = jnp.einsum("bji,bjk->bik", cols, whole, preferred_element_type=full)
    step = to_half(jnp.einsum("bij,bjk->bik", left_root, whole, preferred_element_type=full))
    step = jnp.einsum("bij,bjk->bik", step, right_root, preferred_element_type=full)
    squares = jnp.sum(step * step, axis=(1, 2))
    squares = gather_low(squares, "dp").reshape(-1)
    total = squares
    for k in range(1, high_size("dp")):
        total = total + shift_high(squares, "dp", k)
    sent = from_pair(jnp.stack([grad_rows, left_term, right_term, step]))
    return sent, total


def apply_step(weight, left_stat, right_stat, sent, square_total, step_rates):
    order = weight.shape[2]
    sent = sent.astype(full)
    update_scale = lax.rsqrt(square_total / (order * order) + 1e-06) * step_rates
    return (
        sent[0],
        0.95 * left_stat + 0.05 * sent[1],
        0.95 * right_stat + 0.05 * sent[2],
        weight - sent[3] * update_scale[:, None, None],
    )


def sum_all(values):
    values = values + swap_low(values, "mp")
    for axis in ("mp", "dp"):
        if axis == "dp":
            values = values + swap_low(values, "dp")
        base = values
        for k in range(1, high_size(axis)):
            values = values + shift_high(base, axis, k)
    return values


def body_plain(
    tokens,
    keep_mask,
    cotangent,
    w_attn,
    w_fc1,
    w_fc2,
    vectors,
    left_attn,
    right_attn,
    root_left_attn,
    root_right_attn,
    left_fc1,
    right_fc1,
    root_left_fc1,
    root_right_fc1,
    left_fc2,
    right_fc2,
    root_left_fc2,
    root_right_fc2,
):
    image_count, patch_count, width = tokens.shape
    row_count = image_count * patch_count
    order = w_attn.shape[2]
    row_blocks = width // order
    attn_used = gather_attn(w_attn)
    qkv_full = attn_used[:, : 3 * width]
    out_full = attn_used[:, 3 * width :]
    fc1_used = join_cols(gather_fc(w_fc1), row_blocks)
    fc2_used = join_rows(gather_fc(w_fc2), row_blocks)
    left_roots = [to_pair(v) for v in (root_left_attn, root_left_fc1, root_left_fc2)]
    right_roots = [gather_z(to_pair(v)) for v in (root_right_attn, root_right_fc1, root_right_fc2)]
    hidden_local = fc1_used.shape[1]
    flat = tokens.reshape(row_count, width).astype(full)
    keep_rows = keep_mask.reshape(row_count).astype(full)
    row_gate = jax.nn.sigmoid(jnp.sum(flat * vectors[8], axis=-1))
    row_scale = keep_rows * row_gate
    grad_output = cotangent.reshape(row_count, width).astype(full)
    grad_change = row_scale[:, None] * grad_output
    grad_feed = to_half(grad_change)
    slot = jnp.cumsum(keep_mask, axis=1) - 1
    chosen = (
        (slot[:, None, :] == lax.broadcasted_iota(jnp.int32, (1, SLOTS, 1), 1))
        & (keep_mask[:, None, :] > 0)
    ).astype(half)

    def compact(rows):
        rows = rows.reshape(image_count, patch_count, width)
        picked = jnp.einsum("bsr,brd->bsd", chosen, rows, preferred_element_type=full)
        return to_half(picked).reshape(image_count * SLOTS, width)

    def spread(rows):
        rows = rows.reshape(image_count, SLOTS, width)
        return jnp.einsum(
            "bsr,bsd->brd", chosen.astype(full), rows, precision=highest
        ).reshape(row_count, width)

    group_grads = gather_group(compact(grad_feed))
    normed, first_norm_back = jax.vjp(layer_norm, flat, vectors[0], vectors[1])
    normed_half = to_half(normed)
    qkv_bias = jnp.concatenate([vectors[4], jnp.zeros_like(vectors[4]), vectors[5]])
    mixed_half = to_half(dot32(normed_half, qkv_full) + qkv_bias)
    heads_view = mixed_half.reshape(image_count, patch_count, 3, HEADS, width // HEADS)
    queries = heads_view[:, :, 0]
    key_part = heads_view[:, :, 1]
    values = heads_view[:, :, 2]
    attended_half, probs = jax.vmap(attend)(queries, key_part, values, keep_mask)
    attended_flat = attended_half.reshape(row_count, width)
    branch = dot32(attended_flat, out_full) + vectors[6]
    middle = flat + branch
    normed_two, second_norm_back = jax.vjp(layer_norm, middle, vectors[2], vectors[3])
    group_rows = gather_group(compact(to_half(normed_two)))
    up_bias = vectors[9:].reshape(-1)
    offset = lax.axis_index("mp") * hidden_local
    local_bias = lax.dynamic_slice_in_dim(up_bias, offset, hidden_local)
    hidden = dot32(group_rows, fc1_used) + local_bias
    activated, gelu_back = jax.vjp(exact_gelu, hidden)
    activated = to_half(activated)
    grad_active = times_transpose(group_grads, fc2_used)
    grad_hidden = to_half(gelu_back(grad_active)[0])
    mlp_count = image_count * SLOTS
    grad_rows_back = scatter_group(to_half(times_transpose(grad_hidden, fc1_used)), mlp_count)
    feed = spread(scatter_group(to_half(dot32(activated, fc2_used)), mlp_count)) + vectors[7]
    change = branch + feed
    block_out = to_half(flat + row_scale[:, None] * change).reshape(tokens.shape)
    grad_logit = keep_rows * row_gate * (1.0 - row_gate) * jnp.sum(grad_output * change, axis=-1)
    fc1_rows = scatter_fc(split_cols(row_product(group_rows, grad_hidden), order))
    fc2_rows = scatter_fc(split_rows(row_product(activated, group_grads), order))
    up_part = jnp.sum(grad_hidden, axis=0, dtype=full)
    up_bias_grad = lax.dynamic_update_slice_in_dim(jnp.zeros_like(up_bias), up_part, offset, 0)
    sent_fc1, total_fc1 = shampoo_rows(fc1_rows, left_roots[1], right_roots[1])
    sent_fc2, total_fc2 = shampoo_rows(fc2_rows, left_roots[2], right_roots[2])

    grad_normed_two = spread(grad_rows_back)
    grad_middle, grad_gain_two, grad_shift_two = second_norm_back(grad_normed_two)
    grad_branch = to_half(grad_change + grad_middle)
    grad_attended = to_half(times_transpose(grad_branch, out_full))
    grad_out_full = row_product(attended_flat, grad_branch)
    grad_heads = jax.vmap(attend_back)(
        queries,
        key_part,
        values,
        probs,
        grad_attended.reshape(image_count, patch_count, HEADS, -1),
    )
    grad_mixed = to_half(grad_heads.reshape(row_count, 3 * width))
    grad_qkv_full = row_product(normed_half, grad_mixed)
    attn_rows = scatter_attn(
        split_cols(jnp.concatenate([grad_qkv_full, grad_out_full], axis=1), order)
    )
    sent_attn, total_attn = shampoo_rows(attn_rows, left_roots[0], right_roots[0])
    grad_normed = times_transpose(grad_mixed, qkv_full)
    grad_flat, grad_gain_one, grad_shift_one = first_norm_back(grad_normed)
    input_grad = (grad_output + grad_middle + grad_flat + grad_logit[:, None] * vectors[8]).reshape(
        tokens.shape
    )
    mixed_sums = jnp.sum(grad_mixed, axis=0, dtype=full)
    vector_rows = jnp.stack(
        [
            grad_gain_one,
            grad_shift_one,
            grad_gain_two,
            grad_shift_two,
            mixed_sums[:width],
            mixed_sums[2 * width :],
            jnp.sum(grad_branch, axis=0, dtype=full),
            jnp.sum(grad_feed, axis=0, dtype=full),
            jnp.sum(grad_logit[:, None] * flat, axis=0),
        ]
    )
    vector_part = jnp.concatenate([vector_rows, up_bias_grad.reshape(-1, width)], axis=0)
    vector_grad = sum_all(vector_part)

    attn_local = w_attn.shape[0]
    block_index = lax.axis_index("mp") * attn_local + lax.broadcasted_iota(
        jnp.int32, (attn_local,), 0
    )
    attn_rates = jnp.where(
        block_index // row_blocks < 3 * row_blocks, 0.5 * D ** (-0.5), 0.5 * (D // 16) ** (-0.5)
    )
    fc1_rates = jnp.full((w_fc1.shape[0],), 0.5 * D ** (-0.5), full)
    fc2_rates = jnp.full((w_fc2.shape[0],), 0.5 * FF ** (-0.5), full)
    grad_attn, new_left_attn, new_right_attn, new_attn = apply_step(
        w_attn, left_attn, right_attn, sent_attn, total_attn, attn_rates
    )
    grad_fc1, new_left_fc1, new_right_fc1, new_fc1 = apply_step(
        w_fc1, left_fc1, right_fc1, sent_fc1, total_fc1, fc1_rates
    )
    grad_fc2, new_left_fc2, new_right_fc2, new_fc2 = apply_step(
        w_fc2, left_fc2, right_fc2, sent_fc2, total_fc2, fc2_rates
    )
    vector_blocks = vector_grad.reshape(vector_grad.shape[0], -1, BLOCK_VEC)
    block_scale = lax.rsqrt(jnp.mean(vector_blocks * vector_blocks, axis=-1, keepdims=True) + 1e-06)
    new_vectors = vectors - 0.05 * (vector_blocks * block_scale).reshape(vectors.shape)
    return (
        block_out,
        input_grad,
        grad_attn,
        grad_fc1,
        grad_fc2,
        new_left_attn,
        new_right_attn,
        new_left_fc1,
        new_right_fc1,
        new_left_fc2,
        new_right_fc2,
        new_attn,
        new_fc1,
        new_fc2,
        to_half(new_attn),
        to_half(new_fc1),
        to_half(new_fc2),
        vector_grad,
        new_vectors,
    )


def normalized(values):
    centered = values - jnp.mean(values, axis=-1, keepdims=True)
    variance = jnp.mean(centered * centered, axis=-1, keepdims=True)
    scale = lax.rsqrt(variance + 1e-06)
    return centered * scale, scale


def norm_back(grad_hat, hat, scale):
    first = jnp.mean(grad_hat, axis=-1, keepdims=True)
    second = jnp.mean(grad_hat * hat, axis=-1, keepdims=True)
    return scale * (grad_hat - first - hat * second)


def col_sum(values):
    return jnp.sum(values, axis=0, keepdims=True)


def shape(dims, kind=half):
    return jax.ShapeDtypeStruct(dims, kind)


def local_call(kernel, args, outs, scratch=(), in_hbm=(), out_hbm=(), in_smem=(0,), mib=20, micros=0.05):
    def place_of(index, hbm, smem):
        if index in hbm:
            return pl.BlockSpec(memory_space=pltpu.HBM)
        if index in smem:
            return pl.BlockSpec(memory_space=pltpu.SMEM)
        return pl.BlockSpec(memory_space=pltpu.VMEM)

    return pl.pallas_call(
        kernel,
        out_shape=list(outs),
        in_specs=[place_of(i, in_hbm, in_smem) for i in range(len(args))],
        out_specs=[place_of(i, out_hbm, ()) for i in range(len(outs))],
        scratch_shapes=list(scratch),
        compiler_params=pltpu.CompilerParams(vmem_limit_bytes=mib * 2**20),
        cost_estimate=pl.CostEstimate(
            flops=int(micros * 1e9), bytes_accessed=int(micros * 1e6), transcendentals=0
        ),
    )(*args)


def gate_of(tokens, vec_ref):
    return jax.nn.sigmoid(jnp.sum(tokens * vec_ref[8:9, :], axis=-1, keepdims=True))


def keep_of(chosen):
    ones = jnp.ones((chosen.shape[0], 128), half)
    return row_product(chosen, ones)[:, :1]


def prepare_kernel(mask_ref, tok_ref, cot_ref, vec_ref, normed_ref, grad_ref, chosen_ref):
    rows = tok_ref.shape[0]
    tokens = tok_ref[...].astype(full)
    hat, _ = normalized(tokens)
    normed_ref[...] = to_half(hat * vec_ref[0:1, :] + vec_ref[1:2, :])
    mask = mask_ref[...].astype(full)
    upper = lax.broadcasted_iota(jnp.int32, (rows, rows), 0) <= lax.broadcasted_iota(
        jnp.int32, (rows, rows), 1
    )
    count = dot32(
        to_half(jnp.broadcast_to(mask, (16, rows))), jnp.where(upper, 1.0, 0.0).astype(half)
    )
    slot = count[0:1, :] - 1.0
    wanted = lax.broadcasted_iota(jnp.int32, (SLOTS, rows), 0).astype(full)
    chosen = jnp.where((slot == wanted) & (mask > 0.0), 1.0, 0.0).astype(half)
    chosen_ref[...] = chosen
    scale = keep_of(chosen) * gate_of(tokens, vec_ref)
    grad_feed = to_half(scale * cot_ref[...].astype(full))
    grad_ref[...] = to_half(dot32(chosen, grad_feed))


def head_parts(values):
    lane = lax.broadcasted_iota(jnp.int32, values.shape, 1)
    first = lane < values.shape[1] // 2
    zero = jnp.zeros_like(values)
    return jnp.where(first, values, zero), jnp.where(first, zero, values)


def copy_all(copies):
    for copy in copies:
        copy.start()
    for copy in copies:
        copy.wait()


def matrix_of(weights, kind, row_blocks):
    blocks = weights[kind * row_blocks : (kind + 1) * row_blocks]
    return blocks.reshape(row_blocks * blocks.shape[1], blocks.shape[2])


def forward_kernel(order, pieces, place_ref, *refs):
    piece_refs, refs = refs[: len(pieces)], refs[len(pieces) :]
    normed_ref, tok_ref, mask_ref, chosen_ref, vec_ref = refs[:5]
    rows_ref, qkv_ref, probs_ref, attended_ref, branch_ref, weights_hbm = refs[5:11]
    weights, probs_all, sems, out_sem, probs_sem = refs[11:]
    z, x, m = place_ref[0], place_ref[1], place_ref[2]
    piece = piece_refs[0].shape[2]
    width = normed_ref.shape[1]
    row_blocks = width // order
    copies = []
    for ref, (slots, dx, dm) in zip(piece_refs, pieces):
        for index, slot in enumerate(slots):
            row = pl.multiple_of(((z ^ slot) * PAIR + (x ^ dx)) * piece, 16)
            for col in range(row_blocks):
                target = weights.at[
                    pl.ds((m ^ dm) * row_blocks, row_blocks),
                    pl.ds(row, piece),
                    pl.ds(col * order, order),
                ]
                source = ref.at[index, pl.ds(col * row_blocks, row_blocks)]
                copies.append(pltpu.make_async_copy(source, target, sems.at[len(copies)]))
    copy_all(copies)
    keep_whole = pltpu.make_async_copy(weights, weights_hbm, out_sem)
    keep_whole.start()
    normed = normed_ref[...]
    for kind in range(3):
        matrix = matrix_of(weights, kind, row_blocks)
        for start in range(0, width, TILE):
            lanes = slice(start, start + TILE)
            part = dot32(normed, matrix[:, lanes])
            if kind != 1:
                bias_row = 4 if kind == 0 else 5
                part = part + vec_ref[bias_row : bias_row + 1, lanes]
            qkv_ref[:, kind * width + start : kind * width + start + TILE] = to_half(part)
    head = width // HEADS
    scale = jnp.asarray(head ** (-0.5), half)
    allowed = mask_ref[...] > 0
    slabs = width // (2 * head)
    together = 3
    for first in range(0, slabs, together):
        found = []
        for slab in range(first, first + together):
            lanes = slice(slab * 2 * head, (slab + 1) * 2 * head)
            queries = head_parts(qkv_ref[:, lanes] * scale)
            keys = qkv_ref[:, width + lanes.start : width + lanes.stop]
            for index in range(2):
                scores = times_transpose(queries[index], keys)
                found.append(jnp.where(allowed, scores, masked_score))
        found = [jnp.exp(v - jnp.max(v, axis=-1, keepdims=True)) for v in found]
        found = [v * (1.0 / jnp.sum(v, axis=-1, keepdims=True)) for v in found]
        for index, probs in enumerate(found):
            probs_all[2 * first + index] = probs
        for slab in range(first, first + together):
            lanes = slice(slab * 2 * head, (slab + 1) * 2 * head)
            values = head_parts(qkv_ref[:, 2 * width + lanes.start : 2 * width + lanes.stop])
            at = 2 * (slab - first)
            total = dot32(to_half(found[at]), values[0]) + dot32(to_half(found[at + 1]), values[1])
            attended_ref[:, lanes] = to_half(total)
    keep_probs = pltpu.make_async_copy(probs_all, probs_ref, probs_sem)
    keep_probs.start()
    attended = attended_ref[...]
    matrix = matrix_of(weights, 3, row_blocks)
    for start in range(0, width, TILE):
        lanes = slice(start, start + TILE)
        branch_ref[:, lanes] = dot32(attended, matrix[:, lanes]) + vec_ref[6:7, lanes]
    hat, _ = normalized(tok_ref[...].astype(full) + branch_ref[...])
    second = to_half(hat * vec_ref[2:3, :] + vec_ref[3:4, :])
    rows_ref[...] = to_half(dot32(chosen_ref[...], second))
    keep_whole.wait()
    keep_probs.wait()


def bias_row(m, values, count):
    row = lax.broadcasted_iota(jnp.int32, (count, values.shape[1]), 0)
    return jnp.where(row == m, values, 0.0)


def gelu_parts(values):
    cdf = 0.5 * (1.0 + lax.erf(values * 0.7071067811865476))
    density = jnp.exp(-0.5 * values * values) * 0.3989422804014327
    return values * cdf, cdf + values * density


def hidden_kernel(order, group, pieces, place_ref, *refs):
    piece_refs, refs = refs[: len(pieces)], refs[len(pieces) :]
    row_refs, refs = refs[:group], refs[group:]
    grad_refs, refs = refs[: group // PAIR], refs[group // PAIR :]
    vec_ref = refs[0]
    back_refs, refs = refs[1 : 1 + group], refs[1 + group :]
    rows_ref, grads_ref, active_ref, hidden_ref, down_hbm = refs[:5]
    up, down, sems, out_sem = refs[5:]
    z, x, m = place_ref[0], place_ref[1], place_ref[2]
    piece = piece_refs[0].shape[2]
    width = rows_ref.shape[1]
    row_blocks = width // order
    col_blocks = active_ref.shape[1] // order
    local = row_blocks * col_blocks
    bias = jnp.sum(bias_row(m, vec_ref[9:, :], vec_ref.shape[0] - 9), axis=0, keepdims=True)
    copies = []
    for ref, (slots, dx) in zip(piece_refs, pieces):
        for index, slot in enumerate(slots):
            row = pl.multiple_of(((z ^ slot) * PAIR + (x ^ dx)) * piece, 16)
            span = pl.ds(row, piece)
            for col in range(col_blocks):
                lanes = pl.ds(col * order, order)
                source = ref.at[index, pl.ds(col * row_blocks, row_blocks)]
                pairs = [(source, up.at[:, span, lanes])]
                for other in range(row_blocks):
                    source = ref.at[index, local + col * row_blocks + other]
                    pairs.append((source, down.at[col, span, pl.ds(other * order, order)]))
                for source, target in pairs:
                    copies.append(pltpu.make_async_copy(source, target, sems.at[len(copies)]))
    for copy in copies:
        copy.start()
    count = row_refs[0].shape[0]
    for index in range(group):
        rows_ref[index * count : (index + 1) * count, :] = row_refs[index][...]
        grads_ref[index * count : (index + 1) * count, :] = grad_refs[index // PAIR][index % PAIR]
    for copy in copies:
        copy.wait()
    keep_down = pltpu.make_async_copy(down, down_hbm, out_sem)
    keep_down.start()
    up_matrix = matrix_of(up, 0, row_blocks)
    down_matrix = matrix_of(down, 0, col_blocks)
    for start in range(0, active_ref.shape[1], TILE):
        lanes = slice(start, start + TILE)
        hidden = dot32(rows_ref[...], up_matrix[:, lanes]) + bias[:, lanes]
        active, slope = gelu_parts(hidden)
        active_ref[:, lanes] = to_half(active)
        grad = times_transpose(grads_ref[...], down_matrix[lanes, :])
        hidden_ref[:, lanes] = to_half(grad * slope)
    for start in range(0, width, TILE):
        lanes = slice(start, start + TILE)
        total = times_transpose(hidden_ref[...], up_matrix[lanes, :])
        for index in range(group):
            back_refs[index][:, lanes] = to_half(total[index * count : (index + 1) * count, :])
    keep_down.wait()


def share_blocks(place_ref, blocks, kept_ref, *sent_refs):
    own, order, _ = kept_ref.shape
    x = place_ref[1]
    kept_ref[...] = blocks[pl.ds(x * own, own)]
    at = 0
    for ref in sent_refs:
        stop = at + ref.shape[0]
        for block in range(at // order, -(-stop // order)):
            low, high = max(at, block * order), min(stop, (block + 1) * order)
            ref[low - at : high - at] = blocks[
                (1 - x) * own + block, low - block * order : high - block * order, :
            ]
        at = stop


def store_blocks(blocks, order, product, by_rows):
    rows, cols = product.shape[0] // order, product.shape[1] // order
    for row in range(rows):
        for col in range(cols):
            at = row * cols + col if by_rows else col * rows + row
            blocks[at] = to_half(
                product[row * order : (row + 1) * order, col * order : (col + 1) * order]
            )


def up_grads_kernel(order, place_ref, rows_ref, hidden_ref, kept_ref, sent_ref, blocks):
    store_blocks(blocks, order, row_product(rows_ref[...], hidden_ref[...]), False)
    share_blocks(place_ref, blocks, kept_ref, sent_ref)


def down_grads_kernel(order, group, place_ref, grads_ref, active_ref, hidden_ref, down_ref, *refs):
    feed_kept_ref, feed_sent_ref, kept_ref, first_ref, second_ref, bias_ref, blocks = refs
    count = grads_ref.shape[0] // group
    down_matrix = matrix_of(down_ref, 0, down_ref.shape[0])
    for start in range(0, down_matrix.shape[1], TILE):
        lanes = slice(start, start + TILE)
        total = dot32(active_ref[...], down_matrix[:, lanes])
        for index in range(group):
            target = (feed_kept_ref, feed_sent_ref)[index % PAIR]
            target[index // PAIR, :, lanes] = to_half(total[index * count : (index + 1) * count, :])
    store_blocks(blocks, order, row_product(active_ref[...], grads_ref[...]), True)
    share_blocks(place_ref, blocks, kept_ref, first_ref, second_ref)
    bias_ref[...] = col_sum(hidden_ref[...].astype(full))


def backward_kernel(order, group, place_ref, *refs):
    back_refs, refs = refs[:group], refs[group:]
    chosen_ref, tok_ref, cot_ref, branch_ref, vec_ref = refs[:5]
    qkv_ref, probs_ref, attended_ref, normed_ref, weights_hbm = refs[5:10]
    kept_ref, sent_ref, mixed_ref, middle_ref, sums_ref = refs[10:15]
    weights, left, right, grad_attended, probs_all, sem, probs_sem = refs[15:]
    width = tok_ref.shape[1]
    row_blocks = width // order
    fetch = pltpu.make_async_copy(
        weights_hbm.at[pl.ds(3 * row_blocks, row_blocks)], weights, sem
    )
    fetch.start()
    fetch_probs = pltpu.make_async_copy(probs_ref, probs_all, probs_sem)
    fetch_probs.start()
    chosen = chosen_ref[...]
    arrived = back_refs[0][...].astype(full)
    for ref in back_refs[1:]:
        arrived = arrived + ref[...].astype(full)
    high = to_half(arrived)
    low = to_half(arrived - high.astype(full))
    grad_second = row_product(chosen, high) + row_product(chosen, low)
    tokens = tok_ref[...].astype(full)
    hat, scale = normalized(tokens + branch_ref[...])
    grad_middle = norm_back(grad_second * vec_ref[2:3, :], hat, scale)
    middle_ref[...] = grad_middle
    change = keep_of(chosen) * gate_of(tokens, vec_ref) * cot_ref[...].astype(full)
    grad_branch = to_half(change + grad_middle)
    sums_ref[0:1, :] = col_sum(grad_second * hat)
    sums_ref[1:2, :] = col_sum(grad_second)
    sums_ref[2:3, :] = col_sum(grad_branch.astype(full))
    sums_ref[3:4, :] = col_sum(to_half(change).astype(full))
    left[0] = normed_ref[...]
    left[1] = attended_ref[...]
    right[3] = grad_branch
    fetch.wait()
    matrix = matrix_of(weights, 0, row_blocks)
    for start in range(0, width, TILE):
        lanes = slice(start, start + TILE)
        grad_attended[:, lanes] = to_half(times_transpose(grad_branch, matrix[lanes, :]))
    fetch_probs.wait()
    head = width // HEADS
    factor = head ** (-0.5)
    slabs = width // (2 * head)
    together = 3
    for first in range(0, slabs, together):
        grad_scores, probs_half = [], []
        for slab in range(first, first + together):
            start, stop = slab * 2 * head, (slab + 1) * 2 * head
            values = qkv_ref[:, 2 * width + start : 2 * width + stop]
            for index, part in enumerate(head_parts(grad_attended[:, start:stop])):
                probs = probs_all[2 * slab + index]
                grad_probs = times_transpose(part, values)
                inner = jnp.sum(probs * grad_probs, axis=-1, keepdims=True)
                grad_scores.append(to_half(probs * (grad_probs - inner)))
                probs_half.append(to_half(probs))
        for slab in range(first, first + together):
            start, stop = slab * 2 * head, (slab + 1) * 2 * head
            queries = head_parts(qkv_ref[:, start:stop])
            keys = head_parts(qkv_ref[:, width + start : width + stop])
            grads = head_parts(grad_attended[:, start:stop])
            at = 2 * (slab - first)
            sums = [0.0] * 3
            for index in range(2):
                sums[0] = sums[0] + dot32(grad_scores[at + index], keys[index])
                sums[1] = sums[1] + row_product(grad_scores[at + index], queries[index])
                sums[2] = sums[2] + row_product(probs_half[at + index], grads[index])
            right[0, :, start:stop] = to_half(sums[0] * factor)
            right[1, :, start:stop] = to_half(sums[1] * factor)
            right[2, :, start:stop] = to_half(sums[2])
    for kind in range(3):
        mixed_ref[:, kind * width : (kind + 1) * width] = right[kind]
    core = place_ref[3]
    for high_part in range(kept_ref.shape[0]):
        for target, low_part in ((kept_ref, core), (sent_ref, 1 - core)):
            kind = high_part * PAIR + low_part
            product = row_product(left[kind // 3], right[kind])
            store_blocks(target.at[high_part], order, product, False)


def input_kernel(order, group, *refs):
    feed_refs, refs = refs[:group], refs[group:]
    mixed_ref, middle_ref, tok_ref, cot_ref, chosen_ref, vec_ref, branch_ref, weights_hbm = refs[:8]
    out_ref, grad_ref, sums_ref, weights, sem = refs[8:]
    width = tok_ref.shape[1]
    row_blocks = width // order
    fetch = pltpu.make_async_copy(weights_hbm.at[pl.ds(0, weights.shape[0])], weights, sem)
    fetch.start()
    patches = out_ref.shape[0]
    chosen = chosen_ref[...]
    tokens = tok_ref[...].astype(full)
    cotangent = cot_ref[...].astype(full)
    arrived = feed_refs[0][...].astype(full)
    for ref in feed_refs[1:]:
        arrived = arrived + ref[...].astype(full)
    high = to_half(arrived)
    low = to_half(arrived - high.astype(full))
    feed = row_product(chosen, high) + row_product(chosen, low) + vec_ref[7:8, :]
    change = branch_ref[...] + feed
    gate = gate_of(tokens, vec_ref)
    keep = keep_of(chosen)
    out_ref[...] = to_half(tokens + keep * gate * change)[:patches]
    logit = keep * gate * (1.0 - gate) * jnp.sum(cotangent * change, axis=-1, keepdims=True)
    base = cotangent + middle_ref[...] + logit * vec_ref[8:9, :]
    sums_ref[4:5, :] = col_sum(logit * tokens)
    sums_ref[2:3, :] = col_sum(mixed_ref[:, :width].astype(full))
    sums_ref[3:4, :] = col_sum(mixed_ref[:, 2 * width :].astype(full))
    hat, scale = normalized(tokens)
    fetch.wait()
    grad_normed = None
    for kind in range(3):
        part = times_transpose(
            mixed_ref[:, kind * width : (kind + 1) * width], matrix_of(weights, kind, row_blocks)
        )
        grad_normed = part if grad_normed is None else grad_normed + part
    sums_ref[0:1, :] = col_sum(grad_normed * hat)
    sums_ref[1:2, :] = col_sum(grad_normed)
    grad = base + norm_back(grad_normed * vec_ref[0:1, :], hat, scale)
    grad_ref[:, 0, :] = grad[:patches]


def core_sum_kernel(place_ref, kept_ref, came_ref, *out_refs):
    x, m = place_ref[1], place_ref[2]
    own = kept_ref.shape[1] // PAIR
    for index, out_ref in enumerate(out_refs):
        dy, dx = index // PAIR, index % PAIR
        high = (m // PAIR) ^ dy
        for block in range(own):
            at = (x ^ dx) * own + block
            out_ref[block] = to_half(
                kept_ref[high, at].astype(full) + came_ref[high, at].astype(full)
            )


def row_sum_kernel(groups, count, place_ref, *refs):
    ins, outs = refs[: groups * count], refs[groups * count :]
    rows = outs[0].shape[-2]
    near = len(outs) == 2
    slots = outs[0].shape[0] * 2 if near else len(outs)
    for slot in range(slots):
        out_ref = outs[slot % 2].at[slot // 2] if near else outs[slot]
        start = pl.multiple_of((place_ref[0] ^ slot) * rows, 16)
        at = 0
        for group in range(groups):
            parts = ins[group * count : (group + 1) * count]
            for block in range(parts[0].shape[0]):
                total = parts[0][block, pl.ds(start, rows), :].astype(full)
                for ref in parts[1:]:
                    total = total + ref[block, pl.ds(start, rows), :].astype(full)
                out_ref[at] = to_half(total)
                at += 1


def joined_sum_kernel(place_ref, kept_ref, first_ref, second_ref, near_ref, other_ref, came):
    order = came.shape[1]
    at = 0
    for ref in (first_ref, second_ref):
        stop = at + ref.shape[0]
        for block in range(at // order, -(-stop // order)):
            low, high = max(at, block * order), min(stop, (block + 1) * order)
            came[block, low - block * order : high - block * order, :] = ref[low - at : high - at]
        at = stop
    row_sum_kernel(1, 2, place_ref, kept_ref, came, near_ref, other_ref)


def line_blocks(z, refs, target, first=0):
    for slot, ref in enumerate(refs):
        rows = ref.shape[-2]
        start = pl.multiple_of((z ^ slot) * rows, 16)
        for block in range(target.shape[0]):
            target[block, pl.ds(start, rows), :] = ref[first + block]


def line_roots_kernel(place_ref, *refs):
    root_refs, out_ref = refs[:-1], refs[-1]
    for slot, ref in enumerate(root_refs):
        rows = ref.shape[1]
        for block in range(out_ref.shape[0]):
            for part in range(PAIR):
                start = (place_ref[0] ^ slot) * (PAIR * rows) + part * rows
                out_ref[block, pl.ds(pl.multiple_of(start, 16), rows), :] = ref[block * PAIR + part]


def step_parts(z, x, own, whole, step, terms, found, block, kept_ref, sent_ref):
    rows, order = own.shape
    mine = pl.multiple_of(z * rows, 16)
    half_rows = rows // PAIR
    terms[...] = row_product(whole, whole)
    found[0] = own.astype(full)
    found[1] = times_transpose(own, whole)
    found[2] = terms[pl.ds(mine, rows), :]
    found[3] = step
    for target, part in ((kept_ref, x), (sent_ref, 1 - x)):
        start = pl.multiple_of(part * half_rows, 16)
        for kind in range(4):
            target[kind, block] = to_half(found[kind, pl.ds(start, half_rows), :])


def whole_step_kernel(count, left_first, place_ref, *refs):
    grad_refs, refs = refs[:count], refs[count:]
    roots_ref, kept_ref, sent_ref, grads, terms, found, steps = refs
    z, x = place_ref[0], place_ref[1]
    blocks, rows, order = grad_refs[0].shape
    line_blocks(z, grad_refs, grads)
    mine = pl.multiple_of(z * rows, 16)
    for block in range(blocks):
        whole = grads[block]
        step = to_half(dot32(roots_ref[left_first + block], whole))
        step = dot32(step, roots_ref[block])
        mean = jnp.mean(jnp.mean(step * step, axis=1, keepdims=True), axis=0, keepdims=True)
        steps[...] = step * lax.rsqrt(mean + 1e-06)
        step = steps[pl.ds(mine, rows), :]
        step_parts(z, x, grad_refs[0][block], whole, step, terms, found, block, kept_ref, sent_ref)


def step_kernel(count, first, place_ref, *refs):
    grad_refs, refs = refs[:count], refs[count:]
    roots_ref, left_ref, kept_ref, sent_ref, square_ref, grads, terms, found = refs
    z, x = place_ref[0], place_ref[1]
    blocks, rows, order = grad_refs[0].shape
    line_blocks(z, grad_refs, grads)
    square_ref[...] = jnp.zeros_like(square_ref)
    for block in range(blocks):
        whole = grads[block]
        step = to_half(dot32(left_ref[first + block], whole))
        step = dot32(step, roots_ref[first + block])
        total = jnp.sum(jnp.sum(step * step, axis=1, keepdims=True), axis=0, keepdims=True)
        square_ref[block : block + 1, :] = jnp.broadcast_to(total, (1, 128))
        step_parts(z, x, grad_refs[0][block], whole, step, terms, found, block, kept_ref, sent_ref)
        total = jnp.broadcast_to(total, (16, order))
        terms_of = jnp.zeros((16, order), full)
        row = lax.broadcasted_iota(jnp.int32, (16, order), 0)
        for index in range(3):
            part = to_half(total).astype(full)
            terms_of = jnp.where(row == index, part, terms_of)
            total = total - part
        sent_ref[4, block, :16, :] = to_half(terms_of)
        sent_ref[4, block, 16:, :] = jnp.zeros((sent_ref.shape[2] - 16, order), half)


def last_sums_kernel(vec_ref, vec_came_ref, *refs):
    count = len(refs) // 2
    mine_refs, came_refs, out_ref = refs[:count], refs[count:-1], refs[-1]
    blocks = came_refs[0].shape[1]
    out_ref[...] = jnp.zeros_like(out_ref)
    out_ref[: vec_ref.shape[0], :] = vec_ref[...] + vec_came_ref[...]
    for matrix in range(count):
        for block in range(blocks):
            at = 16 + matrix * blocks + block
            out_ref[at : at + 1, :128] = mine_refs[matrix][block : block + 1, :]
            terms = came_refs[matrix][4, block, 0:16, 0:128].astype(full)
            at += count * blocks
            out_ref[at : at + 1, :128] = jnp.sum(terms, axis=0, keepdims=True)


def apply_stats(x, refs, sent_refs, out_refs):
    left_ref, right_ref = refs
    grad_ref, new_left_ref, new_right_ref = out_refs
    own = left_ref.shape[0] // PAIR
    for side, ref in enumerate(sent_refs):
        for block in range(own):
            at = (x ^ side) * own + block
            grad_ref[at] = ref[0, block].astype(full)
            new_left_ref[at] = 0.95 * left_ref[at] + 0.05 * ref[1, block].astype(full)
            new_right_ref[at] = 0.95 * right_ref[at] + 0.05 * ref[2, block].astype(full)


def apply_step_rows(order, rates, x, m, weight_ref, sent_refs, out_refs, total_ref=None, row=0):
    new_ref, half_ref = out_refs
    local = weight_ref.shape[0]
    own = local // PAIR
    for side, ref in enumerate(sent_refs):
        for block in range(own):
            at = (x ^ side) * own + block
            rate = jnp.where(m * local + at < rates[0], rates[1], rates[2])
            if total_ref is not None:
                index = row + side * 2 * own + block
                total = total_ref[index : index + 1, 0:1]
                rate = rate * lax.rsqrt(total / (order * order) + 1e-06)
            new = weight_ref[at] - rate * ref[3, block].astype(full)
            new_ref[at] = new
            half_ref[at] = to_half(new)


def apply_kernel(order, rates, place_ref, weight_ref, left_ref, right_ref, *refs):
    sent_refs, out_refs = refs[:2], refs[2:]
    x, m = place_ref[1], place_ref[2]
    apply_stats(x, (left_ref, right_ref), sent_refs, out_refs[:3])
    apply_step_rows(order, rates, x, m, weight_ref, sent_refs, out_refs[3:])


def stats_kernel(place_ref, left_ref, right_ref, *refs):
    apply_stats(place_ref[1], (left_ref, right_ref), refs[:2], refs[2:])


def last_kernel(order, rates, place_ref, *refs):
    up_weight, down_weight, left_ref, right_ref = refs[:4]
    up_sent, down_sent, total_ref, vec_ref = refs[4:6], refs[6:8], refs[8], refs[9]
    outs = refs[10:]
    x, m = place_ref[1], place_ref[2]
    own = up_weight.shape[0] // PAIR
    apply_step_rows(order, rates[0], x, m, up_weight, up_sent, outs[0:2], total_ref, 16)
    apply_step_rows(order, rates[1], x, m, down_weight, down_sent, outs[2:4], total_ref, 16 + own)
    apply_stats(x, (left_ref, right_ref), down_sent, outs[4:7])
    vector_step(vec_ref, total_ref, outs[7], outs[8])


def vector_part_kernel(place_ref, one_ref, two_ref, bias_ref, out_ref):
    out_ref[0:2, :] = one_ref[0:2, :]
    out_ref[2:4, :] = two_ref[0:2, :]
    out_ref[4:6, :] = one_ref[2:4, :]
    out_ref[6:8, :] = two_ref[2:4, :]
    out_ref[8:9, :] = one_ref[4:5, :]
    out_ref[9:, :] = bias_row(place_ref[2], bias_ref[...], out_ref.shape[0] - 9)


def vector_step(vec_ref, total_ref, grad_ref, new_ref):
    rows = vec_ref.shape[0]
    grad_ref[...] = total_ref[:rows, :]
    for start in range(0, vec_ref.shape[1], BLOCK_VEC):
        lanes = slice(start, start + BLOCK_VEC)
        block = total_ref[:rows, lanes]
        scale = lax.rsqrt(jnp.mean(block * block, axis=-1, keepdims=True) + 1e-06)
        new_ref[:, lanes] = vec_ref[:, lanes] - 0.05 * (block * scale)


def first_kernel(place_ref, *refs):
    ins, refs = refs[:9], refs[9:]
    attn_out, feed_out, kept_ref, sent_ref = refs[:4]
    held, sems = refs[4:]
    copies = [
        pltpu.make_async_copy(ref, held.at[index], sems.at[index])
        for index, ref in enumerate(ins)
    ]
    for copy in copies:
        copy.start()
    local, own = attn_out.shape[0], kept_ref.shape[1]
    x = place_ref[1]
    for index, copy in enumerate(copies):
        copy.wait()
        if index == 0:
            attn_out[...] = to_half(held[index])
        elif index < 3:
            feed_out[(index - 1) * local : index * local] = to_half(held[index])
        else:
            kept_ref[index - 3] = to_half(held[index, pl.ds(x * own, own)])
            sent_ref[index - 3] = to_half(held[index, pl.ds((1 - x) * own, own)])


def bundle_kernel(place_ref, kept_ref, came_ref, feed_ref, left_ref, bundle_ref):
    x = place_ref[1]
    kinds, own, piece, order = kept_ref.shape
    feed = feed_ref.shape[0]
    bundle_ref[:feed] = feed_ref[...]
    for index in range(kinds):
        for block in range(own):
            for side, ref in ((0, kept_ref), (1, came_ref)):
                value = ref[index, block]
                if index < 3:
                    start = pl.multiple_of((x ^ side) * piece, 16)
                    left_ref[index * own + block, pl.ds(start, piece), :] = value
                if index == 0 or index >= 3:
                    at = (index - 3 if index else 3) * own + block
                    bundle_ref[feed + at * PAIR + (x ^ side)] = value


def move(values, dp_mask, mp_mask):
    dp, mp = lax.axis_size("dp"), lax.axis_size("mp")
    if mp_mask == 0:
        return lax.ppermute(values, "dp", [(s, s ^ dp_mask) for s in range(dp)])
    if dp_mask == 0:
        return lax.ppermute(values, "mp", [(s, s ^ mp_mask) for s in range(mp)])
    mask = dp_mask * mp + mp_mask
    return lax.ppermute(values, ("dp", "mp"), [(s, s ^ mask) for s in range(dp * mp)])


def phase(*values):
    return lax.optimization_barrier(values)


def after(values, *others):
    return lax.optimization_barrier((values,) + others)[0]


def body_lines(
    tokens,
    keep_mask,
    cotangent,
    w_attn,
    w_fc1,
    w_fc2,
    vectors,
    left_attn,
    right_attn,
    root_left_attn,
    root_right_attn,
    left_fc1,
    right_fc1,
    root_left_fc1,
    root_right_fc1,
    left_fc2,
    right_fc2,
    root_left_fc2,
    root_right_fc2,
):
    _, patches, width = tokens.shape
    local, piece, order = w_attn.shape
    z_count, group = high_size("dp"), lax.axis_size("mp")
    row_blocks = width // order
    own = local // PAIR
    rows = patches
    line_rows = order // z_count
    total_rows = group * SLOTS
    hidden_width = local // row_blocks * order
    heads = (HEADS, rows, rows)
    others = range(1, group)
    lines = range(1, z_count)
    tok, cot, mask = tokens[0], cotangent[0], keep_mask
    line, member = lax.axis_index("dp"), lax.axis_index("mp")
    place = jnp.stack([line >> 1, line & 1, member, member & 1]).astype(jnp.int32)

    attn_half, feed_half, root_kept, root_sent = local_call(
        first_kernel,
        (
            place,
            *[
                pltpu.with_memory_space_constraint(value, pltpu.HBM)
                for value in (
                    w_attn,
                    w_fc1,
                    w_fc2,
                    root_left_attn,
                    root_left_fc1,
                    root_left_fc2,
                    root_right_attn,
                    root_right_fc1,
                    root_right_fc2,
                )
            ],
        ),
        (
            shape((local, piece, order)),
            shape((2 * local, piece, order)),
            shape((6, own, piece, order)),
            shape((6, own, piece, order)),
        ),
        scratch=(pltpu.VMEM((9, local, piece, order), full), pltpu.SemaphoreType.DMA((9,))),
        in_hbm=range(1, 10),
    )
    line_came = [move(attn_half, k * PAIR, 0) for k in lines]
    root_came = move(root_sent, 1, 0)
    line_came, root_came, attn_half, mask = phase(line_came, root_came, attn_half, mask)

    plane = [(dx, high * PAIR) for high in range(group // PAIR) for dx in range(PAIR)]
    feed_far = move(feed_half, 2 * PAIR, 0)
    left_roots, bundle = local_call(
        bundle_kernel,
        (place, root_kept, root_came, feed_half),
        (
            shape((3 * own, PAIR * piece, order)),
            shape((2 * local + 4 * own * PAIR, piece, order)),
        ),
    )
    bundle_near = move(bundle, PAIR, 0)
    stack = jnp.stack([attn_half, *line_came])
    found = [stack] + [move(stack, dx, dm) for dx, dm in plane[1:]]
    normed, grad_sent, chosen = local_call(
        prepare_kernel,
        (mask, tok, cot, vectors),
        (shape((rows, width)), shape((SLOTS, width)), shape((SLOTS, rows))),
        in_smem=(),
    )
    pieces, piece_info = [], []
    for (dx, dm), part in zip(plane, found):
        pieces += [part, move(part, 0, 1)]
        piece_info += [(range(z_count), dx, dm), (range(z_count), dx, dm + 1)]
    grad_came = move(grad_sent, 0, 1)
    feed_count = 2 * local
    feed_near = jnp.stack([feed_half, bundle_near[:feed_count]])
    roots, roots_near = bundle[feed_count:], bundle_near[feed_count:]
    half_roots = roots.shape[0] // 2
    roots_first, roots_second = roots[:half_roots], roots[half_roots:]

    feed_near_came = move(feed_near, 1, 0)
    feed_last = move(feed_far, PAIR, 0)
    roots_first_far = move(roots_first, 2 * PAIR, 0)
    pair = jnp.stack([grad_sent, grad_came])
    group_grads = [pair] + [move(pair, 0, dm) for dm in range(PAIR, group, PAIR)]
    count = len(pieces)
    rows_sent, qkv, probs, attended, branch, weights = local_call(
        lambda *refs: forward_kernel(order, piece_info, *refs),
        (place, *pieces, normed, tok, mask, chosen, vectors),
        (
            shape((SLOTS, width)),
            shape((rows, 3 * width)),
            shape(heads, full),
            shape((rows, width)),
            shape((rows, width), full),
            shape((group * row_blocks, order, width)),
        ),
        scratch=(
            pltpu.VMEM((group * row_blocks, order, width), half),
            pltpu.VMEM(heads, full),
            pltpu.SemaphoreType.DMA((count * z_count * row_blocks,)),
            pltpu.SemaphoreType.DMA(()),
            pltpu.SemaphoreType.DMA(()),
        ),
        in_hbm=range(1, 1 + count),
        out_hbm=(2, 5),
        micros=8,
    )
    rows_sent, group_grads, feed_last, roots_first_far = phase(
        rows_sent, group_grads, feed_last, roots_first_far
    )

    group_rows = [rows_sent] + [move(rows_sent, 0, k) for k in others]
    feed_far = jnp.stack([feed_far, feed_last])
    feed_far_came = move(feed_far, 1, 0)
    roots_second_far = move(roots_second, 2 * PAIR, 0)

    feed_pieces = [feed_near, feed_near_came, feed_far, feed_far_came]
    feed_info = [((0, 1), 0), ((0, 1), 1), ((2, 3), 0), ((2, 3), 1)]
    outs = local_call(
        lambda *refs: hidden_kernel(order, group, feed_info, *refs),
        (place, *feed_pieces, *group_rows, *group_grads, vectors),
        (shape((SLOTS, width)),) * group
        + (shape((total_rows, width)),) * 2
        + (shape((total_rows, hidden_width)),) * 2
        + (shape((local // row_blocks, order, width)),),
        scratch=(
            pltpu.VMEM((row_blocks, order, hidden_width), half),
            pltpu.VMEM((local // row_blocks, order, width), half),
            pltpu.SemaphoreType.DMA((PAIR * z_count * (local // row_blocks + local),)),
            pltpu.SemaphoreType.DMA(()),
        ),
        in_hbm=(1, 2, 3, 4),
        out_hbm=(group + 4,),
        micros=5,
    )
    back, (all_rows, all_grads, active, grad_hidden, down) = outs[:group], outs[group:]
    back, all_rows = phase(back, all_rows)

    back = [back[0]] + [move(back[k], 0, k) for k in others]
    roots_far = jnp.concatenate([roots_first_far, roots_second_far])
    roots_last = move(roots_far, PAIR, 0)
    all_roots = [roots, roots_near, roots_far, roots_last]
    up_kept, up_sent = local_call(
        lambda *refs: up_grads_kernel(order, *refs),
        (place, all_rows, grad_hidden),
        (shape((own, order, order)), shape((own * order, order))),
        scratch=(pltpu.VMEM((local, order, order), half),),
    )
    up_came = move(up_sent, 1, 0)
    first_rows = order + line_rows
    feed_kept, feed_sent, down_kept, down_first, down_second, bias_sums = local_call(
        lambda *refs: down_grads_kernel(order, group, *refs),
        (place, all_grads, active, grad_hidden, down),
        (shape((group // PAIR, SLOTS, width)),) * 2
        + (shape((own, order, order)),)
        + (shape((first_rows, order)), shape((own * order - first_rows, order)))
        + (shape((1, hidden_width), full),),
        scratch=(pltpu.VMEM((local, order, order), half),),
    )
    back, down_first, down_second, feed_sent, all_roots = phase(
        back, down_first, down_second, feed_sent, all_roots
    )

    (joined_roots,) = local_call(
        line_roots_kernel,
        (place, *all_roots),
        (shape((4 * own, order, order)),),
    )

    def rows_of(*groups):
        blocks = sum(parts[0].shape[0] for parts in groups)
        return local_call(
            lambda *refs: row_sum_kernel(len(groups), len(groups[0]), *refs),
            (place, *[part for parts in groups for part in parts]),
            (shape((blocks, line_rows, order)),) * z_count,
        )

    def pairs_of(*groups):
        blocks = sum(parts[0].shape[0] for parts in groups)
        return local_call(
            lambda *refs: row_sum_kernel(len(groups), len(groups[0]), *refs),
            (place, *[part for parts in groups for part in parts]),
            (shape((z_count // 2, blocks, line_rows, order)),) * 2,
        )

    def add_near(kept, came):
        return [
            to_half(kept[k].astype(full) + came[k].astype(full)) for k in range(z_count // 2)
        ]

    def total_of(parts):
        total = parts[0].astype(full)
        for part in parts[1:]:
            total = total + part.astype(full)
        return to_half(total)

    def step_of(parts, matrix):
        return local_call(
            lambda *refs: step_kernel(z_count, matrix * own, *refs),
            (place, *parts, joined_roots, left_roots),
            (
                shape((4, own, piece, order)),
                shape((5, own, piece, order)),
                shape((8, 128), full),
            ),
            scratch=(
                pltpu.VMEM((own, order, order), half),
                pltpu.VMEM((order, order), full),
                pltpu.VMEM((4, line_rows, order), full),
            ),
            )

    up_near_kept, up_near_sent = pairs_of((up_kept, up_came.reshape(own, order, order)))
    up_near = move(up_near_sent, PAIR, 0)
    down_first_came = move(down_first, 1, 0)
    feed_came = move(feed_sent, 0, 1)
    attn_kept, attn_sent, mixed, grad_middle, sums_two = local_call(
        lambda *refs: backward_kernel(order, group, *refs),
        (place, *back, chosen, tok, cot, branch, vectors, qkv, probs, attended, normed, weights),
        (
            shape((group // PAIR, local, order, order)),
            shape((group // PAIR, local, order, order)),
            shape((rows, 3 * width)),
            shape((rows, width), full),
            shape((4, width), full),
        ),
        scratch=(
            pltpu.VMEM((row_blocks, order, width), half),
            pltpu.VMEM((2, rows, width), half),
            pltpu.VMEM((4, rows, width), half),
            pltpu.VMEM((rows, width), half),
            pltpu.VMEM(heads, full),
            pltpu.SemaphoreType.DMA(()),
            pltpu.SemaphoreType.DMA(()),
        ),
        in_hbm=(1 + group + 6, 1 + group + 9),
        micros=3,
    )
    attn_sent, up_near, down_first_came, feed_came = phase(
        attn_sent, up_near, down_first_came, feed_came
    )

    attn_came = move(attn_sent, 0, 1)
    up_mine, up_other = add_near(up_near_kept, up_near)
    up_far = move(up_other, 2 * PAIR, 0)
    down_second_came = move(down_second, 1, 0)
    feed_pairs = [
        to_half(feed_kept[k].astype(full) + feed_came[k].astype(full))
        for k in range(group // PAIR)
    ]
    feed = [feed_pairs[0]] + [
        move(part, 0, (k + 1) * PAIR) for k, part in enumerate(feed_pairs[1:])
    ]
    core_parts = local_call(
        core_sum_kernel,
        (place, attn_kept, attn_came),
        (shape((own, order, order)),) * group,
    )
    core_parts, up_mine, down_second_came, feed = phase(
        core_parts, up_mine, down_second_came, feed
    )

    attn_came = [move(part, dx, dm) for (dx, dm), part in zip(plane[1:], core_parts[1:])]
    down_near_kept, down_near_sent = local_call(
        joined_sum_kernel,
        (place, down_kept, down_first_came, down_second_came),
        (shape((z_count // 2, own, line_rows, order)),) * 2,
        scratch=(pltpu.VMEM((own, order, order), half),),
    )
    down_near = move(down_near_sent, PAIR, 0)
    up_rows = total_of([up_mine, up_far])
    up_whole_far = move(up_rows, 2 * PAIR, 0)
    block_out, input_grad, sums_one = local_call(
        lambda *refs: input_kernel(order, group // PAIR, *refs),
        (*feed, mixed, grad_middle, tok, cot, chosen, vectors, branch, weights),
        (
            shape((patches, width)),
            shape((patches, 1, width), full),
            shape((5, width), full),
        ),
        scratch=(
            pltpu.VMEM((3 * row_blocks, order, width), half),
            pltpu.SemaphoreType.DMA(()),
        ),
        in_hbm=(group // PAIR + 7,),
        in_smem=(),
    )
    (vector_sum,) = local_call(
        vector_part_kernel,
        (place, sums_one, sums_two, bias_sums),
        (shape(vectors.shape, full),),
    )
    down_mine, down_other = add_near(down_near_kept, down_near)
    down_far = move(down_other, 2 * PAIR, 0)
    up_pair = jnp.stack([up_rows, up_whole_far])
    up_pair_came = move(up_pair, PAIR, 0)
    up_kept, up_sent, up_squares = step_of(
        [up_rows, up_pair_came[0], up_whole_far, up_pair_came[1]], 1
    )
    down_rows = total_of([down_mine, down_far])
    down_whole_far = move(down_rows, 2 * PAIR, 0)
    attn_came, down_rows, down_whole_far, up_sent, vector_sum = phase(
        attn_came, down_rows, down_whole_far, up_sent, vector_sum
    )

    attn_split = rows_of((core_parts[0], *attn_came))
    attn_split = [attn_split[0]] + [move(attn_split[k], k * PAIR, 0) for k in lines]
    down_pair = jnp.stack([down_rows, down_whole_far])
    down_pair_came = move(down_pair, PAIR, 0)
    up_found = move(up_sent, 1, 0)
    down_kept, down_sent, down_squares = step_of(
        [down_rows, down_pair_came[0], down_whole_far, down_pair_came[1]], 2
    )
    vector_sum = vector_sum + move(after(vector_sum, down_pair_came), 0, 1)
    attn_split, up_found, down_sent, vector_sum = phase(
        attn_split, up_found, down_sent, vector_sum
    )

    attn_rows = total_of(attn_split)
    attn_parts = [attn_rows] + [move(attn_rows, k * PAIR, 0) for k in lines]
    down_found = move(down_sent, 1, 0)
    for dm in range(PAIR, group, PAIR):
        vector_sum = vector_sum + move(vector_sum, 0, dm)
    vector_came = move(vector_sum, 1, 0)
    stat = shape(w_fc1.shape, full)
    stats_up = local_call(
        stats_kernel,
        (place, left_fc1, right_fc1, up_kept, up_found),
        (stat,) * 3,
    )
    attn_parts, down_found, vector_came, stats_up = phase(
        attn_parts, down_found, vector_came, stats_up
    )

    kept, sent = local_call(
        lambda *refs: whole_step_kernel(z_count, 3 * own, *refs),
        (place, *attn_parts, joined_roots),
        (shape((4, own, piece, order)),) * 2,
        scratch=(
            pltpu.VMEM((own, order, order), half),
            pltpu.VMEM((order, order), full),
            pltpu.VMEM((4, line_rows, order), full),
            pltpu.VMEM((order, order), full),
        ),
    )
    came = move(sent, 1, 0)
    (last_sums,) = local_call(
        last_sums_kernel,
        (after(vector_sum, sent), vector_came, up_squares, down_squares, up_found, down_found),
        (shape((24, width), full),),
        in_smem=(),
    )
    total = last_sums
    for k in lines:
        total = total + move(last_sums, k * PAIR, 0)

    attn_rates = (3 * row_blocks * row_blocks, 0.5 * D ** (-0.5), 0.5 * (D // 16) ** (-0.5))
    fc_rates = ((0, 0.0, 0.5 * D ** (-0.5)), (0, 0.0, 0.5 * FF ** (-0.5)))
    new_up, half_up, new_down, half_down, *stats_down, vector_grad, new_vectors = local_call(
        lambda *refs: last_kernel(order, fc_rates, *refs),
        (
            place,
            w_fc1,
            w_fc2,
            left_fc2,
            right_fc2,
            up_kept,
            up_found,
            down_kept,
            down_found,
            total,
            vectors,
        ),
        (stat, shape(w_fc1.shape)) * 2 + (stat,) * 3 + (shape(vectors.shape, full),) * 2,
    )
    done_attn = local_call(
        lambda *refs: apply_kernel(order, attn_rates, *refs),
        (place, w_attn, left_attn, right_attn, kept, came),
        (stat,) * 4 + (shape(w_attn.shape),),
    )
    done_fc1 = (*stats_up, new_up, half_up)
    done_fc2 = (*stats_down, new_down, half_down)
    return (
        block_out[None],
        input_grad.transpose(1, 0, 2),
        done_attn[0],
        done_fc1[0],
        done_fc2[0],
        *done_attn[1:3],
        *done_fc1[1:3],
        *done_fc2[1:3],
        done_attn[3],
        done_fc1[3],
        done_fc2[3],
        done_attn[4],
        done_fc1[4],
        done_fc2[4],
        vector_grad,
        new_vectors,
    )


def body(tokens, keep_mask, cotangent, w_attn, *rest):
    local, piece, _ = w_attn.shape
    group = lax.axis_size("mp")
    tiled = piece % 16 == 0 and tokens.shape[0] == 1 and local % (2 * PAIR) == 0
    tiled = tiled and group == 4 and high_size("dp") == 4
    chosen_body = body_lines if tiled else body_plain
    return chosen_body(tokens, keep_mask, cotangent, w_attn, *rest)


def solution(mesh):
    rows = P(("dp", "mp"), None, None)
    blocks = P("mp", "dp", None)
    return jax.shard_map(
        body,
        mesh=mesh,
        in_specs=(rows, P(("dp", "mp"), None), rows)
        + (blocks,) * 3
        + (P(),)
        + (blocks,) * 12,
        out_specs=(rows, rows) + (blocks,) * 15 + (P(), P()),
        check_vma=False,
    )
```

```python
import jax
import jax.numpy as jnp
from jax import lax
from jax.experimental import pallas as pl
from jax.experimental.pallas import tpu as pltpu
from jax.sharding import PartitionSpec as P

D = 768
HEADS = 12
FF = 3072
BLOCK_VEC = 128
KEPT_MOST = 157
SLOTS = 160
TILE = 256
PAIR = 2

highest = lax.Precision.HIGHEST
masked_score = -1e30
half = jnp.bfloat16
full = jnp.float32


def to_half(values):
    return values.astype(half)


def layer_norm(values, gain_row, shift_row):
    centered = values - jnp.mean(values, axis=-1, keepdims=True)
    variance = jnp.mean(centered * centered, axis=-1, keepdims=True)
    return centered * lax.rsqrt(variance + 1e-06) * gain_row + shift_row


def exact_gelu(values):
    return jax.nn.gelu(values, approximate=False)


def dot32(left, right):
    return jnp.dot(left, right, preferred_element_type=full)


def row_product(left_half, right_half):
    return lax.dot_general(
        left_half, right_half, (((0,), (0,)), ((), ())), preferred_element_type=full
    )


def times_transpose(left_half, right_half):
    return lax.dot_general(
        left_half, right_half, (((1,), (1,)), ((), ())), preferred_element_type=full
    )


def swap_low(values, axis):
    count = lax.axis_size(axis)
    return lax.ppermute(values, axis, [(s, s ^ 1) for s in range(count)])


def shift_high(values, axis, step):
    count = lax.axis_size(axis)
    return lax.ppermute(values, axis, [(s, (s + step * PAIR) % count) for s in range(count)])


def high_index(axis):
    return lax.axis_index(axis) // PAIR


def low_index(axis):
    return lax.axis_index(axis) % PAIR


def high_size(axis):
    return lax.axis_size(axis) // PAIR


def pick(values, index, dim=0):
    return lax.dynamic_index_in_dim(values, index, dim, keepdims=False)


def ordered(pieces, index):
    count = len(pieces)
    if count == 2:
        first = index == 0
        return jnp.stack(
            [jnp.where(first, pieces[0], pieces[1]), jnp.where(first, pieces[1], pieces[0])]
        )
    return lax.dynamic_slice_in_dim(jnp.stack(pieces + pieces), (count - index) % count, count, 0)


def gather_low(values, axis):
    return ordered([values, swap_low(values, axis)], low_index(axis))


def gather_high(values, axis):
    count = high_size(axis)
    pieces = [values] + [shift_high(values, axis, -k) for k in range(1, count)]
    return ordered(pieces, high_index(axis))


def scatter_low(values, axis):
    low = low_index(axis)
    arrived = swap_low(pick(values, 1 - low), axis)
    return pick(values, low).astype(full) + arrived.astype(full)


def scatter_high(values, axis):
    count, high = high_size(axis), high_index(axis)
    total = pick(values, high).astype(full)
    for k in range(1, count):
        total = total + shift_high(pick(values, (high + k) % count), axis, k).astype(full)
    return total


def attend(queries, key_part, values, allowed):
    scale_factor = queries.shape[-1] ** (-0.5)
    scores = jnp.einsum("qhd,khd->hqk", queries, key_part, preferred_element_type=full)
    scores = jnp.where(allowed[None, None, :] > 0, scores * scale_factor, masked_score)
    shifted = jnp.exp(scores - jnp.max(scores, axis=-1, keepdims=True))
    probs = shifted / jnp.sum(shifted, axis=-1, keepdims=True)
    attended = jnp.einsum("hqk,khd->qhd", to_half(probs), values, preferred_element_type=full)
    return (to_half(attended), probs)


def attend_back(queries, key_part, values, probs, grad_attended):
    scale_factor = queries.shape[-1] ** (-0.5)
    grad_values = jnp.einsum(
        "hqk,qhd->khd", to_half(probs), grad_attended, preferred_element_type=full
    )
    grad_probs = jnp.einsum("qhd,khd->hqk", grad_attended, values, preferred_element_type=full)
    row_inner = jnp.sum(probs * grad_probs, axis=-1, keepdims=True)
    grad_scores = to_half(probs * (grad_probs - row_inner))
    grad_queries = (
        jnp.einsum("hqk,khd->qhd", grad_scores, key_part, preferred_element_type=full)
        * scale_factor
    )
    grad_keys = (
        jnp.einsum("hqk,qhd->khd", grad_scores, queries, preferred_element_type=full)
        * scale_factor
    )
    return jnp.stack([grad_queries, grad_keys, grad_values], axis=1)


def gather_group(rows):
    pair = jnp.stack([rows, swap_low(rows, "mp")])
    pieces = [pair] + [shift_high(pair, "mp", -k) for k in range(1, high_size("mp"))]
    return jnp.concatenate(pieces, axis=0).reshape(-1, rows.shape[-1])


def scatter_group(rows, row_count):
    pieces = rows.reshape(high_size("mp"), PAIR, row_count, rows.shape[-1])
    pairs = pieces[:, 0].astype(full) + swap_low(pieces[:, 1], "mp").astype(full)
    total = pairs[0]
    for k in range(1, high_size("mp")):
        total = total + shift_high(to_half(pairs[k]), "mp", k).astype(full)
    return total


def halves(values, dim):
    count = values.shape[dim] // 2
    return (
        lax.slice_in_dim(values, 0, count, axis=dim),
        lax.slice_in_dim(values, count, 2 * count, axis=dim),
    )


def gather_attn(blocks):
    local, piece, order = blocks.shape
    lines = gather_high(to_half(blocks), "dp")
    first, second = halves(lines, 0)
    first = gather_high(gather_low(first, "dp"), "mp")
    second = gather_low(gather_high(second, "mp"), "dp")
    both = jnp.concatenate([first, second.swapaxes(0, 1)], axis=2)
    both = gather_low(both, "mp")
    row_blocks = D // order
    both = both.transpose(1, 0, 4, 3, 2, 5, 6)
    both = both.reshape(-1, row_blocks, order, order)
    return both.transpose(1, 2, 0, 3).reshape(D, -1)


def gather_fc(blocks):
    lines = gather_low(gather_high(to_half(blocks), "dp"), "dp")
    lines = lines.transpose(2, 1, 0, 3, 4)
    return lines.reshape(blocks.shape[0], -1, blocks.shape[2])


def split_cols(matrix, order):
    rows, cols = matrix.shape
    return (
        matrix.reshape(rows // order, order, cols // order, order)
        .transpose(2, 0, 1, 3)
        .reshape(-1, order, order)
    )


def split_rows(matrix, order):
    rows, cols = matrix.shape
    return (
        matrix.reshape(rows // order, order, cols // order, order)
        .transpose(0, 2, 1, 3)
        .reshape(-1, order, order)
    )


def join_cols(blocks, row_blocks):
    count, order, _ = blocks.shape
    return (
        blocks.reshape(-1, row_blocks, order, order)
        .transpose(1, 2, 0, 3)
        .reshape(row_blocks * order, -1)
    )


def join_rows(blocks, col_blocks):
    count, order, _ = blocks.shape
    return (
        blocks.reshape(-1, col_blocks, order, order)
        .transpose(0, 2, 1, 3)
        .reshape(-1, col_blocks * order)
    )


def scatter_z(blocks):
    local, order, _ = blocks.shape
    count = high_size("dp")
    by_rows = to_half(blocks).reshape(local, count, order // count, order).swapaxes(0, 1)
    return scatter_high(by_rows, "dp")


def scatter_fc(blocks):
    local, order, _ = blocks.shape
    by_x = to_half(blocks).reshape(PAIR, local // PAIR, order, order)
    return scatter_z(scatter_low(by_x, "dp"))


def scatter_attn(blocks):
    count, order, _ = blocks.shape
    y_count = high_size("mp")
    local = count // (y_count * PAIR)
    by_core = to_half(blocks).reshape(y_count, PAIR, local, order, order).swapaxes(0, 1)
    kept = to_half(scatter_low(by_core, "mp")).reshape(
        y_count, PAIR, local // PAIR, order, order
    )
    first, second = halves(kept, 3)
    first = to_half(scatter_low(first.swapaxes(0, 1), "dp"))
    second = to_half(scatter_high(second, "mp"))
    first = scatter_high(first, "mp")
    second = scatter_low(second, "dp")
    return scatter_z(jnp.concatenate([first, second], axis=1))


def gather_z(rows):
    local, _, order = rows.shape
    return gather_high(to_half(rows), "dp").swapaxes(0, 1).reshape(local, -1, order)


def to_pair(pieces):
    local, piece, order = pieces.shape
    by_x = to_half(pieces).reshape(PAIR, local // PAIR, piece, order)
    low = low_index("dp")
    both = ordered([pick(by_x, low), swap_low(pick(by_x, 1 - low), "dp")], low)
    return both.swapaxes(0, 1).reshape(local // PAIR, PAIR * piece, order)


def from_pair(rows):
    n, local, piece, order = rows.shape
    by_x = to_half(rows).reshape(n, local, PAIR, piece // PAIR, order)
    low = low_index("dp")
    both = ordered([pick(by_x, low, 2), swap_low(pick(by_x, 1 - low, 2), "dp")], low)
    return both.swapaxes(0, 1).reshape(n, PAIR * local, piece // PAIR, order)


def shampoo_rows(grad_rows, left_root, right_root):
    grad_half = to_half(grad_rows)
    whole = gather_z(grad_half)
    rows = grad_rows.shape[1]
    cols = lax.dynamic_slice_in_dim(whole, high_index("dp") * rows, rows, 2)
    left_term = jnp.einsum("bij,bkj->bik", grad_half, whole, preferred_element_type=full)
    right_term = jnp.einsum("bji,bjk->bik", cols, whole, preferred_element_type=full)
    step = to_half(jnp.einsum("bij,bjk->bik", left_root, whole, preferred_element_type=full))
    step = jnp.einsum("bij,bjk->bik", step, right_root, preferred_element_type=full)
    squares = jnp.sum(step * step, axis=(1, 2))
    squares = gather_low(squares, "dp").reshape(-1)
    total = squares
    for k in range(1, high_size("dp")):
        total = total + shift_high(squares, "dp", k)
    sent = from_pair(jnp.stack([grad_rows, left_term, right_term, step]))
    return sent, total


def apply_step(weight, left_stat, right_stat, sent, square_total, step_rates):
    order = weight.shape[2]
    sent = sent.astype(full)
    update_scale = lax.rsqrt(square_total / (order * order) + 1e-06) * step_rates
    return (
        sent[0],
        0.95 * left_stat + 0.05 * sent[1],
        0.95 * right_stat + 0.05 * sent[2],
        weight - sent[3] * update_scale[:, None, None],
    )


def sum_all(values):
    values = values + swap_low(values, "mp")
    for axis in ("mp", "dp"):
        if axis == "dp":
            values = values + swap_low(values, "dp")
        base = values
        for k in range(1, high_size(axis)):
            values = values + shift_high(base, axis, k)
    return values


def body_plain(
    tokens,
    keep_mask,
    cotangent,
    w_attn,
    w_fc1,
    w_fc2,
    vectors,
    left_attn,
    right_attn,
    root_left_attn,
    root_right_attn,
    left_fc1,
    right_fc1,
    root_left_fc1,
    root_right_fc1,
    left_fc2,
    right_fc2,
    root_left_fc2,
    root_right_fc2,
):
    image_count, patch_count, width = tokens.shape
    row_count = image_count * patch_count
    order = w_attn.shape[2]
    row_blocks = width // order
    attn_used = gather_attn(w_attn)
    qkv_full = attn_used[:, : 3 * width]
    out_full = attn_used[:, 3 * width :]
    fc1_used = join_cols(gather_fc(w_fc1), row_blocks)
    fc2_used = join_rows(gather_fc(w_fc2), row_blocks)
    left_roots = [to_pair(v) for v in (root_left_attn, root_left_fc1, root_left_fc2)]
    right_roots = [gather_z(to_pair(v)) for v in (root_right_attn, root_right_fc1, root_right_fc2)]
    hidden_local = fc1_used.shape[1]
    flat = tokens.reshape(row_count, width).astype(full)
    keep_rows = keep_mask.reshape(row_count).astype(full)
    row_gate = jax.nn.sigmoid(jnp.sum(flat * vectors[8], axis=-1))
    row_scale = keep_rows * row_gate
    grad_output = cotangent.reshape(row_count, width).astype(full)
    grad_change = row_scale[:, None] * grad_output
    grad_feed = to_half(grad_change)
    slot = jnp.cumsum(keep_mask, axis=1) - 1
    chosen = (
        (slot[:, None, :] == lax.broadcasted_iota(jnp.int32, (1, SLOTS, 1), 1))
        & (keep_mask[:, None, :] > 0)
    ).astype(half)

    def compact(rows):
        rows = rows.reshape(image_count, patch_count, width)
        picked = jnp.einsum("bsr,brd->bsd", chosen, rows, preferred_element_type=full)
        return to_half(picked).reshape(image_count * SLOTS, width)

    def spread(rows):
        rows = rows.reshape(image_count, SLOTS, width)
        return jnp.einsum(
            "bsr,bsd->brd", chosen.astype(full), rows, precision=highest
        ).reshape(row_count, width)

    group_grads = gather_group(compact(grad_feed))
    normed, first_norm_back = jax.vjp(layer_norm, flat, vectors[0], vectors[1])
    normed_half = to_half(normed)
    qkv_bias = jnp.concatenate([vectors[4], jnp.zeros_like(vectors[4]), vectors[5]])
    mixed_half = to_half(dot32(normed_half, qkv_full) + qkv_bias)
    heads_view = mixed_half.reshape(image_count, patch_count, 3, HEADS, width // HEADS)
    queries = heads_view[:, :, 0]
    key_part = heads_view[:, :, 1]
    values = heads_view[:, :, 2]
    attended_half, probs = jax.vmap(attend)(queries, key_part, values, keep_mask)
    attended_flat = attended_half.reshape(row_count, width)
    branch = dot32(attended_flat, out_full) + vectors[6]
    middle = flat + branch
    normed_two, second_norm_back = jax.vjp(layer_norm, middle, vectors[2], vectors[3])
    group_rows = gather_group(compact(to_half(normed_two)))
    up_bias = vectors[9:].reshape(-1)
    offset = lax.axis_index("mp") * hidden_local
    local_bias = lax.dynamic_slice_in_dim(up_bias, offset, hidden_local)
    hidden = dot32(group_rows, fc1_used) + local_bias
    activated, gelu_back = jax.vjp(exact_gelu, hidden)
    activated = to_half(activated)
    grad_active = times_transpose(group_grads, fc2_used)
    grad_hidden = to_half(gelu_back(grad_active)[0])
    mlp_count = image_count * SLOTS
    grad_rows_back = scatter_group(to_half(times_transpose(grad_hidden, fc1_used)), mlp_count)
    feed = spread(scatter_group(to_half(dot32(activated, fc2_used)), mlp_count)) + vectors[7]
    change = branch + feed
    block_out = to_half(flat + row_scale[:, None] * change).reshape(tokens.shape)
    grad_logit = keep_rows * row_gate * (1.0 - row_gate) * jnp.sum(grad_output * change, axis=-1)
    fc1_rows = scatter_fc(split_cols(row_product(group_rows, grad_hidden), order))
    fc2_rows = scatter_fc(split_rows(row_product(activated, group_grads), order))
    up_part = jnp.sum(grad_hidden, axis=0, dtype=full)
    up_bias_grad = lax.dynamic_update_slice_in_dim(jnp.zeros_like(up_bias), up_part, offset, 0)
    sent_fc1, total_fc1 = shampoo_rows(fc1_rows, left_roots[1], right_roots[1])
    sent_fc2, total_fc2 = shampoo_rows(fc2_rows, left_roots[2], right_roots[2])

    grad_normed_two = spread(grad_rows_back)
    grad_middle, grad_gain_two, grad_shift_two = second_norm_back(grad_normed_two)
    grad_branch = to_half(grad_change + grad_middle)
    grad_attended = to_half(times_transpose(grad_branch, out_full))
    grad_out_full = row_product(attended_flat, grad_branch)
    grad_heads = jax.vmap(attend_back)(
        queries,
        key_part,
        values,
        probs,
        grad_attended.reshape(image_count, patch_count, HEADS, -1),
    )
    grad_mixed = to_half(grad_heads.reshape(row_count, 3 * width))
    grad_qkv_full = row_product(normed_half, grad_mixed)
    attn_rows = scatter_attn(
        split_cols(jnp.concatenate([grad_qkv_full, grad_out_full], axis=1), order)
    )
    sent_attn, total_attn = shampoo_rows(attn_rows, left_roots[0], right_roots[0])
    grad_normed = times_transpose(grad_mixed, qkv_full)
    grad_flat, grad_gain_one, grad_shift_one = first_norm_back(grad_normed)
    input_grad = (grad_output + grad_middle + grad_flat + grad_logit[:, None] * vectors[8]).reshape(
        tokens.shape
    )
    mixed_sums = jnp.sum(grad_mixed, axis=0, dtype=full)
    vector_rows = jnp.stack(
        [
            grad_gain_one,
            grad_shift_one,
            grad_gain_two,
            grad_shift_two,
            mixed_sums[:width],
            mixed_sums[2 * width :],
            jnp.sum(grad_branch, axis=0, dtype=full),
            jnp.sum(grad_feed, axis=0, dtype=full),
            jnp.sum(grad_logit[:, None] * flat, axis=0),
        ]
    )
    vector_part = jnp.concatenate([vector_rows, up_bias_grad.reshape(-1, width)], axis=0)
    vector_grad = sum_all(vector_part)

    attn_local = w_attn.shape[0]
    block_index = lax.axis_index("mp") * attn_local + lax.broadcasted_iota(
        jnp.int32, (attn_local,), 0
    )
    attn_rates = jnp.where(
        block_index // row_blocks < 3 * row_blocks, 0.5 * D ** (-0.5), 0.5 * (D // 16) ** (-0.5)
    )
    fc1_rates = jnp.full((w_fc1.shape[0],), 0.5 * D ** (-0.5), full)
    fc2_rates = jnp.full((w_fc2.shape[0],), 0.5 * FF ** (-0.5), full)
    grad_attn, new_left_attn, new_right_attn, new_attn = apply_step(
        w_attn, left_attn, right_attn, sent_attn, total_attn, attn_rates
    )
    grad_fc1, new_left_fc1, new_right_fc1, new_fc1 = apply_step(
        w_fc1, left_fc1, right_fc1, sent_fc1, total_fc1, fc1_rates
    )
    grad_fc2, new_left_fc2, new_right_fc2, new_fc2 = apply_step(
        w_fc2, left_fc2, right_fc2, sent_fc2, total_fc2, fc2_rates
    )
    vector_blocks = vector_grad.reshape(vector_grad.shape[0], -1, BLOCK_VEC)
    block_scale = lax.rsqrt(jnp.mean(vector_blocks * vector_blocks, axis=-1, keepdims=True) + 1e-06)
    new_vectors = vectors - 0.05 * (vector_blocks * block_scale).reshape(vectors.shape)
    return (
        block_out,
        input_grad,
        grad_attn,
        grad_fc1,
        grad_fc2,
        new_left_attn,
        new_right_attn,
        new_left_fc1,
        new_right_fc1,
        new_left_fc2,
        new_right_fc2,
        new_attn,
        new_fc1,
        new_fc2,
        to_half(new_attn),
        to_half(new_fc1),
        to_half(new_fc2),
        vector_grad,
        new_vectors,
    )


def normalized(values):
    centered = values - jnp.mean(values, axis=-1, keepdims=True)
    variance = jnp.mean(centered * centered, axis=-1, keepdims=True)
    scale = lax.rsqrt(variance + 1e-06)
    return centered * scale, scale


def norm_back(grad_hat, hat, scale):
    first = jnp.mean(grad_hat, axis=-1, keepdims=True)
    second = jnp.mean(grad_hat * hat, axis=-1, keepdims=True)
    return scale * (grad_hat - first - hat * second)


def col_sum(values):
    return jnp.sum(values, axis=0, keepdims=True)


def shape(dims, kind=half):
    return jax.ShapeDtypeStruct(dims, kind)


def local_call(kernel, args, outs, scratch=(), in_hbm=(), out_hbm=(), in_smem=(0,), mib=20, micros=0.05):
    def place_of(index, hbm, smem):
        if index in hbm:
            return pl.BlockSpec(memory_space=pltpu.HBM)
        if index in smem:
            return pl.BlockSpec(memory_space=pltpu.SMEM)
        return pl.BlockSpec(memory_space=pltpu.VMEM)

    return pl.pallas_call(
        kernel,
        out_shape=list(outs),
        in_specs=[place_of(i, in_hbm, in_smem) for i in range(len(args))],
        out_specs=[place_of(i, out_hbm, ()) for i in range(len(outs))],
        scratch_shapes=list(scratch),
        compiler_params=pltpu.CompilerParams(vmem_limit_bytes=mib * 2**20),
        cost_estimate=pl.CostEstimate(
            flops=int(micros * 1e9), bytes_accessed=int(micros * 1e6), transcendentals=0
        ),
    )(*args)


def gate_of(tokens, vec_ref):
    return jax.nn.sigmoid(jnp.sum(tokens * vec_ref[8:9, :], axis=-1, keepdims=True))


def keep_of(chosen):
    ones = jnp.ones((chosen.shape[0], 128), half)
    return row_product(chosen, ones)[:, :1]


def prepare_kernel(mask_ref, tok_ref, cot_ref, vec_ref, normed_ref, grad_ref, chosen_ref):
    rows = tok_ref.shape[0]
    tokens = tok_ref[...].astype(full)
    hat, _ = normalized(tokens)
    normed_ref[...] = to_half(hat * vec_ref[0:1, :] + vec_ref[1:2, :])
    mask = mask_ref[...].astype(full)
    upper = lax.broadcasted_iota(jnp.int32, (rows, rows), 0) <= lax.broadcasted_iota(
        jnp.int32, (rows, rows), 1
    )
    count = dot32(
        to_half(jnp.broadcast_to(mask, (16, rows))), jnp.where(upper, 1.0, 0.0).astype(half)
    )
    slot = count[0:1, :] - 1.0
    wanted = lax.broadcasted_iota(jnp.int32, (SLOTS, rows), 0).astype(full)
    chosen = jnp.where((slot == wanted) & (mask > 0.0), 1.0, 0.0).astype(half)
    chosen_ref[...] = chosen
    scale = keep_of(chosen) * gate_of(tokens, vec_ref)
    grad_feed = to_half(scale * cot_ref[...].astype(full))
    grad_ref[...] = to_half(dot32(chosen, grad_feed))


def head_parts(values):
    lane = lax.broadcasted_iota(jnp.int32, values.shape, 1)
    first = lane < values.shape[1] // 2
    zero = jnp.zeros_like(values)
    return jnp.where(first, values, zero), jnp.where(first, zero, values)


def copy_all(copies):
    for copy in copies:
        copy.start()
    for copy in copies:
        copy.wait()


def matrix_of(weights, kind, row_blocks):
    blocks = weights[kind * row_blocks : (kind + 1) * row_blocks]
    return blocks.reshape(row_blocks * blocks.shape[1], blocks.shape[2])


def forward_kernel(order, pieces, place_ref, *refs):
    piece_refs, refs = refs[: len(pieces)], refs[len(pieces) :]
    normed_ref, tok_ref, mask_ref, chosen_ref, vec_ref = refs[:5]
    rows_ref, qkv_ref, probs_ref, attended_ref, branch_ref, weights_hbm = refs[5:11]
    weights, probs_all, sems, out_sem, probs_sem = refs[11:]
    z, x, m = place_ref[0], place_ref[1], place_ref[2]
    piece = piece_refs[0].shape[2]
    width = normed_ref.shape[1]
    row_blocks = width // order
    copies = []
    for ref, (slots, dx, dm) in zip(piece_refs, pieces):
        for index, slot in enumerate(slots):
            row = pl.multiple_of(((z ^ slot) * PAIR + (x ^ dx)) * piece, 16)
            for col in range(row_blocks):
                target = weights.at[
                    pl.ds((m ^ dm) * row_blocks, row_blocks),
                    pl.ds(row, piece),
                    pl.ds(col * order, order),
                ]
                source = ref.at[index, pl.ds(col * row_blocks, row_blocks)]
                copies.append(pltpu.make_async_copy(source, target, sems.at[len(copies)]))
    copy_all(copies)
    keep_whole = pltpu.make_async_copy(weights, weights_hbm, out_sem)
    keep_whole.start()
    normed = normed_ref[...]
    for kind in range(3):
        matrix = matrix_of(weights, kind, row_blocks)
        for start in range(0, width, TILE):
            lanes = slice(start, start + TILE)
            part = dot32(normed, matrix[:, lanes])
            if kind != 1:
                bias_row = 4 if kind == 0 else 5
                part = part + vec_ref[bias_row : bias_row + 1, lanes]
            qkv_ref[:, kind * width + start : kind * width + start + TILE] = to_half(part)
    head = width // HEADS
    scale = jnp.asarray(head ** (-0.5), half)
    allowed = mask_ref[...] > 0
    slabs = width // (2 * head)
    together = 3
    for first in range(0, slabs, together):
        found = []
        for slab in range(first, first + together):
            lanes = slice(slab * 2 * head, (slab + 1) * 2 * head)
            queries = head_parts(qkv_ref[:, lanes] * scale)
            keys = qkv_ref[:, width + lanes.start : width + lanes.stop]
            for index in range(2):
                scores = times_transpose(queries[index], keys)
                found.append(jnp.where(allowed, scores, masked_score))
        found = [jnp.exp(v - jnp.max(v, axis=-1, keepdims=True)) for v in found]
        found = [v * (1.0 / jnp.sum(v, axis=-1, keepdims=True)) for v in found]
        for index, probs in enumerate(found):
            probs_all[2 * first + index] = probs
        for slab in range(first, first + together):
            lanes = slice(slab * 2 * head, (slab + 1) * 2 * head)
            values = head_parts(qkv_ref[:, 2 * width + lanes.start : 2 * width + lanes.stop])
            at = 2 * (slab - first)
            total = dot32(to_half(found[at]), values[0]) + dot32(to_half(found[at + 1]), values[1])
            attended_ref[:, lanes] = to_half(total)
    keep_probs = pltpu.make_async_copy(probs_all, probs_ref, probs_sem)
    keep_probs.start()
    attended = attended_ref[...]
    matrix = matrix_of(weights, 3, row_blocks)
    for start in range(0, width, TILE):
        lanes = slice(start, start + TILE)
        branch_ref[:, lanes] = dot32(attended, matrix[:, lanes]) + vec_ref[6:7, lanes]
    hat, _ = normalized(tok_ref[...].astype(full) + branch_ref[...])
    second = to_half(hat * vec_ref[2:3, :] + vec_ref[3:4, :])
    rows_ref[...] = to_half(dot32(chosen_ref[...], second))
    keep_whole.wait()
    keep_probs.wait()


def bias_row(m, values, count):
    row = lax.broadcasted_iota(jnp.int32, (count, values.shape[1]), 0)
    return jnp.where(row == m, values, 0.0)


def gelu_parts(values):
    cdf = 0.5 * (1.0 + lax.erf(values * 0.7071067811865476))
    density = jnp.exp(-0.5 * values * values) * 0.3989422804014327
    return values * cdf, cdf + values * density


def hidden_kernel(order, group, pieces, place_ref, *refs):
    piece_refs, refs = refs[: len(pieces)], refs[len(pieces) :]
    row_refs, refs = refs[:group], refs[group:]
    grad_refs, refs = refs[: group // PAIR], refs[group // PAIR :]
    vec_ref = refs[0]
    back_refs, refs = refs[1 : 1 + group], refs[1 + group :]
    rows_ref, grads_ref, active_ref, hidden_ref, down_hbm = refs[:5]
    up, down, sems, out_sem = refs[5:]
    z, x, m = place_ref[0], place_ref[1], place_ref[2]
    piece = piece_refs[0].shape[2]
    width = rows_ref.shape[1]
    row_blocks = width // order
    col_blocks = active_ref.shape[1] // order
    local = row_blocks * col_blocks
    bias = jnp.sum(bias_row(m, vec_ref[9:, :], vec_ref.shape[0] - 9), axis=0, keepdims=True)
    copies = []
    for ref, (slots, dx) in zip(piece_refs, pieces):
        for index, slot in enumerate(slots):
            row = pl.multiple_of(((z ^ slot) * PAIR + (x ^ dx)) * piece, 16)
            span = pl.ds(row, piece)
            for col in range(col_blocks):
                lanes = pl.ds(col * order, order)
                source = ref.at[index, pl.ds(col * row_blocks, row_blocks)]
                pairs = [(source, up.at[:, span, lanes])]
                for other in range(row_blocks):
                    source = ref.at[index, local + col * row_blocks + other]
                    pairs.append((source, down.at[col, span, pl.ds(other * order, order)]))
                for source, target in pairs:
                    copies.append(pltpu.make_async_copy(source, target, sems.at[len(copies)]))
    for copy in copies:
        copy.start()
    count = row_refs[0].shape[0]
    for index in range(group):
        rows_ref[index * count : (index + 1) * count, :] = row_refs[index][...]
        grads_ref[index * count : (index + 1) * count, :] = grad_refs[index // PAIR][index % PAIR]
    for copy in copies:
        copy.wait()
    keep_down = pltpu.make_async_copy(down, down_hbm, out_sem)
    keep_down.start()
    up_matrix = matrix_of(up, 0, row_blocks)
    down_matrix = matrix_of(down, 0, col_blocks)
    for start in range(0, active_ref.shape[1], TILE):
        lanes = slice(start, start + TILE)
        hidden = dot32(rows_ref[...], up_matrix[:, lanes]) + bias[:, lanes]
        active, slope = gelu_parts(hidden)
        active_ref[:, lanes] = to_half(active)
        grad = times_transpose(grads_ref[...], down_matrix[lanes, :])
        hidden_ref[:, lanes] = to_half(grad * slope)
    for start in range(0, width, TILE):
        lanes = slice(start, start + TILE)
        total = times_transpose(hidden_ref[...], up_matrix[lanes, :])
        for index in range(group):
            back_refs[index][:, lanes] = to_half(total[index * count : (index + 1) * count, :])
    keep_down.wait()


def share_blocks(place_ref, blocks, kept_ref, *sent_refs):
    own, order, _ = kept_ref.shape
    x = place_ref[1]
    kept_ref[...] = blocks[pl.ds(x * own, own)]
    at = 0
    for ref in sent_refs:
        stop = at + ref.shape[0]
        for block in range(at // order, -(-stop // order)):
            low, high = max(at, block * order), min(stop, (block + 1) * order)
            ref[low - at : high - at] = blocks[
                (1 - x) * own + block, low - block * order : high - block * order, :
            ]
        at = stop


def store_blocks(blocks, order, product, by_rows):
    rows, cols = product.shape[0] // order, product.shape[1] // order
    for row in range(rows):
        for col in range(cols):
            at = row * cols + col if by_rows else col * rows + row
            blocks[at] = to_half(
                product[row * order : (row + 1) * order, col * order : (col + 1) * order]
            )


def up_grads_kernel(order, place_ref, rows_ref, hidden_ref, kept_ref, sent_ref, blocks):
    store_blocks(blocks, order, row_product(rows_ref[...], hidden_ref[...]), False)
    share_blocks(place_ref, blocks, kept_ref, sent_ref)


def down_grads_kernel(order, group, place_ref, grads_ref, active_ref, hidden_ref, down_ref, *refs):
    feed_kept_ref, feed_sent_ref, kept_ref, first_ref, second_ref, bias_ref, blocks = refs
    count = grads_ref.shape[0] // group
    down_matrix = matrix_of(down_ref, 0, down_ref.shape[0])
    for start in range(0, down_matrix.shape[1], TILE):
        lanes = slice(start, start + TILE)
        total = dot32(active_ref[...], down_matrix[:, lanes])
        for index in range(group):
            target = (feed_kept_ref, feed_sent_ref)[index % PAIR]
            target[index // PAIR, :, lanes] = to_half(total[index * count : (index + 1) * count, :])
    store_blocks(blocks, order, row_product(active_ref[...], grads_ref[...]), True)
    share_blocks(place_ref, blocks, kept_ref, first_ref, second_ref)
    bias_ref[...] = col_sum(hidden_ref[...].astype(full))


def backward_kernel(order, group, place_ref, *refs):
    back_refs, refs = refs[:group], refs[group:]
    chosen_ref, tok_ref, cot_ref, branch_ref, vec_ref = refs[:5]
    qkv_ref, probs_ref, attended_ref, normed_ref, weights_hbm = refs[5:10]
    kept_ref, sent_ref, mixed_ref, middle_ref, sums_ref = refs[10:15]
    weights, left, right, grad_attended, probs_all, sem, probs_sem = refs[15:]
    width = tok_ref.shape[1]
    row_blocks = width // order
    fetch = pltpu.make_async_copy(
        weights_hbm.at[pl.ds(3 * row_blocks, row_blocks)], weights, sem
    )
    fetch.start()
    fetch_probs = pltpu.make_async_copy(probs_ref, probs_all, probs_sem)
    fetch_probs.start()
    chosen = chosen_ref[...]
    arrived = back_refs[0][...].astype(full)
    for ref in back_refs[1:]:
        arrived = arrived + ref[...].astype(full)
    high = to_half(arrived)
    low = to_half(arrived - high.astype(full))
    grad_second = row_product(chosen, high) + row_product(chosen, low)
    tokens = tok_ref[...].astype(full)
    hat, scale = normalized(tokens + branch_ref[...])
    grad_middle = norm_back(grad_second * vec_ref[2:3, :], hat, scale)
    middle_ref[...] = grad_middle
    change = keep_of(chosen) * gate_of(tokens, vec_ref) * cot_ref[...].astype(full)
    grad_branch = to_half(change + grad_middle)
    sums_ref[0:1, :] = col_sum(grad_second * hat)
    sums_ref[1:2, :] = col_sum(grad_second)
    sums_ref[2:3, :] = col_sum(grad_branch.astype(full))
    sums_ref[3:4, :] = col_sum(to_half(change).astype(full))
    left[0] = normed_ref[...]
    left[1] = attended_ref[...]
    right[3] = grad_branch
    fetch.wait()
    matrix = matrix_of(weights, 0, row_blocks)
    for start in range(0, width, TILE):
        lanes = slice(start, start + TILE)
        grad_attended[:, lanes] = to_half(times_transpose(grad_branch, matrix[lanes, :]))
    fetch_probs.wait()
    head = width // HEADS
    factor = head ** (-0.5)
    slabs = width // (2 * head)
    together = 3
    for first in range(0, slabs, together):
        grad_scores, probs_half = [], []
        for slab in range(first, first + together):
            start, stop = slab * 2 * head, (slab + 1) * 2 * head
            values = qkv_ref[:, 2 * width + start : 2 * width + stop]
            for index, part in enumerate(head_parts(grad_attended[:, start:stop])):
                probs = probs_all[2 * slab + index]
                grad_probs = times_transpose(part, values)
                inner = jnp.sum(probs * grad_probs, axis=-1, keepdims=True)
                grad_scores.append(to_half(probs * (grad_probs - inner)))
                probs_half.append(to_half(probs))
        for slab in range(first, first + together):
            start, stop = slab * 2 * head, (slab + 1) * 2 * head
            queries = head_parts(qkv_ref[:, start:stop])
            keys = head_parts(qkv_ref[:, width + start : width + stop])
            grads = head_parts(grad_attended[:, start:stop])
            at = 2 * (slab - first)
            sums = [0.0] * 3
            for index in range(2):
                sums[0] = sums[0] + dot32(grad_scores[at + index], keys[index])
                sums[1] = sums[1] + row_product(grad_scores[at + index], queries[index])
                sums[2] = sums[2] + row_product(probs_half[at + index], grads[index])
            right[0, :, start:stop] = to_half(sums[0] * factor)
            right[1, :, start:stop] = to_half(sums[1] * factor)
            right[2, :, start:stop] = to_half(sums[2])
    for kind in range(3):
        mixed_ref[:, kind * width : (kind + 1) * width] = right[kind]
    core = place_ref[3]
    for high_part in range(kept_ref.shape[0]):
        for target, low_part in ((kept_ref, core), (sent_ref, 1 - core)):
            kind = high_part * PAIR + low_part
            product = row_product(left[kind // 3], right[kind])
            store_blocks(target.at[high_part], order, product, False)


def input_kernel(order, group, *refs):
    feed_refs, refs = refs[:group], refs[group:]
    mixed_ref, middle_ref, tok_ref, cot_ref, chosen_ref, vec_ref, branch_ref, weights_hbm = refs[:8]
    out_ref, grad_ref, sums_ref, weights, sem = refs[8:]
    width = tok_ref.shape[1]
    row_blocks = width // order
    fetch = pltpu.make_async_copy(weights_hbm.at[pl.ds(0, weights.shape[0])], weights, sem)
    fetch.start()
    patches = out_ref.shape[0]
    chosen = chosen_ref[...]
    tokens = tok_ref[...].astype(full)
    cotangent = cot_ref[...].astype(full)
    arrived = feed_refs[0][...].astype(full)
    for ref in feed_refs[1:]:
        arrived = arrived + ref[...].astype(full)
    high = to_half(arrived)
    low = to_half(arrived - high.astype(full))
    feed = row_product(chosen, high) + row_product(chosen, low) + vec_ref[7:8, :]
    change = branch_ref[...] + feed
    gate = gate_of(tokens, vec_ref)
    keep = keep_of(chosen)
    out_ref[...] = to_half(tokens + keep * gate * change)[:patches]
    logit = keep * gate * (1.0 - gate) * jnp.sum(cotangent * change, axis=-1, keepdims=True)
    base = cotangent + middle_ref[...] + logit * vec_ref[8:9, :]
    sums_ref[4:5, :] = col_sum(logit * tokens)
    sums_ref[2:3, :] = col_sum(mixed_ref[:, :width].astype(full))
    sums_ref[3:4, :] = col_sum(mixed_ref[:, 2 * width :].astype(full))
    hat, scale = normalized(tokens)
    fetch.wait()
    grad_normed = None
    for kind in range(3):
        part = times_transpose(
            mixed_ref[:, kind * width : (kind + 1) * width], matrix_of(weights, kind, row_blocks)
        )
        grad_normed = part if grad_normed is None else grad_normed + part
    sums_ref[0:1, :] = col_sum(grad_normed * hat)
    sums_ref[1:2, :] = col_sum(grad_normed)
    grad = base + norm_back(grad_normed * vec_ref[0:1, :], hat, scale)
    grad_ref[:, 0, :] = grad[:patches]


def core_sum_kernel(place_ref, kept_ref, came_ref, *out_refs):
    x, m = place_ref[1], place_ref[2]
    own = kept_ref.shape[1] // PAIR
    for index, out_ref in enumerate(out_refs):
        dy, dx = index // PAIR, index % PAIR
        high = (m // PAIR) ^ dy
        for block in range(own):
            at = (x ^ dx) * own + block
            out_ref[block] = to_half(
                kept_ref[high, at].astype(full) + came_ref[high, at].astype(full)
            )


def row_sum_kernel(groups, count, place_ref, *refs):
    ins, outs = refs[: groups * count], refs[groups * count :]
    rows = outs[0].shape[-2]
    near = len(outs) == 2
    slots = outs[0].shape[0] * 2 if near else len(outs)
    for slot in range(slots):
        out_ref = outs[slot % 2].at[slot // 2] if near else outs[slot]
        start = pl.multiple_of((place_ref[0] ^ slot) * rows, 16)
        at = 0
        for group in range(groups):
            parts = ins[group * count : (group + 1) * count]
            for block in range(parts[0].shape[0]):
                total = parts[0][block, pl.ds(start, rows), :].astype(full)
                for ref in parts[1:]:
                    total = total + ref[block, pl.ds(start, rows), :].astype(full)
                out_ref[at] = to_half(total)
                at += 1


def joined_sum_kernel(place_ref, kept_ref, first_ref, second_ref, near_ref, other_ref, came):
    order = came.shape[1]
    at = 0
    for ref in (first_ref, second_ref):
        stop = at + ref.shape[0]
        for block in range(at // order, -(-stop // order)):
            low, high = max(at, block * order), min(stop, (block + 1) * order)
            came[block, low - block * order : high - block * order, :] = ref[low - at : high - at]
        at = stop
    row_sum_kernel(1, 2, place_ref, kept_ref, came, near_ref, other_ref)


def line_blocks(z, refs, target, first=0):
    for slot, ref in enumerate(refs):
        rows = ref.shape[-2]
        start = pl.multiple_of((z ^ slot) * rows, 16)
        for block in range(target.shape[0]):
            target[block, pl.ds(start, rows), :] = ref[first + block]


def line_roots_kernel(place_ref, *refs):
    root_refs, out_ref = refs[:-1], refs[-1]
    for slot, ref in enumerate(root_refs):
        rows = ref.shape[1]
        for block in range(out_ref.shape[0]):
            for part in range(PAIR):
                start = (place_ref[0] ^ slot) * (PAIR * rows) + part * rows
                out_ref[block, pl.ds(pl.multiple_of(start, 16), rows), :] = ref[block * PAIR + part]


def step_parts(z, x, own, whole, step, terms, found, block, kept_ref, sent_ref):
    rows, order = own.shape
    mine = pl.multiple_of(z * rows, 16)
    half_rows = rows // PAIR
    terms[...] = row_product(whole, whole)
    found[0] = own.astype(full)
    found[1] = times_transpose(own, whole)
    found[2] = terms[pl.ds(mine, rows), :]
    found[3] = step
    for target, part in ((kept_ref, x), (sent_ref, 1 - x)):
        start = pl.multiple_of(part * half_rows, 16)
        for kind in range(4):
            target[kind, block] = to_half(found[kind, pl.ds(start, half_rows), :])


def whole_step_kernel(count, left_first, place_ref, *refs):
    grad_refs, refs = refs[:count], refs[count:]
    roots_ref, kept_ref, sent_ref, grads, terms, found, steps = refs
    z, x = place_ref[0], place_ref[1]
    blocks, rows, order = grad_refs[0].shape
    line_blocks(z, grad_refs, grads)
    mine = pl.multiple_of(z * rows, 16)
    for block in range(blocks):
        whole = grads[block]
        step = to_half(dot32(roots_ref[left_first + block], whole))
        step = dot32(step, roots_ref[block])
        mean = jnp.mean(jnp.mean(step * step, axis=1, keepdims=True), axis=0, keepdims=True)
        steps[...] = step * lax.rsqrt(mean + 1e-06)
        step = steps[pl.ds(mine, rows), :]
        step_parts(z, x, grad_refs[0][block], whole, step, terms, found, block, kept_ref, sent_ref)


def step_kernel(count, first, place_ref, *refs):
    grad_refs, refs = refs[:count], refs[count:]
    roots_ref, left_ref, kept_ref, sent_ref, square_ref, grads, terms, found = refs
    z, x = place_ref[0], place_ref[1]
    blocks, rows, order = grad_refs[0].shape
    line_blocks(z, grad_refs, grads)
    square_ref[...] = jnp.zeros_like(square_ref)
    for block in range(blocks):
        whole = grads[block]
        step = to_half(dot32(left_ref[first + block], whole))
        step = dot32(step, roots_ref[first + block])
        total = jnp.sum(jnp.sum(step * step, axis=1, keepdims=True), axis=0, keepdims=True)
        square_ref[block : block + 1, :] = jnp.broadcast_to(total, (1, 128))
        step_parts(z, x, grad_refs[0][block], whole, step, terms, found, block, kept_ref, sent_ref)
        total = jnp.broadcast_to(total, (16, order))
        terms_of = jnp.zeros((16, order), full)
        row = lax.broadcasted_iota(jnp.int32, (16, order), 0)
        for index in range(3):
            part = to_half(total).astype(full)
            terms_of = jnp.where(row == index, part, terms_of)
            total = total - part
        sent_ref[4, block, :16, :] = to_half(terms_of)
        sent_ref[4, block, 16:, :] = jnp.zeros((sent_ref.shape[2] - 16, order), half)


def last_sums_kernel(vec_ref, vec_came_ref, *refs):
    count = len(refs) // 2
    mine_refs, came_refs, out_ref = refs[:count], refs[count:-1], refs[-1]
    blocks = came_refs[0].shape[1]
    out_ref[...] = jnp.zeros_like(out_ref)
    out_ref[: vec_ref.shape[0], :] = vec_ref[...] + vec_came_ref[...]
    for matrix in range(count):
        for block in range(blocks):
            at = 16 + matrix * blocks + block
            out_ref[at : at + 1, :128] = mine_refs[matrix][block : block + 1, :]
            terms = came_refs[matrix][4, block, 0:16, 0:128].astype(full)
            at += count * blocks
            out_ref[at : at + 1, :128] = jnp.sum(terms, axis=0, keepdims=True)


def apply_stats(x, refs, sent_refs, out_refs):
    left_ref, right_ref = refs
    grad_ref, new_left_ref, new_right_ref = out_refs
    own = left_ref.shape[0] // PAIR
    for side, ref in enumerate(sent_refs):
        for block in range(own):
            at = (x ^ side) * own + block
            grad_ref[at] = ref[0, block].astype(full)
            new_left_ref[at] = 0.95 * left_ref[at] + 0.05 * ref[1, block].astype(full)
            new_right_ref[at] = 0.95 * right_ref[at] + 0.05 * ref[2, block].astype(full)


def apply_step_rows(order, rates, x, m, weight_ref, sent_refs, out_refs, total_ref=None, row=0):
    new_ref, half_ref = out_refs
    local = weight_ref.shape[0]
    own = local // PAIR
    for side, ref in enumerate(sent_refs):
        for block in range(own):
            at = (x ^ side) * own + block
            rate = jnp.where(m * local + at < rates[0], rates[1], rates[2])
            if total_ref is not None:
                index = row + side * 2 * own + block
                total = total_ref[index : index + 1, 0:1]
                rate = rate * lax.rsqrt(total / (order * order) + 1e-06)
            new = weight_ref[at] - rate * ref[3, block].astype(full)
            new_ref[at] = new
            half_ref[at] = to_half(new)


def apply_kernel(order, rates, place_ref, weight_ref, left_ref, right_ref, *refs):
    sent_refs, out_refs = refs[:2], refs[2:]
    x, m = place_ref[1], place_ref[2]
    apply_stats(x, (left_ref, right_ref), sent_refs, out_refs[:3])
    apply_step_rows(order, rates, x, m, weight_ref, sent_refs, out_refs[3:])


def stats_kernel(place_ref, left_ref, right_ref, *refs):
    apply_stats(place_ref[1], (left_ref, right_ref), refs[:2], refs[2:])


def last_kernel(order, rates, place_ref, *refs):
    up_weight, down_weight, left_ref, right_ref = refs[:4]
    up_sent, down_sent, total_ref, vec_ref = refs[4:6], refs[6:8], refs[8], refs[9]
    outs = refs[10:]
    x, m = place_ref[1], place_ref[2]
    own = up_weight.shape[0] // PAIR
    apply_step_rows(order, rates[0], x, m, up_weight, up_sent, outs[0:2], total_ref, 16)
    apply_step_rows(order, rates[1], x, m, down_weight, down_sent, outs[2:4], total_ref, 16 + own)
    apply_stats(x, (left_ref, right_ref), down_sent, outs[4:7])
    vector_step(vec_ref, total_ref, outs[7], outs[8])


def vector_part_kernel(place_ref, one_ref, two_ref, bias_ref, out_ref):
    out_ref[0:2, :] = one_ref[0:2, :]
    out_ref[2:4, :] = two_ref[0:2, :]
    out_ref[4:6, :] = one_ref[2:4, :]
    out_ref[6:8, :] = two_ref[2:4, :]
    out_ref[8:9, :] = one_ref[4:5, :]
    out_ref[9:, :] = bias_row(place_ref[2], bias_ref[...], out_ref.shape[0] - 9)


def vector_step(vec_ref, total_ref, grad_ref, new_ref):
    rows = vec_ref.shape[0]
    grad_ref[...] = total_ref[:rows, :]
    for start in range(0, vec_ref.shape[1], BLOCK_VEC):
        lanes = slice(start, start + BLOCK_VEC)
        block = total_ref[:rows, lanes]
        scale = lax.rsqrt(jnp.mean(block * block, axis=-1, keepdims=True) + 1e-06)
        new_ref[:, lanes] = vec_ref[:, lanes] - 0.05 * (block * scale)


def first_kernel(place_ref, *refs):
    ins, refs = refs[:9], refs[9:]
    attn_out, feed_out, kept_ref, sent_ref = refs[:4]
    held, sems = refs[4:]
    copies = [
        pltpu.make_async_copy(ref, held.at[index], sems.at[index])
        for index, ref in enumerate(ins)
    ]
    for copy in copies:
        copy.start()
    local, own = attn_out.shape[0], kept_ref.shape[1]
    x = place_ref[1]
    for index, copy in enumerate(copies):
        copy.wait()
        if index == 0:
            attn_out[...] = to_half(held[index])
        elif index < 3:
            feed_out[(index - 1) * local : index * local] = to_half(held[index])
        else:
            kept_ref[index - 3] = to_half(held[index, pl.ds(x * own, own)])
            sent_ref[index - 3] = to_half(held[index, pl.ds((1 - x) * own, own)])


def bundle_kernel(place_ref, kept_ref, came_ref, feed_ref, left_ref, bundle_ref):
    x = place_ref[1]
    kinds, own, piece, order = kept_ref.shape
    feed = feed_ref.shape[0]
    bundle_ref[:feed] = feed_ref[...]
    for index in range(kinds):
        for block in range(own):
            for side, ref in ((0, kept_ref), (1, came_ref)):
                value = ref[index, block]
                if index < 3:
                    start = pl.multiple_of((x ^ side) * piece, 16)
                    left_ref[index * own + block, pl.ds(start, piece), :] = value
                if index == 0 or index >= 3:
                    at = (index - 3 if index else 3) * own + block
                    bundle_ref[feed + at * PAIR + (x ^ side)] = value


def move(values, dp_mask, mp_mask):
    dp, mp = lax.axis_size("dp"), lax.axis_size("mp")
    if mp_mask == 0:
        return lax.ppermute(values, "dp", [(s, s ^ dp_mask) for s in range(dp)])
    if dp_mask == 0:
        return lax.ppermute(values, "mp", [(s, s ^ mp_mask) for s in range(mp)])
    mask = dp_mask * mp + mp_mask
    return lax.ppermute(values, ("dp", "mp"), [(s, s ^ mask) for s in range(dp * mp)])


def phase(*values):
    return lax.optimization_barrier(values)


def after(values, *others):
    return lax.optimization_barrier((values,) + others)[0]


def body_lines(
    tokens,
    keep_mask,
    cotangent,
    w_attn,
    w_fc1,
    w_fc2,
    vectors,
    left_attn,
    right_attn,
    root_left_attn,
    root_right_attn,
    left_fc1,
    right_fc1,
    root_left_fc1,
    root_right_fc1,
    left_fc2,
    right_fc2,
    root_left_fc2,
    root_right_fc2,
):
    _, patches, width = tokens.shape
    local, piece, order = w_attn.shape
    z_count, group = high_size("dp"), lax.axis_size("mp")
    row_blocks = width // order
    own = local // PAIR
    rows = patches
    line_rows = order // z_count
    total_rows = group * SLOTS
    hidden_width = local // row_blocks * order
    heads = (HEADS, rows, rows)
    others = range(1, group)
    lines = range(1, z_count)
    tok, cot, mask = tokens[0], cotangent[0], keep_mask
    line, member = lax.axis_index("dp"), lax.axis_index("mp")
    place = jnp.stack([line >> 1, line & 1, member, member & 1]).astype(jnp.int32)

    attn_half, feed_half, root_kept, root_sent = local_call(
        first_kernel,
        (
            place,
            *[
                pltpu.with_memory_space_constraint(value, pltpu.HBM)
                for value in (
                    w_attn,
                    w_fc1,
                    w_fc2,
                    root_left_attn,
                    root_left_fc1,
                    root_left_fc2,
                    root_right_attn,
                    root_right_fc1,
                    root_right_fc2,
                )
            ],
        ),
        (
            shape((local, piece, order)),
            shape((2 * local, piece, order)),
            shape((6, own, piece, order)),
            shape((6, own, piece, order)),
        ),
        scratch=(pltpu.VMEM((9, local, piece, order), full), pltpu.SemaphoreType.DMA((9,))),
        in_hbm=range(1, 10),
    )
    line_came = [move(attn_half, k * PAIR, 0) for k in lines]
    root_came = move(root_sent, 1, 0)
    line_came, root_came, attn_half, mask = phase(line_came, root_came, attn_half, mask)

    plane = [(dx, high * PAIR) for high in range(group // PAIR) for dx in range(PAIR)]
    feed_far = move(feed_half, 2 * PAIR, 0)
    left_roots, bundle = local_call(
        bundle_kernel,
        (place, root_kept, root_came, feed_half),
        (
            shape((3 * own, PAIR * piece, order)),
            shape((2 * local + 4 * own * PAIR, piece, order)),
        ),
    )
    bundle_near = move(bundle, PAIR, 0)
    stack = jnp.stack([attn_half, *line_came])
    found = [stack] + [move(stack, dx, dm) for dx, dm in plane[1:]]
    normed, grad_sent, chosen = local_call(
        prepare_kernel,
        (mask, tok, cot, vectors),
        (shape((rows, width)), shape((SLOTS, width)), shape((SLOTS, rows))),
        in_smem=(),
    )
    pieces, piece_info = [], []
    for (dx, dm), part in zip(plane, found):
        pieces += [part, move(part, 0, 1)]
        piece_info += [(range(z_count), dx, dm), (range(z_count), dx, dm + 1)]
    grad_came = move(grad_sent, 0, 1)
    feed_count = 2 * local
    feed_near = jnp.stack([feed_half, bundle_near[:feed_count]])
    roots, roots_near = bundle[feed_count:], bundle_near[feed_count:]
    half_roots = roots.shape[0] // 2
    roots_first, roots_second = roots[:half_roots], roots[half_roots:]

    feed_near_came = move(feed_near, 1, 0)
    feed_last = move(feed_far, PAIR, 0)
    roots_first_far = move(roots_first, 2 * PAIR, 0)
    pair = jnp.stack([grad_sent, grad_came])
    group_grads = [pair] + [move(pair, 0, dm) for dm in range(PAIR, group, PAIR)]
    count = len(pieces)
    rows_sent, qkv, probs, attended, branch, weights = local_call(
        lambda *refs: forward_kernel(order, piece_info, *refs),
        (place, *pieces, normed, tok, mask, chosen, vectors),
        (
            shape((SLOTS, width)),
            shape((rows, 3 * width)),
            shape(heads, full),
            shape((rows, width)),
            shape((rows, width), full),
            shape((group * row_blocks, order, width)),
        ),
        scratch=(
            pltpu.VMEM((group * row_blocks, order, width), half),
            pltpu.VMEM(heads, full),
            pltpu.SemaphoreType.DMA((count * z_count * row_blocks,)),
            pltpu.SemaphoreType.DMA(()),
            pltpu.SemaphoreType.DMA(()),
        ),
        in_hbm=range(1, 1 + count),
        out_hbm=(2, 5),
        micros=8,
    )
    rows_sent, group_grads, feed_last, roots_first_far = phase(
        rows_sent, group_grads, feed_last, roots_first_far
    )

    rows_y = move(rows_sent, 0, PAIR)
    group_rows = [rows_sent, move(rows_sent, 0, 1), rows_y, move(rows_y, 0, 1)]
    feed_far = jnp.stack([feed_far, feed_last])
    feed_far_came = move(feed_far, 1, 0)
    roots_second_far = move(roots_second, 2 * PAIR, 0)

    feed_pieces = [feed_near, feed_near_came, feed_far, feed_far_came]
    feed_info = [((0, 1), 0), ((0, 1), 1), ((2, 3), 0), ((2, 3), 1)]
    outs = local_call(
        lambda *refs: hidden_kernel(order, group, feed_info, *refs),
        (place, *feed_pieces, *group_rows, *group_grads, vectors),
        (shape((SLOTS, width)),) * group
        + (shape((total_rows, width)),) * 2
        + (shape((total_rows, hidden_width)),) * 2
        + (shape((local // row_blocks, order, width)),),
        scratch=(
            pltpu.VMEM((row_blocks, order, hidden_width), half),
            pltpu.VMEM((local // row_blocks, order, width), half),
            pltpu.SemaphoreType.DMA((PAIR * z_count * (local // row_blocks + local),)),
            pltpu.SemaphoreType.DMA(()),
        ),
        in_hbm=(1, 2, 3, 4),
        out_hbm=(group + 4,),
        micros=5,
    )
    back, (all_rows, all_grads, active, grad_hidden, down) = outs[:group], outs[group:]
    back, all_rows = phase(back, all_rows)

    back = [back[0]] + [move(back[k], 0, k) for k in others]
    roots_far = jnp.concatenate([roots_first_far, roots_second_far])
    roots_last = move(roots_far, PAIR, 0)
    all_roots = [roots, roots_near, roots_far, roots_last]
    up_kept, up_sent = local_call(
        lambda *refs: up_grads_kernel(order, *refs),
        (place, all_rows, grad_hidden),
        (shape((own, order, order)), shape((own * order, order))),
        scratch=(pltpu.VMEM((local, order, order), half),),
    )
    up_came = move(up_sent, 1, 0)
    first_rows = order + line_rows
    feed_kept, feed_sent, down_kept, down_first, down_second, bias_sums = local_call(
        lambda *refs: down_grads_kernel(order, group, *refs),
        (place, all_grads, active, grad_hidden, down),
        (shape((group // PAIR, SLOTS, width)),) * 2
        + (shape((own, order, order)),)
        + (shape((first_rows, order)), shape((own * order - first_rows, order)))
        + (shape((1, hidden_width), full),),
        scratch=(pltpu.VMEM((local, order, order), half),),
    )
    back, down_first, down_second, feed_sent, all_roots = phase(
        back, down_first, down_second, feed_sent, all_roots
    )

    (joined_roots,) = local_call(
        line_roots_kernel,
        (place, *all_roots),
        (shape((4 * own, order, order)),),
    )

    def rows_of(*groups):
        blocks = sum(parts[0].shape[0] for parts in groups)
        return local_call(
            lambda *refs: row_sum_kernel(len(groups), len(groups[0]), *refs),
            (place, *[part for parts in groups for part in parts]),
            (shape((blocks, line_rows, order)),) * z_count,
        )

    def pairs_of(*groups):
        blocks = sum(parts[0].shape[0] for parts in groups)
        return local_call(
            lambda *refs: row_sum_kernel(len(groups), len(groups[0]), *refs),
            (place, *[part for parts in groups for part in parts]),
            (shape((z_count // 2, blocks, line_rows, order)),) * 2,
        )

    def add_near(kept, came):
        return [
            to_half(kept[k].astype(full) + came[k].astype(full)) for k in range(z_count // 2)
        ]

    def total_of(parts):
        total = parts[0].astype(full)
        for part in parts[1:]:
            total = total + part.astype(full)
        return to_half(total)

    def step_of(parts, matrix):
        return local_call(
            lambda *refs: step_kernel(z_count, matrix * own, *refs),
            (place, *parts, joined_roots, left_roots),
            (
                shape((4, own, piece, order)),
                shape((5, own, piece, order)),
                shape((8, 128), full),
            ),
            scratch=(
                pltpu.VMEM((own, order, order), half),
                pltpu.VMEM((order, order), full),
                pltpu.VMEM((4, line_rows, order), full),
            ),
            )

    up_near_kept, up_near_sent = pairs_of((up_kept, up_came.reshape(own, order, order)))
    up_near = move(up_near_sent, PAIR, 0)
    down_first_came = move(down_first, 1, 0)
    feed_came = move(feed_sent, 0, 1)
    attn_kept, attn_sent, mixed, grad_middle, sums_two = local_call(
        lambda *refs: backward_kernel(order, group, *refs),
        (place, *back, chosen, tok, cot, branch, vectors, qkv, probs, attended, normed, weights),
        (
            shape((group // PAIR, local, order, order)),
            shape((group // PAIR, local, order, order)),
            shape((rows, 3 * width)),
            shape((rows, width), full),
            shape((4, width), full),
        ),
        scratch=(
            pltpu.VMEM((row_blocks, order, width), half),
            pltpu.VMEM((2, rows, width), half),
            pltpu.VMEM((4, rows, width), half),
            pltpu.VMEM((rows, width), half),
            pltpu.VMEM(heads, full),
            pltpu.SemaphoreType.DMA(()),
            pltpu.SemaphoreType.DMA(()),
        ),
        in_hbm=(1 + group + 6, 1 + group + 9),
        micros=3,
    )
    attn_sent, up_near, down_first_came, feed_came = phase(
        attn_sent, up_near, down_first_came, feed_came
    )

    attn_came = move(attn_sent, 0, 1)
    up_mine, up_other = add_near(up_near_kept, up_near)
    up_far = move(up_other, 2 * PAIR, 0)
    down_second_came = move(down_second, 1, 0)
    feed_pairs = [
        to_half(feed_kept[k].astype(full) + feed_came[k].astype(full))
        for k in range(group // PAIR)
    ]
    feed = [feed_pairs[0]] + [
        move(part, 0, (k + 1) * PAIR) for k, part in enumerate(feed_pairs[1:])
    ]
    core_parts = local_call(
        core_sum_kernel,
        (place, attn_kept, attn_came),
        (shape((own, order, order)),) * group,
    )
    core_parts, up_mine, down_second_came, feed = phase(
        core_parts, up_mine, down_second_came, feed
    )

    attn_came = [move(part, dx, dm) for (dx, dm), part in zip(plane[1:], core_parts[1:])]
    down_near_kept, down_near_sent = local_call(
        joined_sum_kernel,
        (place, down_kept, down_first_came, down_second_came),
        (shape((z_count // 2, own, line_rows, order)),) * 2,
        scratch=(pltpu.VMEM((own, order, order), half),),
    )
    down_near = move(down_near_sent, PAIR, 0)
    up_rows = total_of([up_mine, up_far])
    up_whole_far = move(up_rows, 2 * PAIR, 0)
    block_out, input_grad, sums_one = local_call(
        lambda *refs: input_kernel(order, group // PAIR, *refs),
        (*feed, mixed, grad_middle, tok, cot, chosen, vectors, branch, weights),
        (
            shape((patches, width)),
            shape((patches, 1, width), full),
            shape((5, width), full),
        ),
        scratch=(
            pltpu.VMEM((3 * row_blocks, order, width), half),
            pltpu.SemaphoreType.DMA(()),
        ),
        in_hbm=(group // PAIR + 7,),
        in_smem=(),
    )
    (vector_sum,) = local_call(
        vector_part_kernel,
        (place, sums_one, sums_two, bias_sums),
        (shape(vectors.shape, full),),
    )
    down_mine, down_other = add_near(down_near_kept, down_near)
    down_far = move(down_other, 2 * PAIR, 0)
    up_pair = jnp.stack([up_rows, up_whole_far])
    up_pair_came = move(up_pair, PAIR, 0)
    up_kept, up_sent, up_squares = step_of(
        [up_rows, up_pair_came[0], up_whole_far, up_pair_came[1]], 1
    )
    down_rows = total_of([down_mine, down_far])
    down_whole_far = move(down_rows, 2 * PAIR, 0)
    attn_came, down_rows, down_whole_far, up_sent, vector_sum = phase(
        attn_came, down_rows, down_whole_far, up_sent, vector_sum
    )

    attn_split = rows_of((core_parts[0], *attn_came))
    attn_split = [attn_split[0]] + [move(attn_split[k], k * PAIR, 0) for k in lines]
    down_pair = jnp.stack([down_rows, down_whole_far])
    down_pair_came = move(down_pair, PAIR, 0)
    up_found = move(up_sent, 1, 0)
    down_kept, down_sent, down_squares = step_of(
        [down_rows, down_pair_came[0], down_whole_far, down_pair_came[1]], 2
    )
    vector_sum = vector_sum + move(after(vector_sum, down_pair_came), 0, 1)
    attn_split, up_found, down_sent, vector_sum = phase(
        attn_split, up_found, down_sent, vector_sum
    )

    attn_rows = total_of(attn_split)
    attn_parts = [attn_rows] + [move(attn_rows, k * PAIR, 0) for k in lines]
    down_found = move(down_sent, 1, 0)
    for dm in range(PAIR, group, PAIR):
        vector_sum = vector_sum + move(vector_sum, 0, dm)
    vector_came = move(vector_sum, 1, 0)
    stat = shape(w_fc1.shape, full)
    stats_up = local_call(
        stats_kernel,
        (place, left_fc1, right_fc1, up_kept, up_found),
        (stat,) * 3,
    )
    attn_parts, down_found, vector_came, stats_up = phase(
        attn_parts, down_found, vector_came, stats_up
    )

    kept, sent = local_call(
        lambda *refs: whole_step_kernel(z_count, 3 * own, *refs),
        (place, *attn_parts, joined_roots),
        (shape((4, own, piece, order)),) * 2,
        scratch=(
            pltpu.VMEM((own, order, order), half),
            pltpu.VMEM((order, order), full),
            pltpu.VMEM((4, line_rows, order), full),
            pltpu.VMEM((order, order), full),
        ),
    )
    came = move(sent, 1, 0)
    (last_sums,) = local_call(
        last_sums_kernel,
        (after(vector_sum, sent), vector_came, up_squares, down_squares, up_found, down_found),
        (shape((24, width), full),),
        in_smem=(),
    )
    total = last_sums
    for k in lines:
        total = total + move(last_sums, k * PAIR, 0)

    attn_rates = (3 * row_blocks * row_blocks, 0.5 * D ** (-0.5), 0.5 * (D // 16) ** (-0.5))
    fc_rates = ((0, 0.0, 0.5 * D ** (-0.5)), (0, 0.0, 0.5 * FF ** (-0.5)))
    new_up, half_up, new_down, half_down, *stats_down, vector_grad, new_vectors = local_call(
        lambda *refs: last_kernel(order, fc_rates, *refs),
        (
            place,
            w_fc1,
            w_fc2,
            left_fc2,
            right_fc2,
            up_kept,
            up_found,
            down_kept,
            down_found,
            total,
            vectors,
        ),
        (stat, shape(w_fc1.shape)) * 2 + (stat,) * 3 + (shape(vectors.shape, full),) * 2,
    )
    done_attn = local_call(
        lambda *refs: apply_kernel(order, attn_rates, *refs),
        (place, w_attn, left_attn, right_attn, kept, came),
        (stat,) * 4 + (shape(w_attn.shape),),
    )
    done_fc1 = (*stats_up, new_up, half_up)
    done_fc2 = (*stats_down, new_down, half_down)
    return (
        block_out[None],
        input_grad.transpose(1, 0, 2),
        done_attn[0],
        done_fc1[0],
        done_fc2[0],
        *done_attn[1:3],
        *done_fc1[1:3],
        *done_fc2[1:3],
        done_attn[3],
        done_fc1[3],
        done_fc2[3],
        done_attn[4],
        done_fc1[4],
        done_fc2[4],
        vector_grad,
        new_vectors,
    )


def body(tokens, keep_mask, cotangent, w_attn, *rest):
    local, piece, _ = w_attn.shape
    group = lax.axis_size("mp")
    tiled = piece % 16 == 0 and tokens.shape[0] == 1 and local % (2 * PAIR) == 0
    tiled = tiled and group == 4 and high_size("dp") == 4
    chosen_body = body_lines if tiled else body_plain
    return chosen_body(tokens, keep_mask, cotangent, w_attn, *rest)


def solution(mesh):
    rows = P(("dp", "mp"), None, None)
    blocks = P("mp", "dp", None)
    return jax.shard_map(
        body,
        mesh=mesh,
        in_specs=(rows, P(("dp", "mp"), None), rows)
        + (blocks,) * 3
        + (P(),)
        + (blocks,) * 12,
        out_specs=(rows, rows) + (blocks,) * 15 + (P(), P()),
        check_vma=False,
    )
```
